32 devices in a mesh: groups: 2 (over y), wide: 16 (over z, x, core), narrow: 1.
Axes of the slice: x: 2, y: 2, z: 4, core: 2. Of those that a mesh axis runs over, the one named last changes fastest.
Arguments:
- pair: bfloat16 [256, 128, 128], P(('groups', 'wide'), 'narrow'), parts along dimension 0, may hold values from -6 to 6
- adjoint: bfloat16 [256, 128, 128], P(('groups', 'wide'), 'narrow'), parts along dimension 0, may hold values from -6 to 6
- mask: int32 [256], P('groups'), parts along dimension 0, may hold values 0 or 1
- chain: int32 [256], P('groups'), parts along dimension 0, may hold values from 0 to 3, never falling along the last dimension, each value on 1 to 64 neighbouring positions
- gain_in: float32 [128], replicated, may hold values from 0.1 to 1.9
- w_proj: bfloat16 [128, 512], replicated, may hold values from -0.5 to 0.5
- w_gate: bfloat16 [128, 128], replicated, may hold values from -0.5 to 0.5
- chain_bias: float32 [2, 128], replicated, may hold values from -4 to 4
- gain_out: float32 [128], replicated, may hold values from 0.1 to 1.9
- w_out: bfloat16 [128, 128], replicated, may hold values from -0.5 to 0.5
Outputs:
- output: bfloat16 [256, 128, 128], P(('groups', 'wide'), 'narrow'), parts along dimension 0
- d_pair: bfloat16 [256, 128, 128], P(('groups', 'wide'), 'narrow'), parts along dimension 0
- d_proj: float32 [256, 512], P('groups'), parts along dimension 0
- d_gate: float32 [256, 128], P('groups'), parts along dimension 0
The draws below stay inside these ranges and needn't reach their ends.
There are 2 independent parts, one for each index of `groups`. The reference program is written for one: setup_inputs(seed, part) draws one part's arguments, and reference() takes and returns one part's arrays. A program takes and returns all parts, laid end to end along the dimension named above; an argument that names none is the same for every part. Nothing has to cross between parts.
All inputs are finite; a program needn't handle non-finite values.
Results may differ from the reference program's by a relative error of at most 0.017.
Values may be sent and summed in bfloat16 or wider, within the bound.
No kernel may reach another device: no remote copies, remote signals or barrier semaphores. Data moves between devices by JAX's collectives and lax.ppermute only.
A program may use at most 64 MiB of HBM per device.

```python
import math
import jax
import jax.numpy as jnp
import numpy as np
from jax import lax

C = 128
H = 128
RESIDUES = 128


def plant(array, stream_key, least, largest):
    spot = [jax.random.randint(jax.random.fold_in(stream_key, axis), (), 0, length) for axis, length in enumerate(array.shape)]
    longest = array.shape.index(max(array.shape))
    next_to = spot[:longest] + [(spot[longest] + 1) % array.shape[longest]] + spot[longest + 1:]
    return array.at[tuple(spot)].set(least).at[tuple(next_to)].set(largest)


def block_levels(stream_key, dims, cuts, smallest, high):
    level, own = 1.0, jax.random.fold_in(stream_key, 6)
    for axis_at, shards_of in cuts:
        heights = jnp.exp(jax.random.uniform(jax.random.fold_in(own, axis_at), (shards_of,), jnp.float32, smallest / len(cuts), high / len(cuts)))
        level = level * jnp.repeat(heights, dims[axis_at] // shards_of).reshape([-1 if axis == axis_at else 1 for axis in range(len(dims))])
    return level


def length_profile(number_of, total, limit, lean):
    portions = [(1 << 20) // math.isqrt(grade ** lean) + 1 for grade in range(2, number_of + 1)]
    surplus, counts = total - limit - (number_of - 1), [1] * (number_of - 1)
    while surplus > 0:
        candidates = [i for i in range(number_of - 1) if counts[i] < limit]
        mass, budget = sum([portions[i] for i in candidates]), surplus
        for i in candidates:
            extra = min(limit - counts[i], max(1, budget * portions[i] // mass), surplus)
            counts[i] = counts[i] + extra
            surplus = surplus - extra
    return np.array([limit] + counts)


def ragged_sizes(rng, number_of, total, reach, slope):
    if number_of == 2:
        one = jax.random.randint(rng, (), max(1, total - reach), min(reach, total - 1) + 1)
        return jnp.stack([one, total - one])
    lengths = jnp.asarray(length_profile(number_of, total, reach, slope), jnp.int32)
    pairs = (number_of - 1) // 2
    giver, receiver = lengths[1:1 + 2 * pairs:2], lengths[2:2 + 2 * pairs:2]
    room = jnp.minimum(giver - 1, reach - receiver)
    moved = jax.random.randint(jax.random.fold_in(rng, 1), (pairs,), 0, 1 << 20) % (room + 1)
    lengths = lengths.at[1:1 + 2 * pairs:2].set(giver - moved).at[2:2 + 2 * pairs:2].set(receiver + moved)
    return lengths[jax.random.permutation(jax.random.fold_in(rng, 2), number_of)]


def bell_draw(key, shape, width, reach, shards=(), kind=jnp.bfloat16):
    level = block_levels(key, shape, shards, -0.22, 0.18) if shards else 1.0
    result = jax.random.normal(key, shape, jnp.float32) * width * level
    return jnp.minimum(jnp.maximum(result, -reach), reach).astype(kind)


def setup_inputs(seed: int = 0, part: int = 0) -> dict:
    arg_keys = jax.random.split(jax.random.key(seed), 11)
    part_splits = jax.random.split(jax.random.fold_in(arg_keys[10], part), 11)
    pair = bell_draw(part_splits[0], (RESIDUES, RESIDUES, C), 1.0, 6.0, ((0, 16),))
    adjoint = bell_draw(part_splits[1], (RESIDUES, RESIDUES, C), 1.0, 6.0, ((0, 16),))
    mask = plant((jax.random.randint(part_splits[2], (RESIDUES,), 0, 8) < 7).astype(jnp.int32), jax.random.fold_in(part_splits[2], 1), 0, 1)
    chain = jnp.searchsorted(jnp.cumsum(ragged_sizes(part_splits[3], 4, RESIDUES, RESIDUES // 2, 0)), jnp.arange(RESIDUES), side="right").astype(jnp.int32)
    gain_in = jnp.clip(1.0 + 0.18 * jax.random.normal(arg_keys[4], (C,), jnp.float32), 0.1, 1.9)
    w_proj = bell_draw(arg_keys[5], (C, 4 * H), C ** -0.5, 0.5)
    w_gate = bell_draw(arg_keys[6], (C, C), C ** -0.5, 0.5)
    chain_bias = bell_draw(arg_keys[7], (2, C), 1.0, 4.0, (), jnp.float32)
    gain_out = jnp.clip(1.0 + 0.18 * jax.random.normal(arg_keys[8], (H,), jnp.float32), 0.1, 1.9)
    w_out = bell_draw(arg_keys[9], (H, C), H ** -0.5, 0.5)
    return dict(pair=pair, adjoint=adjoint, mask=mask, chain=chain, gain_in=gain_in, w_proj=w_proj, w_gate=w_gate, chain_bias=chain_bias, gain_out=gain_out, w_out=w_out)


EPS = 1e-05

def normalize(values, gain):
    centre = values - lax.optimization_barrier(jnp.mean(values, -1, keepdims=True))
    rstd = lax.rsqrt(lax.optimization_barrier(jnp.mean(centre * centre, -1, keepdims=True)) + EPS)
    hat = centre * rstd
    return (hat * gain, hat, rstd)

def norm_back(scaled, hat, rstd):
    return rstd * (scaled - lax.optimization_barrier(jnp.mean(scaled, -1, keepdims=True)) - hat * lax.optimization_barrier(jnp.mean(scaled * hat, -1, keepdims=True)))

def reference(pair, adjoint, mask, chain, gain_in, w_proj, w_gate, chain_bias, gain_out, w_out):
    block = math.gcd(RESIDUES, 32)
    count = RESIDUES // block
    span = math.gcd(H, 8)
    mask_f = mask.astype(jnp.float32)
    pair_blocks = pair.reshape(count, block, RESIDUES, C)
    adj_blocks = adjoint.reshape(count, block, RESIDUES, C)
    mask_blocks = mask_f.reshape(count, block)
    chain_blocks = chain.reshape(count, block)
    starts = jnp.arange(count, dtype=jnp.int32) * block

    def embed(pair_rows, mask_rows):
        zn_f, z_hat, z_rstd = normalize(pair_rows.astype(jnp.float32), gain_in)
        zn = zn_f.astype(jnp.bfloat16)
        cell_mask = (mask_rows[:, None] * mask_f[None, :])[:, :, None]
        return (zn, z_hat, z_rstd, cell_mask)

    def first(items):
        pair_rows, mask_rows = items
        zn, z_hat, z_rstd, cell_mask = embed(pair_rows, mask_rows)
        proj = jnp.dot(zn, w_proj, preferred_element_type=jnp.float32)
        left = (cell_mask * jax.nn.sigmoid(proj[..., H:2 * H]) * proj[..., :H]).astype(jnp.bfloat16)
        right = (cell_mask * jax.nn.sigmoid(proj[..., 3 * H:]) * proj[..., 2 * H:3 * H]).astype(jnp.bfloat16)
        return (jnp.transpose(left, (2, 0, 1)), jnp.transpose(right, (2, 0, 1)))
    lefts, rights = lax.map(first, (pair_blocks, mask_blocks))
    left_t = jnp.transpose(lefts, (1, 0, 2, 3)).reshape(H, RESIDUES, RESIDUES)
    right_t = jnp.transpose(rights, (1, 0, 2, 3)).reshape(H, RESIDUES, RESIDUES)
    left_spans = left_t.reshape(H // span, span, RESIDUES, RESIDUES)
    right_spans = right_t.reshape(H // span, span, RESIDUES, RESIDUES)

    def triangle(items):
        left_part, right_part = items
        return jnp.einsum('hik,hjk->hij', left_part.astype(jnp.float32), right_part.astype(jnp.float32))
    mixed_t = lax.map(triangle, (left_spans, right_spans)).reshape(H, RESIDUES, RESIDUES)

    def second(items):
        pair_rows, adj_rows, mask_rows, chain_rows, start = items
        zn, z_hat, z_rstd, cell_mask = embed(pair_rows, mask_rows)
        mixed = jnp.transpose(lax.dynamic_slice_in_dim(mixed_t, start, block, 1), (1, 2, 0))
        xn_f, x_hat, x_rstd = normalize(mixed, gain_out)
        xn = xn_f.astype(jnp.bfloat16)
        proj_out = jnp.dot(xn, w_out, preferred_element_type=jnp.float32)
        same = (chain_rows[:, None] == chain[None, :])[:, :, None]
        logits = jnp.dot(zn, w_gate, preferred_element_type=jnp.float32) + jnp.where(same, chain_bias[1], chain_bias[0])
        gate = jax.nn.sigmoid(logits)
        output = (gate * proj_out).astype(jnp.bfloat16)
        adj = adj_rows.astype(jnp.float32)
        d_out = (adj * gate).astype(jnp.bfloat16)
        d_logit = (adj * proj_out * gate * (1.0 - gate)).astype(jnp.bfloat16)
        d_xn = jnp.dot(d_out, w_out.T, preferred_element_type=jnp.float32)
        d_mixed = norm_back(d_xn * gain_out, x_hat, x_rstd).astype(jnp.bfloat16)
        return (output, jnp.transpose(d_mixed, (2, 0, 1)), d_logit)
    outputs, d_mixeds, d_logits = lax.map(second, (pair_blocks, adj_blocks, mask_blocks, chain_blocks, starts))
    output = outputs.reshape(RESIDUES, RESIDUES, C)
    d_mixed_t = jnp.transpose(d_mixeds, (1, 0, 2, 3)).reshape(H // span, span, RESIDUES, RESIDUES)

    def third(items):
        grad_part, left_part, right_part = items
        grad_f = grad_part.astype(jnp.float32)
        d_left = jnp.einsum('hij,hjk->hik', grad_f, right_part.astype(jnp.float32))
        d_right = jnp.einsum('hij,hik->hjk', grad_f, left_part.astype(jnp.float32))
        return (d_left, d_right)
    d_lefts, d_rights = lax.map(third, (d_mixed_t, left_spans, right_spans))
    d_left_t = d_lefts.reshape(H, RESIDUES, RESIDUES)
    d_right_t = d_rights.reshape(H, RESIDUES, RESIDUES)

    def fourth(carry, items):
        pair_rows, mask_rows, d_logit, start = items
        zn, z_hat, z_rstd, cell_mask = embed(pair_rows, mask_rows)
        proj = jnp.dot(zn, w_proj, preferred_element_type=jnp.float32)
        a_lin = proj[..., :H]
        sig_a = jax.nn.sigmoid(proj[..., H:2 * H])
        b_lin = proj[..., 2 * H:3 * H]
        sig_b = jax.nn.sigmoid(proj[..., 3 * H:])
        d_left = jnp.transpose(lax.dynamic_slice_in_dim(d_left_t, start, block, 1), (1, 2, 0))
        d_right = jnp.transpose(lax.dynamic_slice_in_dim(d_right_t, start, block, 1), (1, 2, 0))
        d_cells = jnp.concatenate([d_left * cell_mask * sig_a, d_left * cell_mask * a_lin * sig_a * (1.0 - sig_a), d_right * cell_mask * sig_b, d_right * cell_mask * b_lin * sig_b * (1.0 - sig_b)], -1).astype(jnp.bfloat16)
        d_zn = jnp.dot(d_cells, w_proj.T, preferred_element_type=jnp.float32) + jnp.dot(d_logit, w_gate.T, preferred_element_type=jnp.float32)
        d_pair = norm_back(d_zn * gain_in, z_hat, z_rstd).astype(jnp.bfloat16)
        flat_z = zn.reshape(-1, C)
        proj_sum = carry[0] + jnp.dot(flat_z.T, d_cells.reshape(-1, 4 * H), preferred_element_type=jnp.float32)
        gate_sum = carry[1] + jnp.dot(flat_z.T, d_logit.reshape(-1, C), preferred_element_type=jnp.float32)
        return ((proj_sum, gate_sum), d_pair)
    init = (jnp.zeros((C, 4 * H), jnp.float32), jnp.zeros((C, C), jnp.float32))
    sums, d_pairs = lax.scan(fourth, init, (pair_blocks, mask_blocks, d_logits, starts))
    d_pair = d_pairs.reshape(RESIDUES, RESIDUES, C)
    return (output, d_pair, sums[0] / RESIDUES, sums[1] / RESIDUES)
```

```python
import jax
import jax.numpy as jnp
from jax import lax
from jax.sharding import PartitionSpec as P

EPS = 1e-05


def normalize(values, gain, axis):
    centre = values - jnp.mean(values, axis, keepdims=True)
    rstd = lax.rsqrt(jnp.mean(centre * centre, axis, keepdims=True) + EPS)
    hat = centre * rstd
    return (hat * gain, hat, rstd)


def norm_back(scaled, hat, rstd, axis):
    return rstd * (
        scaled
        - jnp.mean(scaled, axis, keepdims=True)
        - hat * jnp.mean(scaled * hat, axis, keepdims=True)
    )


def swap(blocks):
    return lax.all_to_all(blocks, ("wide", "narrow"), split_axis=0, concat_axis=0, tiled=True)


def gather_cells(blocks, n_wide, n_narrow):
    _, own, rows, cols = blocks.shape
    shaped = blocks.reshape(n_wide, n_narrow, own, rows, cols)
    return jnp.transpose(shaped, (2, 0, 3, 1, 4)).reshape(own, n_wide * rows, n_narrow * cols)


def split_cells(field, n_wide, n_narrow):
    own, rows, cols = field.shape
    shaped = field.reshape(own, n_wide, rows // n_wide, n_narrow, cols // n_narrow)
    moved = jnp.transpose(shaped, (1, 3, 0, 2, 4))
    return moved.reshape(n_wide * n_narrow, own, rows // n_wide, cols // n_narrow)


def per_device(pair, adjoint, mask, chain, gain_in, w_proj, w_gate, chain_bias, gain_out, w_out):
    rows, cols, width = pair.shape
    hidden = w_out.shape[0]
    n_wide = lax.axis_size("wide")
    n_narrow = lax.axis_size("narrow")
    residues = rows * n_wide
    devices = n_wide * n_narrow
    own = hidden // devices
    row_start = lax.axis_index("wide") * rows
    col_start = lax.axis_index("narrow") * cols
    mask_f = mask.astype(jnp.float32)
    row_mask = lax.dynamic_slice_in_dim(mask_f, row_start, rows, 0)
    col_mask = lax.dynamic_slice_in_dim(mask_f, col_start, cols, 0)
    cell_mask = (row_mask[:, None] * col_mask[None, :])[None]
    row_chain = lax.dynamic_slice_in_dim(chain, row_start, rows, 0)
    col_chain = lax.dynamic_slice_in_dim(chain, col_start, cols, 0)
    same = (row_chain[:, None] == col_chain[None, :])[:, :, None]
    zn_f, z_hat, z_rstd = normalize(pair.astype(jnp.float32), gain_in, -1)
    zn = zn_f.astype(jnp.bfloat16)
    proj_a = jnp.einsum(
        "ijc,ch->hij", zn, w_proj[:, : 2 * hidden], preferred_element_type=jnp.float32
    )
    proj_b = jnp.einsum(
        "ijc,ch->hij", zn, w_proj[:, 2 * hidden :], preferred_element_type=jnp.float32
    )
    a_lin = proj_a[:hidden]
    sig_a = jax.nn.sigmoid(proj_a[hidden:])
    b_lin = proj_b[:hidden]
    sig_b = jax.nn.sigmoid(proj_b[hidden:])
    left_t = (cell_mask * sig_a * a_lin).astype(jnp.bfloat16)
    right_t = (cell_mask * sig_b * b_lin).astype(jnp.bfloat16)
    pairs = jnp.concatenate(
        [left_t.reshape(devices, own, rows, cols), right_t.reshape(devices, own, rows, cols)], 1
    )
    pairs = gather_cells(swap(pairs), n_wide, n_narrow)
    left_c, right_c = pairs[:own], pairs[own:]
    mixed_c = jnp.einsum("hik,hjk->hij", left_c, right_c, preferred_element_type=jnp.float32)
    mixed_t = swap(split_cells(mixed_c.astype(jnp.bfloat16), n_wide, n_narrow))
    mixed_t = mixed_t.reshape(hidden, rows, cols).astype(jnp.float32)
    xn_f, x_hat, x_rstd = normalize(mixed_t, gain_out[:, None, None], 0)
    xn = xn_f.astype(jnp.bfloat16)
    proj_out = jnp.einsum("hij,hc->ijc", xn, w_out, preferred_element_type=jnp.float32)
    logits = jnp.dot(zn, w_gate, preferred_element_type=jnp.float32) + jnp.where(
        same, chain_bias[1], chain_bias[0]
    )
    gate = jax.nn.sigmoid(logits)
    output = (gate * proj_out).astype(jnp.bfloat16)
    adj = adjoint.astype(jnp.float32)
    d_out = (adj * gate).astype(jnp.bfloat16)
    d_logit = (adj * proj_out * gate * (1.0 - gate)).astype(jnp.bfloat16)
    d_xn = jnp.einsum("ijc,hc->hij", d_out, w_out, preferred_element_type=jnp.float32)
    d_mixed_t = norm_back(d_xn * gain_out[:, None, None], x_hat, x_rstd, 0).astype(jnp.bfloat16)
    d_mixed_c = gather_cells(swap(d_mixed_t.reshape(devices, own, rows, cols)), n_wide, n_narrow)
    d_left_c = jnp.einsum("hij,hjk->hik", d_mixed_c, right_c, preferred_element_type=jnp.float32)
    d_right_c = jnp.einsum("hij,hik->hjk", d_mixed_c, left_c, preferred_element_type=jnp.float32)
    back = jnp.concatenate([d_left_c.astype(jnp.bfloat16), d_right_c.astype(jnp.bfloat16)], 0)
    back = swap(split_cells(back, n_wide, n_narrow))
    d_left = back[:, :own].reshape(hidden, rows, cols).astype(jnp.float32)
    d_right = back[:, own:].reshape(hidden, rows, cols).astype(jnp.float32)
    d_cells_a = jnp.concatenate(
        [d_left * cell_mask * sig_a, d_left * cell_mask * a_lin * sig_a * (1.0 - sig_a)], 0
    ).astype(jnp.bfloat16)
    d_cells_b = jnp.concatenate(
        [d_right * cell_mask * sig_b, d_right * cell_mask * b_lin * sig_b * (1.0 - sig_b)], 0
    ).astype(jnp.bfloat16)
    d_zn = jnp.einsum(
        "hij,ch->ijc", d_cells_a, w_proj[:, : 2 * hidden], preferred_element_type=jnp.float32
    )
    d_zn = d_zn + jnp.einsum(
        "hij,ch->ijc", d_cells_b, w_proj[:, 2 * hidden :], preferred_element_type=jnp.float32
    )
    d_zn = d_zn + jnp.dot(d_logit, w_gate.T, preferred_element_type=jnp.float32)
    d_pair = norm_back(d_zn * gain_in, z_hat, z_rstd, -1).astype(jnp.bfloat16)
    proj_part = jnp.concatenate(
        [
            jnp.einsum("ijc,hij->ch", zn, d_cells_a, preferred_element_type=jnp.float32),
            jnp.einsum("ijc,hij->ch", zn, d_cells_b, preferred_element_type=jnp.float32),
        ],
        1,
    )
    flat_z = zn.reshape(-1, width)
    gate_part = jnp.dot(flat_z.T, d_logit.reshape(-1, width), preferred_element_type=jnp.float32)
    parts = jnp.concatenate([proj_part, gate_part], 1)
    chunk = width // devices
    mine = swap(parts.astype(jnp.bfloat16).reshape(devices, chunk, -1))
    mine = jnp.sum(mine.astype(jnp.float32), 0) / residues
    total = swap(jnp.broadcast_to(mine, (devices,) + mine.shape)).reshape(width, -1)
    return (output, d_pair, total[:, : 4 * hidden], total[:, 4 * hidden :])


def solution(mesh):
    placed = (
        P(("groups", "wide"), "narrow", None),
        P(("groups", "wide"), "narrow", None),
        P("groups"),
        P("groups"),
        P(),
        P(),
        P(),
        P(),
        P(),
        P(),
    )
    return jax.shard_map(
        per_device,
        mesh=mesh,
        in_specs=placed,
        out_specs=(
            P(("groups", "wide"), "narrow", None),
            P(("groups", "wide"), "narrow", None),
            P("groups", None),
            P("groups", None),
        ),
        check_vma=False,
    )
```

```python
import jax
import jax.numpy as jnp
from jax import lax
from jax.sharding import PartitionSpec as P

EPS = 1e-05


def normalize(values, gain, axis):
    centre = values - jnp.mean(values, axis, keepdims=True)
    rstd = lax.rsqrt(jnp.mean(centre * centre, axis, keepdims=True) + EPS)
    hat = centre * rstd
    return (hat * gain, hat, rstd)


def norm_back(scaled, hat, rstd, axis):
    return rstd * (
        scaled
        - jnp.mean(scaled, axis, keepdims=True)
        - hat * jnp.mean(scaled * hat, axis, keepdims=True)
    )


def swap(blocks):
    return lax.all_to_all(blocks, ("wide", "narrow"), split_axis=0, concat_axis=0, tiled=True)


def spread(block, devices):
    axes = ("wide", "narrow")
    if devices > 16:
        return swap(jnp.broadcast_to(block, (devices,) + block.shape))
    got = [block]
    for step in range(1, devices):
        got.append(lax.ppermute(block, axes, [(d, (d - step) % devices) for d in range(devices)]))
    double = jnp.concatenate([jnp.stack(got)] * 2, 0)
    start = devices - lax.axis_index(axes)
    return lax.dynamic_slice_in_dim(double, start, devices, 0)


def gather_cells(blocks, n_wide, n_narrow):
    _, own, rows, cols = blocks.shape
    shaped = blocks.reshape(n_wide, n_narrow, own, rows, cols)
    return jnp.transpose(shaped, (2, 0, 3, 1, 4)).reshape(own, n_wide * rows, n_narrow * cols)


def split_cells(field, n_wide, n_narrow):
    own, rows, cols = field.shape
    shaped = field.reshape(own, n_wide, rows // n_wide, n_narrow, cols // n_narrow)
    moved = jnp.transpose(shaped, (1, 3, 0, 2, 4))
    return moved.reshape(n_wide * n_narrow, own, rows // n_wide, cols // n_narrow)


def per_device(pair, adjoint, mask, chain, gain_in, w_proj, w_gate, chain_bias, gain_out, w_out):
    rows, cols, width = pair.shape
    hidden = w_out.shape[0]
    n_wide = lax.axis_size("wide")
    n_narrow = lax.axis_size("narrow")
    residues = rows * n_wide
    devices = n_wide * n_narrow
    own = hidden // devices
    row_start = lax.axis_index("wide") * rows
    col_start = lax.axis_index("narrow") * cols
    mask_f = mask.astype(jnp.float32)
    row_mask = lax.dynamic_slice_in_dim(mask_f, row_start, rows, 0)
    col_mask = lax.dynamic_slice_in_dim(mask_f, col_start, cols, 0)
    cell_mask = (row_mask[:, None] * col_mask[None, :])[None]
    row_chain = lax.dynamic_slice_in_dim(chain, row_start, rows, 0)
    col_chain = lax.dynamic_slice_in_dim(chain, col_start, cols, 0)
    same = (row_chain[:, None] == col_chain[None, :])[:, :, None]
    zn_f, z_hat, z_rstd = normalize(pair.astype(jnp.float32), gain_in, -1)
    zn = zn_f.astype(jnp.bfloat16)
    proj_a = jnp.einsum(
        "ijc,ch->hij", zn, w_proj[:, : 2 * hidden], preferred_element_type=jnp.float32
    )
    proj_b = jnp.einsum(
        "ijc,ch->hij", zn, w_proj[:, 2 * hidden :], preferred_element_type=jnp.float32
    )
    a_lin = proj_a[:hidden]
    sig_a = jax.nn.sigmoid(proj_a[hidden:])
    b_lin = proj_b[:hidden]
    sig_b = jax.nn.sigmoid(proj_b[hidden:])
    left_t = (cell_mask * sig_a * a_lin).astype(jnp.bfloat16)
    right_t = (cell_mask * sig_b * b_lin).astype(jnp.bfloat16)
    pairs = jnp.concatenate(
        [left_t.reshape(devices, own, rows, cols), right_t.reshape(devices, own, rows, cols)], 1
    )
    pairs = gather_cells(swap(pairs), n_wide, n_narrow)
    left_c, right_c = pairs[:own], pairs[own:]
    mixed_c = jnp.einsum("hik,hjk->hij", left_c, right_c, preferred_element_type=jnp.float32)
    mixed_t = swap(split_cells(mixed_c.astype(jnp.bfloat16), n_wide, n_narrow))
    mixed_t = mixed_t.reshape(hidden, rows, cols).astype(jnp.float32)
    xn_f, x_hat, x_rstd = normalize(mixed_t, gain_out[:, None, None], 0)
    xn = xn_f.astype(jnp.bfloat16)
    proj_out = jnp.einsum("hij,hc->ijc", xn, w_out, preferred_element_type=jnp.float32)
    logits = jnp.dot(zn, w_gate, preferred_element_type=jnp.float32) + jnp.where(
        same, chain_bias[1], chain_bias[0]
    )
    gate = jax.nn.sigmoid(logits)
    output = (gate * proj_out).astype(jnp.bfloat16)
    adj = adjoint.astype(jnp.float32)
    d_out = (adj * gate).astype(jnp.bfloat16)
    d_logit = (adj * proj_out * gate * (1.0 - gate)).astype(jnp.bfloat16)
    d_xn = jnp.einsum("ijc,hc->hij", d_out, w_out, preferred_element_type=jnp.float32)
    d_mixed_t = norm_back(d_xn * gain_out[:, None, None], x_hat, x_rstd, 0).astype(jnp.bfloat16)
    d_mixed_c = gather_cells(swap(d_mixed_t.reshape(devices, own, rows, cols)), n_wide, n_narrow)
    d_left_c = jnp.einsum("hij,hjk->hik", d_mixed_c, right_c, preferred_element_type=jnp.float32)
    d_right_c = jnp.einsum("hij,hik->hjk", d_mixed_c, left_c, preferred_element_type=jnp.float32)
    back = jnp.concatenate([d_left_c.astype(jnp.bfloat16), d_right_c.astype(jnp.bfloat16)], 0)
    back = swap(split_cells(back, n_wide, n_narrow))
    d_left = back[:, :own].reshape(hidden, rows, cols).astype(jnp.float32)
    d_right = back[:, own:].reshape(hidden, rows, cols).astype(jnp.float32)
    d_cells_a = jnp.concatenate(
        [d_left * cell_mask * sig_a, d_left * cell_mask * a_lin * sig_a * (1.0 - sig_a)], 0
    ).astype(jnp.bfloat16)
    d_cells_b = jnp.concatenate(
        [d_right * cell_mask * sig_b, d_right * cell_mask * b_lin * sig_b * (1.0 - sig_b)], 0
    ).astype(jnp.bfloat16)
    d_zn = jnp.einsum(
        "hij,ch->ijc", d_cells_a, w_proj[:, : 2 * hidden], preferred_element_type=jnp.float32
    )
    d_zn = d_zn + jnp.einsum(
        "hij,ch->ijc", d_cells_b, w_proj[:, 2 * hidden :], preferred_element_type=jnp.float32
    )
    d_zn = d_zn + jnp.dot(d_logit, w_gate.T, preferred_element_type=jnp.float32)
    d_pair = norm_back(d_zn * gain_in, z_hat, z_rstd, -1).astype(jnp.bfloat16)
    proj_part = jnp.concatenate(
        [
            jnp.einsum("ijc,hij->ch", zn, d_cells_a, preferred_element_type=jnp.float32),
            jnp.einsum("ijc,hij->ch", zn, d_cells_b, preferred_element_type=jnp.float32),
        ],
        1,
    )
    flat_z = zn.reshape(-1, width)
    gate_part = jnp.dot(flat_z.T, d_logit.reshape(-1, width), preferred_element_type=jnp.float32)
    parts = jnp.concatenate([proj_part, gate_part], 1)
    chunk = width // devices
    mine = swap(parts.astype(jnp.bfloat16).reshape(devices, chunk, -1))
    mine = jnp.sum(mine.astype(jnp.float32), 0) / residues
    total = spread(mine.astype(jnp.bfloat16), devices).reshape(width, -1).astype(jnp.float32)
    return (output, d_pair, total[:, : 4 * hidden], total[:, 4 * hidden :])


def solution(mesh):
    placed = (
        P(("groups", "wide"), "narrow", None),
        P(("groups", "wide"), "narrow", None),
        P("groups"),
        P("groups"),
        P(),
        P(),
        P(),
        P(),
        P(),
        P(),
    )
    return jax.shard_map(
        per_device,
        mesh=mesh,
        in_specs=placed,
        out_specs=(
            P(("groups", "wide"), "narrow", None),
            P(("groups", "wide"), "narrow", None),
            P("groups", None),
            P("groups", None),
        ),
        check_vma=False,
    )
```

```python
import jax
import jax.numpy as jnp
from jax import lax
from jax.sharding import PartitionSpec as P

EPS = 1e-05


def normalize(values, gain, axis):
    centre = values - jnp.mean(values, axis, keepdims=True)
    rstd = lax.rsqrt(jnp.mean(centre * centre, axis, keepdims=True) + EPS)
    hat = centre * rstd
    return (hat * gain, hat, rstd)


def norm_back(scaled, hat, rstd, axis):
    return rstd * (
        scaled
        - jnp.mean(scaled, axis, keepdims=True)
        - hat * jnp.mean(scaled * hat, axis, keepdims=True)
    )


def swap(blocks):
    return lax.all_to_all(blocks, ("wide", "narrow"), split_axis=0, concat_axis=0, tiled=True)


def gather_cells(blocks, n_wide, n_narrow):
    _, own, rows, cols = blocks.shape
    shaped = blocks.reshape(n_wide, n_narrow, own, rows, cols)
    return jnp.transpose(shaped, (2, 0, 3, 1, 4)).reshape(own, n_wide * rows, n_narrow * cols)


def split_cells(field, n_wide, n_narrow):
    own, rows, cols = field.shape
    shaped = field.reshape(own, n_wide, rows // n_wide, n_narrow, cols // n_narrow)
    moved = jnp.transpose(shaped, (1, 3, 0, 2, 4))
    return moved.reshape(n_wide * n_narrow, own, rows // n_wide, cols // n_narrow)


def own_gradient(pair_all, mask_f, gain_in, w_proj, d_left_c, d_right_c, hidden, own):
    width = pair_all.shape[-1]
    zn = normalize(pair_all.astype(jnp.float32), gain_in, -1)[0].astype(jnp.bfloat16)
    first = lax.axis_index("wide") * own
    weights = lax.dynamic_slice_in_dim(w_proj.reshape(width, 4, hidden), first, own, 2)
    proj = jnp.einsum(
        "ijc,cn->nij", zn, weights.reshape(width, 4 * own), preferred_element_type=jnp.float32
    )
    cell_mask = mask_f[:, None] * mask_f[None, :]
    sig_a = jax.nn.sigmoid(proj[own : 2 * own])
    sig_b = jax.nn.sigmoid(proj[3 * own :])
    d_cells = jnp.concatenate(
        [
            d_left_c * cell_mask * sig_a,
            d_left_c * cell_mask * proj[:own] * sig_a * (1.0 - sig_a),
            d_right_c * cell_mask * sig_b,
            d_right_c * cell_mask * proj[2 * own : 3 * own] * sig_b * (1.0 - sig_b),
        ],
        0,
    ).astype(jnp.bfloat16)
    return jnp.einsum("nij,ijc->nc", d_cells, zn, preferred_element_type=jnp.float32)


def per_device(pair, adjoint, mask, chain, gain_in, w_proj, w_gate, chain_bias, gain_out, w_out):
    rows, cols, width = pair.shape
    hidden = w_out.shape[0]
    n_wide = lax.axis_size("wide")
    n_narrow = lax.axis_size("narrow")
    residues = rows * n_wide
    devices = n_wide * n_narrow
    own = hidden // devices
    row_start = lax.axis_index("wide") * rows
    col_start = lax.axis_index("narrow") * cols
    mask_f = mask.astype(jnp.float32)
    row_mask = lax.dynamic_slice_in_dim(mask_f, row_start, rows, 0)
    col_mask = lax.dynamic_slice_in_dim(mask_f, col_start, cols, 0)
    cell_mask = (row_mask[:, None] * col_mask[None, :])[None]
    row_chain = lax.dynamic_slice_in_dim(chain, row_start, rows, 0)
    col_chain = lax.dynamic_slice_in_dim(chain, col_start, cols, 0)
    same = (row_chain[:, None] == col_chain[None, :])[:, :, None]
    whole = devices <= 16 and n_narrow == 1
    if whole:
        pair_all = lax.all_gather(pair, "wide", axis=0, tiled=True)
    zn_f, z_hat, z_rstd = normalize(pair.astype(jnp.float32), gain_in, -1)
    zn = zn_f.astype(jnp.bfloat16)
    proj_a = jnp.einsum(
        "ijc,ch->hij", zn, w_proj[:, : 2 * hidden], preferred_element_type=jnp.float32
    )
    proj_b = jnp.einsum(
        "ijc,ch->hij", zn, w_proj[:, 2 * hidden :], preferred_element_type=jnp.float32
    )
    a_lin = proj_a[:hidden]
    sig_a = jax.nn.sigmoid(proj_a[hidden:])
    b_lin = proj_b[:hidden]
    sig_b = jax.nn.sigmoid(proj_b[hidden:])
    left_t = (cell_mask * sig_a * a_lin).astype(jnp.bfloat16)
    right_t = (cell_mask * sig_b * b_lin).astype(jnp.bfloat16)
    pairs = jnp.concatenate(
        [left_t.reshape(devices, own, rows, cols), right_t.reshape(devices, own, rows, cols)], 1
    )
    pairs = gather_cells(swap(pairs), n_wide, n_narrow)
    left_c, right_c = pairs[:own], pairs[own:]
    mixed_c = jnp.einsum("hik,hjk->hij", left_c, right_c, preferred_element_type=jnp.float32)
    mixed_t = swap(split_cells(mixed_c.astype(jnp.bfloat16), n_wide, n_narrow))
    mixed_t = mixed_t.reshape(hidden, rows, cols).astype(jnp.float32)
    xn_f, x_hat, x_rstd = normalize(mixed_t, gain_out[:, None, None], 0)
    xn = xn_f.astype(jnp.bfloat16)
    proj_out = jnp.einsum("hij,hc->ijc", xn, w_out, preferred_element_type=jnp.float32)
    logits = jnp.dot(zn, w_gate, preferred_element_type=jnp.float32) + jnp.where(
        same, chain_bias[1], chain_bias[0]
    )
    gate = jax.nn.sigmoid(logits)
    output = (gate * proj_out).astype(jnp.bfloat16)
    adj = adjoint.astype(jnp.float32)
    d_out = (adj * gate).astype(jnp.bfloat16)
    d_logit = (adj * proj_out * gate * (1.0 - gate)).astype(jnp.bfloat16)
    d_xn = jnp.einsum("ijc,hc->hij", d_out, w_out, preferred_element_type=jnp.float32)
    d_mixed_t = norm_back(d_xn * gain_out[:, None, None], x_hat, x_rstd, 0).astype(jnp.bfloat16)
    flat_z = zn.reshape(-1, width)
    gate_part = jnp.dot(flat_z.T, d_logit.reshape(-1, width), preferred_element_type=jnp.float32)
    chunk = width // devices
    sent = d_mixed_t.reshape(devices, own, rows, cols)
    if whole:
        gate_rows = gate_part.astype(jnp.bfloat16).reshape(devices, chunk, width)
        sent = swap(jnp.concatenate([sent.reshape(devices, own * rows, cols), gate_rows], 1))
        gate_own = jnp.sum(sent[:, own * rows :].astype(jnp.float32), 0) / residues
        sent = sent[:, : own * rows].reshape(devices, own, rows, cols)
    else:
        sent = swap(sent)
    d_mixed_c = gather_cells(sent, n_wide, n_narrow)
    d_left_c = jnp.einsum("hij,hjk->hik", d_mixed_c, right_c, preferred_element_type=jnp.float32)
    d_right_c = jnp.einsum("hij,hik->hjk", d_mixed_c, left_c, preferred_element_type=jnp.float32)
    back = jnp.concatenate([d_left_c.astype(jnp.bfloat16), d_right_c.astype(jnp.bfloat16)], 0)
    back = split_cells(back, n_wide, n_narrow)
    if whole:
        proj_own = own_gradient(
            pair_all, mask_f, gain_in, w_proj, d_left_c, d_right_c, hidden, own
        ) / residues
        extra = jnp.concatenate([proj_own, gate_own], 0).astype(jnp.bfloat16)
        extra = jnp.broadcast_to(extra, (devices,) + extra.shape)
        back = swap(jnp.concatenate([back.reshape(devices, 2 * own * rows, cols), extra], 1))
        extra = back[:, 2 * own * rows :].astype(jnp.float32)
        back = back[:, : 2 * own * rows].reshape(devices, 2 * own, rows, cols)
    else:
        back = swap(back)
    d_left = back[:, :own].reshape(hidden, rows, cols).astype(jnp.float32)
    d_right = back[:, own:].reshape(hidden, rows, cols).astype(jnp.float32)
    d_cells_a = jnp.concatenate(
        [d_left * cell_mask * sig_a, d_left * cell_mask * a_lin * sig_a * (1.0 - sig_a)], 0
    ).astype(jnp.bfloat16)
    d_cells_b = jnp.concatenate(
        [d_right * cell_mask * sig_b, d_right * cell_mask * b_lin * sig_b * (1.0 - sig_b)], 0
    ).astype(jnp.bfloat16)
    d_zn = jnp.einsum(
        "hij,ch->ijc", d_cells_a, w_proj[:, : 2 * hidden], preferred_element_type=jnp.float32
    )
    d_zn = d_zn + jnp.einsum(
        "hij,ch->ijc", d_cells_b, w_proj[:, 2 * hidden :], preferred_element_type=jnp.float32
    )
    d_zn = d_zn + jnp.dot(d_logit, w_gate.T, preferred_element_type=jnp.float32)
    d_pair = norm_back(d_zn * gain_in, z_hat, z_rstd, -1).astype(jnp.bfloat16)
    if whole:
        d_proj = extra[:, : 4 * own].reshape(devices, 4, own, width)
        d_proj = jnp.transpose(d_proj, (3, 1, 0, 2)).reshape(width, 4 * hidden)
        return (output, d_pair, d_proj, extra[:, 4 * own :].reshape(width, width))
    proj_part = jnp.concatenate(
        [
            jnp.einsum("ijc,hij->ch", zn, d_cells_a, preferred_element_type=jnp.float32),
            jnp.einsum("ijc,hij->ch", zn, d_cells_b, preferred_element_type=jnp.float32),
        ],
        1,
    )
    parts = jnp.concatenate([proj_part, gate_part], 1)
    mine = swap(parts.astype(jnp.bfloat16).reshape(devices, chunk, -1))
    mine = jnp.sum(mine.astype(jnp.float32), 0) / residues
    total = swap(jnp.broadcast_to(mine, (devices,) + mine.shape)).reshape(width, -1)
    return (output, d_pair, total[:, : 4 * hidden], total[:, 4 * hidden :])


def solution(mesh):
    placed = (
        P(("groups", "wide"), "narrow", None),
        P(("groups", "wide"), "narrow", None),
        P("groups"),
        P("groups"),
        P(),
        P(),
        P(),
        P(),
        P(),
        P(),
    )
    return jax.shard_map(
        per_device,
        mesh=mesh,
        in_specs=placed,
        out_specs=(
            P(("groups", "wide"), "narrow", None),
            P(("groups", "wide"), "narrow", None),
            P("groups", None),
            P("groups", None),
        ),
        check_vma=False,
    )
```

```python
import jax
import jax.numpy as jnp
from jax import lax
from jax.sharding import PartitionSpec as P

EPS = 1e-05


def normalize(values, gain, axis):
    centre = values - jnp.mean(values, axis, keepdims=True)
    rstd = lax.rsqrt(jnp.mean(centre * centre, axis, keepdims=True) + EPS)
    hat = centre * rstd
    return (hat * gain, hat, rstd)


def norm_back(scaled, hat, rstd, axis):
    return rstd * (
        scaled
        - jnp.mean(scaled, axis, keepdims=True)
        - hat * jnp.mean(scaled * hat, axis, keepdims=True)
    )


def swap(blocks):
    return lax.all_to_all(blocks, ("wide", "narrow"), split_axis=0, concat_axis=0, tiled=True)


def spread(block, n_wide, n_narrow):
    near = 4
    if n_narrow > 1 or n_wide % near or n_wide > 16:
        copies = (n_wide * n_narrow,) + block.shape
        return swap(jnp.broadcast_to(block, copies))
    far = n_wide // near
    columns = [[f * near + n for f in range(far)] for n in range(near)]
    planes = [[f * near + n for n in range(near)] for f in range(far)]
    got = lax.all_to_all(
        jnp.broadcast_to(block, (far,) + block.shape),
        "wide", 0, 0, axis_index_groups=columns, tiled=True,
    )
    got = lax.all_to_all(
        jnp.broadcast_to(got, (near,) + got.shape),
        "wide", 0, 0, axis_index_groups=planes, tiled=True,
    )
    return jnp.swapaxes(got, 0, 1)


def gather_cells(blocks, n_wide, n_narrow):
    _, own, rows, cols = blocks.shape
    shaped = blocks.reshape(n_wide, n_narrow, own, rows, cols)
    return jnp.transpose(shaped, (2, 0, 3, 1, 4)).reshape(own, n_wide * rows, n_narrow * cols)


def split_cells(field, n_wide, n_narrow):
    own, rows, cols = field.shape
    shaped = field.reshape(own, n_wide, rows // n_wide, n_narrow, cols // n_narrow)
    moved = jnp.transpose(shaped, (1, 3, 0, 2, 4))
    return moved.reshape(n_wide * n_narrow, own, rows // n_wide, cols // n_narrow)


def per_device(pair, adjoint, mask, chain, gain_in, w_proj, w_gate, chain_bias, gain_out, w_out):
    rows, cols, width = pair.shape
    hidden = w_out.shape[0]
    n_wide = lax.axis_size("wide")
    n_narrow = lax.axis_size("narrow")
    residues = rows * n_wide
    devices = n_wide * n_narrow
    own = hidden // devices
    row_start = lax.axis_index("wide") * rows
    col_start = lax.axis_index("narrow") * cols
    mask_f = mask.astype(jnp.float32)
    row_mask = lax.dynamic_slice_in_dim(mask_f, row_start, rows, 0)
    col_mask = lax.dynamic_slice_in_dim(mask_f, col_start, cols, 0)
    cell_mask = (row_mask[:, None] * col_mask[None, :])[None]
    row_chain = lax.dynamic_slice_in_dim(chain, row_start, rows, 0)
    col_chain = lax.dynamic_slice_in_dim(chain, col_start, cols, 0)
    same = (row_chain[:, None] == col_chain[None, :])[:, :, None]
    zn_f, z_hat, z_rstd = normalize(pair.astype(jnp.float32), gain_in, -1)
    zn = zn_f.astype(jnp.bfloat16)
    proj_a = jnp.einsum(
        "ijc,ch->hij", zn, w_proj[:, : 2 * hidden], preferred_element_type=jnp.float32
    )
    proj_b = jnp.einsum(
        "ijc,ch->hij", zn, w_proj[:, 2 * hidden :], preferred_element_type=jnp.float32
    )
    a_lin = proj_a[:hidden]
    sig_a = jax.nn.sigmoid(proj_a[hidden:])
    b_lin = proj_b[:hidden]
    sig_b = jax.nn.sigmoid(proj_b[hidden:])
    left_t = (cell_mask * sig_a * a_lin).astype(jnp.bfloat16)
    right_t = (cell_mask * sig_b * b_lin).astype(jnp.bfloat16)
    pairs = jnp.concatenate(
        [left_t.reshape(devices, own, rows, cols), right_t.reshape(devices, own, rows, cols)], 1
    )
    pairs = gather_cells(swap(pairs), n_wide, n_narrow)
    left_c, right_c = pairs[:own], pairs[own:]
    mixed_c = jnp.einsum("hik,hjk->hij", left_c, right_c, preferred_element_type=jnp.float32)
    mixed_t = swap(split_cells(mixed_c.astype(jnp.bfloat16), n_wide, n_narrow))
    mixed_t = mixed_t.reshape(hidden, rows, cols).astype(jnp.float32)
    xn_f, x_hat, x_rstd = normalize(mixed_t, gain_out[:, None, None], 0)
    xn = xn_f.astype(jnp.bfloat16)
    proj_out = jnp.einsum("hij,hc->ijc", xn, w_out, preferred_element_type=jnp.float32)
    logits = jnp.dot(zn, w_gate, preferred_element_type=jnp.float32) + jnp.where(
        same, chain_bias[1], chain_bias[0]
    )
    gate = jax.nn.sigmoid(logits)
    output = (gate * proj_out).astype(jnp.bfloat16)
    adj = adjoint.astype(jnp.float32)
    d_out = (adj * gate).astype(jnp.bfloat16)
    d_logit = (adj * proj_out * gate * (1.0 - gate)).astype(jnp.bfloat16)
    d_xn = jnp.einsum("ijc,hc->hij", d_out, w_out, preferred_element_type=jnp.float32)
    d_mixed_t = norm_back(d_xn * gain_out[:, None, None], x_hat, x_rstd, 0).astype(jnp.bfloat16)
    d_mixed_c = gather_cells(swap(d_mixed_t.reshape(devices, own, rows, cols)), n_wide, n_narrow)
    d_left_c = jnp.einsum("hij,hjk->hik", d_mixed_c, right_c, preferred_element_type=jnp.float32)
    d_right_c = jnp.einsum("hij,hik->hjk", d_mixed_c, left_c, preferred_element_type=jnp.float32)
    back = jnp.concatenate([d_left_c.astype(jnp.bfloat16), d_right_c.astype(jnp.bfloat16)], 0)
    back = swap(split_cells(back, n_wide, n_narrow))
    d_left = back[:, :own].reshape(hidden, rows, cols).astype(jnp.float32)
    d_right = back[:, own:].reshape(hidden, rows, cols).astype(jnp.float32)
    d_cells_a = jnp.concatenate(
        [d_left * cell_mask * sig_a, d_left * cell_mask * a_lin * sig_a * (1.0 - sig_a)], 0
    ).astype(jnp.bfloat16)
    d_cells_b = jnp.concatenate(
        [d_right * cell_mask * sig_b, d_right * cell_mask * b_lin * sig_b * (1.0 - sig_b)], 0
    ).astype(jnp.bfloat16)
    d_zn = jnp.einsum(
        "hij,ch->ijc", d_cells_a, w_proj[:, : 2 * hidden], preferred_element_type=jnp.float32
    )
    d_zn = d_zn + jnp.einsum(
        "hij,ch->ijc", d_cells_b, w_proj[:, 2 * hidden :], preferred_element_type=jnp.float32
    )
    d_zn = d_zn + jnp.dot(d_logit, w_gate.T, preferred_element_type=jnp.float32)
    d_pair = norm_back(d_zn * gain_in, z_hat, z_rstd, -1).astype(jnp.bfloat16)
    proj_part = jnp.concatenate(
        [
            jnp.einsum("ijc,hij->ch", zn, d_cells_a, preferred_element_type=jnp.float32),
            jnp.einsum("ijc,hij->ch", zn, d_cells_b, preferred_element_type=jnp.float32),
        ],
        1,
    )
    flat_z = zn.reshape(-1, width)
    gate_part = jnp.dot(flat_z.T, d_logit.reshape(-1, width), preferred_element_type=jnp.float32)
    parts = jnp.concatenate([proj_part, gate_part], 1)
    chunk = width // devices
    mine = swap(parts.astype(jnp.bfloat16).reshape(devices, chunk, -1))
    mine = jnp.sum(mine.astype(jnp.float32), 0) / residues
    total = spread(mine.astype(jnp.bfloat16), n_wide, n_narrow).reshape(width, -1)
    total = total.astype(jnp.float32)
    return (output, d_pair, total[:, : 4 * hidden], total[:, 4 * hidden :])


def solution(mesh):
    placed = (
        P(("groups", "wide"), "narrow", None),
        P(("groups", "wide"), "narrow", None),
        P("groups"),
        P("groups"),
        P(),
        P(),
        P(),
        P(),
        P(),
        P(),
    )
    return jax.shard_map(
        per_device,
        mesh=mesh,
        in_specs=placed,
        out_specs=(
            P(("groups", "wide"), "narrow", None),
            P(("groups", "wide"), "narrow", None),
            P("groups", None),
            P("groups", None),
        ),
        check_vma=False,
    )
```

```python
import functools

import jax
import jax.numpy as jnp
from jax import lax
from jax.experimental import pallas as pl
from jax.experimental.pallas import tpu as pltpu
from jax.sharding import PartitionSpec as P

EPS = 1e-05


def normalize(values, gain, axis):
    centre = values - jnp.mean(values, axis, keepdims=True)
    rstd = lax.rsqrt(jnp.mean(centre * centre, axis, keepdims=True) + EPS)
    hat = centre * rstd
    return (hat * gain, hat, rstd)


def norm_back(scaled, hat, rstd, axis):
    return rstd * (
        scaled
        - jnp.mean(scaled, axis, keepdims=True)
        - hat * jnp.mean(scaled * hat, axis, keepdims=True)
    )


def swap(blocks):
    return lax.all_to_all(blocks, ("wide", "narrow"), split_axis=0, concat_axis=0, tiled=True)


def gather_cells(blocks, n_wide, n_narrow):
    _, own, rows, cols = blocks.shape
    shaped = blocks.reshape(n_wide, n_narrow, own, rows, cols)
    return jnp.transpose(shaped, (2, 0, 3, 1, 4)).reshape(own, n_wide * rows, n_narrow * cols)


def split_cells(field, n_wide, n_narrow):
    own, rows, cols = field.shape
    shaped = field.reshape(own, n_wide, rows // n_wide, n_narrow, cols // n_narrow)
    moved = jnp.transpose(shaped, (1, 3, 0, 2, 4))
    return moved.reshape(n_wide * n_narrow, own, rows // n_wide, cols // n_narrow)


BF = jnp.bfloat16
F32 = jnp.float32


def dot(a, b, over=((1,), (0,))):
    return lax.dot_general(a, b, (over, ((), ())), preferred_element_type=F32)


def column(row):
    return jnp.broadcast_to(row, (row.shape[1], row.shape[1])).T


def centred(x):
    centre = x - jnp.mean(x, 0, keepdims=True)
    rstd = lax.rsqrt(jnp.mean(centre * centre, 0, keepdims=True) + EPS)
    return centre * rstd, rstd


def back_t(scaled, hat, rstd):
    inner = hat * jnp.mean(scaled * hat, 0, keepdims=True)
    return rstd * (scaled - jnp.mean(scaled, 0, keepdims=True) - inner)


def two_rows(first, second, devices):
    own, cols = first.shape[0] // devices, first.shape[1]
    shape = (devices, own, cols)
    return jnp.concatenate([first.reshape(shape), second.reshape(shape)], 1).astype(BF)


def apart(block, devices):
    wide = block.astype(F32)
    own, cols = wide.shape[1] // 2, wide.shape[2]
    return [wide[:, at * own : (at + 1) * own].reshape(devices * own, cols) for at in range(2)]


def project_kernel(pair_ref, mask_ref, gain_ref, w_ref, sent_ref, zn_ref):
    devices, depth, _ = sent_ref.shape
    rows, cols, width = pair_ref.shape
    gain = column(gain_ref[...])
    weights = w_ref[...].astype(F32).T.astype(BF)
    hidden = weights.shape[0] // 4
    half = depth // 2
    for two in range(rows // 2):
        pieces = []
        for row in (2 * two, 2 * two + 1):
            hat, _ = centred(pair_ref[row].astype(F32).T)
            zn = (hat * gain).astype(BF)
            zn_ref[:, row * cols : (row + 1) * cols] = zn
            proj = dot(weights, zn)
            mask = mask_ref[row : row + 1, :]
            left = mask * jax.nn.sigmoid(proj[hidden : 2 * hidden]) * proj[:hidden]
            right = mask * jax.nn.sigmoid(proj[3 * hidden :]) * proj[2 * hidden : 3 * hidden]
            pieces.append((left, right))
        at = two * 16
        sent_ref[:, at : at + 16, :] = two_rows(pieces[0][0], pieces[1][0], devices)
        sent_ref[:, half + at : half + at + 16, :] = two_rows(pieces[0][1], pieces[1][1], devices)


def gate_kernel(
    zn_ref, adj_ref, mask_ref, same_ref, w_ref, w_gate_ref, bias_ref, gain_ref, w_out_ref,
    factor_ref, gate_ref, t_ref,
):
    rows, cols, width = adj_ref.shape
    weights = w_ref[...].astype(F32).T.astype(BF)
    hidden = weights.shape[0] // 4
    w_gate = w_gate_ref[...].astype(F32).T.astype(BF)
    across, within = column(bias_ref[0:1, :]), column(bias_ref[1:2, :])
    gain = column(gain_ref[...])
    for row in range(rows):
        lanes = slice(row * cols, (row + 1) * cols)
        zn = zn_ref[:, lanes]
        proj = dot(weights, zn)
        mask = mask_ref[row : row + 1, :]
        for side in range(2):
            lin = proj[2 * side * hidden : (2 * side + 1) * hidden]
            sig = jax.nn.sigmoid(proj[(2 * side + 1) * hidden : (2 * side + 2) * hidden])
            factor_ref[2 * side * hidden : (2 * side + 1) * hidden, lanes] = mask * sig
            factor_ref[(2 * side + 1) * hidden : (2 * side + 2) * hidden, lanes] = (
                mask * lin * sig * (1.0 - sig)
            )
        bias = jnp.where(same_ref[row : row + 1, :] > 0.5, within, across)
        gate = jax.nn.sigmoid(dot(w_gate, zn) + bias).T
        gate_ref[row] = gate
        d_out = (adj_ref[row].astype(F32) * gate).astype(BF)
        t_ref[:, lanes] = dot(w_out_ref[...], d_out, ((1,), (1,))) * gain


def mix_kernel(got_ref, sent_ref, left_ref, right_ref, left_s, right_s, out_s):
    devices, depth, cols = got_ref.shape
    own = left_ref.shape[0]
    half = depth // 2
    count = devices * half // own
    left_s[...] = got_ref[:, :half, :].astype(F32).reshape(devices * half, cols)
    right_s[...] = got_ref[:, half:, :].astype(F32).reshape(devices * half, cols)
    for h in range(own):
        left = left_s[pl.ds(h, count, stride=own), :].astype(BF)
        right = right_s[pl.ds(h, count, stride=own), :].astype(BF)
        left_ref[h] = left
        right_ref[h] = right
        out_s[pl.ds(h, count, stride=own), :] = dot(left, right, ((1,), (1,)))
    sent_ref[...] = out_s[...].reshape(devices, half, cols).astype(BF)


def norm_kernel(got_ref, t_ref, gain_ref, sent_ref, xn_ref):
    devices, depth, cols = got_ref.shape
    gain = column(gain_ref[...])
    for two in range(depth // 16):
        pieces = []
        for part, mixed in enumerate(apart(got_ref[:, two * 16 : two * 16 + 16, :], devices)):
            row = 2 * two + part
            lanes = slice(row * cols, (row + 1) * cols)
            hat, rstd = centred(mixed)
            xn_ref[:, lanes] = (hat * gain).astype(BF)
            pieces.append(back_t(t_ref[:, lanes], hat, rstd))
        sent_ref[:, two * 16 : two * 16 + 16, :] = two_rows(*pieces, devices)


def output_kernel(
    xn_ref, gate_ref, adj_ref, zn_ref, w_out_ref, output_ref, d_logit_ref, part_ref
):
    rows, cols, width = adj_ref.shape
    total = None
    for row in range(rows):
        lanes = slice(row * cols, (row + 1) * cols)
        xn = xn_ref[:, lanes].astype(F32).T.astype(BF)
        proj_out = dot(xn, w_out_ref[...])
        gate = gate_ref[row]
        output_ref[row] = (gate * proj_out).astype(BF)
        d_logit = (adj_ref[row].astype(F32) * proj_out * gate * (1.0 - gate)).astype(BF)
        d_logit_ref[row] = d_logit
        term = dot(zn_ref[:, lanes], d_logit)
        total = term if total is None else total + term
    part_ref[...] = total


def unmix_kernel(got_ref, left_ref, right_ref, sent_ref, in_s, left_s, right_s):
    devices, half, cols = got_ref.shape
    own = left_ref.shape[0]
    count = devices * half // own
    in_s[...] = got_ref[...].astype(F32).reshape(devices * half, cols)
    for h in range(own):
        grad = in_s[pl.ds(h, count, stride=own), :]
        left_s[pl.ds(h, count, stride=own), :] = dot(grad.astype(BF), right_ref[h])
        right_s[pl.ds(h, count, stride=own), :] = dot(grad.T.astype(BF), left_ref[h])
    sent_ref[:, :half, :] = left_s[...].reshape(devices, half, cols).astype(BF)
    sent_ref[:, half:, :] = right_s[...].reshape(devices, half, cols).astype(BF)


def cells_kernel(got_ref, factor_ref, zn_ref, gate_part_ref, cells_ref, part_ref):
    devices, depth, cols = got_ref.shape
    half = depth // 2
    hidden = factor_ref.shape[0] // 4
    for side in range(2):
        for two in range(half // 16):
            at = side * half + two * 16
            for part, grad in enumerate(apart(got_ref[:, at : at + 16, :], devices)):
                row = 2 * two + part
                lanes = slice(row * cols, (row + 1) * cols)
                for kind in (2 * side, 2 * side + 1):
                    place = slice(kind * hidden, (kind + 1) * hidden)
                    cells_ref[place, lanes] = (grad * factor_ref[place, lanes]).astype(BF)
    total = dot(zn_ref[...], cells_ref[...], ((1,), (1,)))
    part_ref[:, : 4 * hidden] = total.astype(BF)
    part_ref[:, 4 * hidden :] = gate_part_ref[...].astype(BF)


def pair_kernel(cells_ref, d_logit_ref, pair_ref, gain_ref, w_ref, w_gate_ref, d_pair_ref):
    rows, cols, width = pair_ref.shape
    gain = column(gain_ref[...])
    for row in range(rows):
        lanes = slice(row * cols, (row + 1) * cols)
        hat, rstd = centred(pair_ref[row].astype(F32).T)
        d_zn = dot(w_ref[...], cells_ref[:, lanes])
        d_zn = d_zn + dot(w_gate_ref[...], d_logit_ref[row], ((1,), (1,)))
        d_pair_ref[row] = back_t(d_zn * gain, hat, rstd).T.astype(BF)


def sum_kernel(residues, got_ref, sent_ref):
    total = jnp.sum(got_ref[...].astype(F32), 0) / residues
    sent_ref[...] = jnp.broadcast_to(total.astype(BF)[None], sent_ref.shape)


def call(kernel, outs, scratch=(), flops=0, name=None):
    spec = pl.BlockSpec(memory_space=pltpu.VMEM)

    def run(*args):
        moved = sum(a.size * a.dtype.itemsize for a in (*args, *outs))
        return pl.pallas_call(
            kernel,
            out_shape=list(outs),
            in_specs=[spec] * len(args),
            out_specs=[spec] * len(outs),
            scratch_shapes=list(scratch),
            compiler_params=pltpu.CompilerParams(vmem_limit_bytes=32 * 1024 * 1024),
            cost_estimate=pl.CostEstimate(
                flops=flops, bytes_accessed=moved, transcendentals=0
            ),
            name=name,
        )(*args)

    return run


def small_blocks(pair, adjoint, mask, chain, gain_in, w_proj, w_gate, chain_bias, gain_out, w_out):
    rows, cols, width = pair.shape
    hidden = w_out.shape[0]
    devices = lax.axis_size("wide")
    own = hidden // devices
    residues = rows * devices
    cells = rows * cols
    half = rows * own
    shape = jax.ShapeDtypeStruct
    start = lax.axis_index("wide") * rows
    mask_f = mask.astype(F32)
    row_mask = lax.dynamic_slice_in_dim(mask_f, start, rows, 0)
    row_chain = lax.dynamic_slice_in_dim(chain, start, rows, 0)
    cell_mask = row_mask[:, None] * mask_f[None, :]
    same = (row_chain[:, None] == chain[None, :]).astype(F32)
    gain_in, gain_out = gain_in[None], gain_out[None]
    sent, zn = call(
        project_kernel,
        [shape((devices, 2 * half, cols), BF), shape((width, cells), BF)],
        name="project",
    )(pair, cell_mask, gain_in, w_proj)
    got = swap(sent)
    factor, gate, t = call(
        gate_kernel,
        [shape((4 * hidden, cells), F32), shape((rows, cols, width), F32), shape((hidden, cells), F32)],
        flops=2 * 10**9,
        name="gate",
    )(zn, adjoint, cell_mask, same, w_proj, w_gate, chain_bias, gain_out, w_out)
    field = pltpu.VMEM((devices * half, cols), F32)
    channels = shape((own, residues, cols), BF)
    block = shape((devices, half, cols), BF)
    sent, left, right = call(mix_kernel, [block, channels, channels], [field] * 3, name="mix")(got)
    got = swap(sent)
    sent, xn = call(norm_kernel, [block, shape((hidden, cells), BF)], name="norm")(got, t, gain_out)
    got = swap(sent)
    output, d_logit, gate_part = call(
        output_kernel,
        [shape(pair.shape, BF), shape(pair.shape, BF), shape((width, width), F32)],
        flops=2 * 10**9,
        name="output",
    )(xn, gate, adjoint, zn, w_out)
    sent = call(
        unmix_kernel, [shape((devices, 2 * half, cols), BF)], [field] * 3, name="unmix"
    )(got, left, right)[0]
    got = swap(sent)
    d_cells, part = call(
        cells_kernel,
        [shape((4 * hidden, cells), BF), shape((width, 4 * hidden + width), BF)],
        name="cells",
    )(got, factor, zn, gate_part)
    got = swap(part.reshape(devices, width // devices, -1))
    d_pair = call(pair_kernel, [shape(pair.shape, BF)], flops=2 * 10**9, name="pair")(
        d_cells, d_logit, pair, gain_in, w_proj, w_gate
    )[0]
    sent = call(
        functools.partial(sum_kernel, residues), [shape(got.shape, BF)], name="sum"
    )(got)[0]
    total = swap(sent).reshape(width, -1).astype(F32)
    return (output, d_pair, total[:, : 4 * hidden], total[:, 4 * hidden :])


def per_device(pair, adjoint, mask, chain, gain_in, w_proj, w_gate, chain_bias, gain_out, w_out):
    rows, cols, width = pair.shape
    hidden = w_out.shape[0]
    n_wide = lax.axis_size("wide")
    n_narrow = lax.axis_size("narrow")
    if n_narrow == 1 and (rows, cols, width) == (8, 128, 128) and hidden == 8 * n_wide == 128:
        return small_blocks(
            pair, adjoint, mask, chain, gain_in, w_proj, w_gate, chain_bias, gain_out, w_out
        )
    residues = rows * n_wide
    devices = n_wide * n_narrow
    own = hidden // devices
    row_start = lax.axis_index("wide") * rows
    col_start = lax.axis_index("narrow") * cols
    mask_f = mask.astype(jnp.float32)
    row_mask = lax.dynamic_slice_in_dim(mask_f, row_start, rows, 0)
    col_mask = lax.dynamic_slice_in_dim(mask_f, col_start, cols, 0)
    cell_mask = (row_mask[:, None] * col_mask[None, :])[None]
    row_chain = lax.dynamic_slice_in_dim(chain, row_start, rows, 0)
    col_chain = lax.dynamic_slice_in_dim(chain, col_start, cols, 0)
    same = (row_chain[:, None] == col_chain[None, :])[:, :, None]
    zn_f, z_hat, z_rstd = normalize(pair.astype(jnp.float32), gain_in, -1)
    zn = zn_f.astype(jnp.bfloat16)
    proj_a = jnp.einsum(
        "ijc,ch->hij", zn, w_proj[:, : 2 * hidden], preferred_element_type=jnp.float32
    )
    proj_b = jnp.einsum(
        "ijc,ch->hij", zn, w_proj[:, 2 * hidden :], preferred_element_type=jnp.float32
    )
    a_lin = proj_a[:hidden]
    sig_a = jax.nn.sigmoid(proj_a[hidden:])
    b_lin = proj_b[:hidden]
    sig_b = jax.nn.sigmoid(proj_b[hidden:])
    left_t = (cell_mask * sig_a * a_lin).astype(jnp.bfloat16)
    right_t = (cell_mask * sig_b * b_lin).astype(jnp.bfloat16)
    pairs = jnp.concatenate(
        [left_t.reshape(devices, own, rows, cols), right_t.reshape(devices, own, rows, cols)], 1
    )
    pairs = gather_cells(swap(pairs), n_wide, n_narrow)
    left_c, right_c = pairs[:own], pairs[own:]
    mixed_c = jnp.einsum("hik,hjk->hij", left_c, right_c, preferred_element_type=jnp.float32)
    mixed_t = swap(split_cells(mixed_c.astype(jnp.bfloat16), n_wide, n_narrow))
    mixed_t = mixed_t.reshape(hidden, rows, cols).astype(jnp.float32)
    xn_f, x_hat, x_rstd = normalize(mixed_t, gain_out[:, None, None], 0)
    xn = xn_f.astype(jnp.bfloat16)
    proj_out = jnp.einsum("hij,hc->ijc", xn, w_out, preferred_element_type=jnp.float32)
    logits = jnp.dot(zn, w_gate, preferred_element_type=jnp.float32) + jnp.where(
        same, chain_bias[1], chain_bias[0]
    )
    gate = jax.nn.sigmoid(logits)
    output = (gate * proj_out).astype(jnp.bfloat16)
    adj = adjoint.astype(jnp.float32)
    d_out = (adj * gate).astype(jnp.bfloat16)
    d_logit = (adj * proj_out * gate * (1.0 - gate)).astype(jnp.bfloat16)
    d_xn = jnp.einsum("ijc,hc->hij", d_out, w_out, preferred_element_type=jnp.float32)
    d_mixed_t = norm_back(d_xn * gain_out[:, None, None], x_hat, x_rstd, 0).astype(jnp.bfloat16)
    d_mixed_c = gather_cells(swap(d_mixed_t.reshape(devices, own, rows, cols)), n_wide, n_narrow)
    d_left_c = jnp.einsum("hij,hjk->hik", d_mixed_c, right_c, preferred_element_type=jnp.float32)
    d_right_c = jnp.einsum("hij,hik->hjk", d_mixed_c, left_c, preferred_element_type=jnp.float32)
    back = jnp.concatenate([d_left_c.astype(jnp.bfloat16), d_right_c.astype(jnp.bfloat16)], 0)
    back = swap(split_cells(back, n_wide, n_narrow))
    d_left = back[:, :own].reshape(hidden, rows, cols).astype(jnp.float32)
    d_right = back[:, own:].reshape(hidden, rows, cols).astype(jnp.float32)
    d_cells_a = jnp.concatenate(
        [d_left * cell_mask * sig_a, d_left * cell_mask * a_lin * sig_a * (1.0 - sig_a)], 0
    ).astype(jnp.bfloat16)
    d_cells_b = jnp.concatenate(
        [d_right * cell_mask * sig_b, d_right * cell_mask * b_lin * sig_b * (1.0 - sig_b)], 0
    ).astype(jnp.bfloat16)
    d_zn = jnp.einsum(
        "hij,ch->ijc", d_cells_a, w_proj[:, : 2 * hidden], preferred_element_type=jnp.float32
    )
    d_zn = d_zn + jnp.einsum(
        "hij,ch->ijc", d_cells_b, w_proj[:, 2 * hidden :], preferred_element_type=jnp.float32
    )
    d_zn = d_zn + jnp.dot(d_logit, w_gate.T, preferred_element_type=jnp.float32)
    d_pair = norm_back(d_zn * gain_in, z_hat, z_rstd, -1).astype(jnp.bfloat16)
    proj_part = jnp.concatenate(
        [
            jnp.einsum("ijc,hij->ch", zn, d_cells_a, preferred_element_type=jnp.float32),
            jnp.einsum("ijc,hij->ch", zn, d_cells_b, preferred_element_type=jnp.float32),
        ],
        1,
    )
    flat_z = zn.reshape(-1, width)
    gate_part = jnp.dot(flat_z.T, d_logit.reshape(-1, width), preferred_element_type=jnp.float32)
    parts = jnp.concatenate([proj_part, gate_part], 1)
    chunk = width // devices
    mine = swap(parts.astype(jnp.bfloat16).reshape(devices, chunk, -1))
    mine = jnp.sum(mine.astype(jnp.float32), 0) / residues
    mine = mine.astype(jnp.bfloat16)
    total = swap(jnp.broadcast_to(mine, (devices,) + mine.shape)).reshape(width, -1)
    total = total.astype(jnp.float32)
    return (output, d_pair, total[:, : 4 * hidden], total[:, 4 * hidden :])


def solution(mesh):
    placed = (
        P(("groups", "wide"), "narrow", None),
        P(("groups", "wide"), "narrow", None),
        P("groups"),
        P("groups"),
        P(),
        P(),
        P(),
        P(),
        P(),
        P(),
    )
    return jax.shard_map(
        per_device,
        mesh=mesh,
        in_specs=placed,
        out_specs=(
            P(("groups", "wide"), "narrow", None),
            P(("groups", "wide"), "narrow", None),
            P("groups", None),
            P("groups", None),
        ),
        check_vma=False,
    )
```

```python
import functools

import jax
import jax.numpy as jnp
from jax import lax
from jax.experimental import pallas as pl
from jax.experimental.pallas import tpu as pltpu
from jax.sharding import PartitionSpec as P

EPS = 1e-05


def normalize(values, gain, axis):
    centre = values - jnp.mean(values, axis, keepdims=True)
    rstd = lax.rsqrt(jnp.mean(centre * centre, axis, keepdims=True) + EPS)
    hat = centre * rstd
    return (hat * gain, hat, rstd)


def norm_back(scaled, hat, rstd, axis):
    return rstd * (
        scaled
        - jnp.mean(scaled, axis, keepdims=True)
        - hat * jnp.mean(scaled * hat, axis, keepdims=True)
    )


def swap(blocks):
    return lax.all_to_all(blocks, ("wide", "narrow"), split_axis=0, concat_axis=0, tiled=True)


def gather_cells(blocks, n_wide, n_narrow):
    _, own, rows, cols = blocks.shape
    shaped = blocks.reshape(n_wide, n_narrow, own, rows, cols)
    return jnp.transpose(shaped, (2, 0, 3, 1, 4)).reshape(own, n_wide * rows, n_narrow * cols)


def split_cells(field, n_wide, n_narrow):
    own, rows, cols = field.shape
    shaped = field.reshape(own, n_wide, rows // n_wide, n_narrow, cols // n_narrow)
    moved = jnp.transpose(shaped, (1, 3, 0, 2, 4))
    return moved.reshape(n_wide * n_narrow, own, rows // n_wide, cols // n_narrow)


BF = jnp.bfloat16
F32 = jnp.float32


def dot(a, b, over=((1,), (0,))):
    return lax.dot_general(a, b, (over, ((), ())), preferred_element_type=F32)


def column(row):
    return jnp.broadcast_to(row, (row.shape[1], row.shape[1])).T


def centred(x):
    centre = x - jnp.mean(x, 0, keepdims=True)
    rstd = lax.rsqrt(jnp.mean(centre * centre, 0, keepdims=True) + EPS)
    return centre * rstd, rstd


def back_t(scaled, hat, rstd):
    inner = hat * jnp.mean(scaled * hat, 0, keepdims=True)
    return rstd * (scaled - jnp.mean(scaled, 0, keepdims=True) - inner)


def two_rows(first, second, devices):
    own, cols = first.shape[0] // devices, first.shape[1]
    shape = (devices, own, cols)
    return jnp.concatenate([first.reshape(shape), second.reshape(shape)], 1).astype(BF)


def apart(block, devices):
    wide = block.astype(F32)
    own, cols = wide.shape[1] // 2, wide.shape[2]
    return [wide[:, at * own : (at + 1) * own].reshape(devices * own, cols) for at in range(2)]


def project_kernel(
    pair_hbm, mask_hbm, gain_hbm, w_hbm, sent_ref, zn_ref, mask_ref,
    pair_ref, mask_v, mask_s, gain_ref, w_ref, sems, row_sems,
):
    devices, depth, _ = sent_ref.shape
    rows, cols, width = pair_ref.shape
    start = lax.axis_index("wide") * rows
    row_copies = [
        pltpu.make_async_copy(pair_hbm.at[row], pair_ref.at[row], row_sems.at[row])
        for row in range(rows)
    ]
    copies = [
        pltpu.make_async_copy(gain_hbm, gain_ref, sems.at[0]),
        pltpu.make_async_copy(w_hbm, w_ref, sems.at[1]),
        pltpu.make_async_copy(mask_hbm, mask_v, sems.at[2]),
        pltpu.make_async_copy(mask_hbm, mask_s, sems.at[3]),
    ]
    for copy in copies + row_copies:
        copy.start()
    for copy in copies:
        copy.wait()
    mask_f = mask_v[...].astype(F32)
    for row in range(rows):
        mask_ref[row : row + 1, :] = mask_f * mask_s[0, start + row].astype(F32)
    gain = column(gain_ref[...])
    weights = w_ref[...].astype(F32).T.astype(BF)
    hidden = weights.shape[0] // 4
    half = depth // 2
    for two in range(rows // 2):
        pieces = []
        for row in (2 * two, 2 * two + 1):
            row_copies[row].wait()
            hat, _ = centred(pair_ref[row].astype(F32).T)
            zn = (hat * gain).astype(BF)
            zn_ref[:, row * cols : (row + 1) * cols] = zn
            proj = dot(weights, zn)
            mask = mask_ref[row : row + 1, :]
            left = mask * jax.nn.sigmoid(proj[hidden : 2 * hidden]) * proj[:hidden]
            right = mask * jax.nn.sigmoid(proj[3 * hidden :]) * proj[2 * hidden : 3 * hidden]
            pieces.append((left, right))
        at = two * 16
        sent_ref[:, at : at + 16, :] = two_rows(pieces[0][0], pieces[1][0], devices)
        sent_ref[:, half + at : half + at + 16, :] = two_rows(pieces[0][1], pieces[1][1], devices)


def gate_kernel(
    zn_ref, adj_ref, mask_ref, same_ref, w_ref, w_gate_ref, bias_ref, gain_ref, w_out_ref,
    factor_ref, gate_ref, t_ref,
):
    rows, cols, width = adj_ref.shape
    weights = w_ref[...].astype(F32).T.astype(BF)
    hidden = weights.shape[0] // 4
    w_gate = w_gate_ref[...].astype(F32).T.astype(BF)
    across, within = column(bias_ref[0:1, :]), column(bias_ref[1:2, :])
    gain = column(gain_ref[...])
    for row in range(rows):
        lanes = slice(row * cols, (row + 1) * cols)
        zn = zn_ref[:, lanes]
        proj = dot(weights, zn)
        mask = mask_ref[row : row + 1, :]
        for side in range(2):
            lin = proj[2 * side * hidden : (2 * side + 1) * hidden]
            sig = jax.nn.sigmoid(proj[(2 * side + 1) * hidden : (2 * side + 2) * hidden])
            factor_ref[2 * side * hidden : (2 * side + 1) * hidden, lanes] = mask * sig
            factor_ref[(2 * side + 1) * hidden : (2 * side + 2) * hidden, lanes] = (
                mask * lin * sig * (1.0 - sig)
            )
        bias = jnp.where(same_ref[row : row + 1, :] > 0.5, within, across)
        gate = jax.nn.sigmoid(dot(w_gate, zn) + bias).T
        gate_ref[row] = gate
        d_out = (adj_ref[row].astype(F32) * gate).astype(BF)
        t_ref[:, lanes] = dot(w_out_ref[...], d_out, ((1,), (1,))) * gain


def mix_kernel(got_ref, sent_ref, left_ref, right_ref, left_s, right_s, out_s):
    devices, depth, cols = got_ref.shape
    own = left_ref.shape[0]
    half = depth // 2
    count = devices * half // own
    left_s[...] = got_ref[:, :half, :].astype(F32).reshape(devices * half, cols)
    right_s[...] = got_ref[:, half:, :].astype(F32).reshape(devices * half, cols)
    for h in range(own):
        left = left_s[pl.ds(h, count, stride=own), :].astype(BF)
        right = right_s[pl.ds(h, count, stride=own), :].astype(BF)
        left_ref[h] = left
        right_ref[h] = right
        out_s[pl.ds(h, count, stride=own), :] = dot(left, right, ((1,), (1,)))
    sent_ref[...] = out_s[...].reshape(devices, half, cols).astype(BF)


def norm_kernel(got_ref, t_ref, gain_ref, sent_ref, xn_ref):
    devices, depth, cols = got_ref.shape
    gain = column(gain_ref[...])
    for two in range(depth // 16):
        pieces = []
        for part, mixed in enumerate(apart(got_ref[:, two * 16 : two * 16 + 16, :], devices)):
            row = 2 * two + part
            lanes = slice(row * cols, (row + 1) * cols)
            hat, rstd = centred(mixed)
            xn_ref[:, lanes] = (hat * gain).astype(BF)
            pieces.append(back_t(t_ref[:, lanes], hat, rstd))
        sent_ref[:, two * 16 : two * 16 + 16, :] = two_rows(*pieces, devices)


def output_kernel(
    xn_ref, gate_ref, adj_ref, zn_ref, w_out_ref, output_ref, d_logit_ref, part_ref
):
    rows, cols, width = adj_ref.shape
    total = None
    for row in range(rows):
        lanes = slice(row * cols, (row + 1) * cols)
        xn = xn_ref[:, lanes].astype(F32).T.astype(BF)
        proj_out = dot(xn, w_out_ref[...])
        gate = gate_ref[row]
        output_ref[row] = (gate * proj_out).astype(BF)
        d_logit = (adj_ref[row].astype(F32) * proj_out * gate * (1.0 - gate)).astype(BF)
        d_logit_ref[row] = d_logit
        term = dot(zn_ref[:, lanes], d_logit)
        total = term if total is None else total + term
    part_ref[...] = total


def unmix_kernel(got_ref, left_ref, right_ref, sent_ref, in_s, left_s, right_s):
    devices, half, cols = got_ref.shape
    own = left_ref.shape[0]
    count = devices * half // own
    in_s[...] = got_ref[...].astype(F32).reshape(devices * half, cols)
    for h in range(own):
        grad = in_s[pl.ds(h, count, stride=own), :]
        left_s[pl.ds(h, count, stride=own), :] = dot(grad.astype(BF), right_ref[h])
        right_s[pl.ds(h, count, stride=own), :] = dot(grad.T.astype(BF), left_ref[h])
    sent_ref[:, :half, :] = left_s[...].reshape(devices, half, cols).astype(BF)
    sent_ref[:, half:, :] = right_s[...].reshape(devices, half, cols).astype(BF)


def cells_kernel(got_ref, factor_ref, zn_ref, gate_part_ref, cells_ref, part_ref):
    devices, depth, cols = got_ref.shape
    half = depth // 2
    hidden = factor_ref.shape[0] // 4
    for side in range(2):
        for two in range(half // 16):
            at = side * half + two * 16
            for part, grad in enumerate(apart(got_ref[:, at : at + 16, :], devices)):
                row = 2 * two + part
                lanes = slice(row * cols, (row + 1) * cols)
                for kind in (2 * side, 2 * side + 1):
                    place = slice(kind * hidden, (kind + 1) * hidden)
                    cells_ref[place, lanes] = (grad * factor_ref[place, lanes]).astype(BF)
    total = dot(zn_ref[...], cells_ref[...], ((1,), (1,)))
    part_ref[:, : 4 * hidden] = total.astype(BF)
    part_ref[:, 4 * hidden :] = gate_part_ref[...].astype(BF)


def pair_kernel(cells_ref, d_logit_ref, pair_ref, gain_ref, w_ref, w_gate_ref, d_pair_ref):
    rows, cols, width = pair_ref.shape
    gain = column(gain_ref[...])
    for row in range(rows):
        lanes = slice(row * cols, (row + 1) * cols)
        hat, rstd = centred(pair_ref[row].astype(F32).T)
        d_zn = dot(w_ref[...], cells_ref[:, lanes])
        d_zn = d_zn + dot(w_gate_ref[...], d_logit_ref[row], ((1,), (1,)))
        d_pair_ref[row] = back_t(d_zn * gain, hat, rstd).T.astype(BF)


def sum_kernel(residues, got_ref, sent_ref):
    total = jnp.sum(got_ref[...].astype(F32), 0) / residues
    sent_ref[...] = jnp.broadcast_to(total.astype(BF)[None], sent_ref.shape)


def finish_kernel(got_ref, proj_ref, gate_ref):
    devices, chunk, depth = got_ref.shape
    wide = proj_ref.shape[1]
    total = got_ref[...].astype(F32).reshape(devices * chunk, depth)
    proj_ref[...] = total[:, :wide]
    gate_ref[...] = total[:, wide:]


def call(kernel, outs, scratch=(), flops=0, name=None, space=pltpu.VMEM):
    spec = pl.BlockSpec(memory_space=pltpu.VMEM)

    def run(*args):
        moved = sum(a.size * a.dtype.itemsize for a in (*args, *outs))
        return pl.pallas_call(
            kernel,
            out_shape=list(outs),
            in_specs=[pl.BlockSpec(memory_space=space)] * len(args),
            out_specs=[spec] * len(outs),
            scratch_shapes=list(scratch),
            compiler_params=pltpu.CompilerParams(vmem_limit_bytes=12 * 1024 * 1024),
            cost_estimate=pl.CostEstimate(
                flops=flops, bytes_accessed=moved, transcendentals=0
            ),
            name=name,
        )(*args)

    return run


def small_blocks(pair, adjoint, mask, chain, gain_in, w_proj, w_gate, chain_bias, gain_out, w_out):
    rows, cols, width = pair.shape
    hidden = w_out.shape[0]
    devices = lax.axis_size("wide")
    own = hidden // devices
    residues = rows * devices
    cells = rows * cols
    half = rows * own
    shape = jax.ShapeDtypeStruct
    start = lax.axis_index("wide") * rows
    row_chain = lax.dynamic_slice_in_dim(chain, start, rows, 0)
    same = (row_chain[:, None] == chain[None, :]).astype(F32)
    gain_in, gain_out = gain_in[None], gain_out[None]
    sent, zn, cell_mask = call(
        project_kernel,
        [shape((devices, 2 * half, cols), BF), shape((width, cells), BF), shape((rows, cols), F32)],
        [
            pltpu.VMEM(pair.shape, BF),
            pltpu.VMEM((1, residues), jnp.int32),
            pltpu.SMEM((1, residues), jnp.int32),
            pltpu.VMEM(gain_in.shape, F32),
            pltpu.VMEM(w_proj.shape, BF),
            pltpu.SemaphoreType.DMA((4,)),
            pltpu.SemaphoreType.DMA((rows,)),
        ],
        name="project",
        space=pl.ANY,
    )(pair, mask[None], gain_in, w_proj)
    got = swap(sent)
    factor, gate, t = call(
        gate_kernel,
        [shape((4 * hidden, cells), F32), shape((rows, cols, width), F32), shape((hidden, cells), F32)],
        flops=2 * 10**9,
        name="gate",
    )(zn, adjoint, cell_mask, same, w_proj, w_gate, chain_bias, gain_out, w_out)
    field = pltpu.VMEM((devices * half, cols), F32)
    channels = shape((own, residues, cols), BF)
    block = shape((devices, half, cols), BF)
    sent, left, right = call(mix_kernel, [block, channels, channels], [field] * 3, name="mix")(got)
    got = swap(sent)
    sent, xn = call(norm_kernel, [block, shape((hidden, cells), BF)], name="norm")(got, t, gain_out)
    got = swap(sent)
    output, d_logit, gate_part = call(
        output_kernel,
        [shape(pair.shape, BF), shape(pair.shape, BF), shape((width, width), F32)],
        flops=2 * 10**9,
        name="output",
    )(xn, gate, adjoint, zn, w_out)
    sent = call(
        unmix_kernel, [shape((devices, 2 * half, cols), BF)], [field] * 3, name="unmix"
    )(got, left, right)[0]
    got = swap(sent)
    d_cells, part = call(
        cells_kernel,
        [shape((4 * hidden, cells), BF), shape((width, 4 * hidden + width), BF)],
        name="cells",
    )(got, factor, zn, gate_part)
    got = swap(part.reshape(devices, width // devices, -1))
    d_pair = call(pair_kernel, [shape(pair.shape, BF)], flops=2 * 10**9, name="pair")(
        d_cells, d_logit, pair, gain_in, w_proj, w_gate
    )[0]
    sent = call(
        functools.partial(sum_kernel, residues), [shape(got.shape, BF)], name="sum"
    )(got)[0]
    d_proj, d_gate = call(
        finish_kernel, [shape((width, 4 * hidden), F32), shape((width, width), F32)], name="finish"
    )(swap(sent))
    return (output, d_pair, d_proj, d_gate)


def per_device(pair, adjoint, mask, chain, gain_in, w_proj, w_gate, chain_bias, gain_out, w_out):
    rows, cols, width = pair.shape
    hidden = w_out.shape[0]
    n_wide = lax.axis_size("wide")
    n_narrow = lax.axis_size("narrow")
    if n_narrow == 1 and (rows, cols, width) == (8, 128, 128) and hidden == 8 * n_wide == 128:
        return small_blocks(
            pair, adjoint, mask, chain, gain_in, w_proj, w_gate, chain_bias, gain_out, w_out
        )
    residues = rows * n_wide
    devices = n_wide * n_narrow
    own = hidden // devices
    row_start = lax.axis_index("wide") * rows
    col_start = lax.axis_index("narrow") * cols
    mask_f = mask.astype(jnp.float32)
    row_mask = lax.dynamic_slice_in_dim(mask_f, row_start, rows, 0)
    col_mask = lax.dynamic_slice_in_dim(mask_f, col_start, cols, 0)
    cell_mask = (row_mask[:, None] * col_mask[None, :])[None]
    row_chain = lax.dynamic_slice_in_dim(chain, row_start, rows, 0)
    col_chain = lax.dynamic_slice_in_dim(chain, col_start, cols, 0)
    same = (row_chain[:, None] == col_chain[None, :])[:, :, None]
    zn_f, z_hat, z_rstd = normalize(pair.astype(jnp.float32), gain_in, -1)
    zn = zn_f.astype(jnp.bfloat16)
    proj_a = jnp.einsum(
        "ijc,ch->hij", zn, w_proj[:, : 2 * hidden], preferred_element_type=jnp.float32
    )
    proj_b = jnp.einsum(
        "ijc,ch->hij", zn, w_proj[:, 2 * hidden :], preferred_element_type=jnp.float32
    )
    a_lin = proj_a[:hidden]
    sig_a = jax.nn.sigmoid(proj_a[hidden:])
    b_lin = proj_b[:hidden]
    sig_b = jax.nn.sigmoid(proj_b[hidden:])
    left_t = (cell_mask * sig_a * a_lin).astype(jnp.bfloat16)
    right_t = (cell_mask * sig_b * b_lin).astype(jnp.bfloat16)
    pairs = jnp.concatenate(
        [left_t.reshape(devices, own, rows, cols), right_t.reshape(devices, own, rows, cols)], 1
    )
    pairs = gather_cells(swap(pairs), n_wide, n_narrow)
    left_c, right_c = pairs[:own], pairs[own:]
    mixed_c = jnp.einsum("hik,hjk->hij", left_c, right_c, preferred_element_type=jnp.float32)
    mixed_t = swap(split_cells(mixed_c.astype(jnp.bfloat16), n_wide, n_narrow))
    mixed_t = mixed_t.reshape(hidden, rows, cols).astype(jnp.float32)
    xn_f, x_hat, x_rstd = normalize(mixed_t, gain_out[:, None, None], 0)
    xn = xn_f.astype(jnp.bfloat16)
    proj_out = jnp.einsum("hij,hc->ijc", xn, w_out, preferred_element_type=jnp.float32)
    logits = jnp.dot(zn, w_gate, preferred_element_type=jnp.float32) + jnp.where(
        same, chain_bias[1], chain_bias[0]
    )
    gate = jax.nn.sigmoid(logits)
    output = (gate * proj_out).astype(jnp.bfloat16)
    adj = adjoint.astype(jnp.float32)
    d_out = (adj * gate).astype(jnp.bfloat16)
    d_logit = (adj * proj_out * gate * (1.0 - gate)).astype(jnp.bfloat16)
    d_xn = jnp.einsum("ijc,hc->hij", d_out, w_out, preferred_element_type=jnp.float32)
    d_mixed_t = norm_back(d_xn * gain_out[:, None, None], x_hat, x_rstd, 0).astype(jnp.bfloat16)
    d_mixed_c = gather_cells(swap(d_mixed_t.reshape(devices, own, rows, cols)), n_wide, n_narrow)
    d_left_c = jnp.einsum("hij,hjk->hik", d_mixed_c, right_c, preferred_element_type=jnp.float32)
    d_right_c = jnp.einsum("hij,hik->hjk", d_mixed_c, left_c, preferred_element_type=jnp.float32)
    back = jnp.concatenate([d_left_c.astype(jnp.bfloat16), d_right_c.astype(jnp.bfloat16)], 0)
    back = swap(split_cells(back, n_wide, n_narrow))
    d_left = back[:, :own].reshape(hidden, rows, cols).astype(jnp.float32)
    d_right = back[:, own:].reshape(hidden, rows, cols).astype(jnp.float32)
    d_cells_a = jnp.concatenate(
        [d_left * cell_mask * sig_a, d_left * cell_mask * a_lin * sig_a * (1.0 - sig_a)], 0
    ).astype(jnp.bfloat16)
    d_cells_b = jnp.concatenate(
        [d_right * cell_mask * sig_b, d_right * cell_mask * b_lin * sig_b * (1.0 - sig_b)], 0
    ).astype(jnp.bfloat16)
    d_zn = jnp.einsum(
        "hij,ch->ijc", d_cells_a, w_proj[:, : 2 * hidden], preferred_element_type=jnp.float32
    )
    d_zn = d_zn + jnp.einsum(
        "hij,ch->ijc", d_cells_b, w_proj[:, 2 * hidden :], preferred_element_type=jnp.float32
    )
    d_zn = d_zn + jnp.dot(d_logit, w_gate.T, preferred_element_type=jnp.float32)
    d_pair = norm_back(d_zn * gain_in, z_hat, z_rstd, -1).astype(jnp.bfloat16)
    proj_part = jnp.concatenate(
        [
            jnp.einsum("ijc,hij->ch", zn, d_cells_a, preferred_element_type=jnp.float32),
            jnp.einsum("ijc,hij->ch", zn, d_cells_b, preferred_element_type=jnp.float32),
        ],
        1,
    )
    flat_z = zn.reshape(-1, width)
    gate_part = jnp.dot(flat_z.T, d_logit.reshape(-1, width), preferred_element_type=jnp.float32)
    parts = jnp.concatenate([proj_part, gate_part], 1)
    chunk = width // devices
    mine = swap(parts.astype(jnp.bfloat16).reshape(devices, chunk, -1))
    mine = jnp.sum(mine.astype(jnp.float32), 0) / residues
    mine = mine.astype(jnp.bfloat16)
    total = swap(jnp.broadcast_to(mine, (devices,) + mine.shape)).reshape(width, -1)
    total = total.astype(jnp.float32)
    return (output, d_pair, total[:, : 4 * hidden], total[:, 4 * hidden :])


def solution(mesh):
    placed = (
        P(("groups", "wide"), "narrow", None),
        P(("groups", "wide"), "narrow", None),
        P("groups"),
        P("groups"),
        P(),
        P(),
        P(),
        P(),
        P(),
        P(),
    )
    return jax.shard_map(
        per_device,
        mesh=mesh,
        in_specs=placed,
        out_specs=(
            P(("groups", "wide"), "narrow", None),
            P(("groups", "wide"), "narrow", None),
            P("groups", None),
            P("groups", None),
        ),
        check_vma=False,
    )
```

```python
import functools

import jax
import jax.numpy as jnp
from jax import lax
from jax.experimental import pallas as pl
from jax.experimental.pallas import tpu as pltpu
from jax.sharding import PartitionSpec as P

EPS = 1e-05


def normalize(values, gain, axis):
    centre = values - jnp.mean(values, axis, keepdims=True)
    rstd = lax.rsqrt(jnp.mean(centre * centre, axis, keepdims=True) + EPS)
    hat = centre * rstd
    return (hat * gain, hat, rstd)


def norm_back(scaled, hat, rstd, axis):
    return rstd * (
        scaled
        - jnp.mean(scaled, axis, keepdims=True)
        - hat * jnp.mean(scaled * hat, axis, keepdims=True)
    )


def swap(blocks):
    return lax.all_to_all(blocks, ("wide", "narrow"), split_axis=0, concat_axis=0, tiled=True)


def gather_cells(blocks, n_wide, n_narrow):
    _, own, rows, cols = blocks.shape
    shaped = blocks.reshape(n_wide, n_narrow, own, rows, cols)
    return jnp.transpose(shaped, (2, 0, 3, 1, 4)).reshape(own, n_wide * rows, n_narrow * cols)


def split_cells(field, n_wide, n_narrow):
    own, rows, cols = field.shape
    shaped = field.reshape(own, n_wide, rows // n_wide, n_narrow, cols // n_narrow)
    moved = jnp.transpose(shaped, (1, 3, 0, 2, 4))
    return moved.reshape(n_wide * n_narrow, own, rows // n_wide, cols // n_narrow)


BF = jnp.bfloat16
F32 = jnp.float32


def dot(a, b, over=((1,), (0,))):
    return lax.dot_general(a, b, (over, ((), ())), preferred_element_type=F32)


def column(row):
    return jnp.broadcast_to(row, (row.shape[1], row.shape[1])).T


def centred(x):
    centre = x - jnp.mean(x, 0, keepdims=True)
    rstd = lax.rsqrt(jnp.mean(centre * centre, 0, keepdims=True) + EPS)
    return centre * rstd, rstd


def back_t(scaled, hat, rstd):
    inner = hat * jnp.mean(scaled * hat, 0, keepdims=True)
    return rstd * (scaled - jnp.mean(scaled, 0, keepdims=True) - inner)


def two_rows(first, second, devices):
    own, cols = first.shape[0] // devices, first.shape[1]
    shape = (devices, own, cols)
    return jnp.concatenate([first.reshape(shape), second.reshape(shape)], 1).astype(BF)


def apart(block, devices):
    wide = block.astype(F32)
    own, cols = wide.shape[1] // 2, wide.shape[2]
    return [wide[:, at * own : (at + 1) * own].reshape(devices * own, cols) for at in range(2)]


def project_kernel(
    pair_hbm, mask_hbm, gain_hbm, w_hbm, sent_ref, zn_ref, mask_ref,
    pair_ref, mask_v, gain_ref, w_ref, sems, row_sems,
):
    devices, depth, _ = sent_ref.shape
    rows, cols, width = pair_ref.shape
    start = lax.axis_index("wide") * rows
    row_copies = [
        pltpu.make_async_copy(pair_hbm.at[row], pair_ref.at[row], row_sems.at[row])
        for row in range(rows)
    ]
    copies = [
        pltpu.make_async_copy(gain_hbm, gain_ref, sems.at[0]),
        pltpu.make_async_copy(w_hbm, w_ref, sems.at[1]),
        pltpu.make_async_copy(mask_hbm, mask_v, sems.at[2]),
    ]
    for copy in copies + row_copies:
        copy.start()
    for copy in copies:
        copy.wait()
    mask_f = mask_v[...].astype(F32)
    shape = (rows, mask_f.shape[1])
    lane = lax.broadcasted_iota(jnp.int32, shape, 1)
    own = lane == start + lax.broadcasted_iota(jnp.int32, shape, 0)
    mask_ref[...] = mask_f * jnp.sum(jnp.where(own, mask_f, 0.0), 1, keepdims=True)
    gain = column(gain_ref[...])
    weights = w_ref[...].astype(F32).T.astype(BF)
    hidden = weights.shape[0] // 4
    half = depth // 2
    for two in range(rows // 2):
        pieces = []
        for row in (2 * two, 2 * two + 1):
            row_copies[row].wait()
            hat, _ = centred(pair_ref[row].astype(F32).T)
            zn = (hat * gain).astype(BF)
            zn_ref[:, row * cols : (row + 1) * cols] = zn
            proj = dot(weights, zn)
            mask = mask_ref[row : row + 1, :]
            left = mask * jax.nn.sigmoid(proj[hidden : 2 * hidden]) * proj[:hidden]
            right = mask * jax.nn.sigmoid(proj[3 * hidden :]) * proj[2 * hidden : 3 * hidden]
            pieces.append((left, right))
        at = two * 16
        sent_ref[:, at : at + 16, :] = two_rows(pieces[0][0], pieces[1][0], devices)
        sent_ref[:, half + at : half + at + 16, :] = two_rows(pieces[0][1], pieces[1][1], devices)


def gate_kernel(
    zn_ref, adj_ref, mask_ref, same_ref, w_ref, w_gate_ref, bias_ref, gain_ref, w_out_ref,
    factor_ref, gate_ref, t_ref,
):
    rows, cols, width = adj_ref.shape
    weights = w_ref[...].astype(F32).T.astype(BF)
    hidden = weights.shape[0] // 4
    w_gate = w_gate_ref[...].astype(F32).T.astype(BF)
    across, within = column(bias_ref[0:1, :]), column(bias_ref[1:2, :])
    gain = column(gain_ref[...])
    for row in range(rows):
        lanes = slice(row * cols, (row + 1) * cols)
        zn = zn_ref[:, lanes]
        proj = dot(weights, zn)
        mask = mask_ref[row : row + 1, :]
        for side in range(2):
            lin = proj[2 * side * hidden : (2 * side + 1) * hidden]
            sig = jax.nn.sigmoid(proj[(2 * side + 1) * hidden : (2 * side + 2) * hidden])
            factor_ref[2 * side * hidden : (2 * side + 1) * hidden, lanes] = (mask * sig).astype(BF)
            factor_ref[(2 * side + 1) * hidden : (2 * side + 2) * hidden, lanes] = (
                mask * lin * sig * (1.0 - sig)
            ).astype(BF)
        bias = jnp.where(same_ref[row : row + 1, :] > 0.5, within, across)
        gate = jax.nn.sigmoid(dot(w_gate, zn) + bias).T
        gate_ref[row] = gate
        d_out = (adj_ref[row].astype(F32) * gate).astype(BF)
        t_ref[:, lanes] = (dot(w_out_ref[...], d_out, ((1,), (1,))) * gain).astype(BF)


def mix_kernel(got_ref, sent_ref, left_ref, right_ref, left_s, right_s, out_s):
    devices, depth, cols = got_ref.shape
    own = left_ref.shape[0]
    half = depth // 2
    count = devices * half // own
    left_s[...] = got_ref[:, :half, :].astype(F32).reshape(devices * half, cols)
    right_s[...] = got_ref[:, half:, :].astype(F32).reshape(devices * half, cols)
    for h in range(own):
        left = left_s[pl.ds(h, count, stride=own), :].astype(BF)
        right = right_s[pl.ds(h, count, stride=own), :].astype(BF)
        left_ref[h] = left
        right_ref[h] = right
        out_s[pl.ds(h, count, stride=own), :] = dot(left, right, ((1,), (1,)))
    sent_ref[...] = out_s[...].reshape(devices, half, cols).astype(BF)


def norm_kernel(got_ref, t_ref, gain_ref, sent_ref, xn_ref):
    devices, depth, cols = got_ref.shape
    gain = column(gain_ref[...])
    for two in range(depth // 16):
        pieces = []
        for part, mixed in enumerate(apart(got_ref[:, two * 16 : two * 16 + 16, :], devices)):
            row = 2 * two + part
            lanes = slice(row * cols, (row + 1) * cols)
            hat, rstd = centred(mixed)
            xn_ref[:, lanes] = (hat * gain).astype(BF)
            pieces.append(back_t(t_ref[:, lanes].astype(F32), hat, rstd))
        sent_ref[:, two * 16 : two * 16 + 16, :] = two_rows(*pieces, devices)


def output_kernel(
    xn_ref, gate_ref, adj_ref, zn_ref, w_out_ref, output_ref, d_logit_ref, part_ref
):
    rows, cols, width = adj_ref.shape
    total = None
    for row in range(rows):
        lanes = slice(row * cols, (row + 1) * cols)
        xn = xn_ref[:, lanes].astype(F32).T.astype(BF)
        proj_out = dot(xn, w_out_ref[...])
        gate = gate_ref[row]
        output_ref[row] = (gate * proj_out).astype(BF)
        d_logit = (adj_ref[row].astype(F32) * proj_out * gate * (1.0 - gate)).astype(BF)
        d_logit_ref[row] = d_logit
        term = dot(zn_ref[:, lanes], d_logit)
        total = term if total is None else total + term
    part_ref[...] = total


def unmix_kernel(got_ref, left_ref, right_ref, sent_ref, in_s, left_s, right_s):
    devices, half, cols = got_ref.shape
    own = left_ref.shape[0]
    count = devices * half // own
    in_s[...] = got_ref[...].astype(F32).reshape(devices * half, cols)
    for h in range(own):
        grad = in_s[pl.ds(h, count, stride=own), :]
        left_s[pl.ds(h, count, stride=own), :] = dot(grad.astype(BF), right_ref[h])
        right_s[pl.ds(h, count, stride=own), :] = dot(grad.T.astype(BF), left_ref[h])
    sent_ref[:, :half, :] = left_s[...].reshape(devices, half, cols).astype(BF)
    sent_ref[:, half:, :] = right_s[...].reshape(devices, half, cols).astype(BF)


def cells_kernel(got_ref, factor_ref, zn_ref, gate_part_ref, cells_ref, part_ref):
    devices, depth, cols = got_ref.shape
    half = depth // 2
    hidden = factor_ref.shape[0] // 4
    for side in range(2):
        for two in range(half // 16):
            at = side * half + two * 16
            for part, grad in enumerate(apart(got_ref[:, at : at + 16, :], devices)):
                row = 2 * two + part
                lanes = slice(row * cols, (row + 1) * cols)
                for kind in (2 * side, 2 * side + 1):
                    place = slice(kind * hidden, (kind + 1) * hidden)
                    cells_ref[place, lanes] = (grad * factor_ref[place, lanes].astype(F32)).astype(BF)
    total = dot(zn_ref[...], cells_ref[...], ((1,), (1,)))
    part_ref[:, : 4 * hidden] = total.astype(BF)
    part_ref[:, 4 * hidden :] = gate_part_ref[...].astype(BF)


def pair_kernel(cells_ref, d_logit_ref, pair_ref, gain_ref, w_ref, w_gate_ref, d_pair_ref):
    rows, cols, width = pair_ref.shape
    gain = column(gain_ref[...])
    for row in range(rows):
        lanes = slice(row * cols, (row + 1) * cols)
        hat, rstd = centred(pair_ref[row].astype(F32).T)
        d_zn = dot(w_ref[...], cells_ref[:, lanes])
        d_zn = d_zn + dot(w_gate_ref[...], d_logit_ref[row], ((1,), (1,)))
        d_pair_ref[row] = back_t(d_zn * gain, hat, rstd).T.astype(BF)


def sum_kernel(residues, got_ref, sent_ref):
    total = jnp.sum(got_ref[...].astype(F32), 0) / residues
    sent_ref[...] = jnp.broadcast_to(total.astype(BF)[None], sent_ref.shape)


def finish_kernel(got_ref, proj_ref, gate_ref):
    devices, chunk, depth = got_ref.shape
    wide = proj_ref.shape[1]
    total = got_ref[...].astype(F32).reshape(devices * chunk, depth)
    proj_ref[...] = total[:, :wide]
    gate_ref[...] = total[:, wide:]


def call(kernel, outs, scratch=(), flops=0, name=None, space=pltpu.VMEM):
    spec = pl.BlockSpec(memory_space=pltpu.VMEM)

    def run(*args):
        moved = sum(a.size * a.dtype.itemsize for a in (*args, *outs))
        return pl.pallas_call(
            kernel,
            out_shape=list(outs),
            in_specs=[pl.BlockSpec(memory_space=space)] * len(args),
            out_specs=[spec] * len(outs),
            scratch_shapes=list(scratch),
            compiler_params=pltpu.CompilerParams(vmem_limit_bytes=12 * 1024 * 1024),
            cost_estimate=pl.CostEstimate(
                flops=flops, bytes_accessed=moved, transcendentals=0
            ),
            name=name,
        )(*args)

    return run


def small_blocks(pair, adjoint, mask, chain, gain_in, w_proj, w_gate, chain_bias, gain_out, w_out):
    rows, cols, width = pair.shape
    hidden = w_out.shape[0]
    devices = lax.axis_size("wide")
    own = hidden // devices
    residues = rows * devices
    cells = rows * cols
    half = rows * own
    shape = jax.ShapeDtypeStruct
    start = lax.axis_index("wide") * rows
    row_chain = lax.dynamic_slice_in_dim(chain, start, rows, 0)
    same = (row_chain[:, None] == chain[None, :]).astype(F32)
    gain_in, gain_out = gain_in[None], gain_out[None]
    sent, zn, cell_mask = call(
        project_kernel,
        [shape((devices, 2 * half, cols), BF), shape((width, cells), BF), shape((rows, cols), F32)],
        [
            pltpu.VMEM(pair.shape, BF),
            pltpu.VMEM((1, residues), jnp.int32),
            pltpu.VMEM(gain_in.shape, F32),
            pltpu.VMEM(w_proj.shape, BF),
            pltpu.SemaphoreType.DMA((3,)),
            pltpu.SemaphoreType.DMA((rows,)),
        ],
        name="project",
        space=pltpu.HBM,
    )(pair, mask[None], gain_in, w_proj)
    got = swap(sent)
    factor, gate, t = call(
        gate_kernel,
        [shape((4 * hidden, cells), BF), shape((rows, cols, width), F32), shape((hidden, cells), BF)],
        flops=2 * 10**9,
        name="gate",
    )(zn, adjoint, cell_mask, same, w_proj, w_gate, chain_bias, gain_out, w_out)
    field = pltpu.VMEM((devices * half, cols), F32)
    channels = shape((own, residues, cols), BF)
    block = shape((devices, half, cols), BF)
    sent, left, right = call(mix_kernel, [block, channels, channels], [field] * 3, name="mix")(got)
    got = swap(sent)
    sent, xn = call(norm_kernel, [block, shape((hidden, cells), BF)], name="norm")(got, t, gain_out)
    got = swap(sent)
    output, d_logit, gate_part = call(
        output_kernel,
        [shape(pair.shape, BF), shape(pair.shape, BF), shape((width, width), F32)],
        flops=2 * 10**9,
        name="output",
    )(xn, gate, adjoint, zn, w_out)
    sent = call(
        unmix_kernel, [shape((devices, 2 * half, cols), BF)], [field] * 3, name="unmix"
    )(got, left, right)[0]
    got = swap(sent)
    d_cells, part = call(
        cells_kernel,
        [shape((4 * hidden, cells), BF), shape((width, 4 * hidden + width), BF)],
        name="cells",
    )(got, factor, zn, gate_part)
    got = swap(part.reshape(devices, width // devices, -1))
    d_pair = call(pair_kernel, [shape(pair.shape, BF)], flops=2 * 10**9, name="pair")(
        d_cells, d_logit, pair, gain_in, w_proj, w_gate
    )[0]
    sent = call(
        functools.partial(sum_kernel, residues), [shape(got.shape, BF)], name="sum"
    )(got)[0]
    d_proj, d_gate = call(
        finish_kernel, [shape((width, 4 * hidden), F32), shape((width, width), F32)], name="finish"
    )(swap(sent))
    return (output, d_pair, d_proj, d_gate)


def per_device(pair, adjoint, mask, chain, gain_in, w_proj, w_gate, chain_bias, gain_out, w_out):
    rows, cols, width = pair.shape
    hidden = w_out.shape[0]
    n_wide = lax.axis_size("wide")
    n_narrow = lax.axis_size("narrow")
    if n_narrow == 1 and (rows, cols, width) == (8, 128, 128) and hidden == 8 * n_wide == 128:
        return small_blocks(
            pair, adjoint, mask, chain, gain_in, w_proj, w_gate, chain_bias, gain_out, w_out
        )
    residues = rows * n_wide
    devices = n_wide * n_narrow
    own = hidden // devices
    row_start = lax.axis_index("wide") * rows
    col_start = lax.axis_index("narrow") * cols
    mask_f = mask.astype(jnp.float32)
    row_mask = lax.dynamic_slice_in_dim(mask_f, row_start, rows, 0)
    col_mask = lax.dynamic_slice_in_dim(mask_f, col_start, cols, 0)
    cell_mask = (row_mask[:, None] * col_mask[None, :])[None]
    row_chain = lax.dynamic_slice_in_dim(chain, row_start, rows, 0)
    col_chain = lax.dynamic_slice_in_dim(chain, col_start, cols, 0)
    same = (row_chain[:, None] == col_chain[None, :])[:, :, None]
    zn_f, z_hat, z_rstd = normalize(pair.astype(jnp.float32), gain_in, -1)
    zn = zn_f.astype(jnp.bfloat16)
    proj_a = jnp.einsum(
        "ijc,ch->hij", zn, w_proj[:, : 2 * hidden], preferred_element_type=jnp.float32
    )
    proj_b = jnp.einsum(
        "ijc,ch->hij", zn, w_proj[:, 2 * hidden :], preferred_element_type=jnp.float32
    )
    a_lin = proj_a[:hidden]
    sig_a = jax.nn.sigmoid(proj_a[hidden:])
    b_lin = proj_b[:hidden]
    sig_b = jax.nn.sigmoid(proj_b[hidden:])
    left_t = (cell_mask * sig_a * a_lin).astype(jnp.bfloat16)
    right_t = (cell_mask * sig_b * b_lin).astype(jnp.bfloat16)
    pairs = jnp.concatenate(
        [left_t.reshape(devices, own, rows, cols), right_t.reshape(devices, own, rows, cols)], 1
    )
    pairs = gather_cells(swap(pairs), n_wide, n_narrow)
    left_c, right_c = pairs[:own], pairs[own:]
    mixed_c = jnp.einsum("hik,hjk->hij", left_c, right_c, preferred_element_type=jnp.float32)
    mixed_t = swap(split_cells(mixed_c.astype(jnp.bfloat16), n_wide, n_narrow))
    mixed_t = mixed_t.reshape(hidden, rows, cols).astype(jnp.float32)
    xn_f, x_hat, x_rstd = normalize(mixed_t, gain_out[:, None, None], 0)
    xn = xn_f.astype(jnp.bfloat16)
    proj_out = jnp.einsum("hij,hc->ijc", xn, w_out, preferred_element_type=jnp.float32)
    logits = jnp.dot(zn, w_gate, preferred_element_type=jnp.float32) + jnp.where(
        same, chain_bias[1], chain_bias[0]
    )
    gate = jax.nn.sigmoid(logits)
    output = (gate * proj_out).astype(jnp.bfloat16)
    adj = adjoint.astype(jnp.float32)
    d_out = (adj * gate).astype(jnp.bfloat16)
    d_logit = (adj * proj_out * gate * (1.0 - gate)).astype(jnp.bfloat16)
    d_xn = jnp.einsum("ijc,hc->hij", d_out, w_out, preferred_element_type=jnp.float32)
    d_mixed_t = norm_back(d_xn * gain_out[:, None, None], x_hat, x_rstd, 0).astype(jnp.bfloat16)
    d_mixed_c = gather_cells(swap(d_mixed_t.reshape(devices, own, rows, cols)), n_wide, n_narrow)
    d_left_c = jnp.einsum("hij,hjk->hik", d_mixed_c, right_c, preferred_element_type=jnp.float32)
    d_right_c = jnp.einsum("hij,hik->hjk", d_mixed_c, left_c, preferred_element_type=jnp.float32)
    back = jnp.concatenate([d_left_c.astype(jnp.bfloat16), d_right_c.astype(jnp.bfloat16)], 0)
    back = swap(split_cells(back, n_wide, n_narrow))
    d_left = back[:, :own].reshape(hidden, rows, cols).astype(jnp.float32)
    d_right = back[:, own:].reshape(hidden, rows, cols).astype(jnp.float32)
    d_cells_a = jnp.concatenate(
        [d_left * cell_mask * sig_a, d_left * cell_mask * a_lin * sig_a * (1.0 - sig_a)], 0
    ).astype(jnp.bfloat16)
    d_cells_b = jnp.concatenate(
        [d_right * cell_mask * sig_b, d_right * cell_mask * b_lin * sig_b * (1.0 - sig_b)], 0
    ).astype(jnp.bfloat16)
    d_zn = jnp.einsum(
        "hij,ch->ijc", d_cells_a, w_proj[:, : 2 * hidden], preferred_element_type=jnp.float32
    )
    d_zn = d_zn + jnp.einsum(
        "hij,ch->ijc", d_cells_b, w_proj[:, 2 * hidden :], preferred_element_type=jnp.float32
    )
    d_zn = d_zn + jnp.dot(d_logit, w_gate.T, preferred_element_type=jnp.float32)
    d_pair = norm_back(d_zn * gain_in, z_hat, z_rstd, -1).astype(jnp.bfloat16)
    proj_part = jnp.concatenate(
        [
            jnp.einsum("ijc,hij->ch", zn, d_cells_a, preferred_element_type=jnp.float32),
            jnp.einsum("ijc,hij->ch", zn, d_cells_b, preferred_element_type=jnp.float32),
        ],
        1,
    )
    flat_z = zn.reshape(-1, width)
    gate_part = jnp.dot(flat_z.T, d_logit.reshape(-1, width), preferred_element_type=jnp.float32)
    parts = jnp.concatenate([proj_part, gate_part], 1)
    chunk = width // devices
    mine = swap(parts.astype(jnp.bfloat16).reshape(devices, chunk, -1))
    mine = jnp.sum(mine.astype(jnp.float32), 0) / residues
    mine = mine.astype(jnp.bfloat16)
    total = swap(jnp.broadcast_to(mine, (devices,) + mine.shape)).reshape(width, -1)
    total = total.astype(jnp.float32)
    return (output, d_pair, total[:, : 4 * hidden], total[:, 4 * hidden :])


def solution(mesh):
    placed = (
        P(("groups", "wide"), "narrow", None),
        P(("groups", "wide"), "narrow", None),
        P("groups"),
        P("groups"),
        P(),
        P(),
        P(),
        P(),
        P(),
        P(),
    )
    return jax.shard_map(
        per_device,
        mesh=mesh,
        in_specs=placed,
        out_specs=(
            P(("groups", "wide"), "narrow", None),
            P(("groups", "wide"), "narrow", None),
            P("groups", None),
            P("groups", None),
        ),
        check_vma=False,
    )
```

```python
import functools

import jax
import jax.numpy as jnp
from jax import lax
from jax.experimental import pallas as pl
from jax.experimental.pallas import tpu as pltpu
from jax.sharding import PartitionSpec as P

EPS = 1e-05


def normalize(values, gain, axis):
    centre = values - jnp.mean(values, axis, keepdims=True)
    rstd = lax.rsqrt(jnp.mean(centre * centre, axis, keepdims=True) + EPS)
    hat = centre * rstd
    return (hat * gain, hat, rstd)


def norm_back(scaled, hat, rstd, axis):
    return rstd * (
        scaled
        - jnp.mean(scaled, axis, keepdims=True)
        - hat * jnp.mean(scaled * hat, axis, keepdims=True)
    )


def swap(blocks):
    return lax.all_to_all(blocks, ("wide", "narrow"), split_axis=0, concat_axis=0, tiled=True)


def gather_cells(blocks, n_wide, n_narrow):
    _, own, rows, cols = blocks.shape
    shaped = blocks.reshape(n_wide, n_narrow, own, rows, cols)
    return jnp.transpose(shaped, (2, 0, 3, 1, 4)).reshape(own, n_wide * rows, n_narrow * cols)


def split_cells(field, n_wide, n_narrow):
    own, rows, cols = field.shape
    shaped = field.reshape(own, n_wide, rows // n_wide, n_narrow, cols // n_narrow)
    moved = jnp.transpose(shaped, (1, 3, 0, 2, 4))
    return moved.reshape(n_wide * n_narrow, own, rows // n_wide, cols // n_narrow)


BF = jnp.bfloat16
F32 = jnp.float32


def dot(a, b, over=((1,), (0,))):
    return lax.dot_general(a, b, (over, ((), ())), preferred_element_type=F32)


def column(row):
    return jnp.broadcast_to(row, (row.shape[1], row.shape[1])).T


def centred(x):
    centre = x - jnp.mean(x, 0, keepdims=True)
    rstd = lax.rsqrt(jnp.mean(centre * centre, 0, keepdims=True) + EPS)
    return centre * rstd, rstd


def back_t(scaled, hat, rstd):
    inner = hat * jnp.mean(scaled * hat, 0, keepdims=True)
    return rstd * (scaled - jnp.mean(scaled, 0, keepdims=True) - inner)


def two_rows(first, second, devices):
    own, cols = first.shape[0] // devices, first.shape[1]
    shape = (devices, own, cols)
    return jnp.concatenate([first.reshape(shape), second.reshape(shape)], 1).astype(BF)


def apart(block, devices):
    wide = block.astype(F32)
    own, cols = wide.shape[1] // 2, wide.shape[2]
    return [wide[:, at * own : (at + 1) * own].reshape(devices * own, cols) for at in range(2)]


def project_kernel(
    pair_hbm, mask_hbm, gain_hbm, w_hbm, sent_ref, zn_ref, mask_ref,
    pair_ref, mask_v, gain_ref, w_ref, sems, row_sems,
):
    devices, depth, _ = sent_ref.shape
    rows, cols, width = pair_ref.shape
    start = lax.axis_index("wide") * rows
    row_copies = [
        pltpu.make_async_copy(pair_hbm.at[row], pair_ref.at[row], row_sems.at[row])
        for row in range(rows)
    ]
    copies = [
        pltpu.make_async_copy(gain_hbm, gain_ref, sems.at[0]),
        pltpu.make_async_copy(w_hbm, w_ref, sems.at[1]),
        pltpu.make_async_copy(mask_hbm, mask_v, sems.at[2]),
    ]
    for copy in copies + row_copies:
        copy.start()
    for copy in copies:
        copy.wait()
    mask_f = mask_v[...].astype(F32)
    shape = (rows, mask_f.shape[1])
    lane = lax.broadcasted_iota(jnp.int32, shape, 1)
    own = lane == start + lax.broadcasted_iota(jnp.int32, shape, 0)
    mask_ref[...] = mask_f * jnp.sum(jnp.where(own, mask_f, 0.0), 1, keepdims=True)
    gain = column(gain_ref[...])
    weights = w_ref[...].astype(F32).T.astype(BF)
    hidden = weights.shape[0] // 4
    half = depth // 2
    for two in range(rows // 2):
        pieces = []
        for row in (2 * two, 2 * two + 1):
            row_copies[row].wait()
            hat, _ = centred(pair_ref[row].astype(F32).T)
            zn = (hat * gain).astype(BF)
            zn_ref[:, row * cols : (row + 1) * cols] = zn
            proj = dot(weights, zn)
            mask = mask_ref[row : row + 1, :]
            left = mask * jax.nn.sigmoid(proj[hidden : 2 * hidden]) * proj[:hidden]
            right = mask * jax.nn.sigmoid(proj[3 * hidden :]) * proj[2 * hidden : 3 * hidden]
            pieces.append((left, right))
        at = two * 16
        sent_ref[:, at : at + 16, :] = two_rows(pieces[0][0], pieces[1][0], devices)
        sent_ref[:, half + at : half + at + 16, :] = two_rows(pieces[0][1], pieces[1][1], devices)


def gate_kernel(
    zn_ref, adj_ref, mask_ref, same_ref, w_ref, w_gate_ref, bias_ref, gain_ref, w_out_ref,
    factor_ref, gate_ref, t_ref,
):
    rows, cols, width = adj_ref.shape
    weights = w_ref[...].astype(F32).T.astype(BF)
    hidden = weights.shape[0] // 4
    w_gate = w_gate_ref[...].astype(F32).T.astype(BF)
    across, within = column(bias_ref[0:1, :]), column(bias_ref[1:2, :])
    gain = column(gain_ref[...])
    for row in range(rows):
        lanes = slice(row * cols, (row + 1) * cols)
        zn = zn_ref[:, lanes]
        proj = dot(weights, zn)
        mask = mask_ref[row : row + 1, :]
        for side in range(2):
            lin = proj[2 * side * hidden : (2 * side + 1) * hidden]
            sig = jax.nn.sigmoid(proj[(2 * side + 1) * hidden : (2 * side + 2) * hidden])
            factor_ref[2 * side * hidden : (2 * side + 1) * hidden, lanes] = (mask * sig).astype(BF)
            factor_ref[(2 * side + 1) * hidden : (2 * side + 2) * hidden, lanes] = (
                mask * lin * sig * (1.0 - sig)
            ).astype(BF)
        bias = jnp.where(same_ref[row : row + 1, :] > 0.5, within, across)
        gate = jax.nn.sigmoid(dot(w_gate, zn) + bias).T
        gate_ref[row] = gate
        d_out = (adj_ref[row].astype(F32) * gate).astype(BF)
        t_ref[:, lanes] = (dot(w_out_ref[...], d_out, ((1,), (1,))) * gain).astype(BF)


def mix_kernel(got_ref, sent_ref, left_ref, right_ref, left_s, right_s, out_s):
    devices, depth, cols = got_ref.shape
    own = left_ref.shape[0]
    half = depth // 2
    count = devices * half // own
    left_s[...] = got_ref[:, :half, :].astype(F32).reshape(devices * half, cols)
    right_s[...] = got_ref[:, half:, :].astype(F32).reshape(devices * half, cols)
    for h in range(own):
        left = left_s[pl.ds(h, count, stride=own), :].astype(BF)
        right = right_s[pl.ds(h, count, stride=own), :].astype(BF)
        left_ref[h] = left
        right_ref[h] = right
        out_s[pl.ds(h, count, stride=own), :] = dot(left, right, ((1,), (1,)))
    sent_ref[...] = out_s[...].reshape(devices, half, cols).astype(BF)


def norm_kernel(got_ref, t_ref, gain_ref, sent_ref, xn_ref):
    devices, depth, cols = got_ref.shape
    gain = column(gain_ref[...])
    for two in range(depth // 16):
        pieces = []
        for part, mixed in enumerate(apart(got_ref[:, two * 16 : two * 16 + 16, :], devices)):
            row = 2 * two + part
            lanes = slice(row * cols, (row + 1) * cols)
            hat, rstd = centred(mixed)
            xn_ref[:, lanes] = (hat * gain).astype(BF)
            pieces.append(back_t(t_ref[:, lanes].astype(F32), hat, rstd))
        sent_ref[:, two * 16 : two * 16 + 16, :] = two_rows(*pieces, devices)


def output_kernel(
    xn_ref, gate_ref, adj_ref, zn_ref, w_out_ref, output_ref, d_logit_ref, part_ref
):
    rows, cols, width = adj_ref.shape
    total = None
    for row in range(rows):
        lanes = slice(row * cols, (row + 1) * cols)
        xn = xn_ref[:, lanes].astype(F32).T.astype(BF)
        proj_out = dot(xn, w_out_ref[...])
        gate = gate_ref[row]
        output_ref[row] = (gate * proj_out).astype(BF)
        d_logit = (adj_ref[row].astype(F32) * proj_out * gate * (1.0 - gate)).astype(BF)
        d_logit_ref[row] = d_logit
        term = dot(zn_ref[:, lanes], d_logit)
        total = term if total is None else total + term
    part_ref[...] = total


def unmix_kernel(got_ref, left_ref, right_ref, sent_ref, in_s, left_s, right_s):
    devices, half, cols = got_ref.shape
    own = left_ref.shape[0]
    count = devices * half // own
    in_s[...] = got_ref[...].astype(F32).reshape(devices * half, cols)
    for h in range(own):
        grad = in_s[pl.ds(h, count, stride=own), :]
        left_s[pl.ds(h, count, stride=own), :] = dot(grad.astype(BF), right_ref[h])
        right_s[pl.ds(h, count, stride=own), :] = dot(grad.T.astype(BF), left_ref[h])
    sent_ref[:, :half, :] = left_s[...].reshape(devices, half, cols).astype(BF)
    sent_ref[:, half:, :] = right_s[...].reshape(devices, half, cols).astype(BF)


def cells_kernel(got_ref, factor_ref, zn_ref, gate_part_ref, cells_ref, part_ref):
    devices, depth, cols = got_ref.shape
    half = depth // 2
    hidden = factor_ref.shape[0] // 4
    for side in range(2):
        for two in range(half // 16):
            at = side * half + two * 16
            for part, grad in enumerate(apart(got_ref[:, at : at + 16, :], devices)):
                row = 2 * two + part
                lanes = slice(row * cols, (row + 1) * cols)
                for kind in (2 * side, 2 * side + 1):
                    place = slice(kind * hidden, (kind + 1) * hidden)
                    cells_ref[place, lanes] = (grad * factor_ref[place, lanes].astype(F32)).astype(BF)
    total = dot(zn_ref[...], cells_ref[...], ((1,), (1,)))
    part_ref[:, : 4 * hidden] = total.astype(BF)
    part_ref[:, 4 * hidden :] = gate_part_ref[...].astype(BF)


def pair_kernel(cells_ref, d_logit_ref, pair_ref, gain_ref, w_ref, w_gate_ref, d_pair_ref):
    rows, cols, width = pair_ref.shape
    gain = column(gain_ref[...])
    for row in range(rows):
        lanes = slice(row * cols, (row + 1) * cols)
        hat, rstd = centred(pair_ref[row].astype(F32).T)
        d_zn = dot(w_ref[...], cells_ref[:, lanes])
        d_zn = d_zn + dot(w_gate_ref[...], d_logit_ref[row], ((1,), (1,)))
        d_pair_ref[row] = back_t(d_zn * gain, hat, rstd).T.astype(BF)


def sum_kernel(residues, got_ref, sent_ref):
    total = jnp.sum(got_ref[...].astype(F32), 0) / residues
    sent_ref[...] = jnp.broadcast_to(total.astype(BF)[None], sent_ref.shape)


def finish_kernel(got_ref, proj_ref, gate_ref):
    devices, chunk, depth = got_ref.shape
    wide = proj_ref.shape[1]
    total = got_ref[...].astype(F32).reshape(devices * chunk, depth)
    proj_ref[...] = total[:, :wide]
    gate_ref[...] = total[:, wide:]


def call(kernel, outs, scratch=(), flops=0, name=None, space=pltpu.VMEM, mib=12):
    spec = pl.BlockSpec(memory_space=pltpu.VMEM)

    def run(*args):
        moved = sum(a.size * a.dtype.itemsize for a in (*args, *outs))
        return pl.pallas_call(
            kernel,
            out_shape=list(outs),
            in_specs=[pl.BlockSpec(memory_space=space)] * len(args),
            out_specs=[spec] * len(outs),
            scratch_shapes=list(scratch),
            compiler_params=pltpu.CompilerParams(vmem_limit_bytes=mib * 1024 * 1024),
            cost_estimate=pl.CostEstimate(
                flops=flops, bytes_accessed=moved, transcendentals=0
            ),
            name=name,
        )(*args)

    return run


def small_blocks(pair, adjoint, mask, chain, gain_in, w_proj, w_gate, chain_bias, gain_out, w_out):
    rows, cols, width = pair.shape
    hidden = w_out.shape[0]
    devices = lax.axis_size("wide")
    own = hidden // devices
    residues = rows * devices
    cells = rows * cols
    half = rows * own
    shape = jax.ShapeDtypeStruct
    start = lax.axis_index("wide") * rows
    row_chain = lax.dynamic_slice_in_dim(chain, start, rows, 0)
    same = (row_chain[:, None] == chain[None, :]).astype(F32)
    gain_in, gain_out = gain_in[None], gain_out[None]
    sent, zn, cell_mask = call(
        project_kernel,
        [shape((devices, 2 * half, cols), BF), shape((width, cells), BF), shape((rows, cols), F32)],
        [
            pltpu.VMEM(pair.shape, BF),
            pltpu.VMEM((1, residues), jnp.int32),
            pltpu.VMEM(gain_in.shape, F32),
            pltpu.VMEM(w_proj.shape, BF),
            pltpu.SemaphoreType.DMA((3,)),
            pltpu.SemaphoreType.DMA((rows,)),
        ],
        name="project",
        space=pltpu.HBM,
        mib=56,
    )(pair, mask[None], gain_in, w_proj)
    got = swap(sent)
    factor, gate, t = call(
        gate_kernel,
        [shape((4 * hidden, cells), BF), shape((rows, cols, width), F32), shape((hidden, cells), BF)],
        flops=2 * 10**9,
        name="gate",
    )(zn, adjoint, cell_mask, same, w_proj, w_gate, chain_bias, gain_out, w_out)
    field = pltpu.VMEM((devices * half, cols), F32)
    channels = shape((own, residues, cols), BF)
    block = shape((devices, half, cols), BF)
    sent, left, right = call(mix_kernel, [block, channels, channels], [field] * 3, name="mix")(got)
    got = swap(sent)
    sent, xn = call(norm_kernel, [block, shape((hidden, cells), BF)], name="norm")(got, t, gain_out)
    got = swap(sent)
    output, d_logit, gate_part = call(
        output_kernel,
        [shape(pair.shape, BF), shape(pair.shape, BF), shape((width, width), F32)],
        flops=2 * 10**9,
        name="output",
    )(xn, gate, adjoint, zn, w_out)
    sent = call(
        unmix_kernel, [shape((devices, 2 * half, cols), BF)], [field] * 3, name="unmix"
    )(got, left, right)[0]
    got = swap(sent)
    d_cells, part = call(
        cells_kernel,
        [shape((4 * hidden, cells), BF), shape((width, 4 * hidden + width), BF)],
        name="cells",
    )(got, factor, zn, gate_part)
    got = swap(part.reshape(devices, width // devices, -1))
    d_pair = call(pair_kernel, [shape(pair.shape, BF)], flops=2 * 10**9, name="pair")(
        d_cells, d_logit, pair, gain_in, w_proj, w_gate
    )[0]
    sent = call(
        functools.partial(sum_kernel, residues), [shape(got.shape, BF)], name="sum"
    )(got)[0]
    d_proj, d_gate = call(
        finish_kernel, [shape((width, 4 * hidden), F32), shape((width, width), F32)], name="finish"
    )(swap(sent))
    return (output, d_pair, d_proj, d_gate)


def per_device(pair, adjoint, mask, chain, gain_in, w_proj, w_gate, chain_bias, gain_out, w_out):
    rows, cols, width = pair.shape
    hidden = w_out.shape[0]
    n_wide = lax.axis_size("wide")
    n_narrow = lax.axis_size("narrow")
    if n_narrow == 1 and (rows, cols, width) == (8, 128, 128) and hidden == 8 * n_wide == 128:
        return small_blocks(
            pair, adjoint, mask, chain, gain_in, w_proj, w_gate, chain_bias, gain_out, w_out
        )
    residues = rows * n_wide
    devices = n_wide * n_narrow
    own = hidden // devices
    row_start = lax.axis_index("wide") * rows
    col_start = lax.axis_index("narrow") * cols
    mask_f = mask.astype(jnp.float32)
    row_mask = lax.dynamic_slice_in_dim(mask_f, row_start, rows, 0)
    col_mask = lax.dynamic_slice_in_dim(mask_f, col_start, cols, 0)
    cell_mask = (row_mask[:, None] * col_mask[None, :])[None]
    row_chain = lax.dynamic_slice_in_dim(chain, row_start, rows, 0)
    col_chain = lax.dynamic_slice_in_dim(chain, col_start, cols, 0)
    same = (row_chain[:, None] == col_chain[None, :])[:, :, None]
    zn_f, z_hat, z_rstd = normalize(pair.astype(jnp.float32), gain_in, -1)
    zn = zn_f.astype(jnp.bfloat16)
    proj_a = jnp.einsum(
        "ijc,ch->hij", zn, w_proj[:, : 2 * hidden], preferred_element_type=jnp.float32
    )
    proj_b = jnp.einsum(
        "ijc,ch->hij", zn, w_proj[:, 2 * hidden :], preferred_element_type=jnp.float32
    )
    a_lin = proj_a[:hidden]
    sig_a = jax.nn.sigmoid(proj_a[hidden:])
    b_lin = proj_b[:hidden]
    sig_b = jax.nn.sigmoid(proj_b[hidden:])
    left_t = (cell_mask * sig_a * a_lin).astype(jnp.bfloat16)
    right_t = (cell_mask * sig_b * b_lin).astype(jnp.bfloat16)
    pairs = jnp.concatenate(
        [left_t.reshape(devices, own, rows, cols), right_t.reshape(devices, own, rows, cols)], 1
    )
    pairs = gather_cells(swap(pairs), n_wide, n_narrow)
    left_c, right_c = pairs[:own], pairs[own:]
    mixed_c = jnp.einsum("hik,hjk->hij", left_c, right_c, preferred_element_type=jnp.float32)
    mixed_t = swap(split_cells(mixed_c.astype(jnp.bfloat16), n_wide, n_narrow))
    mixed_t = mixed_t.reshape(hidden, rows, cols).astype(jnp.float32)
    xn_f, x_hat, x_rstd = normalize(mixed_t, gain_out[:, None, None], 0)
    xn = xn_f.astype(jnp.bfloat16)
    proj_out = jnp.einsum("hij,hc->ijc", xn, w_out, preferred_element_type=jnp.float32)
    logits = jnp.dot(zn, w_gate, preferred_element_type=jnp.float32) + jnp.where(
        same, chain_bias[1], chain_bias[0]
    )
    gate = jax.nn.sigmoid(logits)
    output = (gate * proj_out).astype(jnp.bfloat16)
    adj = adjoint.astype(jnp.float32)
    d_out = (adj * gate).astype(jnp.bfloat16)
    d_logit = (adj * proj_out * gate * (1.0 - gate)).astype(jnp.bfloat16)
    d_xn = jnp.einsum("ijc,hc->hij", d_out, w_out, preferred_element_type=jnp.float32)
    d_mixed_t = norm_back(d_xn * gain_out[:, None, None], x_hat, x_rstd, 0).astype(jnp.bfloat16)
    d_mixed_c = gather_cells(swap(d_mixed_t.reshape(devices, own, rows, cols)), n_wide, n_narrow)
    d_left_c = jnp.einsum("hij,hjk->hik", d_mixed_c, right_c, preferred_element_type=jnp.float32)
    d_right_c = jnp.einsum("hij,hik->hjk", d_mixed_c, left_c, preferred_element_type=jnp.float32)
    back = jnp.concatenate([d_left_c.astype(jnp.bfloat16), d_right_c.astype(jnp.bfloat16)], 0)
    back = swap(split_cells(back, n_wide, n_narrow))
    d_left = back[:, :own].reshape(hidden, rows, cols).astype(jnp.float32)
    d_right = back[:, own:].reshape(hidden, rows, cols).astype(jnp.float32)
    d_cells_a = jnp.concatenate(
        [d_left * cell_mask * sig_a, d_left * cell_mask * a_lin * sig_a * (1.0 - sig_a)], 0
    ).astype(jnp.bfloat16)
    d_cells_b = jnp.concatenate(
        [d_right * cell_mask * sig_b, d_right * cell_mask * b_lin * sig_b * (1.0 - sig_b)], 0
    ).astype(jnp.bfloat16)
    d_zn = jnp.einsum(
        "hij,ch->ijc", d_cells_a, w_proj[:, : 2 * hidden], preferred_element_type=jnp.float32
    )
    d_zn = d_zn + jnp.einsum(
        "hij,ch->ijc", d_cells_b, w_proj[:, 2 * hidden :], preferred_element_type=jnp.float32
    )
    d_zn = d_zn + jnp.dot(d_logit, w_gate.T, preferred_element_type=jnp.float32)
    d_pair = norm_back(d_zn * gain_in, z_hat, z_rstd, -1).astype(jnp.bfloat16)
    proj_part = jnp.concatenate(
        [
            jnp.einsum("ijc,hij->ch", zn, d_cells_a, preferred_element_type=jnp.float32),
            jnp.einsum("ijc,hij->ch", zn, d_cells_b, preferred_element_type=jnp.float32),
        ],
        1,
    )
    flat_z = zn.reshape(-1, width)
    gate_part = jnp.dot(flat_z.T, d_logit.reshape(-1, width), preferred_element_type=jnp.float32)
    parts = jnp.concatenate([proj_part, gate_part], 1)
    chunk = width // devices
    mine = swap(parts.astype(jnp.bfloat16).reshape(devices, chunk, -1))
    mine = jnp.sum(mine.astype(jnp.float32), 0) / residues
    mine = mine.astype(jnp.bfloat16)
    total = swap(jnp.broadcast_to(mine, (devices,) + mine.shape)).reshape(width, -1)
    total = total.astype(jnp.float32)
    return (output, d_pair, total[:, : 4 * hidden], total[:, 4 * hidden :])


def solution(mesh):
    placed = (
        P(("groups", "wide"), "narrow", None),
        P(("groups", "wide"), "narrow", None),
        P("groups"),
        P("groups"),
        P(),
        P(),
        P(),
        P(),
        P(),
        P(),
    )
    return jax.shard_map(
        per_device,
        mesh=mesh,
        in_specs=placed,
        out_specs=(
            P(("groups", "wide"), "narrow", None),
            P(("groups", "wide"), "narrow", None),
            P("groups", None),
            P("groups", None),
        ),
        check_vma=False,
    )
```

```python
import functools

import jax
import jax.numpy as jnp
from jax import lax
from jax.experimental import pallas as pl
from jax.experimental.pallas import tpu as pltpu
from jax.sharding import PartitionSpec as P

EPS = 1e-05


def normalize(values, gain, axis):
    centre = values - jnp.mean(values, axis, keepdims=True)
    rstd = lax.rsqrt(jnp.mean(centre * centre, axis, keepdims=True) + EPS)
    hat = centre * rstd
    return (hat * gain, hat, rstd)


def norm_back(scaled, hat, rstd, axis):
    return rstd * (
        scaled
        - jnp.mean(scaled, axis, keepdims=True)
        - hat * jnp.mean(scaled * hat, axis, keepdims=True)
    )


def swap(blocks):
    return lax.all_to_all(blocks, ("wide", "narrow"), split_axis=0, concat_axis=0, tiled=True)


def gather_cells(blocks, n_wide, n_narrow):
    _, own, rows, cols = blocks.shape
    shaped = blocks.reshape(n_wide, n_narrow, own, rows, cols)
    return jnp.transpose(shaped, (2, 0, 3, 1, 4)).reshape(own, n_wide * rows, n_narrow * cols)


def split_cells(field, n_wide, n_narrow):
    own, rows, cols = field.shape
    shaped = field.reshape(own, n_wide, rows // n_wide, n_narrow, cols // n_narrow)
    moved = jnp.transpose(shaped, (1, 3, 0, 2, 4))
    return moved.reshape(n_wide * n_narrow, own, rows // n_wide, cols // n_narrow)


BF = jnp.bfloat16
F32 = jnp.float32


def dot(a, b, over=((1,), (0,))):
    return lax.dot_general(a, b, (over, ((), ())), preferred_element_type=F32)


def column(row):
    return jnp.broadcast_to(row, (row.shape[1], row.shape[1])).T


def centred(x):
    centre = x - jnp.mean(x, 0, keepdims=True)
    rstd = lax.rsqrt(jnp.mean(centre * centre, 0, keepdims=True) + EPS)
    return centre * rstd, rstd


def back_t(scaled, hat, rstd):
    inner = hat * jnp.mean(scaled * hat, 0, keepdims=True)
    return rstd * (scaled - jnp.mean(scaled, 0, keepdims=True) - inner)


def two_rows(first, second, devices):
    own, cols = first.shape[0] // devices, first.shape[1]
    shape = (devices, own, cols)
    return jnp.concatenate([first.reshape(shape), second.reshape(shape)], 1).astype(BF)


def apart(block, devices):
    wide = block.astype(F32)
    own, cols = wide.shape[1] // 2, wide.shape[2]
    return [wide[:, at * own : (at + 1) * own].reshape(devices * own, cols) for at in range(2)]


def project_kernel(
    pair_hbm, mask_hbm, gain_hbm, w_hbm, sent_ref, zn_ref, mask_ref,
    pair_ref, mask_v, gain_ref, w_ref, sems,
):
    devices, depth, _ = sent_ref.shape
    rows, cols, width = pair_ref.shape
    start = lax.axis_index("wide") * rows
    copies = [
        pltpu.make_async_copy(gain_hbm, gain_ref, sems.at[0]),
        pltpu.make_async_copy(w_hbm, w_ref, sems.at[1]),
        pltpu.make_async_copy(mask_hbm, mask_v, sems.at[2]),
        pltpu.make_async_copy(pair_hbm, pair_ref, sems.at[3]),
    ]
    for copy in copies:
        copy.start()
    for copy in copies:
        copy.wait()
    mask_f = mask_v[...].astype(F32)
    shape = (rows, mask_f.shape[1])
    lane = lax.broadcasted_iota(jnp.int32, shape, 1)
    own = lane == start + lax.broadcasted_iota(jnp.int32, shape, 0)
    mask_ref[...] = mask_f * jnp.sum(jnp.where(own, mask_f, 0.0), 1, keepdims=True)
    gain = column(gain_ref[...])
    weights = w_ref[...].astype(F32).T.astype(BF)
    hidden = weights.shape[0] // 4
    half = depth // 2
    for two in range(rows // 2):
        pieces = []
        for row in (2 * two, 2 * two + 1):
            hat, _ = centred(pair_ref[row].astype(F32).T)
            zn = (hat * gain).astype(BF)
            zn_ref[:, row * cols : (row + 1) * cols] = zn
            proj = dot(weights, zn)
            mask = mask_ref[row : row + 1, :]
            left = mask * jax.nn.sigmoid(proj[hidden : 2 * hidden]) * proj[:hidden]
            right = mask * jax.nn.sigmoid(proj[3 * hidden :]) * proj[2 * hidden : 3 * hidden]
            pieces.append((left, right))
        at = two * 16
        sent_ref[:, at : at + 16, :] = two_rows(pieces[0][0], pieces[1][0], devices)
        sent_ref[:, half + at : half + at + 16, :] = two_rows(pieces[0][1], pieces[1][1], devices)


def gate_kernel(
    zn_ref, adj_ref, mask_ref, same_ref, w_ref, w_gate_ref, bias_ref, gain_ref, w_out_ref,
    factor_ref, gate_ref, t_ref,
):
    rows, cols, width = adj_ref.shape
    weights = w_ref[...].astype(F32).T.astype(BF)
    hidden = weights.shape[0] // 4
    w_gate = w_gate_ref[...].astype(F32).T.astype(BF)
    across, within = column(bias_ref[0:1, :]), column(bias_ref[1:2, :])
    gain = column(gain_ref[...])
    for row in range(rows):
        lanes = slice(row * cols, (row + 1) * cols)
        zn = zn_ref[:, lanes]
        proj = dot(weights, zn)
        mask = mask_ref[row : row + 1, :]
        for side in range(2):
            lin = proj[2 * side * hidden : (2 * side + 1) * hidden]
            sig = jax.nn.sigmoid(proj[(2 * side + 1) * hidden : (2 * side + 2) * hidden])
            factor_ref[2 * side * hidden : (2 * side + 1) * hidden, lanes] = (mask * sig).astype(BF)
            factor_ref[(2 * side + 1) * hidden : (2 * side + 2) * hidden, lanes] = (
                mask * lin * sig * (1.0 - sig)
            ).astype(BF)
        bias = jnp.where(same_ref[row : row + 1, :] > 0.5, within, across)
        gate = jax.nn.sigmoid(dot(w_gate, zn) + bias).T
        gate_ref[row] = gate
        d_out = (adj_ref[row].astype(F32) * gate).astype(BF)
        t_ref[:, lanes] = (dot(w_out_ref[...], d_out, ((1,), (1,))) * gain).astype(BF)


def mix_kernel(got_ref, sent_ref, left_ref, right_ref, left_s, right_s, out_s):
    devices, depth, cols = got_ref.shape
    own = left_ref.shape[0]
    half = depth // 2
    count = devices * half // own
    left_s[...] = got_ref[:, :half, :].astype(F32).reshape(devices * half, cols)
    right_s[...] = got_ref[:, half:, :].astype(F32).reshape(devices * half, cols)
    for h in range(own):
        left = left_s[pl.ds(h, count, stride=own), :].astype(BF)
        right = right_s[pl.ds(h, count, stride=own), :].astype(BF)
        left_ref[h] = left
        right_ref[h] = right
        out_s[pl.ds(h, count, stride=own), :] = dot(left, right, ((1,), (1,)))
    sent_ref[...] = out_s[...].reshape(devices, half, cols).astype(BF)


def norm_kernel(got_ref, t_ref, gain_ref, sent_ref, xn_ref):
    devices, depth, cols = got_ref.shape
    gain = column(gain_ref[...])
    for two in range(depth // 16):
        pieces = []
        for part, mixed in enumerate(apart(got_ref[:, two * 16 : two * 16 + 16, :], devices)):
            row = 2 * two + part
            lanes = slice(row * cols, (row + 1) * cols)
            hat, rstd = centred(mixed)
            xn_ref[:, lanes] = (hat * gain).astype(BF)
            pieces.append(back_t(t_ref[:, lanes].astype(F32), hat, rstd))
        sent_ref[:, two * 16 : two * 16 + 16, :] = two_rows(*pieces, devices)


def output_kernel(
    xn_ref, gate_ref, adj_ref, zn_ref, w_out_ref, output_ref, d_logit_ref, part_ref
):
    rows, cols, width = adj_ref.shape
    total = None
    for row in range(rows):
        lanes = slice(row * cols, (row + 1) * cols)
        xn = xn_ref[:, lanes].astype(F32).T.astype(BF)
        proj_out = dot(xn, w_out_ref[...])
        gate = gate_ref[row]
        output_ref[row] = (gate * proj_out).astype(BF)
        d_logit = (adj_ref[row].astype(F32) * proj_out * gate * (1.0 - gate)).astype(BF)
        d_logit_ref[row] = d_logit
        term = dot(zn_ref[:, lanes], d_logit)
        total = term if total is None else total + term
    part_ref[...] = total


def unmix_kernel(got_ref, left_ref, right_ref, sent_ref, in_s, left_s, right_s):
    devices, half, cols = got_ref.shape
    own = left_ref.shape[0]
    count = devices * half // own
    in_s[...] = got_ref[...].astype(F32).reshape(devices * half, cols)
    for h in range(own):
        grad = in_s[pl.ds(h, count, stride=own), :]
        left_s[pl.ds(h, count, stride=own), :] = dot(grad.astype(BF), right_ref[h])
        right_s[pl.ds(h, count, stride=own), :] = dot(grad.T.astype(BF), left_ref[h])
    sent_ref[:, :half, :] = left_s[...].reshape(devices, half, cols).astype(BF)
    sent_ref[:, half:, :] = right_s[...].reshape(devices, half, cols).astype(BF)


def cells_kernel(got_ref, factor_ref, zn_ref, gate_part_ref, cells_ref, part_ref):
    devices, depth, cols = got_ref.shape
    half = depth // 2
    hidden = factor_ref.shape[0] // 4
    for side in range(2):
        for two in range(half // 16):
            at = side * half + two * 16
            for part, grad in enumerate(apart(got_ref[:, at : at + 16, :], devices)):
                row = 2 * two + part
                lanes = slice(row * cols, (row + 1) * cols)
                for kind in (2 * side, 2 * side + 1):
                    place = slice(kind * hidden, (kind + 1) * hidden)
                    cells_ref[place, lanes] = (grad * factor_ref[place, lanes].astype(F32)).astype(BF)
    total = dot(zn_ref[...], cells_ref[...], ((1,), (1,)))
    part_ref[:, : 4 * hidden] = total.astype(BF)
    part_ref[:, 4 * hidden :] = gate_part_ref[...].astype(BF)


def pair_kernel(cells_ref, d_logit_ref, pair_ref, gain_ref, w_ref, w_gate_ref, d_pair_ref):
    rows, cols, width = pair_ref.shape
    gain = column(gain_ref[...])
    for row in range(rows):
        lanes = slice(row * cols, (row + 1) * cols)
        hat, rstd = centred(pair_ref[row].astype(F32).T)
        d_zn = dot(w_ref[...], cells_ref[:, lanes])
        d_zn = d_zn + dot(w_gate_ref[...], d_logit_ref[row], ((1,), (1,)))
        d_pair_ref[row] = back_t(d_zn * gain, hat, rstd).T.astype(BF)


def sum_kernel(residues, got_ref, sent_ref):
    total = jnp.sum(got_ref[...].astype(F32), 0) / residues
    sent_ref[...] = jnp.broadcast_to(total.astype(BF)[None], sent_ref.shape)


def finish_kernel(got_ref, proj_ref, gate_ref):
    devices, chunk, depth = got_ref.shape
    wide = proj_ref.shape[1]
    total = got_ref[...].astype(F32).reshape(devices * chunk, depth)
    proj_ref[...] = total[:, :wide]
    gate_ref[...] = total[:, wide:]


def call(kernel, outs, scratch=(), flops=0, name=None, space=pltpu.VMEM, mib=12):
    spec = pl.BlockSpec(memory_space=pltpu.VMEM)

    def run(*args):
        moved = sum(a.size * a.dtype.itemsize for a in (*args, *outs))
        return pl.pallas_call(
            kernel,
            out_shape=list(outs),
            in_specs=[pl.BlockSpec(memory_space=space)] * len(args),
            out_specs=[spec] * len(outs),
            scratch_shapes=list(scratch),
            compiler_params=pltpu.CompilerParams(vmem_limit_bytes=mib * 1024 * 1024),
            cost_estimate=pl.CostEstimate(
                flops=flops, bytes_accessed=moved, transcendentals=0
            ),
            name=name,
        )(*args)

    return run


def small_blocks(pair, adjoint, mask, chain, gain_in, w_proj, w_gate, chain_bias, gain_out, w_out):
    rows, cols, width = pair.shape
    hidden = w_out.shape[0]
    devices = lax.axis_size("wide")
    own = hidden // devices
    residues = rows * devices
    cells = rows * cols
    half = rows * own
    shape = jax.ShapeDtypeStruct
    start = lax.axis_index("wide") * rows
    row_chain = lax.dynamic_slice_in_dim(chain, start, rows, 0)
    same = (row_chain[:, None] == chain[None, :]).astype(F32)
    gain_in, gain_out = gain_in[None], gain_out[None]
    sent, zn, cell_mask = call(
        project_kernel,
        [shape((devices, 2 * half, cols), BF), shape((width, cells), BF), shape((rows, cols), F32)],
        [
            pltpu.VMEM(pair.shape, BF),
            pltpu.VMEM((1, residues), jnp.int32),
            pltpu.VMEM(gain_in.shape, F32),
            pltpu.VMEM(w_proj.shape, BF),
            pltpu.SemaphoreType.DMA((4,)),
        ],
        name="project",
        space=pltpu.HBM,
        mib=56,
    )(pair, mask[None], gain_in, w_proj)
    got = swap(sent)
    factor, gate, t = call(
        gate_kernel,
        [shape((4 * hidden, cells), BF), shape((rows, cols, width), F32), shape((hidden, cells), BF)],
        flops=2 * 10**9,
        name="gate",
    )(zn, adjoint, cell_mask, same, w_proj, w_gate, chain_bias, gain_out, w_out)
    field = pltpu.VMEM((devices * half, cols), F32)
    channels = shape((own, residues, cols), BF)
    block = shape((devices, half, cols), BF)
    got, t = lax.optimization_barrier((got, t))
    sent, left, right = call(mix_kernel, [block, channels, channels], [field] * 3, name="mix")(got)
    got = swap(sent)
    sent, xn = call(norm_kernel, [block, shape((hidden, cells), BF)], name="norm")(got, t, gain_out)
    got = swap(sent)
    output, d_logit, gate_part = call(
        output_kernel,
        [shape(pair.shape, BF), shape(pair.shape, BF), shape((width, width), F32)],
        flops=2 * 10**9,
        name="output",
    )(xn, gate, adjoint, zn, w_out)
    got, gate_part = lax.optimization_barrier((got, gate_part))
    sent = call(
        unmix_kernel, [shape((devices, 2 * half, cols), BF)], [field] * 3, name="unmix"
    )(got, left, right)[0]
    got = swap(sent)
    d_cells, part = call(
        cells_kernel,
        [shape((4 * hidden, cells), BF), shape((width, 4 * hidden + width), BF)],
        name="cells",
    )(got, factor, zn, gate_part)
    got = swap(part.reshape(devices, width // devices, -1))
    d_pair = call(pair_kernel, [shape(pair.shape, BF)], flops=2 * 10**9, name="pair")(
        d_cells, d_logit, pair, gain_in, w_proj, w_gate
    )[0]
    sent = call(
        functools.partial(sum_kernel, residues), [shape(got.shape, BF)], name="sum"
    )(got)[0]
    d_proj, d_gate = call(
        finish_kernel, [shape((width, 4 * hidden), F32), shape((width, width), F32)], name="finish"
    )(swap(sent))
    return (output, d_pair, d_proj, d_gate)


def per_device(pair, adjoint, mask, chain, gain_in, w_proj, w_gate, chain_bias, gain_out, w_out):
    rows, cols, width = pair.shape
    hidden = w_out.shape[0]
    n_wide = lax.axis_size("wide")
    n_narrow = lax.axis_size("narrow")
    if n_narrow == 1 and (rows, cols, width) == (8, 128, 128) and hidden == 8 * n_wide == 128:
        return small_blocks(
            pair, adjoint, mask, chain, gain_in, w_proj, w_gate, chain_bias, gain_out, w_out
        )
    residues = rows * n_wide
    devices = n_wide * n_narrow
    own = hidden // devices
    row_start = lax.axis_index("wide") * rows
    col_start = lax.axis_index("narrow") * cols
    mask_f = mask.astype(jnp.float32)
    row_mask = lax.dynamic_slice_in_dim(mask_f, row_start, rows, 0)
    col_mask = lax.dynamic_slice_in_dim(mask_f, col_start, cols, 0)
    cell_mask = (row_mask[:, None] * col_mask[None, :])[None]
    row_chain = lax.dynamic_slice_in_dim(chain, row_start, rows, 0)
    col_chain = lax.dynamic_slice_in_dim(chain, col_start, cols, 0)
    same = (row_chain[:, None] == col_chain[None, :])[:, :, None]
    zn_f, z_hat, z_rstd = normalize(pair.astype(jnp.float32), gain_in, -1)
    zn = zn_f.astype(jnp.bfloat16)
    proj_a = jnp.einsum(
        "ijc,ch->hij", zn, w_proj[:, : 2 * hidden], preferred_element_type=jnp.float32
    )
    proj_b = jnp.einsum(
        "ijc,ch->hij", zn, w_proj[:, 2 * hidden :], preferred_element_type=jnp.float32
    )
    a_lin = proj_a[:hidden]
    sig_a = jax.nn.sigmoid(proj_a[hidden:])
    b_lin = proj_b[:hidden]
    sig_b = jax.nn.sigmoid(proj_b[hidden:])
    left_t = (cell_mask * sig_a * a_lin).astype(jnp.bfloat16)
    right_t = (cell_mask * sig_b * b_lin).astype(jnp.bfloat16)
    pairs = jnp.concatenate(
        [left_t.reshape(devices, own, rows, cols), right_t.reshape(devices, own, rows, cols)], 1
    )
    pairs = gather_cells(swap(pairs), n_wide, n_narrow)
    left_c, right_c = pairs[:own], pairs[own:]
    mixed_c = jnp.einsum("hik,hjk->hij", left_c, right_c, preferred_element_type=jnp.float32)
    mixed_t = swap(split_cells(mixed_c.astype(jnp.bfloat16), n_wide, n_narrow))
    mixed_t = mixed_t.reshape(hidden, rows, cols).astype(jnp.float32)
    xn_f, x_hat, x_rstd = normalize(mixed_t, gain_out[:, None, None], 0)
    xn = xn_f.astype(jnp.bfloat16)
    proj_out = jnp.einsum("hij,hc->ijc", xn, w_out, preferred_element_type=jnp.float32)
    logits = jnp.dot(zn, w_gate, preferred_element_type=jnp.float32) + jnp.where(
        same, chain_bias[1], chain_bias[0]
    )
    gate = jax.nn.sigmoid(logits)
    output = (gate * proj_out).astype(jnp.bfloat16)
    adj = adjoint.astype(jnp.float32)
    d_out = (adj * gate).astype(jnp.bfloat16)
    d_logit = (adj * proj_out * gate * (1.0 - gate)).astype(jnp.bfloat16)
    d_xn = jnp.einsum("ijc,hc->hij", d_out, w_out, preferred_element_type=jnp.float32)
    d_mixed_t = norm_back(d_xn * gain_out[:, None, None], x_hat, x_rstd, 0).astype(jnp.bfloat16)
    d_mixed_c = gather_cells(swap(d_mixed_t.reshape(devices, own, rows, cols)), n_wide, n_narrow)
    d_left_c = jnp.einsum("hij,hjk->hik", d_mixed_c, right_c, preferred_element_type=jnp.float32)
    d_right_c = jnp.einsum("hij,hik->hjk", d_mixed_c, left_c, preferred_element_type=jnp.float32)
    back = jnp.concatenate([d_left_c.astype(jnp.bfloat16), d_right_c.astype(jnp.bfloat16)], 0)
    back = swap(split_cells(back, n_wide, n_narrow))
    d_left = back[:, :own].reshape(hidden, rows, cols).astype(jnp.float32)
    d_right = back[:, own:].reshape(hidden, rows, cols).astype(jnp.float32)
    d_cells_a = jnp.concatenate(
        [d_left * cell_mask * sig_a, d_left * cell_mask * a_lin * sig_a * (1.0 - sig_a)], 0
    ).astype(jnp.bfloat16)
    d_cells_b = jnp.concatenate(
        [d_right * cell_mask * sig_b, d_right * cell_mask * b_lin * sig_b * (1.0 - sig_b)], 0
    ).astype(jnp.bfloat16)
    d_zn = jnp.einsum(
        "hij,ch->ijc", d_cells_a, w_proj[:, : 2 * hidden], preferred_element_type=jnp.float32
    )
    d_zn = d_zn + jnp.einsum(
        "hij,ch->ijc", d_cells_b, w_proj[:, 2 * hidden :], preferred_element_type=jnp.float32
    )
    d_zn = d_zn + jnp.dot(d_logit, w_gate.T, preferred_element_type=jnp.float32)
    d_pair = norm_back(d_zn * gain_in, z_hat, z_rstd, -1).astype(jnp.bfloat16)
    proj_part = jnp.concatenate(
        [
            jnp.einsum("ijc,hij->ch", zn, d_cells_a, preferred_element_type=jnp.float32),
            jnp.einsum("ijc,hij->ch", zn, d_cells_b, preferred_element_type=jnp.float32),
        ],
        1,
    )
    flat_z = zn.reshape(-1, width)
    gate_part = jnp.dot(flat_z.T, d_logit.reshape(-1, width), preferred_element_type=jnp.float32)
    parts = jnp.concatenate([proj_part, gate_part], 1)
    chunk = width // devices
    mine = swap(parts.astype(jnp.bfloat16).reshape(devices, chunk, -1))
    mine = jnp.sum(mine.astype(jnp.float32), 0) / residues
    mine = mine.astype(jnp.bfloat16)
    total = swap(jnp.broadcast_to(mine, (devices,) + mine.shape)).reshape(width, -1)
    total = total.astype(jnp.float32)
    return (output, d_pair, total[:, : 4 * hidden], total[:, 4 * hidden :])


def solution(mesh):
    placed = (
        P(("groups", "wide"), "narrow", None),
        P(("groups", "wide"), "narrow", None),
        P("groups"),
        P("groups"),
        P(),
        P(),
        P(),
        P(),
        P(),
        P(),
    )
    return jax.shard_map(
        per_device,
        mesh=mesh,
        in_specs=placed,
        out_specs=(
            P(("groups", "wide"), "narrow", None),
            P(("groups", "wide"), "narrow", None),
            P("groups", None),
            P("groups", None),
        ),
        check_vma=False,
    )
```

```python
import functools

import jax
import jax.numpy as jnp
from jax import lax
from jax.experimental import pallas as pl
from jax.experimental.pallas import tpu as pltpu
from jax.sharding import PartitionSpec as P

EPS = 1e-05


def normalize(values, gain, axis):
    centre = values - jnp.mean(values, axis, keepdims=True)
    rstd = lax.rsqrt(jnp.mean(centre * centre, axis, keepdims=True) + EPS)
    hat = centre * rstd
    return (hat * gain, hat, rstd)


def norm_back(scaled, hat, rstd, axis):
    return rstd * (
        scaled
        - jnp.mean(scaled, axis, keepdims=True)
        - hat * jnp.mean(scaled * hat, axis, keepdims=True)
    )


def swap(blocks):
    return lax.all_to_all(blocks, ("wide", "narrow"), split_axis=0, concat_axis=0, tiled=True)


def gather_cells(blocks, n_wide, n_narrow):
    _, own, rows, cols = blocks.shape
    shaped = blocks.reshape(n_wide, n_narrow, own, rows, cols)
    return jnp.transpose(shaped, (2, 0, 3, 1, 4)).reshape(own, n_wide * rows, n_narrow * cols)


def split_cells(field, n_wide, n_narrow):
    own, rows, cols = field.shape
    shaped = field.reshape(own, n_wide, rows // n_wide, n_narrow, cols // n_narrow)
    moved = jnp.transpose(shaped, (1, 3, 0, 2, 4))
    return moved.reshape(n_wide * n_narrow, own, rows // n_wide, cols // n_narrow)


BF = jnp.bfloat16
F32 = jnp.float32


def dot(a, b, over=((1,), (0,))):
    return lax.dot_general(a, b, (over, ((), ())), preferred_element_type=F32)


def column(row):
    return jnp.broadcast_to(row, (row.shape[1], row.shape[1])).T


def centred(x):
    centre = x - jnp.mean(x, 0, keepdims=True)
    rstd = lax.rsqrt(jnp.mean(centre * centre, 0, keepdims=True) + EPS)
    return centre * rstd, rstd


def back_t(scaled, hat, rstd):
    inner = hat * jnp.mean(scaled * hat, 0, keepdims=True)
    return rstd * (scaled - jnp.mean(scaled, 0, keepdims=True) - inner)


def two_rows(first, second, devices):
    own, cols = first.shape[0] // devices, first.shape[1]
    shape = (devices, own, cols)
    return jnp.concatenate([first.reshape(shape), second.reshape(shape)], 1).astype(BF)


def apart(block, devices):
    wide = block.astype(F32)
    own, cols = wide.shape[1] // 2, wide.shape[2]
    return [wide[:, at * own : (at + 1) * own].reshape(devices * own, cols) for at in range(2)]


def project_kernel(
    pair_hbm, mask_hbm, gain_hbm, w_hbm, sent_ref, zn_ref, mask_ref,
    pair_ref, mask_v, gain_ref, w_ref, sems,
):
    devices, depth, _ = sent_ref.shape
    rows, cols, width = pair_ref.shape
    start = lax.axis_index("wide") * rows
    copies = [
        pltpu.make_async_copy(gain_hbm, gain_ref, sems.at[0]),
        pltpu.make_async_copy(w_hbm, w_ref, sems.at[1]),
        pltpu.make_async_copy(mask_hbm, mask_v, sems.at[2]),
        pltpu.make_async_copy(pair_hbm, pair_ref, sems.at[3]),
    ]
    for copy in copies:
        copy.start()
    for copy in copies:
        copy.wait()
    mask_f = mask_v[...].astype(F32)
    shape = (rows, mask_f.shape[1])
    lane = lax.broadcasted_iota(jnp.int32, shape, 1)
    own = lane == start + lax.broadcasted_iota(jnp.int32, shape, 0)
    mask_ref[...] = mask_f * jnp.sum(jnp.where(own, mask_f, 0.0), 1, keepdims=True)
    gain = column(gain_ref[...])
    weights = w_ref[...].astype(F32).T.astype(BF)
    hidden = weights.shape[0] // 4
    half = depth // 2
    for two in range(rows // 2):
        pieces = []
        for row in (2 * two, 2 * two + 1):
            hat, _ = centred(pair_ref[row].astype(F32).T)
            zn = (hat * gain).astype(BF)
            zn_ref[:, row * cols : (row + 1) * cols] = zn
            proj = dot(weights, zn)
            mask = mask_ref[row : row + 1, :]
            left = mask * jax.nn.sigmoid(proj[hidden : 2 * hidden]) * proj[:hidden]
            right = mask * jax.nn.sigmoid(proj[3 * hidden :]) * proj[2 * hidden : 3 * hidden]
            pieces.append((left, right))
        at = two * 16
        sent_ref[:, at : at + 16, :] = two_rows(pieces[0][0], pieces[1][0], devices)
        sent_ref[:, half + at : half + at + 16, :] = two_rows(pieces[0][1], pieces[1][1], devices)


def gate_kernel(
    zn_ref, adj_ref, mask_ref, same_ref, w_ref, w_gate_ref, bias_ref, gain_ref, w_out_ref,
    factor_ref, gate_ref, t_ref,
):
    rows, cols, width = adj_ref.shape
    weights = w_ref[...].astype(F32).T.astype(BF)
    hidden = weights.shape[0] // 4
    w_gate = w_gate_ref[...].astype(F32).T.astype(BF)
    across, within = column(bias_ref[0:1, :]), column(bias_ref[1:2, :])
    gain = column(gain_ref[...])
    for row in range(rows):
        lanes = slice(row * cols, (row + 1) * cols)
        zn = zn_ref[:, lanes]
        proj = dot(weights, zn)
        mask = mask_ref[row : row + 1, :]
        for side in range(2):
            lin = proj[2 * side * hidden : (2 * side + 1) * hidden]
            sig = jax.nn.sigmoid(proj[(2 * side + 1) * hidden : (2 * side + 2) * hidden])
            factor_ref[2 * side * hidden : (2 * side + 1) * hidden, lanes] = (mask * sig).astype(BF)
            factor_ref[(2 * side + 1) * hidden : (2 * side + 2) * hidden, lanes] = (
                mask * lin * sig * (1.0 - sig)
            ).astype(BF)
        bias = jnp.where(same_ref[row : row + 1, :] > 0.5, within, across)
        gate = jax.nn.sigmoid(dot(w_gate, zn) + bias).T
        gate_ref[row] = gate
        d_out = (adj_ref[row].astype(F32) * gate).astype(BF)
        t_ref[:, lanes] = (dot(w_out_ref[...], d_out, ((1,), (1,))) * gain).astype(BF)


def mix_kernel(got_ref, sent_ref, left_ref, right_ref, left_s, right_s, out_s):
    devices, depth, cols = got_ref.shape
    own = left_ref.shape[0]
    half = depth // 2
    count = devices * half // own
    left_s[...] = got_ref[:, :half, :].astype(F32).reshape(devices * half, cols)
    right_s[...] = got_ref[:, half:, :].astype(F32).reshape(devices * half, cols)
    for h in range(own):
        left = left_s[pl.ds(h, count, stride=own), :].astype(BF)
        right = right_s[pl.ds(h, count, stride=own), :].astype(BF)
        left_ref[h] = left
        right_ref[h] = right
        out_s[pl.ds(h, count, stride=own), :] = dot(left, right, ((1,), (1,)))
    sent_ref[...] = out_s[...].reshape(devices, half, cols).astype(BF)


def norm_kernel(got_ref, t_ref, gain_ref, sent_ref, xn_ref):
    devices, depth, cols = got_ref.shape
    gain = column(gain_ref[...])
    for two in range(depth // 16):
        pieces = []
        for part, mixed in enumerate(apart(got_ref[:, two * 16 : two * 16 + 16, :], devices)):
            row = 2 * two + part
            lanes = slice(row * cols, (row + 1) * cols)
            hat, rstd = centred(mixed)
            xn_ref[:, lanes] = (hat * gain).astype(BF)
            pieces.append(back_t(t_ref[:, lanes].astype(F32), hat, rstd))
        sent_ref[:, two * 16 : two * 16 + 16, :] = two_rows(*pieces, devices)


def output_kernel(
    xn_ref, gate_ref, adj_ref, zn_ref, w_out_ref, output_ref, d_logit_ref, part_ref
):
    rows, cols, width = adj_ref.shape
    total = None
    for row in range(rows):
        lanes = slice(row * cols, (row + 1) * cols)
        xn = xn_ref[:, lanes].astype(F32).T.astype(BF)
        proj_out = dot(xn, w_out_ref[...])
        gate = gate_ref[row]
        output_ref[row] = (gate * proj_out).astype(BF)
        d_logit = (adj_ref[row].astype(F32) * proj_out * gate * (1.0 - gate)).astype(BF)
        d_logit_ref[row] = d_logit
        term = dot(zn_ref[:, lanes], d_logit)
        total = term if total is None else total + term
    part_ref[...] = total


def unmix_kernel(got_ref, left_ref, right_ref, sent_ref, in_s, left_s, right_s):
    devices, half, cols = got_ref.shape
    own = left_ref.shape[0]
    count = devices * half // own
    in_s[...] = got_ref[...].astype(F32).reshape(devices * half, cols)
    for h in range(own):
        grad = in_s[pl.ds(h, count, stride=own), :]
        left_s[pl.ds(h, count, stride=own), :] = dot(grad.astype(BF), right_ref[h])
        right_s[pl.ds(h, count, stride=own), :] = dot(grad.T.astype(BF), left_ref[h])
    sent_ref[:, :half, :] = left_s[...].reshape(devices, half, cols).astype(BF)
    sent_ref[:, half:, :] = right_s[...].reshape(devices, half, cols).astype(BF)


def cells_kernel(got_ref, factor_ref, zn_ref, gate_part_ref, cells_ref, part_ref):
    devices, depth, cols = got_ref.shape
    half = depth // 2
    hidden = factor_ref.shape[0] // 4
    for side in range(2):
        for two in range(half // 16):
            at = side * half + two * 16
            for part, grad in enumerate(apart(got_ref[:, at : at + 16, :], devices)):
                row = 2 * two + part
                lanes = slice(row * cols, (row + 1) * cols)
                for kind in (2 * side, 2 * side + 1):
                    place = slice(kind * hidden, (kind + 1) * hidden)
                    cells_ref[place, lanes] = (grad * factor_ref[place, lanes].astype(F32)).astype(BF)
    total = dot(zn_ref[...], cells_ref[...], ((1,), (1,)))
    part_ref[:, : 4 * hidden] = total.astype(BF)
    part_ref[:, 4 * hidden :] = gate_part_ref[...].astype(BF)


def pair_kernel(cells_ref, d_logit_ref, pair_ref, gain_ref, w_ref, w_gate_ref, d_pair_ref):
    rows, cols, width = pair_ref.shape
    gain = column(gain_ref[...])
    for row in range(rows):
        lanes = slice(row * cols, (row + 1) * cols)
        hat, rstd = centred(pair_ref[row].astype(F32).T)
        d_zn = dot(w_ref[...], cells_ref[:, lanes])
        d_zn = d_zn + dot(w_gate_ref[...], d_logit_ref[row], ((1,), (1,)))
        d_pair_ref[row] = back_t(d_zn * gain, hat, rstd).T.astype(BF)


def sum_kernel(residues, got_ref, sent_ref):
    total = jnp.sum(got_ref[...].astype(F32), 0) / residues
    sent_ref[...] = jnp.broadcast_to(total.astype(BF)[None], sent_ref.shape)


def finish_kernel(got_ref, proj_ref, gate_ref):
    devices, chunk, depth = got_ref.shape
    wide = proj_ref.shape[1]
    total = got_ref[...].astype(F32).reshape(devices * chunk, depth)
    proj_ref[...] = total[:, :wide]
    gate_ref[...] = total[:, wide:]


def call(kernel, outs, scratch=(), flops=0, name=None, space=pltpu.VMEM, mib=12):
    spec = pl.BlockSpec(memory_space=pltpu.VMEM)

    def run(*args):
        moved = sum(a.size * a.dtype.itemsize for a in (*args, *outs))
        return pl.pallas_call(
            kernel,
            out_shape=list(outs),
            in_specs=[pl.BlockSpec(memory_space=space)] * len(args),
            out_specs=[spec] * len(outs),
            scratch_shapes=list(scratch),
            compiler_params=pltpu.CompilerParams(vmem_limit_bytes=mib * 1024 * 1024),
            cost_estimate=pl.CostEstimate(
                flops=flops, bytes_accessed=moved, transcendentals=0
            ),
            name=name,
        )(*args)

    return run


def small_blocks(pair, adjoint, mask, chain, gain_in, w_proj, w_gate, chain_bias, gain_out, w_out):
    rows, cols, width = pair.shape
    hidden = w_out.shape[0]
    devices = lax.axis_size("wide")
    own = hidden // devices
    residues = rows * devices
    cells = rows * cols
    half = rows * own
    shape = jax.ShapeDtypeStruct
    start = lax.axis_index("wide") * rows
    row_chain = lax.dynamic_slice_in_dim(chain, start, rows, 0)
    same = (row_chain[:, None] == chain[None, :]).astype(F32)
    gain_in, gain_out = gain_in[None], gain_out[None]
    sent, zn, cell_mask = call(
        project_kernel,
        [shape((devices, 2 * half, cols), BF), shape((width, cells), BF), shape((rows, cols), F32)],
        [
            pltpu.VMEM(pair.shape, BF),
            pltpu.VMEM((1, residues), jnp.int32),
            pltpu.VMEM(gain_in.shape, F32),
            pltpu.VMEM(w_proj.shape, BF),
            pltpu.SemaphoreType.DMA((4,)),
        ],
        name="project",
        space=pltpu.HBM,
        mib=56,
    )(pair, mask[None], gain_in, w_proj)
    got = swap(sent)
    factor, gate, t = call(
        gate_kernel,
        [shape((4 * hidden, cells), BF), shape((rows, cols, width), F32), shape((hidden, cells), BF)],
        flops=2 * 10**9,
        name="gate",
    )(zn, adjoint, cell_mask, same, w_proj, w_gate, chain_bias, gain_out, w_out)
    field = pltpu.VMEM((devices * half, cols), F32)
    channels = shape((own, residues, cols), BF)
    block = shape((devices, half, cols), BF)
    got, t = lax.optimization_barrier((got, t))
    sent, left, right = call(mix_kernel, [block, channels, channels], [field] * 3, name="mix")(got)
    got = swap(sent)
    sent, xn = call(norm_kernel, [block, shape((hidden, cells), BF)], name="norm")(got, t, gain_out)
    got = swap(sent)
    output, d_logit, gate_part = call(
        output_kernel,
        [shape(pair.shape, BF), shape(pair.shape, BF), shape((width, width), F32)],
        flops=2 * 10**9,
        name="output",
    )(xn, gate, adjoint, zn, w_out)
    got, gate_part = lax.optimization_barrier((got, gate_part))
    sent = call(
        unmix_kernel, [shape((devices, 2 * half, cols), BF)], [field] * 3, name="unmix"
    )(got, left, right)[0]
    got = swap(sent)
    d_cells, part = call(
        cells_kernel,
        [shape((4 * hidden, cells), BF), shape((width, 4 * hidden + width), BF)],
        name="cells",
    )(got, factor, zn, gate_part)
    got = swap(part.reshape(devices, width // devices, -1))
    d_pair = call(pair_kernel, [shape(pair.shape, BF)], flops=2 * 10**9, name="pair")(
        d_cells, d_logit, pair, gain_in, w_proj, w_gate
    )[0]
    got, d_pair = lax.optimization_barrier((got, d_pair))
    sent = call(
        functools.partial(sum_kernel, residues), [shape(got.shape, BF)], name="sum"
    )(got)[0]
    d_proj, d_gate = call(
        finish_kernel, [shape((width, 4 * hidden), F32), shape((width, width), F32)], name="finish"
    )(swap(sent))
    return (output, d_pair, d_proj, d_gate)


def per_device(pair, adjoint, mask, chain, gain_in, w_proj, w_gate, chain_bias, gain_out, w_out):
    rows, cols, width = pair.shape
    hidden = w_out.shape[0]
    n_wide = lax.axis_size("wide")
    n_narrow = lax.axis_size("narrow")
    if n_narrow == 1 and (rows, cols, width) == (8, 128, 128) and hidden == 8 * n_wide == 128:
        return small_blocks(
            pair, adjoint, mask, chain, gain_in, w_proj, w_gate, chain_bias, gain_out, w_out
        )
    residues = rows * n_wide
    devices = n_wide * n_narrow
    own = hidden // devices
    row_start = lax.axis_index("wide") * rows
    col_start = lax.axis_index("narrow") * cols
    mask_f = mask.astype(jnp.float32)
    row_mask = lax.dynamic_slice_in_dim(mask_f, row_start, rows, 0)
    col_mask = lax.dynamic_slice_in_dim(mask_f, col_start, cols, 0)
    cell_mask = (row_mask[:, None] * col_mask[None, :])[None]
    row_chain = lax.dynamic_slice_in_dim(chain, row_start, rows, 0)
    col_chain = lax.dynamic_slice_in_dim(chain, col_start, cols, 0)
    same = (row_chain[:, None] == col_chain[None, :])[:, :, None]
    zn_f, z_hat, z_rstd = normalize(pair.astype(jnp.float32), gain_in, -1)
    zn = zn_f.astype(jnp.bfloat16)
    proj_a = jnp.einsum(
        "ijc,ch->hij", zn, w_proj[:, : 2 * hidden], preferred_element_type=jnp.float32
    )
    proj_b = jnp.einsum(
        "ijc,ch->hij", zn, w_proj[:, 2 * hidden :], preferred_element_type=jnp.float32
    )
    a_lin = proj_a[:hidden]
    sig_a = jax.nn.sigmoid(proj_a[hidden:])
    b_lin = proj_b[:hidden]
    sig_b = jax.nn.sigmoid(proj_b[hidden:])
    left_t = (cell_mask * sig_a * a_lin).astype(jnp.bfloat16)
    right_t = (cell_mask * sig_b * b_lin).astype(jnp.bfloat16)
    pairs = jnp.concatenate(
        [left_t.reshape(devices, own, rows, cols), right_t.reshape(devices, own, rows, cols)], 1
    )
    pairs = gather_cells(swap(pairs), n_wide, n_narrow)
    left_c, right_c = pairs[:own], pairs[own:]
    mixed_c = jnp.einsum("hik,hjk->hij", left_c, right_c, preferred_element_type=jnp.float32)
    mixed_t = swap(split_cells(mixed_c.astype(jnp.bfloat16), n_wide, n_narrow))
    mixed_t = mixed_t.reshape(hidden, rows, cols).astype(jnp.float32)
    xn_f, x_hat, x_rstd = normalize(mixed_t, gain_out[:, None, None], 0)
    xn = xn_f.astype(jnp.bfloat16)
    proj_out = jnp.einsum("hij,hc->ijc", xn, w_out, preferred_element_type=jnp.float32)
    logits = jnp.dot(zn, w_gate, preferred_element_type=jnp.float32) + jnp.where(
        same, chain_bias[1], chain_bias[0]
    )
    gate = jax.nn.sigmoid(logits)
    output = (gate * proj_out).astype(jnp.bfloat16)
    adj = adjoint.astype(jnp.float32)
    d_out = (adj * gate).astype(jnp.bfloat16)
    d_logit = (adj * proj_out * gate * (1.0 - gate)).astype(jnp.bfloat16)
    d_xn = jnp.einsum("ijc,hc->hij", d_out, w_out, preferred_element_type=jnp.float32)
    d_mixed_t = norm_back(d_xn * gain_out[:, None, None], x_hat, x_rstd, 0).astype(jnp.bfloat16)
    d_mixed_c = gather_cells(swap(d_mixed_t.reshape(devices, own, rows, cols)), n_wide, n_narrow)
    d_left_c = jnp.einsum("hij,hjk->hik", d_mixed_c, right_c, preferred_element_type=jnp.float32)
    d_right_c = jnp.einsum("hij,hik->hjk", d_mixed_c, left_c, preferred_element_type=jnp.float32)
    back = jnp.concatenate([d_left_c.astype(jnp.bfloat16), d_right_c.astype(jnp.bfloat16)], 0)
    back = swap(split_cells(back, n_wide, n_narrow))
    d_left = back[:, :own].reshape(hidden, rows, cols).astype(jnp.float32)
    d_right = back[:, own:].reshape(hidden, rows, cols).astype(jnp.float32)
    d_cells_a = jnp.concatenate(
        [d_left * cell_mask * sig_a, d_left * cell_mask * a_lin * sig_a * (1.0 - sig_a)], 0
    ).astype(jnp.bfloat16)
    d_cells_b = jnp.concatenate(
        [d_right * cell_mask * sig_b, d_right * cell_mask * b_lin * sig_b * (1.0 - sig_b)], 0
    ).astype(jnp.bfloat16)
    d_zn = jnp.einsum(
        "hij,ch->ijc", d_cells_a, w_proj[:, : 2 * hidden], preferred_element_type=jnp.float32
    )
    d_zn = d_zn + jnp.einsum(
        "hij,ch->ijc", d_cells_b, w_proj[:, 2 * hidden :], preferred_element_type=jnp.float32
    )
    d_zn = d_zn + jnp.dot(d_logit, w_gate.T, preferred_element_type=jnp.float32)
    d_pair = norm_back(d_zn * gain_in, z_hat, z_rstd, -1).astype(jnp.bfloat16)
    proj_part = jnp.concatenate(
        [
            jnp.einsum("ijc,hij->ch", zn, d_cells_a, preferred_element_type=jnp.float32),
            jnp.einsum("ijc,hij->ch", zn, d_cells_b, preferred_element_type=jnp.float32),
        ],
        1,
    )
    flat_z = zn.reshape(-1, width)
    gate_part = jnp.dot(flat_z.T, d_logit.reshape(-1, width), preferred_element_type=jnp.float32)
    parts = jnp.concatenate([proj_part, gate_part], 1)
    chunk = width // devices
    mine = swap(parts.astype(jnp.bfloat16).reshape(devices, chunk, -1))
    mine = jnp.sum(mine.astype(jnp.float32), 0) / residues
    mine = mine.astype(jnp.bfloat16)
    total = swap(jnp.broadcast_to(mine, (devices,) + mine.shape)).reshape(width, -1)
    total = total.astype(jnp.float32)
    return (output, d_pair, total[:, : 4 * hidden], total[:, 4 * hidden :])


def solution(mesh):
    placed = (
        P(("groups", "wide"), "narrow", None),
        P(("groups", "wide"), "narrow", None),
        P("groups"),
        P("groups"),
        P(),
        P(),
        P(),
        P(),
        P(),
        P(),
    )
    return jax.shard_map(
        per_device,
        mesh=mesh,
        in_specs=placed,
        out_specs=(
            P(("groups", "wide"), "narrow", None),
            P(("groups", "wide"), "narrow", None),
            P("groups", None),
            P("groups", None),
        ),
        check_vma=False,
    )
```

```python
import functools

import jax
import jax.numpy as jnp
from jax import lax
from jax.experimental import pallas as pl
from jax.experimental.pallas import tpu as pltpu
from jax.sharding import PartitionSpec as P

EPS = 1e-05


def normalize(values, gain, axis):
    centre = values - jnp.mean(values, axis, keepdims=True)
    rstd = lax.rsqrt(jnp.mean(centre * centre, axis, keepdims=True) + EPS)
    hat = centre * rstd
    return (hat * gain, hat, rstd)


def norm_back(scaled, hat, rstd, axis):
    return rstd * (
        scaled
        - jnp.mean(scaled, axis, keepdims=True)
        - hat * jnp.mean(scaled * hat, axis, keepdims=True)
    )


def swap(blocks):
    return lax.all_to_all(blocks, ("wide", "narrow"), split_axis=0, concat_axis=0, tiled=True)


def gather_cells(blocks, n_wide, n_narrow):
    _, own, rows, cols = blocks.shape
    shaped = blocks.reshape(n_wide, n_narrow, own, rows, cols)
    return jnp.transpose(shaped, (2, 0, 3, 1, 4)).reshape(own, n_wide * rows, n_narrow * cols)


def split_cells(field, n_wide, n_narrow):
    own, rows, cols = field.shape
    shaped = field.reshape(own, n_wide, rows // n_wide, n_narrow, cols // n_narrow)
    moved = jnp.transpose(shaped, (1, 3, 0, 2, 4))
    return moved.reshape(n_wide * n_narrow, own, rows // n_wide, cols // n_narrow)


BF = jnp.bfloat16
F32 = jnp.float32


def dot(a, b, over=((1,), (0,))):
    return lax.dot_general(a, b, (over, ((), ())), preferred_element_type=F32)


def column(row):
    return jnp.broadcast_to(row, (row.shape[1], row.shape[1])).T


def centred(x):
    centre = x - jnp.mean(x, 0, keepdims=True)
    rstd = lax.rsqrt(jnp.mean(centre * centre, 0, keepdims=True) + EPS)
    return centre * rstd, rstd


def back_t(scaled, hat, rstd):
    inner = hat * jnp.mean(scaled * hat, 0, keepdims=True)
    return rstd * (scaled - jnp.mean(scaled, 0, keepdims=True) - inner)


def two_rows(first, second, devices):
    own, cols = first.shape[0] // devices, first.shape[1]
    shape = (devices, own, cols)
    return jnp.concatenate([first.reshape(shape), second.reshape(shape)], 1).astype(BF)


def apart(block, devices):
    wide = block.astype(F32)
    own, cols = wide.shape[1] // 2, wide.shape[2]
    return [wide[:, at * own : (at + 1) * own].reshape(devices * own, cols) for at in range(2)]


def project_kernel(
    pair_hbm, mask_hbm, gain_hbm, w_hbm, sent_ref, zn_ref, mask_ref,
    pair_ref, mask_v, gain_ref, w_ref, sems,
):
    devices, depth, _ = sent_ref.shape
    rows, cols, width = pair_ref.shape
    start = lax.axis_index("wide") * rows
    copies = [
        pltpu.make_async_copy(gain_hbm, gain_ref, sems.at[0]),
        pltpu.make_async_copy(w_hbm, w_ref, sems.at[1]),
        pltpu.make_async_copy(mask_hbm, mask_v, sems.at[2]),
        pltpu.make_async_copy(pair_hbm, pair_ref, sems.at[3]),
    ]
    for copy in copies:
        copy.start()
    for copy in copies:
        copy.wait()
    mask_f = mask_v[...].astype(F32)
    shape = (rows, mask_f.shape[1])
    lane = lax.broadcasted_iota(jnp.int32, shape, 1)
    own = lane == start + lax.broadcasted_iota(jnp.int32, shape, 0)
    mask_ref[...] = mask_f * jnp.sum(jnp.where(own, mask_f, 0.0), 1, keepdims=True)
    gain = column(gain_ref[...])
    weights = w_ref[...].astype(F32).T.astype(BF)
    hidden = weights.shape[0] // 4
    half = depth // 2
    for two in range(rows // 2):
        pieces = []
        for row in (2 * two, 2 * two + 1):
            hat, _ = centred(pair_ref[row].astype(F32).T)
            zn = (hat * gain).astype(BF)
            zn_ref[:, row * cols : (row + 1) * cols] = zn
            proj = dot(weights, zn)
            mask = mask_ref[row : row + 1, :]
            left = mask * jax.nn.sigmoid(proj[hidden : 2 * hidden]) * proj[:hidden]
            right = mask * jax.nn.sigmoid(proj[3 * hidden :]) * proj[2 * hidden : 3 * hidden]
            pieces.append((left, right))
        at = two * 16
        sent_ref[:, at : at + 16, :] = two_rows(pieces[0][0], pieces[1][0], devices)
        sent_ref[:, half + at : half + at + 16, :] = two_rows(pieces[0][1], pieces[1][1], devices)


def gate_kernel(
    zn_ref, adj_ref, mask_ref, same_ref, w_ref, w_gate_ref, bias_ref, gain_ref, w_out_ref,
    factor_ref, gate_ref, t_ref,
):
    rows, cols, width = adj_ref.shape
    weights = w_ref[...].astype(F32).T.astype(BF)
    hidden = weights.shape[0] // 4
    w_gate = w_gate_ref[...].astype(F32).T.astype(BF)
    across, within = column(bias_ref[0:1, :]), column(bias_ref[1:2, :])
    gain = column(gain_ref[...])
    for row in range(rows):
        lanes = slice(row * cols, (row + 1) * cols)
        zn = zn_ref[:, lanes]
        proj = dot(weights, zn)
        mask = mask_ref[row : row + 1, :]
        for side in range(2):
            lin = proj[2 * side * hidden : (2 * side + 1) * hidden]
            sig = jax.nn.sigmoid(proj[(2 * side + 1) * hidden : (2 * side + 2) * hidden])
            factor_ref[2 * side * hidden : (2 * side + 1) * hidden, lanes] = (mask * sig).astype(BF)
            factor_ref[(2 * side + 1) * hidden : (2 * side + 2) * hidden, lanes] = (
                mask * lin * sig * (1.0 - sig)
            ).astype(BF)
        bias = jnp.where(same_ref[row : row + 1, :] > 0.5, within, across)
        gate = jax.nn.sigmoid(dot(w_gate, zn) + bias).T
        gate_ref[row] = gate
        d_out = (adj_ref[row].astype(F32) * gate).astype(BF)
        t_ref[:, lanes] = (dot(w_out_ref[...], d_out, ((1,), (1,))) * gain).astype(BF)


def mix_kernel(got_ref, sent_ref, left_ref, right_ref, left_s, right_s, out_s):
    devices, depth, cols = got_ref.shape
    own = left_ref.shape[0]
    half = depth // 2
    count = devices * half // own
    left_s[...] = got_ref[:, :half, :].astype(F32).reshape(devices * half, cols)
    right_s[...] = got_ref[:, half:, :].astype(F32).reshape(devices * half, cols)
    for h in range(own):
        left = left_s[pl.ds(h, count, stride=own), :].astype(BF)
        right = right_s[pl.ds(h, count, stride=own), :].astype(BF)
        left_ref[h] = left
        right_ref[h] = right
        out_s[pl.ds(h, count, stride=own), :] = dot(left, right, ((1,), (1,)))
    sent_ref[...] = out_s[...].reshape(devices, half, cols).astype(BF)


def norm_kernel(got_ref, t_ref, gain_ref, sent_ref, xn_ref):
    devices, depth, cols = got_ref.shape
    gain = column(gain_ref[...])
    for two in range(depth // 16):
        pieces = []
        for part, mixed in enumerate(apart(got_ref[:, two * 16 : two * 16 + 16, :], devices)):
            row = 2 * two + part
            lanes = slice(row * cols, (row + 1) * cols)
            hat, rstd = centred(mixed)
            xn_ref[:, lanes] = (hat * gain).astype(BF)
            pieces.append(back_t(t_ref[:, lanes].astype(F32), hat, rstd))
        sent_ref[:, two * 16 : two * 16 + 16, :] = two_rows(*pieces, devices)


def output_kernel(
    xn_ref, gate_ref, adj_ref, zn_ref, w_out_ref, output_ref, d_logit_ref, part_ref
):
    rows, cols, width = adj_ref.shape
    total = None
    for row in range(rows):
        lanes = slice(row * cols, (row + 1) * cols)
        xn = xn_ref[:, lanes].astype(F32).T.astype(BF)
        proj_out = dot(xn, w_out_ref[...])
        gate = gate_ref[row]
        output_ref[row] = (gate * proj_out).astype(BF)
        d_logit = (adj_ref[row].astype(F32) * proj_out * gate * (1.0 - gate)).astype(BF)
        d_logit_ref[row] = d_logit
        term = dot(zn_ref[:, lanes], d_logit)
        total = term if total is None else total + term
    part_ref[...] = total


def unmix_kernel(got_ref, left_ref, right_ref, sent_ref, in_s, left_s, right_s):
    devices, half, cols = got_ref.shape
    own = left_ref.shape[0]
    count = devices * half // own
    in_s[...] = got_ref[...].astype(F32).reshape(devices * half, cols)
    for h in range(own):
        grad = in_s[pl.ds(h, count, stride=own), :]
        left_s[pl.ds(h, count, stride=own), :] = dot(grad.astype(BF), right_ref[h])
        right_s[pl.ds(h, count, stride=own), :] = dot(grad.T.astype(BF), left_ref[h])
    sent_ref[:, :half, :] = left_s[...].reshape(devices, half, cols).astype(BF)
    sent_ref[:, half:, :] = right_s[...].reshape(devices, half, cols).astype(BF)


def cells_kernel(
    got_ref, factor_ref, zn_ref, gate_part_ref, w_ref, d_zn_ref, part_ref, cells_ref
):
    devices, depth, cols = got_ref.shape
    half = depth // 2
    hidden = factor_ref.shape[0] // 4
    for side in range(2):
        for two in range(half // 16):
            at = side * half + two * 16
            for part, grad in enumerate(apart(got_ref[:, at : at + 16, :], devices)):
                row = 2 * two + part
                lanes = slice(row * cols, (row + 1) * cols)
                for kind in (2 * side, 2 * side + 1):
                    place = slice(kind * hidden, (kind + 1) * hidden)
                    cells_ref[place, lanes] = (grad * factor_ref[place, lanes].astype(F32)).astype(BF)
    total = dot(zn_ref[...], cells_ref[...], ((1,), (1,)))
    part_ref[:, : 4 * hidden] = total.astype(BF)
    part_ref[:, 4 * hidden :] = gate_part_ref[...].astype(BF)
    d_zn_ref[...] = dot(w_ref[...], cells_ref[...]).astype(BF)


def pair_kernel(d_zn_ref, d_logit_ref, pair_ref, gain_ref, w_gate_ref, d_pair_ref):
    rows, cols, width = pair_ref.shape
    gain = column(gain_ref[...])
    for row in range(rows):
        lanes = slice(row * cols, (row + 1) * cols)
        hat, rstd = centred(pair_ref[row].astype(F32).T)
        d_zn = d_zn_ref[:, lanes].astype(F32)
        d_zn = d_zn + dot(w_gate_ref[...], d_logit_ref[row], ((1,), (1,)))
        d_pair_ref[row] = back_t(d_zn * gain, hat, rstd).T.astype(BF)


def sum_kernel(residues, got_ref, sent_ref):
    total = jnp.sum(got_ref[...].astype(F32), 0) / residues
    sent_ref[...] = jnp.broadcast_to(total.astype(BF)[None], sent_ref.shape)


def finish_kernel(got_ref, proj_ref, gate_ref):
    devices, chunk, depth = got_ref.shape
    wide = proj_ref.shape[1]
    total = got_ref[...].astype(F32).reshape(devices * chunk, depth)
    proj_ref[...] = total[:, :wide]
    gate_ref[...] = total[:, wide:]


def call(kernel, outs, scratch=(), flops=0, name=None, space=pltpu.VMEM, mib=12):
    spec = pl.BlockSpec(memory_space=pltpu.VMEM)

    def run(*args):
        moved = sum(a.size * a.dtype.itemsize for a in (*args, *outs))
        return pl.pallas_call(
            kernel,
            out_shape=list(outs),
            in_specs=[pl.BlockSpec(memory_space=space)] * len(args),
            out_specs=[spec] * len(outs),
            scratch_shapes=list(scratch),
            compiler_params=pltpu.CompilerParams(vmem_limit_bytes=mib * 1024 * 1024),
            cost_estimate=pl.CostEstimate(
                flops=flops, bytes_accessed=moved, transcendentals=0
            ),
            name=name,
        )(*args)

    return run


def small_blocks(pair, adjoint, mask, chain, gain_in, w_proj, w_gate, chain_bias, gain_out, w_out):
    rows, cols, width = pair.shape
    hidden = w_out.shape[0]
    devices = lax.axis_size("wide")
    own = hidden // devices
    residues = rows * devices
    cells = rows * cols
    half = rows * own
    shape = jax.ShapeDtypeStruct
    start = lax.axis_index("wide") * rows
    row_chain = lax.dynamic_slice_in_dim(chain, start, rows, 0)
    same = (row_chain[:, None] == chain[None, :]).astype(F32)
    gain_in, gain_out = gain_in[None], gain_out[None]
    sent, zn, cell_mask = call(
        project_kernel,
        [shape((devices, 2 * half, cols), BF), shape((width, cells), BF), shape((rows, cols), F32)],
        [
            pltpu.VMEM(pair.shape, BF),
            pltpu.VMEM((1, residues), jnp.int32),
            pltpu.VMEM(gain_in.shape, F32),
            pltpu.VMEM(w_proj.shape, BF),
            pltpu.SemaphoreType.DMA((4,)),
        ],
        name="project",
        space=pltpu.HBM,
        mib=56,
    )(pair, mask[None], gain_in, w_proj)
    got = swap(sent)
    factor, gate, t = call(
        gate_kernel,
        [shape((4 * hidden, cells), BF), shape((rows, cols, width), F32), shape((hidden, cells), BF)],
        flops=2 * 10**9,
        name="gate",
    )(zn, adjoint, cell_mask, same, w_proj, w_gate, chain_bias, gain_out, w_out)
    field = pltpu.VMEM((devices * half, cols), F32)
    channels = shape((own, residues, cols), BF)
    block = shape((devices, half, cols), BF)
    got, t = lax.optimization_barrier((got, t))
    sent, left, right = call(mix_kernel, [block, channels, channels], [field] * 3, name="mix")(got)
    got = swap(sent)
    sent, xn = call(norm_kernel, [block, shape((hidden, cells), BF)], name="norm")(got, t, gain_out)
    got = swap(sent)
    output, d_logit, gate_part = call(
        output_kernel,
        [shape(pair.shape, BF), shape(pair.shape, BF), shape((width, width), F32)],
        flops=2 * 10**9,
        name="output",
    )(xn, gate, adjoint, zn, w_out)
    got, gate_part = lax.optimization_barrier((got, gate_part))
    sent = call(
        unmix_kernel, [shape((devices, 2 * half, cols), BF)], [field] * 3, name="unmix"
    )(got, left, right)[0]
    got = swap(sent)
    d_zn, part = call(
        cells_kernel,
        [shape((width, cells), BF), shape((width, 4 * hidden + width), BF)],
        [pltpu.VMEM((4 * hidden, cells), BF)],
        name="cells",
    )(got, factor, zn, gate_part, w_proj)
    got = swap(part.reshape(devices, width // devices, -1))
    d_pair = call(pair_kernel, [shape(pair.shape, BF)], flops=2 * 10**9, name="pair")(
        d_zn, d_logit, pair, gain_in, w_gate
    )[0]
    got, d_pair = lax.optimization_barrier((got, d_pair))
    sent = call(
        functools.partial(sum_kernel, residues), [shape(got.shape, BF)], name="sum"
    )(got)[0]
    d_proj, d_gate = call(
        finish_kernel, [shape((width, 4 * hidden), F32), shape((width, width), F32)], name="finish"
    )(swap(sent))
    return (output, d_pair, d_proj, d_gate)


def per_device(pair, adjoint, mask, chain, gain_in, w_proj, w_gate, chain_bias, gain_out, w_out):
    rows, cols, width = pair.shape
    hidden = w_out.shape[0]
    n_wide = lax.axis_size("wide")
    n_narrow = lax.axis_size("narrow")
    if n_narrow == 1 and (rows, cols, width) == (8, 128, 128) and hidden == 8 * n_wide == 128:
        return small_blocks(
            pair, adjoint, mask, chain, gain_in, w_proj, w_gate, chain_bias, gain_out, w_out
        )
    residues = rows * n_wide
    devices = n_wide * n_narrow
    own = hidden // devices
    row_start = lax.axis_index("wide") * rows
    col_start = lax.axis_index("narrow") * cols
    mask_f = mask.astype(jnp.float32)
    row_mask = lax.dynamic_slice_in_dim(mask_f, row_start, rows, 0)
    col_mask = lax.dynamic_slice_in_dim(mask_f, col_start, cols, 0)
    cell_mask = (row_mask[:, None] * col_mask[None, :])[None]
    row_chain = lax.dynamic_slice_in_dim(chain, row_start, rows, 0)
    col_chain = lax.dynamic_slice_in_dim(chain, col_start, cols, 0)
    same = (row_chain[:, None] == col_chain[None, :])[:, :, None]
    zn_f, z_hat, z_rstd = normalize(pair.astype(jnp.float32), gain_in, -1)
    zn = zn_f.astype(jnp.bfloat16)
    proj_a = jnp.einsum(
        "ijc,ch->hij", zn, w_proj[:, : 2 * hidden], preferred_element_type=jnp.float32
    )
    proj_b = jnp.einsum(
        "ijc,ch->hij", zn, w_proj[:, 2 * hidden :], preferred_element_type=jnp.float32
    )
    a_lin = proj_a[:hidden]
    sig_a = jax.nn.sigmoid(proj_a[hidden:])
    b_lin = proj_b[:hidden]
    sig_b = jax.nn.sigmoid(proj_b[hidden:])
    left_t = (cell_mask * sig_a * a_lin).astype(jnp.bfloat16)
    right_t = (cell_mask * sig_b * b_lin).astype(jnp.bfloat16)
    pairs = jnp.concatenate(
        [left_t.reshape(devices, own, rows, cols), right_t.reshape(devices, own, rows, cols)], 1
    )
    pairs = gather_cells(swap(pairs), n_wide, n_narrow)
    left_c, right_c = pairs[:own], pairs[own:]
    mixed_c = jnp.einsum("hik,hjk->hij", left_c, right_c, preferred_element_type=jnp.float32)
    mixed_t = swap(split_cells(mixed_c.astype(jnp.bfloat16), n_wide, n_narrow))
    mixed_t = mixed_t.reshape(hidden, rows, cols).astype(jnp.float32)
    xn_f, x_hat, x_rstd = normalize(mixed_t, gain_out[:, None, None], 0)
    xn = xn_f.astype(jnp.bfloat16)
    proj_out = jnp.einsum("hij,hc->ijc", xn, w_out, preferred_element_type=jnp.float32)
    logits = jnp.dot(zn, w_gate, preferred_element_type=jnp.float32) + jnp.where(
        same, chain_bias[1], chain_bias[0]
    )
    gate = jax.nn.sigmoid(logits)
    output = (gate * proj_out).astype(jnp.bfloat16)
    adj = adjoint.astype(jnp.float32)
    d_out = (adj * gate).astype(jnp.bfloat16)
    d_logit = (adj * proj_out * gate * (1.0 - gate)).astype(jnp.bfloat16)
    d_xn = jnp.einsum("ijc,hc->hij", d_out, w_out, preferred_element_type=jnp.float32)
    d_mixed_t = norm_back(d_xn * gain_out[:, None, None], x_hat, x_rstd, 0).astype(jnp.bfloat16)
    d_mixed_c = gather_cells(swap(d_mixed_t.reshape(devices, own, rows, cols)), n_wide, n_narrow)
    d_left_c = jnp.einsum("hij,hjk->hik", d_mixed_c, right_c, preferred_element_type=jnp.float32)
    d_right_c = jnp.einsum("hij,hik->hjk", d_mixed_c, left_c, preferred_element_type=jnp.float32)
    back = jnp.concatenate([d_left_c.astype(jnp.bfloat16), d_right_c.astype(jnp.bfloat16)], 0)
    back = swap(split_cells(back, n_wide, n_narrow))
    d_left = back[:, :own].reshape(hidden, rows, cols).astype(jnp.float32)
    d_right = back[:, own:].reshape(hidden, rows, cols).astype(jnp.float32)
    d_cells_a = jnp.concatenate(
        [d_left * cell_mask * sig_a, d_left * cell_mask * a_lin * sig_a * (1.0 - sig_a)], 0
    ).astype(jnp.bfloat16)
    d_cells_b = jnp.concatenate(
        [d_right * cell_mask * sig_b, d_right * cell_mask * b_lin * sig_b * (1.0 - sig_b)], 0
    ).astype(jnp.bfloat16)
    d_zn = jnp.einsum(
        "hij,ch->ijc", d_cells_a, w_proj[:, : 2 * hidden], preferred_element_type=jnp.float32
    )
    d_zn = d_zn + jnp.einsum(
        "hij,ch->ijc", d_cells_b, w_proj[:, 2 * hidden :], preferred_element_type=jnp.float32
    )
    d_zn = d_zn + jnp.dot(d_logit, w_gate.T, preferred_element_type=jnp.float32)
    d_pair = norm_back(d_zn * gain_in, z_hat, z_rstd, -1).astype(jnp.bfloat16)
    proj_part = jnp.concatenate(
        [
            jnp.einsum("ijc,hij->ch", zn, d_cells_a, preferred_element_type=jnp.float32),
            jnp.einsum("ijc,hij->ch", zn, d_cells_b, preferred_element_type=jnp.float32),
        ],
        1,
    )
    flat_z = zn.reshape(-1, width)
    gate_part = jnp.dot(flat_z.T, d_logit.reshape(-1, width), preferred_element_type=jnp.float32)
    parts = jnp.concatenate([proj_part, gate_part], 1)
    chunk = width // devices
    mine = swap(parts.astype(jnp.bfloat16).reshape(devices, chunk, -1))
    mine = jnp.sum(mine.astype(jnp.float32), 0) / residues
    mine = mine.astype(jnp.bfloat16)
    total = swap(jnp.broadcast_to(mine, (devices,) + mine.shape)).reshape(width, -1)
    total = total.astype(jnp.float32)
    return (output, d_pair, total[:, : 4 * hidden], total[:, 4 * hidden :])


def solution(mesh):
    placed = (
        P(("groups", "wide"), "narrow", None),
        P(("groups", "wide"), "narrow", None),
        P("groups"),
        P("groups"),
        P(),
        P(),
        P(),
        P(),
        P(),
        P(),
    )
    return jax.shard_map(
        per_device,
        mesh=mesh,
        in_specs=placed,
        out_specs=(
            P(("groups", "wide"), "narrow", None),
            P(("groups", "wide"), "narrow", None),
            P("groups", None),
            P("groups", None),
        ),
        check_vma=False,
    )
```

```python
import functools

import jax
import jax.numpy as jnp
from jax import lax
from jax.experimental import pallas as pl
from jax.experimental.pallas import tpu as pltpu
from jax.sharding import PartitionSpec as P

EPS = 1e-05


def normalize(values, gain, axis):
    centre = values - jnp.mean(values, axis, keepdims=True)
    rstd = lax.rsqrt(jnp.mean(centre * centre, axis, keepdims=True) + EPS)
    hat = centre * rstd
    return (hat * gain, hat, rstd)


def norm_back(scaled, hat, rstd, axis):
    return rstd * (
        scaled
        - jnp.mean(scaled, axis, keepdims=True)
        - hat * jnp.mean(scaled * hat, axis, keepdims=True)
    )


def swap(blocks):
    return lax.all_to_all(blocks, ("wide", "narrow"), split_axis=0, concat_axis=0, tiled=True)


def gather_cells(blocks, n_wide, n_narrow):
    _, own, rows, cols = blocks.shape
    shaped = blocks.reshape(n_wide, n_narrow, own, rows, cols)
    return jnp.transpose(shaped, (2, 0, 3, 1, 4)).reshape(own, n_wide * rows, n_narrow * cols)


def split_cells(field, n_wide, n_narrow):
    own, rows, cols = field.shape
    shaped = field.reshape(own, n_wide, rows // n_wide, n_narrow, cols // n_narrow)
    moved = jnp.transpose(shaped, (1, 3, 0, 2, 4))
    return moved.reshape(n_wide * n_narrow, own, rows // n_wide, cols // n_narrow)


BF = jnp.bfloat16
F32 = jnp.float32


def dot(a, b, over=((1,), (0,))):
    return lax.dot_general(a, b, (over, ((), ())), preferred_element_type=F32)


def column(row):
    return jnp.broadcast_to(row, (row.shape[1], row.shape[1])).T


def centred(x):
    centre = x - jnp.mean(x, 0, keepdims=True)
    rstd = lax.rsqrt(jnp.mean(centre * centre, 0, keepdims=True) + EPS)
    return centre * rstd, rstd


def back_t(scaled, hat, rstd):
    inner = hat * jnp.mean(scaled * hat, 0, keepdims=True)
    return rstd * (scaled - jnp.mean(scaled, 0, keepdims=True) - inner)


def two_rows(first, second, devices):
    own, cols = first.shape[0] // devices, first.shape[1]
    shape = (devices, own, cols)
    return jnp.concatenate([first.reshape(shape), second.reshape(shape)], 1).astype(BF)


def apart(block, devices):
    wide = block.astype(F32)
    own, cols = wide.shape[1] // 2, wide.shape[2]
    return [wide[:, at * own : (at + 1) * own].reshape(devices * own, cols) for at in range(2)]


def project_kernel(
    pair_hbm, mask_hbm, gain_hbm, w_hbm, sent_ref, zn_ref, mask_ref,
    pair_ref, mask_v, gain_ref, w_ref, sems,
):
    devices, depth, _ = sent_ref.shape
    rows, cols, width = pair_ref.shape
    start = lax.axis_index("wide") * rows
    copies = [
        pltpu.make_async_copy(gain_hbm, gain_ref, sems.at[0]),
        pltpu.make_async_copy(w_hbm, w_ref, sems.at[1]),
        pltpu.make_async_copy(mask_hbm, mask_v, sems.at[2]),
        pltpu.make_async_copy(pair_hbm, pair_ref, sems.at[3]),
    ]
    for copy in copies:
        copy.start()
    for copy in copies:
        copy.wait()
    mask_f = mask_v[...].astype(F32)
    shape = (rows, mask_f.shape[1])
    lane = lax.broadcasted_iota(jnp.int32, shape, 1)
    own = lane == start + lax.broadcasted_iota(jnp.int32, shape, 0)
    mask_ref[...] = mask_f * jnp.sum(jnp.where(own, mask_f, 0.0), 1, keepdims=True)
    gain = column(gain_ref[...])
    weights = w_ref[...].astype(F32).T.astype(BF)
    hidden = weights.shape[0] // 4
    half = depth // 2
    for two in range(rows // 2):
        pieces = []
        for row in (2 * two, 2 * two + 1):
            hat, _ = centred(pair_ref[row].astype(F32).T)
            zn = (hat * gain).astype(BF)
            zn_ref[:, row * cols : (row + 1) * cols] = zn
            proj = dot(weights, zn)
            mask = mask_ref[row : row + 1, :]
            left = mask * jax.nn.sigmoid(proj[hidden : 2 * hidden]) * proj[:hidden]
            right = mask * jax.nn.sigmoid(proj[3 * hidden :]) * proj[2 * hidden : 3 * hidden]
            pieces.append((left, right))
        at = two * 16
        sent_ref[:, at : at + 16, :] = two_rows(pieces[0][0], pieces[1][0], devices)
        sent_ref[:, half + at : half + at + 16, :] = two_rows(pieces[0][1], pieces[1][1], devices)


def gate_kernel(
    zn_ref, adj_ref, mask_ref, same_ref, w_ref, w_gate_ref, bias_ref, gain_ref, w_out_ref,
    factor_ref, gate_ref, t_ref,
):
    rows, cols, width = adj_ref.shape
    weights = w_ref[...].astype(F32).T.astype(BF)
    hidden = weights.shape[0] // 4
    w_gate = w_gate_ref[...].astype(F32).T.astype(BF)
    across, within = column(bias_ref[0:1, :]), column(bias_ref[1:2, :])
    gain = column(gain_ref[...])
    for row in range(rows):
        lanes = slice(row * cols, (row + 1) * cols)
        zn = zn_ref[:, lanes]
        proj = dot(weights, zn)
        mask = mask_ref[row : row + 1, :]
        for side in range(2):
            lin = proj[2 * side * hidden : (2 * side + 1) * hidden]
            sig = jax.nn.sigmoid(proj[(2 * side + 1) * hidden : (2 * side + 2) * hidden])
            factor_ref[2 * side * hidden : (2 * side + 1) * hidden, lanes] = (mask * sig).astype(BF)
            factor_ref[(2 * side + 1) * hidden : (2 * side + 2) * hidden, lanes] = (
                mask * lin * sig * (1.0 - sig)
            ).astype(BF)
        bias = jnp.where(same_ref[row : row + 1, :] > 0.5, within, across)
        gate = jax.nn.sigmoid(dot(w_gate, zn) + bias).T
        gate_ref[row] = gate
        d_out = (adj_ref[row].astype(F32) * gate).astype(BF)
        t = dot(w_out_ref[...], d_out, ((1,), (1,))) * gain
        t_ref[:, lanes] = (t - jnp.mean(t, 0, keepdims=True)).astype(BF)


def mix_kernel(got_ref, sent_ref, left_ref, right_ref, left_s, right_s, out_s):
    devices, depth, cols = got_ref.shape
    own = left_ref.shape[0]
    half = depth // 2
    count = devices * half // own
    left_s[...] = got_ref[:, :half, :].astype(F32).reshape(devices * half, cols)
    right_s[...] = got_ref[:, half:, :].astype(F32).reshape(devices * half, cols)
    for h in range(own):
        left = left_s[pl.ds(h, count, stride=own), :].astype(BF)
        right = right_s[pl.ds(h, count, stride=own), :].astype(BF)
        left_ref[h] = left
        right_ref[h] = right
        out_s[pl.ds(h, count, stride=own), :] = dot(left, right, ((1,), (1,)))
    sent_ref[...] = out_s[...].reshape(devices, half, cols).astype(BF)


def norm_kernel(got_ref, t_ref, gain_ref, sent_ref, xn_ref):
    devices, depth, cols = got_ref.shape
    gain = column(gain_ref[...])
    for two in range(depth // 16):
        pieces = []
        for part, mixed in enumerate(apart(got_ref[:, two * 16 : two * 16 + 16, :], devices)):
            row = 2 * two + part
            lanes = slice(row * cols, (row + 1) * cols)
            hat, rstd = centred(mixed)
            xn_ref[:, lanes] = (hat * gain).astype(BF)
            pieces.append(back_t(t_ref[:, lanes].astype(F32), hat, rstd))
        sent_ref[:, two * 16 : two * 16 + 16, :] = two_rows(*pieces, devices)


def output_kernel(
    xn_ref, gate_ref, adj_ref, zn_ref, w_out_ref, output_ref, d_logit_ref, part_ref
):
    rows, cols, width = adj_ref.shape
    total = None
    for row in range(rows):
        lanes = slice(row * cols, (row + 1) * cols)
        xn = xn_ref[:, lanes].astype(F32).T.astype(BF)
        proj_out = dot(xn, w_out_ref[...])
        gate = gate_ref[row]
        output_ref[row] = (gate * proj_out).astype(BF)
        d_logit = (adj_ref[row].astype(F32) * proj_out * gate * (1.0 - gate)).astype(BF)
        d_logit_ref[row] = d_logit
        term = dot(zn_ref[:, lanes], d_logit)
        total = term if total is None else total + term
    part_ref[...] = total


def unmix_kernel(got_ref, left_ref, right_ref, sent_ref, in_s, left_s, right_s):
    devices, half, cols = got_ref.shape
    own = left_ref.shape[0]
    count = devices * half // own
    in_s[...] = got_ref[...].astype(F32).reshape(devices * half, cols)
    for h in range(own):
        grad = in_s[pl.ds(h, count, stride=own), :]
        left_s[pl.ds(h, count, stride=own), :] = dot(grad.astype(BF), right_ref[h])
        right_s[pl.ds(h, count, stride=own), :] = dot(grad.T.astype(BF), left_ref[h])
    sent_ref[:, :half, :] = left_s[...].reshape(devices, half, cols).astype(BF)
    sent_ref[:, half:, :] = right_s[...].reshape(devices, half, cols).astype(BF)


def cells_kernel(
    got_ref, factor_ref, zn_ref, gate_part_ref, w_ref, gain_ref, u_ref, part_ref, cells_ref
):
    devices, depth, cols = got_ref.shape
    half = depth // 2
    hidden = factor_ref.shape[0] // 4
    for side in range(2):
        for two in range(half // 16):
            at = side * half + two * 16
            for part, grad in enumerate(apart(got_ref[:, at : at + 16, :], devices)):
                row = 2 * two + part
                lanes = slice(row * cols, (row + 1) * cols)
                for kind in (2 * side, 2 * side + 1):
                    place = slice(kind * hidden, (kind + 1) * hidden)
                    cells_ref[place, lanes] = (grad * factor_ref[place, lanes].astype(F32)).astype(BF)
    total = dot(zn_ref[...], cells_ref[...], ((1,), (1,)))
    part_ref[:, : 4 * hidden] = total.astype(BF)
    part_ref[:, 4 * hidden :] = gate_part_ref[...].astype(BF)
    u = dot(w_ref[...], cells_ref[...]) * column(gain_ref[...])[:, :1]
    u_ref[...] = (u - jnp.mean(u, 0, keepdims=True)).astype(BF)


def pair_kernel(u_ref, d_logit_ref, pair_ref, gain_ref, w_gate_ref, d_pair_ref):
    rows, cols, width = pair_ref.shape
    gain = column(gain_ref[...])
    for row in range(rows):
        lanes = slice(row * cols, (row + 1) * cols)
        hat, rstd = centred(pair_ref[row].astype(F32).T)
        u = dot(w_gate_ref[...], d_logit_ref[row], ((1,), (1,))) * gain
        u = u + u_ref[:, lanes].astype(F32)
        d_pair_ref[row] = back_t(u, hat, rstd).T.astype(BF)


def sum_kernel(residues, got_ref, sent_ref):
    total = jnp.sum(got_ref[...].astype(F32), 0) / residues
    sent_ref[...] = jnp.broadcast_to(total.astype(BF)[None], sent_ref.shape)


def finish_kernel(got_ref, proj_ref, gate_ref):
    devices, chunk, depth = got_ref.shape
    wide = proj_ref.shape[1]
    total = got_ref[...].astype(F32).reshape(devices * chunk, depth)
    proj_ref[...] = total[:, :wide]
    gate_ref[...] = total[:, wide:]


def call(kernel, outs, scratch=(), flops=0, name=None, space=pltpu.VMEM, mib=12):
    spec = pl.BlockSpec(memory_space=pltpu.VMEM)

    def run(*args):
        moved = sum(a.size * a.dtype.itemsize for a in (*args, *outs))
        return pl.pallas_call(
            kernel,
            out_shape=list(outs),
            in_specs=[pl.BlockSpec(memory_space=space)] * len(args),
            out_specs=[spec] * len(outs),
            scratch_shapes=list(scratch),
            compiler_params=pltpu.CompilerParams(vmem_limit_bytes=mib * 1024 * 1024),
            cost_estimate=pl.CostEstimate(
                flops=flops, bytes_accessed=moved, transcendentals=0
            ),
            name=name,
        )(*args)

    return run


def small_blocks(pair, adjoint, mask, chain, gain_in, w_proj, w_gate, chain_bias, gain_out, w_out):
    rows, cols, width = pair.shape
    hidden = w_out.shape[0]
    devices = lax.axis_size("wide")
    own = hidden // devices
    residues = rows * devices
    cells = rows * cols
    half = rows * own
    shape = jax.ShapeDtypeStruct
    start = lax.axis_index("wide") * rows
    row_chain = lax.dynamic_slice_in_dim(chain, start, rows, 0)
    same = (row_chain[:, None] == chain[None, :]).astype(F32)
    gain_in, gain_out = gain_in[None], gain_out[None]
    sent, zn, cell_mask = call(
        project_kernel,
        [shape((devices, 2 * half, cols), BF), shape((width, cells), BF), shape((rows, cols), F32)],
        [
            pltpu.VMEM(pair.shape, BF),
            pltpu.VMEM((1, residues), jnp.int32),
            pltpu.VMEM(gain_in.shape, F32),
            pltpu.VMEM(w_proj.shape, BF),
            pltpu.SemaphoreType.DMA((4,)),
        ],
        name="project",
        space=pltpu.HBM,
        mib=56,
    )(pair, mask[None], gain_in, w_proj)
    got = swap(sent)
    factor, gate, t = call(
        gate_kernel,
        [shape((4 * hidden, cells), BF), shape((rows, cols, width), F32), shape((hidden, cells), BF)],
        flops=2 * 10**9,
        name="gate",
    )(zn, adjoint, cell_mask, same, w_proj, w_gate, chain_bias, gain_out, w_out)
    field = pltpu.VMEM((devices * half, cols), F32)
    channels = shape((own, residues, cols), BF)
    block = shape((devices, half, cols), BF)
    got, t = lax.optimization_barrier((got, t))
    sent, left, right = call(mix_kernel, [block, channels, channels], [field] * 3, name="mix")(got)
    got = swap(sent)
    sent, xn = call(norm_kernel, [block, shape((hidden, cells), BF)], name="norm")(got, t, gain_out)
    got = swap(sent)
    output, d_logit, gate_part = call(
        output_kernel,
        [shape(pair.shape, BF), shape(pair.shape, BF), shape((width, width), F32)],
        flops=2 * 10**9,
        name="output",
    )(xn, gate, adjoint, zn, w_out)
    got, gate_part = lax.optimization_barrier((got, gate_part))
    sent = call(
        unmix_kernel, [shape((devices, 2 * half, cols), BF)], [field] * 3, name="unmix"
    )(got, left, right)[0]
    got = swap(sent)
    u, part = call(
        cells_kernel,
        [shape((width, cells), BF), shape((width, 4 * hidden + width), BF)],
        [pltpu.VMEM((4 * hidden, cells), BF)],
        name="cells",
    )(got, factor, zn, gate_part, w_proj, gain_in)
    got = swap(part.reshape(devices, width // devices, -1))
    d_pair = call(pair_kernel, [shape(pair.shape, BF)], flops=2 * 10**9, name="pair")(
        u, d_logit, pair, gain_in, w_gate
    )[0]
    got, d_pair = lax.optimization_barrier((got, d_pair))
    sent = call(
        functools.partial(sum_kernel, residues), [shape(got.shape, BF)], name="sum"
    )(got)[0]
    d_proj, d_gate = call(
        finish_kernel, [shape((width, 4 * hidden), F32), shape((width, width), F32)], name="finish"
    )(swap(sent))
    return (output, d_pair, d_proj, d_gate)


def per_device(pair, adjoint, mask, chain, gain_in, w_proj, w_gate, chain_bias, gain_out, w_out):
    rows, cols, width = pair.shape
    hidden = w_out.shape[0]
    n_wide = lax.axis_size("wide")
    n_narrow = lax.axis_size("narrow")
    if n_narrow == 1 and (rows, cols, width) == (8, 128, 128) and hidden == 8 * n_wide == 128:
        return small_blocks(
            pair, adjoint, mask, chain, gain_in, w_proj, w_gate, chain_bias, gain_out, w_out
        )
    residues = rows * n_wide
    devices = n_wide * n_narrow
    own = hidden // devices
    row_start = lax.axis_index("wide") * rows
    col_start = lax.axis_index("narrow") * cols
    mask_f = mask.astype(jnp.float32)
    row_mask = lax.dynamic_slice_in_dim(mask_f, row_start, rows, 0)
    col_mask = lax.dynamic_slice_in_dim(mask_f, col_start, cols, 0)
    cell_mask = (row_mask[:, None] * col_mask[None, :])[None]
    row_chain = lax.dynamic_slice_in_dim(chain, row_start, rows, 0)
    col_chain = lax.dynamic_slice_in_dim(chain, col_start, cols, 0)
    same = (row_chain[:, None] == col_chain[None, :])[:, :, None]
    zn_f, z_hat, z_rstd = normalize(pair.astype(jnp.float32), gain_in, -1)
    zn = zn_f.astype(jnp.bfloat16)
    proj_a = jnp.einsum(
        "ijc,ch->hij", zn, w_proj[:, : 2 * hidden], preferred_element_type=jnp.float32
    )
    proj_b = jnp.einsum(
        "ijc,ch->hij", zn, w_proj[:, 2 * hidden :], preferred_element_type=jnp.float32
    )
    a_lin = proj_a[:hidden]
    sig_a = jax.nn.sigmoid(proj_a[hidden:])
    b_lin = proj_b[:hidden]
    sig_b = jax.nn.sigmoid(proj_b[hidden:])
    left_t = (cell_mask * sig_a * a_lin).astype(jnp.bfloat16)
    right_t = (cell_mask * sig_b * b_lin).astype(jnp.bfloat16)
    pairs = jnp.concatenate(
        [left_t.reshape(devices, own, rows, cols), right_t.reshape(devices, own, rows, cols)], 1
    )
    pairs = gather_cells(swap(pairs), n_wide, n_narrow)
    left_c, right_c = pairs[:own], pairs[own:]
    mixed_c = jnp.einsum("hik,hjk->hij", left_c, right_c, preferred_element_type=jnp.float32)
    mixed_t = swap(split_cells(mixed_c.astype(jnp.bfloat16), n_wide, n_narrow))
    mixed_t = mixed_t.reshape(hidden, rows, cols).astype(jnp.float32)
    xn_f, x_hat, x_rstd = normalize(mixed_t, gain_out[:, None, None], 0)
    xn = xn_f.astype(jnp.bfloat16)
    proj_out = jnp.einsum("hij,hc->ijc", xn, w_out, preferred_element_type=jnp.float32)
    logits = jnp.dot(zn, w_gate, preferred_element_type=jnp.float32) + jnp.where(
        same, chain_bias[1], chain_bias[0]
    )
    gate = jax.nn.sigmoid(logits)
    output = (gate * proj_out).astype(jnp.bfloat16)
    adj = adjoint.astype(jnp.float32)
    d_out = (adj * gate).astype(jnp.bfloat16)
    d_logit = (adj * proj_out * gate * (1.0 - gate)).astype(jnp.bfloat16)
    d_xn = jnp.einsum("ijc,hc->hij", d_out, w_out, preferred_element_type=jnp.float32)
    d_mixed_t = norm_back(d_xn * gain_out[:, None, None], x_hat, x_rstd, 0).astype(jnp.bfloat16)
    d_mixed_c = gather_cells(swap(d_mixed_t.reshape(devices, own, rows, cols)), n_wide, n_narrow)
    d_left_c = jnp.einsum("hij,hjk->hik", d_mixed_c, right_c, preferred_element_type=jnp.float32)
    d_right_c = jnp.einsum("hij,hik->hjk", d_mixed_c, left_c, preferred_element_type=jnp.float32)
    back = jnp.concatenate([d_left_c.astype(jnp.bfloat16), d_right_c.astype(jnp.bfloat16)], 0)
    back = swap(split_cells(back, n_wide, n_narrow))
    d_left = back[:, :own].reshape(hidden, rows, cols).astype(jnp.float32)
    d_right = back[:, own:].reshape(hidden, rows, cols).astype(jnp.float32)
    d_cells_a = jnp.concatenate(
        [d_left * cell_mask * sig_a, d_left * cell_mask * a_lin * sig_a * (1.0 - sig_a)], 0
    ).astype(jnp.bfloat16)
    d_cells_b = jnp.concatenate(
        [d_right * cell_mask * sig_b, d_right * cell_mask * b_lin * sig_b * (1.0 - sig_b)], 0
    ).astype(jnp.bfloat16)
    d_zn = jnp.einsum(
        "hij,ch->ijc", d_cells_a, w_proj[:, : 2 * hidden], preferred_element_type=jnp.float32
    )
    d_zn = d_zn + jnp.einsum(
        "hij,ch->ijc", d_cells_b, w_proj[:, 2 * hidden :], preferred_element_type=jnp.float32
    )
    d_zn = d_zn + jnp.dot(d_logit, w_gate.T, preferred_element_type=jnp.float32)
    d_pair = norm_back(d_zn * gain_in, z_hat, z_rstd, -1).astype(jnp.bfloat16)
    proj_part = jnp.concatenate(
        [
            jnp.einsum("ijc,hij->ch", zn, d_cells_a, preferred_element_type=jnp.float32),
            jnp.einsum("ijc,hij->ch", zn, d_cells_b, preferred_element_type=jnp.float32),
        ],
        1,
    )
    flat_z = zn.reshape(-1, width)
    gate_part = jnp.dot(flat_z.T, d_logit.reshape(-1, width), preferred_element_type=jnp.float32)
    parts = jnp.concatenate([proj_part, gate_part], 1)
    chunk = width // devices
    mine = swap(parts.astype(jnp.bfloat16).reshape(devices, chunk, -1))
    mine = jnp.sum(mine.astype(jnp.float32), 0) / residues
    mine = mine.astype(jnp.bfloat16)
    total = swap(jnp.broadcast_to(mine, (devices,) + mine.shape)).reshape(width, -1)
    total = total.astype(jnp.float32)
    return (output, d_pair, total[:, : 4 * hidden], total[:, 4 * hidden :])


def solution(mesh):
    placed = (
        P(("groups", "wide"), "narrow", None),
        P(("groups", "wide"), "narrow", None),
        P("groups"),
        P("groups"),
        P(),
        P(),
        P(),
        P(),
        P(),
        P(),
    )
    return jax.shard_map(
        per_device,
        mesh=mesh,
        in_specs=placed,
        out_specs=(
            P(("groups", "wide"), "narrow", None),
            P(("groups", "wide"), "narrow", None),
            P("groups", None),
            P("groups", None),
        ),
        check_vma=False,
    )
```

```python
import functools

import jax
import jax.numpy as jnp
from jax import lax
from jax.experimental import pallas as pl
from jax.experimental.pallas import tpu as pltpu
from jax.sharding import PartitionSpec as P

EPS = 1e-05


def normalize(values, gain, axis):
    centre = values - jnp.mean(values, axis, keepdims=True)
    rstd = lax.rsqrt(jnp.mean(centre * centre, axis, keepdims=True) + EPS)
    hat = centre * rstd
    return (hat * gain, hat, rstd)


def norm_back(scaled, hat, rstd, axis):
    return rstd * (
        scaled
        - jnp.mean(scaled, axis, keepdims=True)
        - hat * jnp.mean(scaled * hat, axis, keepdims=True)
    )


def swap(blocks):
    return lax.all_to_all(blocks, ("wide", "narrow"), split_axis=0, concat_axis=0, tiled=True)


def gather_cells(blocks, n_wide, n_narrow):
    _, own, rows, cols = blocks.shape
    shaped = blocks.reshape(n_wide, n_narrow, own, rows, cols)
    return jnp.transpose(shaped, (2, 0, 3, 1, 4)).reshape(own, n_wide * rows, n_narrow * cols)


def split_cells(field, n_wide, n_narrow):
    own, rows, cols = field.shape
    shaped = field.reshape(own, n_wide, rows // n_wide, n_narrow, cols // n_narrow)
    moved = jnp.transpose(shaped, (1, 3, 0, 2, 4))
    return moved.reshape(n_wide * n_narrow, own, rows // n_wide, cols // n_narrow)


BF = jnp.bfloat16
F32 = jnp.float32


def dot(a, b, over=((1,), (0,))):
    return lax.dot_general(a, b, (over, ((), ())), preferred_element_type=F32)


def column(row):
    return jnp.broadcast_to(row, (row.shape[1], row.shape[1])).T


def centred(x):
    centre = x - jnp.mean(x, 0, keepdims=True)
    rstd = lax.rsqrt(jnp.mean(centre * centre, 0, keepdims=True) + EPS)
    return centre * rstd, rstd


def back_t(scaled, hat, rstd):
    inner = hat * jnp.mean(scaled * hat, 0, keepdims=True)
    return rstd * (scaled - jnp.mean(scaled, 0, keepdims=True) - inner)


def two_rows(first, second, devices):
    own, cols = first.shape[0] // devices, first.shape[1]
    shape = (devices, own, cols)
    return jnp.concatenate([first.reshape(shape), second.reshape(shape)], 1).astype(BF)


def apart(block, devices):
    wide = block.astype(F32)
    own, cols = wide.shape[1] // 2, wide.shape[2]
    return [wide[:, at * own : (at + 1) * own].reshape(devices * own, cols) for at in range(2)]


def project_kernel(
    pair_hbm, mask_hbm, gain_hbm, w_hbm, sent_ref, zn_ref, mask_ref,
    pair_ref, mask_v, gain_ref, w_ref, sems,
):
    devices, depth, _ = sent_ref.shape
    rows, cols, width = pair_ref.shape
    start = lax.axis_index("wide") * rows
    copies = [
        pltpu.make_async_copy(gain_hbm, gain_ref, sems.at[0]),
        pltpu.make_async_copy(w_hbm, w_ref, sems.at[1]),
        pltpu.make_async_copy(mask_hbm, mask_v, sems.at[2]),
        pltpu.make_async_copy(pair_hbm, pair_ref, sems.at[3]),
    ]
    for copy in copies:
        copy.start()
    for copy in copies:
        copy.wait()
    mask_f = mask_v[...].astype(F32)
    shape = (rows, mask_f.shape[1])
    lane = lax.broadcasted_iota(jnp.int32, shape, 1)
    own = lane == start + lax.broadcasted_iota(jnp.int32, shape, 0)
    mask_ref[...] = mask_f * jnp.sum(jnp.where(own, mask_f, 0.0), 1, keepdims=True)
    gain = column(gain_ref[...])
    weights = w_ref[...].astype(F32).T.astype(BF)
    hidden = weights.shape[0] // 4
    half = depth // 2
    for two in range(rows // 2):
        pieces = []
        for row in (2 * two, 2 * two + 1):
            hat, _ = centred(pair_ref[row].astype(F32).T)
            zn = (hat * gain).astype(BF)
            zn_ref[:, row * cols : (row + 1) * cols] = zn
            proj = dot(weights, zn)
            mask = mask_ref[row : row + 1, :]
            left = mask * jax.nn.sigmoid(proj[hidden : 2 * hidden]) * proj[:hidden]
            right = mask * jax.nn.sigmoid(proj[3 * hidden :]) * proj[2 * hidden : 3 * hidden]
            pieces.append((left, right))
        at = two * 16
        sent_ref[:, at : at + 16, :] = two_rows(pieces[0][0], pieces[1][0], devices)
        sent_ref[:, half + at : half + at + 16, :] = two_rows(pieces[0][1], pieces[1][1], devices)


def gate_kernel(
    zn_ref, adj_ref, mask_ref, same_ref, w_ref, w_gate_ref, bias_ref, gain_ref, w_out_ref,
    gain_in_ref, factor_ref, gate_ref, t_ref, columns_ref,
):
    rows, cols, width = adj_ref.shape
    weights = w_ref[...].astype(F32).T.astype(BF)
    hidden = weights.shape[0] // 4
    w_gate = w_gate_ref[...].astype(F32).T.astype(BF)
    across, within = column(bias_ref[0:1, :]), column(bias_ref[1:2, :])
    gain = column(gain_ref[...])
    columns_ref[...] = column(gain_in_ref[...])
    for row in range(rows):
        lanes = slice(row * cols, (row + 1) * cols)
        zn = zn_ref[:, lanes]
        proj = dot(weights, zn)
        mask = mask_ref[row : row + 1, :]
        for side in range(2):
            lin = proj[2 * side * hidden : (2 * side + 1) * hidden]
            sig = jax.nn.sigmoid(proj[(2 * side + 1) * hidden : (2 * side + 2) * hidden])
            factor_ref[2 * side * hidden : (2 * side + 1) * hidden, lanes] = (mask * sig).astype(BF)
            factor_ref[(2 * side + 1) * hidden : (2 * side + 2) * hidden, lanes] = (
                mask * lin * sig * (1.0 - sig)
            ).astype(BF)
        bias = jnp.where(same_ref[row : row + 1, :] > 0.5, within, across)
        gate = jax.nn.sigmoid(dot(w_gate, zn) + bias).T
        gate_ref[row] = gate
        d_out = (adj_ref[row].astype(F32) * gate).astype(BF)
        t = dot(w_out_ref[...], d_out, ((1,), (1,))) * gain
        t_ref[:, lanes] = (t - jnp.mean(t, 0, keepdims=True)).astype(BF)


def mix_kernel(got_ref, sent_ref, left_ref, right_ref, left_s, right_s, out_s):
    devices, depth, cols = got_ref.shape
    own = left_ref.shape[0]
    half = depth // 2
    count = devices * half // own
    left_s[...] = got_ref[:, :half, :].astype(F32).reshape(devices * half, cols)
    right_s[...] = got_ref[:, half:, :].astype(F32).reshape(devices * half, cols)
    for h in range(own):
        left = left_s[pl.ds(h, count, stride=own), :].astype(BF)
        right = right_s[pl.ds(h, count, stride=own), :].astype(BF)
        left_ref[h] = left
        right_ref[h] = right
        out_s[pl.ds(h, count, stride=own), :] = dot(left, right, ((1,), (1,)))
    sent_ref[...] = out_s[...].reshape(devices, half, cols).astype(BF)


def norm_kernel(got_ref, t_ref, gain_ref, sent_ref, xn_ref):
    devices, depth, cols = got_ref.shape
    gain = column(gain_ref[...])
    for two in range(depth // 16):
        pieces = []
        for part, mixed in enumerate(apart(got_ref[:, two * 16 : two * 16 + 16, :], devices)):
            row = 2 * two + part
            lanes = slice(row * cols, (row + 1) * cols)
            hat, rstd = centred(mixed)
            xn_ref[:, lanes] = (hat * gain).astype(BF)
            pieces.append(back_t(t_ref[:, lanes].astype(F32), hat, rstd))
        sent_ref[:, two * 16 : two * 16 + 16, :] = two_rows(*pieces, devices)


def output_kernel(
    xn_ref, gate_ref, adj_ref, zn_ref, w_out_ref, output_ref, d_logit_ref, part_ref
):
    rows, cols, width = adj_ref.shape
    total = None
    for row in range(rows):
        lanes = slice(row * cols, (row + 1) * cols)
        xn = xn_ref[:, lanes].astype(F32).T.astype(BF)
        proj_out = dot(xn, w_out_ref[...])
        gate = gate_ref[row]
        output_ref[row] = (gate * proj_out).astype(BF)
        d_logit = (adj_ref[row].astype(F32) * proj_out * gate * (1.0 - gate)).astype(BF)
        d_logit_ref[row] = d_logit
        term = dot(zn_ref[:, lanes], d_logit)
        total = term if total is None else total + term
    part_ref[...] = total


def unmix_kernel(got_ref, left_ref, right_ref, sent_ref, in_s, left_s, right_s):
    devices, half, cols = got_ref.shape
    own = left_ref.shape[0]
    count = devices * half // own
    in_s[...] = got_ref[...].astype(F32).reshape(devices * half, cols)
    for h in range(own):
        grad = in_s[pl.ds(h, count, stride=own), :]
        left_s[pl.ds(h, count, stride=own), :] = dot(grad.astype(BF), right_ref[h])
        right_s[pl.ds(h, count, stride=own), :] = dot(grad.T.astype(BF), left_ref[h])
    sent_ref[:, :half, :] = left_s[...].reshape(devices, half, cols).astype(BF)
    sent_ref[:, half:, :] = right_s[...].reshape(devices, half, cols).astype(BF)


def cells_kernel(
    got_ref, factor_ref, zn_ref, gate_part_ref, w_ref, columns_ref, u_ref, part_ref, cells_ref
):
    devices, depth, cols = got_ref.shape
    half = depth // 2
    hidden = factor_ref.shape[0] // 4
    for side in range(2):
        for two in range(half // 16):
            at = side * half + two * 16
            for part, grad in enumerate(apart(got_ref[:, at : at + 16, :], devices)):
                row = 2 * two + part
                lanes = slice(row * cols, (row + 1) * cols)
                for kind in (2 * side, 2 * side + 1):
                    place = slice(kind * hidden, (kind + 1) * hidden)
                    cells_ref[place, lanes] = (grad * factor_ref[place, lanes].astype(F32)).astype(BF)
    total = dot(zn_ref[...], cells_ref[...], ((1,), (1,)))
    part_ref[:, : 4 * hidden] = total.astype(BF)
    part_ref[:, 4 * hidden :] = gate_part_ref[...].astype(BF)
    u = dot(w_ref[...], cells_ref[...]) * columns_ref[:, :1]
    u_ref[...] = (u - jnp.mean(u, 0, keepdims=True)).astype(BF)


def pair_kernel(u_ref, d_logit_ref, pair_ref, gain_ref, w_gate_ref, d_pair_ref):
    rows, cols, width = pair_ref.shape
    gain = column(gain_ref[...])
    for row in range(rows):
        lanes = slice(row * cols, (row + 1) * cols)
        hat, rstd = centred(pair_ref[row].astype(F32).T)
        u = dot(w_gate_ref[...], d_logit_ref[row], ((1,), (1,))) * gain
        u = u + u_ref[:, lanes].astype(F32)
        d_pair_ref[row] = back_t(u, hat, rstd).T.astype(BF)


def sum_kernel(residues, got_ref, sent_ref):
    total = jnp.sum(got_ref[...].astype(F32), 0) / residues
    sent_ref[...] = jnp.broadcast_to(total.astype(BF)[None], sent_ref.shape)


def finish_kernel(got_ref, proj_ref, gate_ref):
    devices, chunk, depth = got_ref.shape
    wide = proj_ref.shape[1]
    total = got_ref[...].astype(F32).reshape(devices * chunk, depth)
    proj_ref[...] = total[:, :wide]
    gate_ref[...] = total[:, wide:]


def call(kernel, outs, scratch=(), flops=0, name=None, space=pltpu.VMEM, mib=12):
    spec = pl.BlockSpec(memory_space=pltpu.VMEM)

    def run(*args):
        moved = sum(a.size * a.dtype.itemsize for a in (*args, *outs))
        return pl.pallas_call(
            kernel,
            out_shape=list(outs),
            in_specs=[pl.BlockSpec(memory_space=space)] * len(args),
            out_specs=[spec] * len(outs),
            scratch_shapes=list(scratch),
            compiler_params=pltpu.CompilerParams(vmem_limit_bytes=mib * 1024 * 1024),
            cost_estimate=pl.CostEstimate(
                flops=flops, bytes_accessed=moved, transcendentals=0
            ),
            name=name,
        )(*args)

    return run


def small_blocks(pair, adjoint, mask, chain, gain_in, w_proj, w_gate, chain_bias, gain_out, w_out):
    rows, cols, width = pair.shape
    hidden = w_out.shape[0]
    devices = lax.axis_size("wide")
    own = hidden // devices
    residues = rows * devices
    cells = rows * cols
    half = rows * own
    shape = jax.ShapeDtypeStruct
    start = lax.axis_index("wide") * rows
    row_chain = lax.dynamic_slice_in_dim(chain, start, rows, 0)
    same = (row_chain[:, None] == chain[None, :]).astype(F32)
    gain_in, gain_out = gain_in[None], gain_out[None]
    sent, zn, cell_mask = call(
        project_kernel,
        [shape((devices, 2 * half, cols), BF), shape((width, cells), BF), shape((rows, cols), F32)],
        [
            pltpu.VMEM(pair.shape, BF),
            pltpu.VMEM((1, residues), jnp.int32),
            pltpu.VMEM(gain_in.shape, F32),
            pltpu.VMEM(w_proj.shape, BF),
            pltpu.SemaphoreType.DMA((4,)),
        ],
        name="project",
        space=pltpu.HBM,
        mib=56,
    )(pair, mask[None], gain_in, w_proj)
    got = swap(sent)
    factor, gate, t, columns = call(
        gate_kernel,
        [shape((4 * hidden, cells), BF), shape((rows, cols, width), F32), shape((hidden, cells), BF), shape((width, width), F32)],
        flops=2 * 10**9,
        name="gate",
    )(zn, adjoint, cell_mask, same, w_proj, w_gate, chain_bias, gain_out, w_out, gain_in)
    field = pltpu.VMEM((devices * half, cols), F32)
    channels = shape((own, residues, cols), BF)
    block = shape((devices, half, cols), BF)
    got, t = lax.optimization_barrier((got, t))
    sent, left, right = call(mix_kernel, [block, channels, channels], [field] * 3, name="mix")(got)
    got = swap(sent)
    sent, xn = call(norm_kernel, [block, shape((hidden, cells), BF)], name="norm")(got, t, gain_out)
    got = swap(sent)
    output, d_logit, gate_part = call(
        output_kernel,
        [shape(pair.shape, BF), shape(pair.shape, BF), shape((width, width), F32)],
        flops=2 * 10**9,
        name="output",
    )(xn, gate, adjoint, zn, w_out)
    got, gate_part = lax.optimization_barrier((got, gate_part))
    sent = call(
        unmix_kernel, [shape((devices, 2 * half, cols), BF)], [field] * 3, name="unmix"
    )(got, left, right)[0]
    got = swap(sent)
    u, part = call(
        cells_kernel,
        [shape((width, cells), BF), shape((width, 4 * hidden + width), BF)],
        [pltpu.VMEM((4 * hidden, cells), BF)],
        name="cells",
    )(got, factor, zn, gate_part, w_proj, columns)
    got = swap(part.reshape(devices, width // devices, -1))
    d_pair = call(pair_kernel, [shape(pair.shape, BF)], flops=2 * 10**9, name="pair")(
        u, d_logit, pair, gain_in, w_gate
    )[0]
    got, d_pair = lax.optimization_barrier((got, d_pair))
    sent = call(
        functools.partial(sum_kernel, residues), [shape(got.shape, BF)], name="sum"
    )(got)[0]
    d_proj, d_gate = call(
        finish_kernel, [shape((width, 4 * hidden), F32), shape((width, width), F32)], name="finish"
    )(swap(sent))
    return (output, d_pair, d_proj, d_gate)


def per_device(pair, adjoint, mask, chain, gain_in, w_proj, w_gate, chain_bias, gain_out, w_out):
    rows, cols, width = pair.shape
    hidden = w_out.shape[0]
    n_wide = lax.axis_size("wide")
    n_narrow = lax.axis_size("narrow")
    if n_narrow == 1 and (rows, cols, width) == (8, 128, 128) and hidden == 8 * n_wide == 128:
        return small_blocks(
            pair, adjoint, mask, chain, gain_in, w_proj, w_gate, chain_bias, gain_out, w_out
        )
    residues = rows * n_wide
    devices = n_wide * n_narrow
    own = hidden // devices
    row_start = lax.axis_index("wide") * rows
    col_start = lax.axis_index("narrow") * cols
    mask_f = mask.astype(jnp.float32)
    row_mask = lax.dynamic_slice_in_dim(mask_f, row_start, rows, 0)
    col_mask = lax.dynamic_slice_in_dim(mask_f, col_start, cols, 0)
    cell_mask = (row_mask[:, None] * col_mask[None, :])[None]
    row_chain = lax.dynamic_slice_in_dim(chain, row_start, rows, 0)
    col_chain = lax.dynamic_slice_in_dim(chain, col_start, cols, 0)
    same = (row_chain[:, None] == col_chain[None, :])[:, :, None]
    zn_f, z_hat, z_rstd = normalize(pair.astype(jnp.float32), gain_in, -1)
    zn = zn_f.astype(jnp.bfloat16)
    proj_a = jnp.einsum(
        "ijc,ch->hij", zn, w_proj[:, : 2 * hidden], preferred_element_type=jnp.float32
    )
    proj_b = jnp.einsum(
        "ijc,ch->hij", zn, w_proj[:, 2 * hidden :], preferred_element_type=jnp.float32
    )
    a_lin = proj_a[:hidden]
    sig_a = jax.nn.sigmoid(proj_a[hidden:])
    b_lin = proj_b[:hidden]
    sig_b = jax.nn.sigmoid(proj_b[hidden:])
    left_t = (cell_mask * sig_a * a_lin).astype(jnp.bfloat16)
    right_t = (cell_mask * sig_b * b_lin).astype(jnp.bfloat16)
    pairs = jnp.concatenate(
        [left_t.reshape(devices, own, rows, cols), right_t.reshape(devices, own, rows, cols)], 1
    )
    pairs = gather_cells(swap(pairs), n_wide, n_narrow)
    left_c, right_c = pairs[:own], pairs[own:]
    mixed_c = jnp.einsum("hik,hjk->hij", left_c, right_c, preferred_element_type=jnp.float32)
    mixed_t = swap(split_cells(mixed_c.astype(jnp.bfloat16), n_wide, n_narrow))
    mixed_t = mixed_t.reshape(hidden, rows, cols).astype(jnp.float32)
    xn_f, x_hat, x_rstd = normalize(mixed_t, gain_out[:, None, None], 0)
    xn = xn_f.astype(jnp.bfloat16)
    proj_out = jnp.einsum("hij,hc->ijc", xn, w_out, preferred_element_type=jnp.float32)
    logits = jnp.dot(zn, w_gate, preferred_element_type=jnp.float32) + jnp.where(
        same, chain_bias[1], chain_bias[0]
    )
    gate = jax.nn.sigmoid(logits)
    output = (gate * proj_out).astype(jnp.bfloat16)
    adj = adjoint.astype(jnp.float32)
    d_out = (adj * gate).astype(jnp.bfloat16)
    d_logit = (adj * proj_out * gate * (1.0 - gate)).astype(jnp.bfloat16)
    d_xn = jnp.einsum("ijc,hc->hij", d_out, w_out, preferred_element_type=jnp.float32)
    d_mixed_t = norm_back(d_xn * gain_out[:, None, None], x_hat, x_rstd, 0).astype(jnp.bfloat16)
    d_mixed_c = gather_cells(swap(d_mixed_t.reshape(devices, own, rows, cols)), n_wide, n_narrow)
    d_left_c = jnp.einsum("hij,hjk->hik", d_mixed_c, right_c, preferred_element_type=jnp.float32)
    d_right_c = jnp.einsum("hij,hik->hjk", d_mixed_c, left_c, preferred_element_type=jnp.float32)
    back = jnp.concatenate([d_left_c.astype(jnp.bfloat16), d_right_c.astype(jnp.bfloat16)], 0)
    back = swap(split_cells(back, n_wide, n_narrow))
    d_left = back[:, :own].reshape(hidden, rows, cols).astype(jnp.float32)
    d_right = back[:, own:].reshape(hidden, rows, cols).astype(jnp.float32)
    d_cells_a = jnp.concatenate(
        [d_left * cell_mask * sig_a, d_left * cell_mask * a_lin * sig_a * (1.0 - sig_a)], 0
    ).astype(jnp.bfloat16)
    d_cells_b = jnp.concatenate(
        [d_right * cell_mask * sig_b, d_right * cell_mask * b_lin * sig_b * (1.0 - sig_b)], 0
    ).astype(jnp.bfloat16)
    d_zn = jnp.einsum(
        "hij,ch->ijc", d_cells_a, w_proj[:, : 2 * hidden], preferred_element_type=jnp.float32
    )
    d_zn = d_zn + jnp.einsum(
        "hij,ch->ijc", d_cells_b, w_proj[:, 2 * hidden :], preferred_element_type=jnp.float32
    )
    d_zn = d_zn + jnp.dot(d_logit, w_gate.T, preferred_element_type=jnp.float32)
    d_pair = norm_back(d_zn * gain_in, z_hat, z_rstd, -1).astype(jnp.bfloat16)
    proj_part = jnp.concatenate(
        [
            jnp.einsum("ijc,hij->ch", zn, d_cells_a, preferred_element_type=jnp.float32),
            jnp.einsum("ijc,hij->ch", zn, d_cells_b, preferred_element_type=jnp.float32),
        ],
        1,
    )
    flat_z = zn.reshape(-1, width)
    gate_part = jnp.dot(flat_z.T, d_logit.reshape(-1, width), preferred_element_type=jnp.float32)
    parts = jnp.concatenate([proj_part, gate_part], 1)
    chunk = width // devices
    mine = swap(parts.astype(jnp.bfloat16).reshape(devices, chunk, -1))
    mine = jnp.sum(mine.astype(jnp.float32), 0) / residues
    mine = mine.astype(jnp.bfloat16)
    total = swap(jnp.broadcast_to(mine, (devices,) + mine.shape)).reshape(width, -1)
    total = total.astype(jnp.float32)
    return (output, d_pair, total[:, : 4 * hidden], total[:, 4 * hidden :])


def solution(mesh):
    placed = (
        P(("groups", "wide"), "narrow", None),
        P(("groups", "wide"), "narrow", None),
        P("groups"),
        P("groups"),
        P(),
        P(),
        P(),
        P(),
        P(),
        P(),
    )
    return jax.shard_map(
        per_device,
        mesh=mesh,
        in_specs=placed,
        out_specs=(
            P(("groups", "wide"), "narrow", None),
            P(("groups", "wide"), "narrow", None),
            P("groups", None),
            P("groups", None),
        ),
        check_vma=False,
    )
```

```python
import functools

import jax
import jax.numpy as jnp
from jax import lax
from jax.experimental import pallas as pl
from jax.experimental.pallas import tpu as pltpu
from jax.sharding import PartitionSpec as P

EPS = 1e-05


def normalize(values, gain, axis):
    centre = values - jnp.mean(values, axis, keepdims=True)
    rstd = lax.rsqrt(jnp.mean(centre * centre, axis, keepdims=True) + EPS)
    hat = centre * rstd
    return (hat * gain, hat, rstd)


def norm_back(scaled, hat, rstd, axis):
    return rstd * (
        scaled
        - jnp.mean(scaled, axis, keepdims=True)
        - hat * jnp.mean(scaled * hat, axis, keepdims=True)
    )


def swap(blocks):
    return lax.all_to_all(blocks, ("wide", "narrow"), split_axis=0, concat_axis=0, tiled=True)


def gather_cells(blocks, n_wide, n_narrow):
    _, own, rows, cols = blocks.shape
    shaped = blocks.reshape(n_wide, n_narrow, own, rows, cols)
    return jnp.transpose(shaped, (2, 0, 3, 1, 4)).reshape(own, n_wide * rows, n_narrow * cols)


def split_cells(field, n_wide, n_narrow):
    own, rows, cols = field.shape
    shaped = field.reshape(own, n_wide, rows // n_wide, n_narrow, cols // n_narrow)
    moved = jnp.transpose(shaped, (1, 3, 0, 2, 4))
    return moved.reshape(n_wide * n_narrow, own, rows // n_wide, cols // n_narrow)


BF = jnp.bfloat16
F32 = jnp.float32


def dot(a, b, over=((1,), (0,))):
    return lax.dot_general(a, b, (over, ((), ())), preferred_element_type=F32)


def column(row):
    return jnp.broadcast_to(row, (row.shape[1], row.shape[1])).T


def centred(x):
    centre = x - jnp.mean(x, 0, keepdims=True)
    rstd = lax.rsqrt(jnp.mean(centre * centre, 0, keepdims=True) + EPS)
    return centre * rstd, rstd


def back_t(scaled, hat, rstd):
    inner = hat * jnp.mean(scaled * hat, 0, keepdims=True)
    return rstd * (scaled - jnp.mean(scaled, 0, keepdims=True) - inner)


def two_rows(first, second, devices):
    own, cols = first.shape[0] // devices, first.shape[1]
    shape = (devices, own, cols)
    return jnp.concatenate([first.reshape(shape), second.reshape(shape)], 1).astype(BF)


def apart(block, devices):
    wide = block.astype(F32)
    own, cols = wide.shape[1] // 2, wide.shape[2]
    return [wide[:, at * own : (at + 1) * own].reshape(devices * own, cols) for at in range(2)]


def project_kernel(
    pair_hbm, mask_hbm, gain_hbm, w_hbm, sent_ref, zn_ref, mask_ref,
    pair_ref, mask_v, gain_ref, w_ref, sems,
):
    devices, depth, _ = sent_ref.shape
    rows, cols, width = pair_ref.shape
    start = lax.axis_index("wide") * rows
    copies = [
        pltpu.make_async_copy(gain_hbm, gain_ref, sems.at[0]),
        pltpu.make_async_copy(w_hbm, w_ref, sems.at[1]),
        pltpu.make_async_copy(mask_hbm, mask_v, sems.at[2]),
        pltpu.make_async_copy(pair_hbm, pair_ref, sems.at[3]),
    ]
    for copy in copies:
        copy.start()
    for copy in copies:
        copy.wait()
    mask_f = mask_v[...].astype(F32)
    shape = (rows, mask_f.shape[1])
    lane = lax.broadcasted_iota(jnp.int32, shape, 1)
    own = lane == start + lax.broadcasted_iota(jnp.int32, shape, 0)
    mask_ref[...] = mask_f * jnp.sum(jnp.where(own, mask_f, 0.0), 1, keepdims=True)
    gain = column(gain_ref[...])
    weights = w_ref[...].astype(F32).T.astype(BF)
    hidden = weights.shape[0] // 4
    half = depth // 2
    for two in range(rows // 2):
        pieces = []
        for row in (2 * two, 2 * two + 1):
            hat, _ = centred(pair_ref[row].astype(F32).T)
            zn = (hat * gain).astype(BF)
            zn_ref[:, row * cols : (row + 1) * cols] = zn
            proj = dot(weights, zn)
            mask = mask_ref[row : row + 1, :]
            left = mask * jax.nn.sigmoid(proj[hidden : 2 * hidden]) * proj[:hidden]
            right = mask * jax.nn.sigmoid(proj[3 * hidden :]) * proj[2 * hidden : 3 * hidden]
            pieces.append((left, right))
        at = two * 16
        sent_ref[:, at : at + 16, :] = two_rows(pieces[0][0], pieces[1][0], devices)
        sent_ref[:, half + at : half + at + 16, :] = two_rows(pieces[0][1], pieces[1][1], devices)


def gate_kernel(
    zn_ref, adj_ref, mask_ref, same_ref, w_ref, w_gate_ref, bias_ref, gain_ref, w_out_ref,
    gain_in_ref, factor_ref, gate_ref, t_ref, columns_ref,
):
    rows, cols, width = adj_ref.shape
    weights = w_ref[...].astype(F32).T.astype(BF)
    hidden = weights.shape[0] // 4
    w_gate = w_gate_ref[...].astype(F32).T.astype(BF)
    across, within = column(bias_ref[0:1, :]), column(bias_ref[1:2, :])
    gain = column(gain_ref[...])
    columns_ref[...] = column(gain_in_ref[...])
    for row in range(rows):
        lanes = slice(row * cols, (row + 1) * cols)
        zn = zn_ref[:, lanes]
        proj = dot(weights, zn)
        mask = mask_ref[row : row + 1, :]
        for side in range(2):
            lin = proj[2 * side * hidden : (2 * side + 1) * hidden]
            sig = jax.nn.sigmoid(proj[(2 * side + 1) * hidden : (2 * side + 2) * hidden])
            factor_ref[2 * side * hidden : (2 * side + 1) * hidden, lanes] = (mask * sig).astype(BF)
            factor_ref[(2 * side + 1) * hidden : (2 * side + 2) * hidden, lanes] = (
                mask * lin * sig * (1.0 - sig)
            ).astype(BF)
        bias = jnp.where(same_ref[row : row + 1, :] > 0.5, within, across)
        gate = jax.nn.sigmoid(dot(w_gate, zn) + bias).T
        gate_ref[row] = gate
        d_out = (adj_ref[row].astype(F32) * gate).astype(BF)
        t = dot(w_out_ref[...], d_out, ((1,), (1,))) * gain
        t_ref[:, lanes] = (t - jnp.mean(t, 0, keepdims=True)).astype(BF)


def mix_kernel(got_ref, sent_ref, left_ref, right_ref, left_s, right_s, out_s):
    devices, depth, cols = got_ref.shape
    own = left_ref.shape[0]
    half = depth // 2
    count = devices * half // own
    left_s[...] = got_ref[:, :half, :].astype(F32).reshape(devices * half, cols)
    right_s[...] = got_ref[:, half:, :].astype(F32).reshape(devices * half, cols)
    for h in range(own):
        left = left_s[pl.ds(h, count, stride=own), :].astype(BF)
        right = right_s[pl.ds(h, count, stride=own), :].astype(BF)
        left_ref[h] = left
        right_ref[h] = right
        out_s[pl.ds(h, count, stride=own), :] = dot(left, right, ((1,), (1,)))
    sent_ref[...] = out_s[...].reshape(devices, half, cols).astype(BF)


def norm_kernel(got_ref, t_ref, gain_ref, sent_out, xn_ref, sent_ref, sems):
    devices, depth, cols = got_ref.shape
    gain = column(gain_ref[...])
    copies = []
    for two in range(depth // 16):
        pieces = []
        for part, mixed in enumerate(apart(got_ref[:, two * 16 : two * 16 + 16, :], devices)):
            row = 2 * two + part
            lanes = slice(row * cols, (row + 1) * cols)
            hat, rstd = centred(mixed)
            xn_ref[:, lanes] = (hat * gain).astype(BF)
            pieces.append(back_t(t_ref[:, lanes].astype(F32), hat, rstd))
        sent_ref[:, two * 16 : two * 16 + 16, :] = two_rows(*pieces, devices)
        place = (slice(None), pl.ds(two * 16, 16))
        copies.append(
            pltpu.make_async_copy(sent_ref.at[place], sent_out.at[place], sems.at[two])
        )
        copies[-1].start()
    for copy in copies:
        copy.wait()


def output_kernel(
    xn_ref, gate_ref, adj_ref, zn_ref, w_out_ref, output_ref, d_logit_ref, part_ref
):
    rows, cols, width = adj_ref.shape
    total = None
    for row in range(rows):
        lanes = slice(row * cols, (row + 1) * cols)
        xn = xn_ref[:, lanes].astype(F32).T.astype(BF)
        proj_out = dot(xn, w_out_ref[...])
        gate = gate_ref[row]
        output_ref[row] = (gate * proj_out).astype(BF)
        d_logit = (adj_ref[row].astype(F32) * proj_out * gate * (1.0 - gate)).astype(BF)
        d_logit_ref[row] = d_logit
        term = dot(zn_ref[:, lanes], d_logit)
        total = term if total is None else total + term
    part_ref[...] = total


def unmix_kernel(got_ref, left_ref, right_ref, sent_ref, in_s, left_s, right_s):
    devices, half, cols = got_ref.shape
    own = left_ref.shape[0]
    count = devices * half // own
    in_s[...] = got_ref[...].astype(F32).reshape(devices * half, cols)
    for h in range(own):
        grad = in_s[pl.ds(h, count, stride=own), :]
        left_s[pl.ds(h, count, stride=own), :] = dot(grad.astype(BF), right_ref[h])
        right_s[pl.ds(h, count, stride=own), :] = dot(grad.T.astype(BF), left_ref[h])
    sent_ref[:, :half, :] = left_s[...].reshape(devices, half, cols).astype(BF)
    sent_ref[:, half:, :] = right_s[...].reshape(devices, half, cols).astype(BF)


def cells_kernel(
    got_ref, factor_ref, zn_ref, gate_part_ref, w_ref, columns_ref, u_ref, part_out,
    cells_ref, part_ref, sem,
):
    devices, depth, cols = got_ref.shape
    half = depth // 2
    hidden = factor_ref.shape[0] // 4
    for side in range(2):
        for two in range(half // 16):
            at = side * half + two * 16
            for part, grad in enumerate(apart(got_ref[:, at : at + 16, :], devices)):
                row = 2 * two + part
                lanes = slice(row * cols, (row + 1) * cols)
                for kind in (2 * side, 2 * side + 1):
                    place = slice(kind * hidden, (kind + 1) * hidden)
                    cells_ref[place, lanes] = (grad * factor_ref[place, lanes].astype(F32)).astype(BF)
    total = dot(zn_ref[...], cells_ref[...], ((1,), (1,)))
    part_ref[:, : 4 * hidden] = total.astype(BF)
    part_ref[:, 4 * hidden :] = gate_part_ref[...].astype(BF)
    copy = pltpu.make_async_copy(part_ref, part_out, sem)
    copy.start()
    u = dot(w_ref[...], cells_ref[...]) * columns_ref[:, :1]
    u_ref[...] = (u - jnp.mean(u, 0, keepdims=True)).astype(BF)
    copy.wait()


def pair_kernel(u_ref, d_logit_ref, pair_ref, gain_ref, w_gate_ref, d_pair_ref):
    rows, cols, width = pair_ref.shape
    gain = column(gain_ref[...])
    for row in range(rows):
        lanes = slice(row * cols, (row + 1) * cols)
        hat, rstd = centred(pair_ref[row].astype(F32).T)
        u = dot(w_gate_ref[...], d_logit_ref[row], ((1,), (1,))) * gain
        u = u + u_ref[:, lanes].astype(F32)
        d_pair_ref[row] = back_t(u, hat, rstd).T.astype(BF)


def sum_kernel(residues, got_ref, sent_ref):
    total = jnp.sum(got_ref[...].astype(F32), 0) / residues
    sent_ref[...] = jnp.broadcast_to(total.astype(BF)[None], sent_ref.shape)


def finish_kernel(got_ref, proj_ref, gate_ref):
    devices, chunk, depth = got_ref.shape
    wide = proj_ref.shape[1]
    total = got_ref[...].astype(F32).reshape(devices * chunk, depth)
    proj_ref[...] = total[:, :wide]
    gate_ref[...] = total[:, wide:]


def call(kernel, outs, scratch=(), flops=0, name=None, space=pltpu.VMEM, mib=12, away=()):
    spec = pl.BlockSpec(memory_space=pltpu.VMEM)

    def run(*args):
        moved = sum(a.size * a.dtype.itemsize for a in (*args, *outs))
        return pl.pallas_call(
            kernel,
            out_shape=list(outs),
            in_specs=[pl.BlockSpec(memory_space=space)] * len(args),
            out_specs=[pl.BlockSpec(memory_space=pl.ANY) if i in away else spec for i in range(len(outs))],
            scratch_shapes=list(scratch),
            compiler_params=pltpu.CompilerParams(vmem_limit_bytes=mib * 1024 * 1024),
            cost_estimate=pl.CostEstimate(
                flops=flops, bytes_accessed=moved, transcendentals=0
            ),
            name=name,
        )(*args)

    return run


def small_blocks(pair, adjoint, mask, chain, gain_in, w_proj, w_gate, chain_bias, gain_out, w_out):
    rows, cols, width = pair.shape
    hidden = w_out.shape[0]
    devices = lax.axis_size("wide")
    own = hidden // devices
    residues = rows * devices
    cells = rows * cols
    half = rows * own
    shape = jax.ShapeDtypeStruct
    start = lax.axis_index("wide") * rows
    row_chain = lax.dynamic_slice_in_dim(chain, start, rows, 0)
    same = (row_chain[:, None] == chain[None, :]).astype(F32)
    gain_in, gain_out = gain_in[None], gain_out[None]
    sent, zn, cell_mask = call(
        project_kernel,
        [shape((devices, 2 * half, cols), BF), shape((width, cells), BF), shape((rows, cols), F32)],
        [
            pltpu.VMEM(pair.shape, BF),
            pltpu.VMEM((1, residues), jnp.int32),
            pltpu.VMEM(gain_in.shape, F32),
            pltpu.VMEM(w_proj.shape, BF),
            pltpu.SemaphoreType.DMA((4,)),
        ],
        name="project",
        space=pltpu.HBM,
        mib=56,
    )(pair, mask[None], gain_in, w_proj)
    got = swap(sent)
    factor, gate, t, columns = call(
        gate_kernel,
        [shape((4 * hidden, cells), BF), shape((rows, cols, width), F32), shape((hidden, cells), BF), shape((width, width), F32)],
        flops=2 * 10**9,
        name="gate",
    )(zn, adjoint, cell_mask, same, w_proj, w_gate, chain_bias, gain_out, w_out, gain_in)
    field = pltpu.VMEM((devices * half, cols), F32)
    channels = shape((own, residues, cols), BF)
    block = shape((devices, half, cols), BF)
    got, t = lax.optimization_barrier((got, t))
    sent, left, right = call(mix_kernel, [block, channels, channels], [field] * 3, name="mix")(got)
    got = swap(sent)
    sent, xn = call(
        norm_kernel,
        [block, shape((hidden, cells), BF)],
        [pltpu.VMEM(block.shape, BF), pltpu.SemaphoreType.DMA((half // 16,))],
        name="norm",
        away=(0,),
    )(got, t, gain_out)
    got = swap(sent)
    output, d_logit, gate_part = call(
        output_kernel,
        [shape(pair.shape, BF), shape(pair.shape, BF), shape((width, width), F32)],
        flops=2 * 10**9,
        name="output",
    )(xn, gate, adjoint, zn, w_out)
    got, gate_part = lax.optimization_barrier((got, gate_part))
    sent = call(
        unmix_kernel, [shape((devices, 2 * half, cols), BF)], [field] * 3, name="unmix"
    )(got, left, right)[0]
    got = swap(sent)
    u, part = call(
        cells_kernel,
        [shape((width, cells), BF), shape((width, 4 * hidden + width), BF)],
        [
            pltpu.VMEM((4 * hidden, cells), BF),
            pltpu.VMEM((width, 4 * hidden + width), BF),
            pltpu.SemaphoreType.DMA,
        ],
        name="cells",
        away=(1,),
    )(got, factor, zn, gate_part, w_proj, columns)
    got = swap(part.reshape(devices, width // devices, -1))
    d_pair = call(pair_kernel, [shape(pair.shape, BF)], flops=2 * 10**9, name="pair")(
        u, d_logit, pair, gain_in, w_gate
    )[0]
    got, d_pair = lax.optimization_barrier((got, d_pair))
    sent = call(
        functools.partial(sum_kernel, residues), [shape(got.shape, BF)], name="sum"
    )(got)[0]
    d_proj, d_gate = call(
        finish_kernel, [shape((width, 4 * hidden), F32), shape((width, width), F32)], name="finish"
    )(swap(sent))
    return (output, d_pair, d_proj, d_gate)


def per_device(pair, adjoint, mask, chain, gain_in, w_proj, w_gate, chain_bias, gain_out, w_out):
    rows, cols, width = pair.shape
    hidden = w_out.shape[0]
    n_wide = lax.axis_size("wide")
    n_narrow = lax.axis_size("narrow")
    if n_narrow == 1 and (rows, cols, width) == (8, 128, 128) and hidden == 8 * n_wide == 128:
        return small_blocks(
            pair, adjoint, mask, chain, gain_in, w_proj, w_gate, chain_bias, gain_out, w_out
        )
    residues = rows * n_wide
    devices = n_wide * n_narrow
    own = hidden // devices
    row_start = lax.axis_index("wide") * rows
    col_start = lax.axis_index("narrow") * cols
    mask_f = mask.astype(jnp.float32)
    row_mask = lax.dynamic_slice_in_dim(mask_f, row_start, rows, 0)
    col_mask = lax.dynamic_slice_in_dim(mask_f, col_start, cols, 0)
    cell_mask = (row_mask[:, None] * col_mask[None, :])[None]
    row_chain = lax.dynamic_slice_in_dim(chain, row_start, rows, 0)
    col_chain = lax.dynamic_slice_in_dim(chain, col_start, cols, 0)
    same = (row_chain[:, None] == col_chain[None, :])[:, :, None]
    zn_f, z_hat, z_rstd = normalize(pair.astype(jnp.float32), gain_in, -1)
    zn = zn_f.astype(jnp.bfloat16)
    proj_a = jnp.einsum(
        "ijc,ch->hij", zn, w_proj[:, : 2 * hidden], preferred_element_type=jnp.float32
    )
    proj_b = jnp.einsum(
        "ijc,ch->hij", zn, w_proj[:, 2 * hidden :], preferred_element_type=jnp.float32
    )
    a_lin = proj_a[:hidden]
    sig_a = jax.nn.sigmoid(proj_a[hidden:])
    b_lin = proj_b[:hidden]
    sig_b = jax.nn.sigmoid(proj_b[hidden:])
    left_t = (cell_mask * sig_a * a_lin).astype(jnp.bfloat16)
    right_t = (cell_mask * sig_b * b_lin).astype(jnp.bfloat16)
    pairs = jnp.concatenate(
        [left_t.reshape(devices, own, rows, cols), right_t.reshape(devices, own, rows, cols)], 1
    )
    pairs = gather_cells(swap(pairs), n_wide, n_narrow)
    left_c, right_c = pairs[:own], pairs[own:]
    mixed_c = jnp.einsum("hik,hjk->hij", left_c, right_c, preferred_element_type=jnp.float32)
    mixed_t = swap(split_cells(mixed_c.astype(jnp.bfloat16), n_wide, n_narrow))
    mixed_t = mixed_t.reshape(hidden, rows, cols).astype(jnp.float32)
    xn_f, x_hat, x_rstd = normalize(mixed_t, gain_out[:, None, None], 0)
    xn = xn_f.astype(jnp.bfloat16)
    proj_out = jnp.einsum("hij,hc->ijc", xn, w_out, preferred_element_type=jnp.float32)
    logits = jnp.dot(zn, w_gate, preferred_element_type=jnp.float32) + jnp.where(
        same, chain_bias[1], chain_bias[0]
    )
    gate = jax.nn.sigmoid(logits)
    output = (gate * proj_out).astype(jnp.bfloat16)
    adj = adjoint.astype(jnp.float32)
    d_out = (adj * gate).astype(jnp.bfloat16)
    d_logit = (adj * proj_out * gate * (1.0 - gate)).astype(jnp.bfloat16)
    d_xn = jnp.einsum("ijc,hc->hij", d_out, w_out, preferred_element_type=jnp.float32)
    d_mixed_t = norm_back(d_xn * gain_out[:, None, None], x_hat, x_rstd, 0).astype(jnp.bfloat16)
    d_mixed_c = gather_cells(swap(d_mixed_t.reshape(devices, own, rows, cols)), n_wide, n_narrow)
    d_left_c = jnp.einsum("hij,hjk->hik", d_mixed_c, right_c, preferred_element_type=jnp.float32)
    d_right_c = jnp.einsum("hij,hik->hjk", d_mixed_c, left_c, preferred_element_type=jnp.float32)
    back = jnp.concatenate([d_left_c.astype(jnp.bfloat16), d_right_c.astype(jnp.bfloat16)], 0)
    back = swap(split_cells(back, n_wide, n_narrow))
    d_left = back[:, :own].reshape(hidden, rows, cols).astype(jnp.float32)
    d_right = back[:, own:].reshape(hidden, rows, cols).astype(jnp.float32)
    d_cells_a = jnp.concatenate(
        [d_left * cell_mask * sig_a, d_left * cell_mask * a_lin * sig_a * (1.0 - sig_a)], 0
    ).astype(jnp.bfloat16)
    d_cells_b = jnp.concatenate(
        [d_right * cell_mask * sig_b, d_right * cell_mask * b_lin * sig_b * (1.0 - sig_b)], 0
    ).astype(jnp.bfloat16)
    d_zn = jnp.einsum(
        "hij,ch->ijc", d_cells_a, w_proj[:, : 2 * hidden], preferred_element_type=jnp.float32
    )
    d_zn = d_zn + jnp.einsum(
        "hij,ch->ijc", d_cells_b, w_proj[:, 2 * hidden :], preferred_element_type=jnp.float32
    )
    d_zn = d_zn + jnp.dot(d_logit, w_gate.T, preferred_element_type=jnp.float32)
    d_pair = norm_back(d_zn * gain_in, z_hat, z_rstd, -1).astype(jnp.bfloat16)
    proj_part = jnp.concatenate(
        [
            jnp.einsum("ijc,hij->ch", zn, d_cells_a, preferred_element_type=jnp.float32),
            jnp.einsum("ijc,hij->ch", zn, d_cells_b, preferred_element_type=jnp.float32),
        ],
        1,
    )
    flat_z = zn.reshape(-1, width)
    gate_part = jnp.dot(flat_z.T, d_logit.reshape(-1, width), preferred_element_type=jnp.float32)
    parts = jnp.concatenate([proj_part, gate_part], 1)
    chunk = width // devices
    mine = swap(parts.astype(jnp.bfloat16).reshape(devices, chunk, -1))
    mine = jnp.sum(mine.astype(jnp.float32), 0) / residues
    mine = mine.astype(jnp.bfloat16)
    total = swap(jnp.broadcast_to(mine, (devices,) + mine.shape)).reshape(width, -1)
    total = total.astype(jnp.float32)
    return (output, d_pair, total[:, : 4 * hidden], total[:, 4 * hidden :])


def solution(mesh):
    placed = (
        P(("groups", "wide"), "narrow", None),
        P(("groups", "wide"), "narrow", None),
        P("groups"),
        P("groups"),
        P(),
        P(),
        P(),
        P(),
        P(),
        P(),
    )
    return jax.shard_map(
        per_device,
        mesh=mesh,
        in_specs=placed,
        out_specs=(
            P(("groups", "wide"), "narrow", None),
            P(("groups", "wide"), "narrow", None),
            P("groups", None),
            P("groups", None),
        ),
        check_vma=False,
    )
```

```python
import functools

import jax
import jax.numpy as jnp
from jax import lax
from jax.experimental import pallas as pl
from jax.experimental.pallas import tpu as pltpu
from jax.sharding import PartitionSpec as P

EPS = 1e-05


def normalize(values, gain, axis):
    centre = values - jnp.mean(values, axis, keepdims=True)
    rstd = lax.rsqrt(jnp.mean(centre * centre, axis, keepdims=True) + EPS)
    hat = centre * rstd
    return (hat * gain, hat, rstd)


def norm_back(scaled, hat, rstd, axis):
    return rstd * (
        scaled
        - jnp.mean(scaled, axis, keepdims=True)
        - hat * jnp.mean(scaled * hat, axis, keepdims=True)
    )


def swap(blocks):
    return lax.all_to_all(blocks, ("wide", "narrow"), split_axis=0, concat_axis=0, tiled=True)


def gather_cells(blocks, n_wide, n_narrow):
    _, own, rows, cols = blocks.shape
    shaped = blocks.reshape(n_wide, n_narrow, own, rows, cols)
    return jnp.transpose(shaped, (2, 0, 3, 1, 4)).reshape(own, n_wide * rows, n_narrow * cols)


def split_cells(field, n_wide, n_narrow):
    own, rows, cols = field.shape
    shaped = field.reshape(own, n_wide, rows // n_wide, n_narrow, cols // n_narrow)
    moved = jnp.transpose(shaped, (1, 3, 0, 2, 4))
    return moved.reshape(n_wide * n_narrow, own, rows // n_wide, cols // n_narrow)


BF = jnp.bfloat16
F32 = jnp.float32


def dot(a, b, over=((1,), (0,))):
    return lax.dot_general(a, b, (over, ((), ())), preferred_element_type=F32)


def column(row):
    return jnp.broadcast_to(row, (row.shape[1], row.shape[1])).T


def centred(x):
    centre = x - jnp.mean(x, 0, keepdims=True)
    rstd = lax.rsqrt(jnp.mean(centre * centre, 0, keepdims=True) + EPS)
    return centre * rstd, rstd


def back_t(scaled, hat, rstd):
    inner = hat * jnp.mean(scaled * hat, 0, keepdims=True)
    return rstd * (scaled - jnp.mean(scaled, 0, keepdims=True) - inner)


def two_rows(first, second, devices):
    own, cols = first.shape[0] // devices, first.shape[1]
    shape = (devices, own, cols)
    return jnp.concatenate([first.reshape(shape), second.reshape(shape)], 1).astype(BF)


def apart(block, devices):
    wide = block.astype(F32)
    own, cols = wide.shape[1] // 2, wide.shape[2]
    return [wide[:, at * own : (at + 1) * own].reshape(devices * own, cols) for at in range(2)]


def project_kernel(
    pair_hbm, mask_hbm, gain_hbm, w_hbm, sent_ref, zn_ref, mask_ref,
    pair_ref, mask_v, gain_ref, w_ref, sems,
):
    devices, depth, _ = sent_ref.shape
    rows, cols, width = pair_ref.shape
    start = lax.axis_index("wide") * rows
    copies = [
        pltpu.make_async_copy(gain_hbm, gain_ref, sems.at[0]),
        pltpu.make_async_copy(w_hbm, w_ref, sems.at[1]),
        pltpu.make_async_copy(mask_hbm, mask_v, sems.at[2]),
        pltpu.make_async_copy(pair_hbm, pair_ref, sems.at[3]),
    ]
    for copy in copies:
        copy.start()
    for copy in copies:
        copy.wait()
    mask_f = mask_v[...].astype(F32)
    shape = (rows, mask_f.shape[1])
    lane = lax.broadcasted_iota(jnp.int32, shape, 1)
    own = lane == start + lax.broadcasted_iota(jnp.int32, shape, 0)
    mask_ref[...] = mask_f * jnp.sum(jnp.where(own, mask_f, 0.0), 1, keepdims=True)
    gain = column(gain_ref[...])
    weights = w_ref[...].astype(F32).T.astype(BF)
    hidden = weights.shape[0] // 4
    half = depth // 2
    for two in range(rows // 2):
        pieces = []
        for row in (2 * two, 2 * two + 1):
            hat, _ = centred(pair_ref[row].astype(F32).T)
            zn = (hat * gain).astype(BF)
            zn_ref[:, row * cols : (row + 1) * cols] = zn
            proj = dot(weights, zn)
            mask = mask_ref[row : row + 1, :]
            left = mask * jax.nn.sigmoid(proj[hidden : 2 * hidden]) * proj[:hidden]
            right = mask * jax.nn.sigmoid(proj[3 * hidden :]) * proj[2 * hidden : 3 * hidden]
            pieces.append((left, right))
        at = two * 16
        sent_ref[:, at : at + 16, :] = two_rows(pieces[0][0], pieces[1][0], devices)
        sent_ref[:, half + at : half + at + 16, :] = two_rows(pieces[0][1], pieces[1][1], devices)


def gate_kernel(
    zn_ref, adj_ref, mask_ref, same_ref, w_ref, w_gate_ref, bias_ref, gain_ref, w_out_ref,
    gain_in_ref, factor_ref, gate_ref, t_ref, columns_ref,
):
    rows, cols, width = adj_ref.shape
    weights = w_ref[...].astype(F32).T.astype(BF)
    hidden = weights.shape[0] // 4
    w_gate = w_gate_ref[...].astype(F32).T.astype(BF)
    across, within = column(bias_ref[0:1, :]), column(bias_ref[1:2, :])
    gain = column(gain_ref[...])
    columns_ref[...] = column(gain_in_ref[...])
    for row in range(rows):
        lanes = slice(row * cols, (row + 1) * cols)
        zn = zn_ref[:, lanes]
        proj = dot(weights, zn)
        mask = mask_ref[row : row + 1, :]
        for side in range(2):
            lin = proj[2 * side * hidden : (2 * side + 1) * hidden]
            sig = jax.nn.sigmoid(proj[(2 * side + 1) * hidden : (2 * side + 2) * hidden])
            factor_ref[2 * side * hidden : (2 * side + 1) * hidden, lanes] = (mask * sig).astype(BF)
            factor_ref[(2 * side + 1) * hidden : (2 * side + 2) * hidden, lanes] = (
                mask * lin * sig * (1.0 - sig)
            ).astype(BF)
        bias = jnp.where(same_ref[row : row + 1, :] > 0.5, within, across)
        gate = jax.nn.sigmoid(dot(w_gate, zn) + bias).T
        gate_ref[row] = gate
        d_out = (adj_ref[row].astype(F32) * gate).astype(BF)
        t = dot(w_out_ref[...], d_out, ((1,), (1,))) * gain
        t_ref[:, lanes] = (t - jnp.mean(t, 0, keepdims=True)).astype(BF)


def mix_kernel(got_ref, sent_ref, left_ref, right_ref, left_s, right_s, out_s):
    devices, depth, cols = got_ref.shape
    own = left_ref.shape[0]
    half = depth // 2
    count = devices * half // own
    left_s[...] = got_ref[:, :half, :].astype(F32).reshape(devices * half, cols)
    right_s[...] = got_ref[:, half:, :].astype(F32).reshape(devices * half, cols)
    for h in range(own):
        left = left_s[pl.ds(h, count, stride=own), :].astype(BF)
        right = right_s[pl.ds(h, count, stride=own), :].astype(BF)
        left_ref[h] = left
        right_ref[h] = right
        out_s[pl.ds(h, count, stride=own), :] = dot(left, right, ((1,), (1,)))
    sent_ref[...] = out_s[...].reshape(devices, half, cols).astype(BF)


def norm_kernel(
    got_ref, t_ref, gain_ref, gate_ref, adj_ref, zn_ref, w_out_ref,
    sent_ref, xn_ref, d_logit_ref, part_ref,
):
    devices, depth, cols = got_ref.shape
    gain = column(gain_ref[...])
    total = None
    for two in range(depth // 16):
        pieces = []
        for part, mixed in enumerate(apart(got_ref[:, two * 16 : two * 16 + 16, :], devices)):
            row = 2 * two + part
            lanes = slice(row * cols, (row + 1) * cols)
            hat, rstd = centred(mixed)
            pieces.append(back_t(t_ref[:, lanes].astype(F32), hat, rstd))
            scaled = hat * gain
            xn_ref[:, lanes] = scaled.astype(BF)
            proj_out = dot(scaled.T.astype(BF), w_out_ref[...])
            gate = gate_ref[row]
            d_logit = (adj_ref[row].astype(F32) * proj_out * gate * (1.0 - gate)).astype(BF)
            d_logit_ref[row] = d_logit
            term = dot(zn_ref[:, lanes], d_logit)
            total = term if total is None else total + term
        sent_ref[:, two * 16 : two * 16 + 16, :] = two_rows(*pieces, devices)
    part_ref[...] = total


def output_kernel(xn_ref, gate_ref, w_out_ref, output_ref):
    rows, cols, width = gate_ref.shape
    for row in range(rows):
        lanes = slice(row * cols, (row + 1) * cols)
        xn = xn_ref[:, lanes].astype(F32).T.astype(BF)
        output_ref[row] = (gate_ref[row] * dot(xn, w_out_ref[...])).astype(BF)


def unmix_kernel(got_ref, left_ref, right_ref, sent_ref, in_s, left_s, right_s):
    devices, half, cols = got_ref.shape
    own = left_ref.shape[0]
    count = devices * half // own
    in_s[...] = got_ref[...].astype(F32).reshape(devices * half, cols)
    for h in range(own):
        grad = in_s[pl.ds(h, count, stride=own), :]
        left_s[pl.ds(h, count, stride=own), :] = dot(grad.astype(BF), right_ref[h])
        right_s[pl.ds(h, count, stride=own), :] = dot(grad.T.astype(BF), left_ref[h])
    sent_ref[:, :half, :] = left_s[...].reshape(devices, half, cols).astype(BF)
    sent_ref[:, half:, :] = right_s[...].reshape(devices, half, cols).astype(BF)


def cells_kernel(
    got_ref, factor_ref, zn_ref, gate_part_ref, w_ref, columns_ref, u_ref, part_ref, cells_ref
):
    devices, depth, cols = got_ref.shape
    half = depth // 2
    hidden = factor_ref.shape[0] // 4
    for side in range(2):
        for two in range(half // 16):
            at = side * half + two * 16
            for part, grad in enumerate(apart(got_ref[:, at : at + 16, :], devices)):
                row = 2 * two + part
                lanes = slice(row * cols, (row + 1) * cols)
                for kind in (2 * side, 2 * side + 1):
                    place = slice(kind * hidden, (kind + 1) * hidden)
                    cells_ref[place, lanes] = (grad * factor_ref[place, lanes].astype(F32)).astype(BF)
    total = dot(zn_ref[...], cells_ref[...], ((1,), (1,)))
    part_ref[:, : 4 * hidden] = total.astype(BF)
    part_ref[:, 4 * hidden :] = gate_part_ref[...].astype(BF)
    u = dot(w_ref[...], cells_ref[...]) * columns_ref[:, :1]
    u_ref[...] = (u - jnp.mean(u, 0, keepdims=True)).astype(BF)


def pair_kernel(u_ref, d_logit_ref, pair_ref, gain_ref, w_gate_ref, d_pair_ref):
    rows, cols, width = pair_ref.shape
    gain = column(gain_ref[...])
    for row in range(rows):
        lanes = slice(row * cols, (row + 1) * cols)
        hat, rstd = centred(pair_ref[row].astype(F32).T)
        u = dot(w_gate_ref[...], d_logit_ref[row], ((1,), (1,))) * gain
        u = u + u_ref[:, lanes].astype(F32)
        d_pair_ref[row] = back_t(u, hat, rstd).T.astype(BF)


def sum_kernel(residues, got_ref, sent_ref):
    total = jnp.sum(got_ref[...].astype(F32), 0) / residues
    sent_ref[...] = jnp.broadcast_to(total.astype(BF)[None], sent_ref.shape)


def finish_kernel(got_ref, proj_ref, gate_ref):
    devices, chunk, depth = got_ref.shape
    wide = proj_ref.shape[1]
    total = got_ref[...].astype(F32).reshape(devices * chunk, depth)
    proj_ref[...] = total[:, :wide]
    gate_ref[...] = total[:, wide:]


def call(kernel, outs, scratch=(), flops=0, name=None, space=pltpu.VMEM, mib=12):
    spec = pl.BlockSpec(memory_space=pltpu.VMEM)

    def run(*args):
        moved = sum(a.size * a.dtype.itemsize for a in (*args, *outs))
        return pl.pallas_call(
            kernel,
            out_shape=list(outs),
            in_specs=[pl.BlockSpec(memory_space=space)] * len(args),
            out_specs=[spec] * len(outs),
            scratch_shapes=list(scratch),
            compiler_params=pltpu.CompilerParams(vmem_limit_bytes=mib * 1024 * 1024),
            cost_estimate=pl.CostEstimate(
                flops=flops, bytes_accessed=moved, transcendentals=0
            ),
            name=name,
        )(*args)

    return run


def small_blocks(pair, adjoint, mask, chain, gain_in, w_proj, w_gate, chain_bias, gain_out, w_out):
    rows, cols, width = pair.shape
    hidden = w_out.shape[0]
    devices = lax.axis_size("wide")
    own = hidden // devices
    residues = rows * devices
    cells = rows * cols
    half = rows * own
    shape = jax.ShapeDtypeStruct
    start = lax.axis_index("wide") * rows
    row_chain = lax.dynamic_slice_in_dim(chain, start, rows, 0)
    same = (row_chain[:, None] == chain[None, :]).astype(F32)
    gain_in, gain_out = gain_in[None], gain_out[None]
    sent, zn, cell_mask = call(
        project_kernel,
        [shape((devices, 2 * half, cols), BF), shape((width, cells), BF), shape((rows, cols), F32)],
        [
            pltpu.VMEM(pair.shape, BF),
            pltpu.VMEM((1, residues), jnp.int32),
            pltpu.VMEM(gain_in.shape, F32),
            pltpu.VMEM(w_proj.shape, BF),
            pltpu.SemaphoreType.DMA((4,)),
        ],
        name="project",
        space=pltpu.HBM,
        mib=56,
    )(pair, mask[None], gain_in, w_proj)
    got = swap(sent)
    factor, gate, t, columns = call(
        gate_kernel,
        [shape((4 * hidden, cells), BF), shape((rows, cols, width), F32), shape((hidden, cells), BF), shape((width, width), F32)],
        flops=2 * 10**9,
        name="gate",
    )(zn, adjoint, cell_mask, same, w_proj, w_gate, chain_bias, gain_out, w_out, gain_in)
    field = pltpu.VMEM((devices * half, cols), F32)
    channels = shape((own, residues, cols), BF)
    block = shape((devices, half, cols), BF)
    got, t = lax.optimization_barrier((got, t))
    sent, left, right = call(mix_kernel, [block, channels, channels], [field] * 3, name="mix")(got)
    got = swap(sent)
    sent, xn, d_logit, gate_part = call(
        norm_kernel,
        [block, shape((hidden, cells), BF), shape(pair.shape, BF), shape((width, width), F32)],
        name="norm",
    )(got, t, gain_out, gate, adjoint, zn, w_out)
    got = swap(sent)
    sent = call(
        unmix_kernel, [shape((devices, 2 * half, cols), BF)], [field] * 3, name="unmix"
    )(got, left, right)[0]
    got = swap(sent)
    u, part = call(
        cells_kernel,
        [shape((width, cells), BF), shape((width, 4 * hidden + width), BF)],
        [pltpu.VMEM((4 * hidden, cells), BF)],
        name="cells",
    )(got, factor, zn, gate_part, w_proj, columns)
    got = swap(part.reshape(devices, width // devices, -1))
    d_pair = call(pair_kernel, [shape(pair.shape, BF)], flops=2 * 10**9, name="pair")(
        u, d_logit, pair, gain_in, w_gate
    )[0]
    output = call(output_kernel, [shape(pair.shape, BF)], flops=2 * 10**9, name="output")(
        xn, gate, w_out
    )[0]
    got, d_pair, output = lax.optimization_barrier((got, d_pair, output))
    sent = call(
        functools.partial(sum_kernel, residues), [shape(got.shape, BF)], name="sum"
    )(got)[0]
    d_proj, d_gate = call(
        finish_kernel, [shape((width, 4 * hidden), F32), shape((width, width), F32)], name="finish"
    )(swap(sent))
    return (output, d_pair, d_proj, d_gate)


def per_device(pair, adjoint, mask, chain, gain_in, w_proj, w_gate, chain_bias, gain_out, w_out):
    rows, cols, width = pair.shape
    hidden = w_out.shape[0]
    n_wide = lax.axis_size("wide")
    n_narrow = lax.axis_size("narrow")
    if n_narrow == 1 and (rows, cols, width) == (8, 128, 128) and hidden == 8 * n_wide == 128:
        return small_blocks(
            pair, adjoint, mask, chain, gain_in, w_proj, w_gate, chain_bias, gain_out, w_out
        )
    residues = rows * n_wide
    devices = n_wide * n_narrow
    own = hidden // devices
    row_start = lax.axis_index("wide") * rows
    col_start = lax.axis_index("narrow") * cols
    mask_f = mask.astype(jnp.float32)
    row_mask = lax.dynamic_slice_in_dim(mask_f, row_start, rows, 0)
    col_mask = lax.dynamic_slice_in_dim(mask_f, col_start, cols, 0)
    cell_mask = (row_mask[:, None] * col_mask[None, :])[None]
    row_chain = lax.dynamic_slice_in_dim(chain, row_start, rows, 0)
    col_chain = lax.dynamic_slice_in_dim(chain, col_start, cols, 0)
    same = (row_chain[:, None] == col_chain[None, :])[:, :, None]
    zn_f, z_hat, z_rstd = normalize(pair.astype(jnp.float32), gain_in, -1)
    zn = zn_f.astype(jnp.bfloat16)
    proj_a = jnp.einsum(
        "ijc,ch->hij", zn, w_proj[:, : 2 * hidden], preferred_element_type=jnp.float32
    )
    proj_b = jnp.einsum(
        "ijc,ch->hij", zn, w_proj[:, 2 * hidden :], preferred_element_type=jnp.float32
    )
    a_lin = proj_a[:hidden]
    sig_a = jax.nn.sigmoid(proj_a[hidden:])
    b_lin = proj_b[:hidden]
    sig_b = jax.nn.sigmoid(proj_b[hidden:])
    left_t = (cell_mask * sig_a * a_lin).astype(jnp.bfloat16)
    right_t = (cell_mask * sig_b * b_lin).astype(jnp.bfloat16)
    pairs = jnp.concatenate(
        [left_t.reshape(devices, own, rows, cols), right_t.reshape(devices, own, rows, cols)], 1
    )
    pairs = gather_cells(swap(pairs), n_wide, n_narrow)
    left_c, right_c = pairs[:own], pairs[own:]
    mixed_c = jnp.einsum("hik,hjk->hij", left_c, right_c, preferred_element_type=jnp.float32)
    mixed_t = swap(split_cells(mixed_c.astype(jnp.bfloat16), n_wide, n_narrow))
    mixed_t = mixed_t.reshape(hidden, rows, cols).astype(jnp.float32)
    xn_f, x_hat, x_rstd = normalize(mixed_t, gain_out[:, None, None], 0)
    xn = xn_f.astype(jnp.bfloat16)
    proj_out = jnp.einsum("hij,hc->ijc", xn, w_out, preferred_element_type=jnp.float32)
    logits = jnp.dot(zn, w_gate, preferred_element_type=jnp.float32) + jnp.where(
        same, chain_bias[1], chain_bias[0]
    )
    gate = jax.nn.sigmoid(logits)
    output = (gate * proj_out).astype(jnp.bfloat16)
    adj = adjoint.astype(jnp.float32)
    d_out = (adj * gate).astype(jnp.bfloat16)
    d_logit = (adj * proj_out * gate * (1.0 - gate)).astype(jnp.bfloat16)
    d_xn = jnp.einsum("ijc,hc->hij", d_out, w_out, preferred_element_type=jnp.float32)
    d_mixed_t = norm_back(d_xn * gain_out[:, None, None], x_hat, x_rstd, 0).astype(jnp.bfloat16)
    d_mixed_c = gather_cells(swap(d_mixed_t.reshape(devices, own, rows, cols)), n_wide, n_narrow)
    d_left_c = jnp.einsum("hij,hjk->hik", d_mixed_c, right_c, preferred_element_type=jnp.float32)
    d_right_c = jnp.einsum("hij,hik->hjk", d_mixed_c, left_c, preferred_element_type=jnp.float32)
    back = jnp.concatenate([d_left_c.astype(jnp.bfloat16), d_right_c.astype(jnp.bfloat16)], 0)
    back = swap(split_cells(back, n_wide, n_narrow))
    d_left = back[:, :own].reshape(hidden, rows, cols).astype(jnp.float32)
    d_right = back[:, own:].reshape(hidden, rows, cols).astype(jnp.float32)
    d_cells_a = jnp.concatenate(
        [d_left * cell_mask * sig_a, d_left * cell_mask * a_lin * sig_a * (1.0 - sig_a)], 0
    ).astype(jnp.bfloat16)
    d_cells_b = jnp.concatenate(
        [d_right * cell_mask * sig_b, d_right * cell_mask * b_lin * sig_b * (1.0 - sig_b)], 0
    ).astype(jnp.bfloat16)
    d_zn = jnp.einsum(
        "hij,ch->ijc", d_cells_a, w_proj[:, : 2 * hidden], preferred_element_type=jnp.float32
    )
    d_zn = d_zn + jnp.einsum(
        "hij,ch->ijc", d_cells_b, w_proj[:, 2 * hidden :], preferred_element_type=jnp.float32
    )
    d_zn = d_zn + jnp.dot(d_logit, w_gate.T, preferred_element_type=jnp.float32)
    d_pair = norm_back(d_zn * gain_in, z_hat, z_rstd, -1).astype(jnp.bfloat16)
    proj_part = jnp.concatenate(
        [
            jnp.einsum("ijc,hij->ch", zn, d_cells_a, preferred_element_type=jnp.float32),
            jnp.einsum("ijc,hij->ch", zn, d_cells_b, preferred_element_type=jnp.float32),
        ],
        1,
    )
    flat_z = zn.reshape(-1, width)
    gate_part = jnp.dot(flat_z.T, d_logit.reshape(-1, width), preferred_element_type=jnp.float32)
    parts = jnp.concatenate([proj_part, gate_part], 1)
    chunk = width // devices
    mine = swap(parts.astype(jnp.bfloat16).reshape(devices, chunk, -1))
    mine = jnp.sum(mine.astype(jnp.float32), 0) / residues
    mine = mine.astype(jnp.bfloat16)
    total = swap(jnp.broadcast_to(mine, (devices,) + mine.shape)).reshape(width, -1)
    total = total.astype(jnp.float32)
    return (output, d_pair, total[:, : 4 * hidden], total[:, 4 * hidden :])


def solution(mesh):
    placed = (
        P(("groups", "wide"), "narrow", None),
        P(("groups", "wide"), "narrow", None),
        P("groups"),
        P("groups"),
        P(),
        P(),
        P(),
        P(),
        P(),
        P(),
    )
    return jax.shard_map(
        per_device,
        mesh=mesh,
        in_specs=placed,
        out_specs=(
            P(("groups", "wide"), "narrow", None),
            P(("groups", "wide"), "narrow", None),
            P("groups", None),
            P("groups", None),
        ),
        check_vma=False,
    )
```

```python
import functools

import jax
import jax.numpy as jnp
from jax import lax
from jax.experimental import pallas as pl
from jax.experimental.pallas import tpu as pltpu
from jax.sharding import PartitionSpec as P

EPS = 1e-05


def normalize(values, gain, axis):
    centre = values - jnp.mean(values, axis, keepdims=True)
    rstd = lax.rsqrt(jnp.mean(centre * centre, axis, keepdims=True) + EPS)
    hat = centre * rstd
    return (hat * gain, hat, rstd)


def norm_back(scaled, hat, rstd, axis):
    return rstd * (
        scaled
        - jnp.mean(scaled, axis, keepdims=True)
        - hat * jnp.mean(scaled * hat, axis, keepdims=True)
    )


def swap(blocks):
    return lax.all_to_all(blocks, ("wide", "narrow"), split_axis=0, concat_axis=0, tiled=True)


def gather_cells(blocks, n_wide, n_narrow):
    _, own, rows, cols = blocks.shape
    shaped = blocks.reshape(n_wide, n_narrow, own, rows, cols)
    return jnp.transpose(shaped, (2, 0, 3, 1, 4)).reshape(own, n_wide * rows, n_narrow * cols)


def split_cells(field, n_wide, n_narrow):
    own, rows, cols = field.shape
    shaped = field.reshape(own, n_wide, rows // n_wide, n_narrow, cols // n_narrow)
    moved = jnp.transpose(shaped, (1, 3, 0, 2, 4))
    return moved.reshape(n_wide * n_narrow, own, rows // n_wide, cols // n_narrow)


BF = jnp.bfloat16
F32 = jnp.float32


def dot(a, b, over=((1,), (0,))):
    return lax.dot_general(a, b, (over, ((), ())), preferred_element_type=F32)


def column(row):
    return jnp.broadcast_to(row, (row.shape[1], row.shape[1])).T


def centred(x):
    centre = x - jnp.mean(x, 0, keepdims=True)
    rstd = lax.rsqrt(jnp.mean(centre * centre, 0, keepdims=True) + EPS)
    return centre * rstd, rstd


def back_t(scaled, hat, rstd):
    inner = hat * jnp.mean(scaled * hat, 0, keepdims=True)
    return rstd * (scaled - jnp.mean(scaled, 0, keepdims=True) - inner)


def two_rows(first, second, devices):
    own, cols = first.shape[0] // devices, first.shape[1]
    shape = (devices, own, cols)
    return jnp.concatenate([first.reshape(shape), second.reshape(shape)], 1).astype(BF)


def apart(block, devices):
    wide = block.astype(F32)
    own, cols = wide.shape[1] // 2, wide.shape[2]
    return [wide[:, at * own : (at + 1) * own].reshape(devices * own, cols) for at in range(2)]


def project_kernel(
    pair_hbm, mask_hbm, gain_hbm, w_hbm, sent_ref, zn_ref, mask_ref,
    pair_ref, mask_v, gain_ref, w_ref, sems,
):
    devices, depth, _ = sent_ref.shape
    rows, cols, width = pair_ref.shape
    start = lax.axis_index("wide") * rows
    copies = [
        pltpu.make_async_copy(gain_hbm, gain_ref, sems.at[0]),
        pltpu.make_async_copy(w_hbm, w_ref, sems.at[1]),
        pltpu.make_async_copy(mask_hbm, mask_v, sems.at[2]),
        pltpu.make_async_copy(pair_hbm, pair_ref, sems.at[3]),
    ]
    for copy in copies:
        copy.start()
    for copy in copies:
        copy.wait()
    mask_f = mask_v[...].astype(F32)
    shape = (rows, mask_f.shape[1])
    lane = lax.broadcasted_iota(jnp.int32, shape, 1)
    own = lane == start + lax.broadcasted_iota(jnp.int32, shape, 0)
    mask_ref[...] = mask_f * jnp.sum(jnp.where(own, mask_f, 0.0), 1, keepdims=True)
    gain = column(gain_ref[...])
    weights = w_ref[...].astype(F32).T.astype(BF)
    hidden = weights.shape[0] // 4
    half = depth // 2
    for two in range(rows // 2):
        pieces = []
        for row in (2 * two, 2 * two + 1):
            hat, _ = centred(pair_ref[row].astype(F32).T)
            zn = (hat * gain).astype(BF)
            zn_ref[:, row * cols : (row + 1) * cols] = zn
            proj = dot(weights, zn)
            mask = mask_ref[row : row + 1, :]
            left = mask * jax.nn.sigmoid(proj[hidden : 2 * hidden]) * proj[:hidden]
            right = mask * jax.nn.sigmoid(proj[3 * hidden :]) * proj[2 * hidden : 3 * hidden]
            pieces.append((left, right))
        at = two * 16
        sent_ref[:, at : at + 16, :] = two_rows(pieces[0][0], pieces[1][0], devices)
        sent_ref[:, half + at : half + at + 16, :] = two_rows(pieces[0][1], pieces[1][1], devices)


def gate_kernel(
    zn_ref, adj_ref, mask_ref, same_ref, w_ref, w_gate_ref, bias_ref, gain_ref, w_out_ref,
    gain_in_ref, factor_ref, gate_ref, t_ref, columns_ref,
):
    rows, cols, width = adj_ref.shape
    weights = w_ref[...].astype(F32).T.astype(BF)
    hidden = weights.shape[0] // 4
    w_gate = w_gate_ref[...].astype(F32).T.astype(BF)
    across, within = column(bias_ref[0:1, :]), column(bias_ref[1:2, :])
    gain = column(gain_ref[...])
    columns_ref[...] = column(gain_in_ref[...])
    for row in range(rows):
        lanes = slice(row * cols, (row + 1) * cols)
        zn = zn_ref[:, lanes]
        proj = dot(weights, zn)
        mask = mask_ref[row : row + 1, :]
        for side in range(2):
            lin = proj[2 * side * hidden : (2 * side + 1) * hidden]
            sig = jax.nn.sigmoid(proj[(2 * side + 1) * hidden : (2 * side + 2) * hidden])
            factor_ref[2 * side * hidden : (2 * side + 1) * hidden, lanes] = (mask * sig).astype(BF)
            factor_ref[(2 * side + 1) * hidden : (2 * side + 2) * hidden, lanes] = (
                mask * lin * sig * (1.0 - sig)
            ).astype(BF)
        bias = jnp.where(same_ref[row : row + 1, :] > 0.5, within, across)
        gate = jax.nn.sigmoid(dot(w_gate, zn) + bias).T
        gate_ref[row] = gate
        d_out = (adj_ref[row].astype(F32) * gate).astype(BF)
        t = dot(w_out_ref[...], d_out, ((1,), (1,))) * gain
        t_ref[:, lanes] = (t - jnp.mean(t, 0, keepdims=True)).astype(BF)


def mix_kernel(got_ref, sent_ref, left_ref, right_ref, left_s, right_s, out_s):
    devices, depth, cols = got_ref.shape
    own = left_ref.shape[0]
    half = depth // 2
    count = devices * half // own
    left_s[...] = got_ref[:, :half, :].astype(F32).reshape(devices * half, cols)
    right_s[...] = got_ref[:, half:, :].astype(F32).reshape(devices * half, cols)
    for h in range(own):
        left = left_s[pl.ds(h, count, stride=own), :].astype(BF)
        right = right_s[pl.ds(h, count, stride=own), :].astype(BF)
        left_ref[h] = left
        right_ref[h] = right
        out_s[pl.ds(h, count, stride=own), :] = dot(left, right, ((1,), (1,)))
    sent_ref[...] = out_s[...].reshape(devices, half, cols).astype(BF)


def norm_kernel(
    got_ref, t_ref, gain_ref, gate_ref, adj_ref, zn_ref, w_out_ref,
    sent_ref, output_ref, d_logit_ref, part_ref,
):
    devices, depth, cols = got_ref.shape
    gain = column(gain_ref[...])
    total = None
    for two in range(depth // 16):
        pieces = []
        for part, mixed in enumerate(apart(got_ref[:, two * 16 : two * 16 + 16, :], devices)):
            row = 2 * two + part
            lanes = slice(row * cols, (row + 1) * cols)
            hat, rstd = centred(mixed)
            pieces.append(back_t(t_ref[:, lanes].astype(F32), hat, rstd))
            proj_out = dot((hat * gain).T.astype(BF), w_out_ref[...])
            gate = gate_ref[row]
            output_ref[row] = (gate * proj_out).astype(BF)
            d_logit = (adj_ref[row].astype(F32) * proj_out * gate * (1.0 - gate)).astype(BF)
            d_logit_ref[row] = d_logit
            term = dot(zn_ref[:, lanes], d_logit)
            total = term if total is None else total + term
        sent_ref[:, two * 16 : two * 16 + 16, :] = two_rows(*pieces, devices)
    part_ref[...] = total


def unmix_kernel(got_ref, left_ref, right_ref, sent_ref, in_s, left_s, right_s):
    devices, half, cols = got_ref.shape
    own = left_ref.shape[0]
    count = devices * half // own
    in_s[...] = got_ref[...].astype(F32).reshape(devices * half, cols)
    for h in range(own):
        grad = in_s[pl.ds(h, count, stride=own), :]
        left_s[pl.ds(h, count, stride=own), :] = dot(grad.astype(BF), right_ref[h])
        right_s[pl.ds(h, count, stride=own), :] = dot(grad.T.astype(BF), left_ref[h])
    sent_ref[:, :half, :] = left_s[...].reshape(devices, half, cols).astype(BF)
    sent_ref[:, half:, :] = right_s[...].reshape(devices, half, cols).astype(BF)


def cells_kernel(
    got_ref, factor_ref, zn_ref, gate_part_ref, w_ref, columns_ref, u_ref, part_ref, cells_ref
):
    devices, depth, cols = got_ref.shape
    half = depth // 2
    hidden = factor_ref.shape[0] // 4
    for side in range(2):
        for two in range(half // 16):
            at = side * half + two * 16
            for part, grad in enumerate(apart(got_ref[:, at : at + 16, :], devices)):
                row = 2 * two + part
                lanes = slice(row * cols, (row + 1) * cols)
                for kind in (2 * side, 2 * side + 1):
                    place = slice(kind * hidden, (kind + 1) * hidden)
                    cells_ref[place, lanes] = (grad * factor_ref[place, lanes].astype(F32)).astype(BF)
    total = dot(zn_ref[...], cells_ref[...], ((1,), (1,)))
    part_ref[:, : 4 * hidden] = total.astype(BF)
    part_ref[:, 4 * hidden :] = gate_part_ref[...].astype(BF)
    u = dot(w_ref[...], cells_ref[...]) * columns_ref[:, :1]
    u_ref[...] = (u - jnp.mean(u, 0, keepdims=True)).astype(BF)


def sum_kernel(residues, got_ref, sent_ref):
    total = jnp.sum(got_ref[...].astype(F32), 0) / residues
    sent_ref[...] = jnp.broadcast_to(total.astype(BF)[None], sent_ref.shape)


def finish_kernel(
    got_ref, output_ref, u_ref, d_logit_ref, pair_ref, gain_ref, w_gate_ref,
    output_out, d_pair_out, proj_out, gate_out,
    d_pair_ref, proj_ref, gate_ref, sems, row_sems,
):
    devices, chunk, depth = got_ref.shape
    rows, cols, width = pair_ref.shape
    wide = proj_ref.shape[1]
    copies = [pltpu.make_async_copy(output_ref, output_out, sems.at[0])]
    copies[0].start()
    total = got_ref[...].astype(F32).reshape(devices * chunk, depth)
    proj_ref[...] = total[:, :wide]
    gate_ref[...] = total[:, wide:]
    copies.append(pltpu.make_async_copy(proj_ref, proj_out, sems.at[1]))
    copies.append(pltpu.make_async_copy(gate_ref, gate_out, sems.at[2]))
    copies[1].start()
    copies[2].start()
    gain = column(gain_ref[...])
    half = rows // 2
    for row in range(rows):
        lanes = slice(row * cols, (row + 1) * cols)
        hat, rstd = centred(pair_ref[row].astype(F32).T)
        u = dot(w_gate_ref[...], d_logit_ref[row], ((1,), (1,))) * gain
        u = u + u_ref[:, lanes].astype(F32)
        d_pair_ref[row] = back_t(u, hat, rstd).T.astype(BF)
        if row + 1 in (half, rows):
            place = pl.ds(row + 1 - half, half)
            at = row // half
            copies.append(
                pltpu.make_async_copy(d_pair_ref.at[place], d_pair_out.at[place], row_sems.at[at])
            )
            copies[-1].start()
    for copy in copies:
        copy.wait()


def call(kernel, outs, scratch=(), flops=0, name=None, space=pltpu.VMEM, mib=12, away=()):
    spec = pl.BlockSpec(memory_space=pltpu.VMEM)

    def run(*args):
        moved = sum(a.size * a.dtype.itemsize for a in (*args, *outs))
        return pl.pallas_call(
            kernel,
            out_shape=list(outs),
            in_specs=[pl.BlockSpec(memory_space=space)] * len(args),
            out_specs=[pl.BlockSpec(memory_space=pl.ANY) if i in away else spec for i in range(len(outs))],
            scratch_shapes=list(scratch),
            compiler_params=pltpu.CompilerParams(vmem_limit_bytes=mib * 1024 * 1024),
            cost_estimate=pl.CostEstimate(
                flops=flops, bytes_accessed=moved, transcendentals=0
            ),
            name=name,
        )(*args)

    return run


def small_blocks(pair, adjoint, mask, chain, gain_in, w_proj, w_gate, chain_bias, gain_out, w_out):
    rows, cols, width = pair.shape
    hidden = w_out.shape[0]
    devices = lax.axis_size("wide")
    own = hidden // devices
    residues = rows * devices
    cells = rows * cols
    half = rows * own
    shape = jax.ShapeDtypeStruct
    start = lax.axis_index("wide") * rows
    row_chain = lax.dynamic_slice_in_dim(chain, start, rows, 0)
    same = (row_chain[:, None] == chain[None, :]).astype(F32)
    gain_in, gain_out = gain_in[None], gain_out[None]
    sent, zn, cell_mask = call(
        project_kernel,
        [shape((devices, 2 * half, cols), BF), shape((width, cells), BF), shape((rows, cols), F32)],
        [
            pltpu.VMEM(pair.shape, BF),
            pltpu.VMEM((1, residues), jnp.int32),
            pltpu.VMEM(gain_in.shape, F32),
            pltpu.VMEM(w_proj.shape, BF),
            pltpu.SemaphoreType.DMA((4,)),
        ],
        name="project",
        space=pltpu.HBM,
        mib=56,
    )(pair, mask[None], gain_in, w_proj)
    got = swap(sent)
    factor, gate, t, columns = call(
        gate_kernel,
        [shape((4 * hidden, cells), BF), shape((rows, cols, width), F32), shape((hidden, cells), BF), shape((width, width), F32)],
        flops=2 * 10**9,
        name="gate",
    )(zn, adjoint, cell_mask, same, w_proj, w_gate, chain_bias, gain_out, w_out, gain_in)
    field = pltpu.VMEM((devices * half, cols), F32)
    channels = shape((own, residues, cols), BF)
    block = shape((devices, half, cols), BF)
    got, t = lax.optimization_barrier((got, t))
    sent, left, right = call(mix_kernel, [block, channels, channels], [field] * 3, name="mix")(got)
    got = swap(sent)
    sent, output, d_logit, gate_part = call(
        norm_kernel,
        [block, shape(pair.shape, BF), shape(pair.shape, BF), shape((width, width), F32)],
        name="norm",
    )(got, t, gain_out, gate, adjoint, zn, w_out)
    got = swap(sent)
    sent = call(
        unmix_kernel, [shape((devices, 2 * half, cols), BF)], [field] * 3, name="unmix"
    )(got, left, right)[0]
    got = swap(sent)
    u, part = call(
        cells_kernel,
        [shape((width, cells), BF), shape((width, 4 * hidden + width), BF)],
        [pltpu.VMEM((4 * hidden, cells), BF)],
        name="cells",
    )(got, factor, zn, gate_part, w_proj, columns)
    got = swap(part.reshape(devices, width // devices, -1))
    sent = call(
        functools.partial(sum_kernel, residues), [shape(got.shape, BF)], name="sum"
    )(got)[0]
    return tuple(
        call(
            finish_kernel,
            [
                shape(pair.shape, BF),
                shape(pair.shape, BF),
                shape((width, 4 * hidden), F32),
                shape((width, width), F32),
            ],
            [
                pltpu.VMEM(pair.shape, BF),
                pltpu.VMEM((width, 4 * hidden), F32),
                pltpu.VMEM((width, width), F32),
                pltpu.SemaphoreType.DMA((3,)),
                pltpu.SemaphoreType.DMA((2,)),
            ],
            name="finish",
            away=(0, 1, 2, 3),
        )(swap(sent), output, u, d_logit, pair, gain_in, w_gate)
    )


def per_device(pair, adjoint, mask, chain, gain_in, w_proj, w_gate, chain_bias, gain_out, w_out):
    rows, cols, width = pair.shape
    hidden = w_out.shape[0]
    n_wide = lax.axis_size("wide")
    n_narrow = lax.axis_size("narrow")
    if n_narrow == 1 and (rows, cols, width) == (8, 128, 128) and hidden == 8 * n_wide == 128:
        return small_blocks(
            pair, adjoint, mask, chain, gain_in, w_proj, w_gate, chain_bias, gain_out, w_out
        )
    residues = rows * n_wide
    devices = n_wide * n_narrow
    own = hidden // devices
    row_start = lax.axis_index("wide") * rows
    col_start = lax.axis_index("narrow") * cols
    mask_f = mask.astype(jnp.float32)
    row_mask = lax.dynamic_slice_in_dim(mask_f, row_start, rows, 0)
    col_mask = lax.dynamic_slice_in_dim(mask_f, col_start, cols, 0)
    cell_mask = (row_mask[:, None] * col_mask[None, :])[None]
    row_chain = lax.dynamic_slice_in_dim(chain, row_start, rows, 0)
    col_chain = lax.dynamic_slice_in_dim(chain, col_start, cols, 0)
    same = (row_chain[:, None] == col_chain[None, :])[:, :, None]
    zn_f, z_hat, z_rstd = normalize(pair.astype(jnp.float32), gain_in, -1)
    zn = zn_f.astype(jnp.bfloat16)
    proj_a = jnp.einsum(
        "ijc,ch->hij", zn, w_proj[:, : 2 * hidden], preferred_element_type=jnp.float32
    )
    proj_b = jnp.einsum(
        "ijc,ch->hij", zn, w_proj[:, 2 * hidden :], preferred_element_type=jnp.float32
    )
    a_lin = proj_a[:hidden]
    sig_a = jax.nn.sigmoid(proj_a[hidden:])
    b_lin = proj_b[:hidden]
    sig_b = jax.nn.sigmoid(proj_b[hidden:])
    left_t = (cell_mask * sig_a * a_lin).astype(jnp.bfloat16)
    right_t = (cell_mask * sig_b * b_lin).astype(jnp.bfloat16)
    pairs = jnp.concatenate(
        [left_t.reshape(devices, own, rows, cols), right_t.reshape(devices, own, rows, cols)], 1
    )
    pairs = gather_cells(swap(pairs), n_wide, n_narrow)
    left_c, right_c = pairs[:own], pairs[own:]
    mixed_c = jnp.einsum("hik,hjk->hij", left_c, right_c, preferred_element_type=jnp.float32)
    mixed_t = swap(split_cells(mixed_c.astype(jnp.bfloat16), n_wide, n_narrow))
    mixed_t = mixed_t.reshape(hidden, rows, cols).astype(jnp.float32)
    xn_f, x_hat, x_rstd = normalize(mixed_t, gain_out[:, None, None], 0)
    xn = xn_f.astype(jnp.bfloat16)
    proj_out = jnp.einsum("hij,hc->ijc", xn, w_out, preferred_element_type=jnp.float32)
    logits = jnp.dot(zn, w_gate, preferred_element_type=jnp.float32) + jnp.where(
        same, chain_bias[1], chain_bias[0]
    )
    gate = jax.nn.sigmoid(logits)
    output = (gate * proj_out).astype(jnp.bfloat16)
    adj = adjoint.astype(jnp.float32)
    d_out = (adj * gate).astype(jnp.bfloat16)
    d_logit = (adj * proj_out * gate * (1.0 - gate)).astype(jnp.bfloat16)
    d_xn = jnp.einsum("ijc,hc->hij", d_out, w_out, preferred_element_type=jnp.float32)
    d_mixed_t = norm_back(d_xn * gain_out[:, None, None], x_hat, x_rstd, 0).astype(jnp.bfloat16)
    d_mixed_c = gather_cells(swap(d_mixed_t.reshape(devices, own, rows, cols)), n_wide, n_narrow)
    d_left_c = jnp.einsum("hij,hjk->hik", d_mixed_c, right_c, preferred_element_type=jnp.float32)
    d_right_c = jnp.einsum("hij,hik->hjk", d_mixed_c, left_c, preferred_element_type=jnp.float32)
    back = jnp.concatenate([d_left_c.astype(jnp.bfloat16), d_right_c.astype(jnp.bfloat16)], 0)
    back = swap(split_cells(back, n_wide, n_narrow))
    d_left = back[:, :own].reshape(hidden, rows, cols).astype(jnp.float32)
    d_right = back[:, own:].reshape(hidden, rows, cols).astype(jnp.float32)
    d_cells_a = jnp.concatenate(
        [d_left * cell_mask * sig_a, d_left * cell_mask * a_lin * sig_a * (1.0 - sig_a)], 0
    ).astype(jnp.bfloat16)
    d_cells_b = jnp.concatenate(
        [d_right * cell_mask * sig_b, d_right * cell_mask * b_lin * sig_b * (1.0 - sig_b)], 0
    ).astype(jnp.bfloat16)
    d_zn = jnp.einsum(
        "hij,ch->ijc", d_cells_a, w_proj[:, : 2 * hidden], preferred_element_type=jnp.float32
    )
    d_zn = d_zn + jnp.einsum(
        "hij,ch->ijc", d_cells_b, w_proj[:, 2 * hidden :], preferred_element_type=jnp.float32
    )
    d_zn = d_zn + jnp.dot(d_logit, w_gate.T, preferred_element_type=jnp.float32)
    d_pair = norm_back(d_zn * gain_in, z_hat, z_rstd, -1).astype(jnp.bfloat16)
    proj_part = jnp.concatenate(
        [
            jnp.einsum("ijc,hij->ch", zn, d_cells_a, preferred_element_type=jnp.float32),
            jnp.einsum("ijc,hij->ch", zn, d_cells_b, preferred_element_type=jnp.float32),
        ],
        1,
    )
    flat_z = zn.reshape(-1, width)
    gate_part = jnp.dot(flat_z.T, d_logit.reshape(-1, width), preferred_element_type=jnp.float32)
    parts = jnp.concatenate([proj_part, gate_part], 1)
    chunk = width // devices
    mine = swap(parts.astype(jnp.bfloat16).reshape(devices, chunk, -1))
    mine = jnp.sum(mine.astype(jnp.float32), 0) / residues
    mine = mine.astype(jnp.bfloat16)
    total = swap(jnp.broadcast_to(mine, (devices,) + mine.shape)).reshape(width, -1)
    total = total.astype(jnp.float32)
    return (output, d_pair, total[:, : 4 * hidden], total[:, 4 * hidden :])


def solution(mesh):
    placed = (
        P(("groups", "wide"), "narrow", None),
        P(("groups", "wide"), "narrow", None),
        P("groups"),
        P("groups"),
        P(),
        P(),
        P(),
        P(),
        P(),
        P(),
    )
    return jax.shard_map(
        per_device,
        mesh=mesh,
        in_specs=placed,
        out_specs=(
            P(("groups", "wide"), "narrow", None),
            P(("groups", "wide"), "narrow", None),
            P("groups", None),
            P("groups", None),
        ),
        check_vma=False,
    )
```

```python
import functools

import jax
import jax.numpy as jnp
from jax import lax
from jax.experimental import pallas as pl
from jax.experimental.pallas import tpu as pltpu
from jax.sharding import PartitionSpec as P

EPS = 1e-05


def normalize(values, gain, axis):
    centre = values - jnp.mean(values, axis, keepdims=True)
    rstd = lax.rsqrt(jnp.mean(centre * centre, axis, keepdims=True) + EPS)
    hat = centre * rstd
    return (hat * gain, hat, rstd)


def norm_back(scaled, hat, rstd, axis):
    return rstd * (
        scaled
        - jnp.mean(scaled, axis, keepdims=True)
        - hat * jnp.mean(scaled * hat, axis, keepdims=True)
    )


def swap(blocks):
    return lax.all_to_all(blocks, ("wide", "narrow"), split_axis=0, concat_axis=0, tiled=True)


def gather_cells(blocks, n_wide, n_narrow):
    _, own, rows, cols = blocks.shape
    shaped = blocks.reshape(n_wide, n_narrow, own, rows, cols)
    return jnp.transpose(shaped, (2, 0, 3, 1, 4)).reshape(own, n_wide * rows, n_narrow * cols)


def split_cells(field, n_wide, n_narrow):
    own, rows, cols = field.shape
    shaped = field.reshape(own, n_wide, rows // n_wide, n_narrow, cols // n_narrow)
    moved = jnp.transpose(shaped, (1, 3, 0, 2, 4))
    return moved.reshape(n_wide * n_narrow, own, rows // n_wide, cols // n_narrow)


BF = jnp.bfloat16
F32 = jnp.float32


def dot(a, b, over=((1,), (0,))):
    return lax.dot_general(a, b, (over, ((), ())), preferred_element_type=F32)


def column(row):
    return jnp.broadcast_to(row, (row.shape[1], row.shape[1])).T


def centred(x):
    centre = x - jnp.mean(x, 0, keepdims=True)
    rstd = lax.rsqrt(jnp.mean(centre * centre, 0, keepdims=True) + EPS)
    return centre * rstd, rstd


def back_t(scaled, hat, rstd):
    inner = hat * jnp.mean(scaled * hat, 0, keepdims=True)
    return rstd * (scaled - jnp.mean(scaled, 0, keepdims=True) - inner)


def two_rows(first, second, devices):
    own, cols = first.shape[0] // devices, first.shape[1]
    shape = (devices, own, cols)
    return jnp.concatenate([first.reshape(shape), second.reshape(shape)], 1).astype(BF)


def apart(block, devices):
    wide = block.astype(F32)
    own, cols = wide.shape[1] // 2, wide.shape[2]
    return [wide[:, at * own : (at + 1) * own].reshape(devices * own, cols) for at in range(2)]


def project_kernel(
    pair_hbm, mask_hbm, gain_hbm, w_hbm, sent_ref, zn_ref, mask_ref,
    pair_ref, mask_v, gain_ref, w_ref, sems,
):
    devices, depth, _ = sent_ref.shape
    rows, cols, width = pair_ref.shape
    start = lax.axis_index("wide") * rows
    copies = [
        pltpu.make_async_copy(gain_hbm, gain_ref, sems.at[0]),
        pltpu.make_async_copy(w_hbm, w_ref, sems.at[1]),
        pltpu.make_async_copy(mask_hbm, mask_v, sems.at[2]),
        pltpu.make_async_copy(pair_hbm, pair_ref, sems.at[3]),
    ]
    for copy in copies:
        copy.start()
    for copy in copies:
        copy.wait()
    mask_f = mask_v[...].astype(F32)
    shape = (rows, mask_f.shape[1])
    lane = lax.broadcasted_iota(jnp.int32, shape, 1)
    own = lane == start + lax.broadcasted_iota(jnp.int32, shape, 0)
    mask_ref[...] = mask_f * jnp.sum(jnp.where(own, mask_f, 0.0), 1, keepdims=True)
    gain = column(gain_ref[...])
    weights = w_ref[...].astype(F32).T.astype(BF)
    hidden = weights.shape[0] // 4
    half = depth // 2
    for two in range(rows // 2):
        pieces = []
        for row in (2 * two, 2 * two + 1):
            hat, _ = centred(pair_ref[row].astype(F32).T)
            zn = (hat * gain).astype(BF)
            zn_ref[:, row * cols : (row + 1) * cols] = zn
            proj = dot(weights, zn)
            mask = mask_ref[row : row + 1, :]
            left = mask * jax.nn.sigmoid(proj[hidden : 2 * hidden]) * proj[:hidden]
            right = mask * jax.nn.sigmoid(proj[3 * hidden :]) * proj[2 * hidden : 3 * hidden]
            pieces.append((left, right))
        at = two * 16
        sent_ref[:, at : at + 16, :] = two_rows(pieces[0][0], pieces[1][0], devices)
        sent_ref[:, half + at : half + at + 16, :] = two_rows(pieces[0][1], pieces[1][1], devices)


def gate_kernel(
    zn_ref, adj_ref, mask_ref, same_ref, w_ref, w_gate_ref, bias_ref, gain_ref, w_out_ref,
    gain_in_ref, pair_ref, factor_ref, gate_ref, t_ref, columns_ref, hat_ref, rstd_ref,
):
    rows, cols, width = adj_ref.shape
    weights = w_ref[...].astype(F32).T.astype(BF)
    hidden = weights.shape[0] // 4
    w_gate = w_gate_ref[...].astype(F32).T.astype(BF)
    across, within = column(bias_ref[0:1, :]), column(bias_ref[1:2, :])
    gain = column(gain_ref[...])
    columns_ref[...] = column(gain_in_ref[...])
    for row in range(rows):
        lanes = slice(row * cols, (row + 1) * cols)
        zn = zn_ref[:, lanes]
        proj = dot(weights, zn)
        mask = mask_ref[row : row + 1, :]
        for side in range(2):
            lin = proj[2 * side * hidden : (2 * side + 1) * hidden]
            sig = jax.nn.sigmoid(proj[(2 * side + 1) * hidden : (2 * side + 2) * hidden])
            factor_ref[2 * side * hidden : (2 * side + 1) * hidden, lanes] = (mask * sig).astype(BF)
            factor_ref[(2 * side + 1) * hidden : (2 * side + 2) * hidden, lanes] = (
                mask * lin * sig * (1.0 - sig)
            ).astype(BF)
        bias = jnp.where(same_ref[row : row + 1, :] > 0.5, within, across)
        gate = jax.nn.sigmoid(dot(w_gate, zn) + bias).T
        gate_ref[row] = gate
        d_out = (adj_ref[row].astype(F32) * gate).astype(BF)
        t = dot(w_out_ref[...], d_out, ((1,), (1,))) * gain
        t_ref[:, lanes] = (t - jnp.mean(t, 0, keepdims=True)).astype(BF)
        hat, rstd = centred(pair_ref[row].astype(F32).T)
        hat_ref[:, lanes] = hat
        rstd_ref[row : row + 1, :] = rstd


def mix_kernel(got_ref, sent_ref, left_ref, right_ref, left_s, right_s, out_s):
    devices, depth, cols = got_ref.shape
    own = left_ref.shape[0]
    half = depth // 2
    count = devices * half // own
    left_s[...] = got_ref[:, :half, :].astype(F32).reshape(devices * half, cols)
    right_s[...] = got_ref[:, half:, :].astype(F32).reshape(devices * half, cols)
    for h in range(own):
        left = left_s[pl.ds(h, count, stride=own), :].astype(BF)
        right = right_s[pl.ds(h, count, stride=own), :].astype(BF)
        left_ref[h] = left
        right_ref[h] = right
        out_s[pl.ds(h, count, stride=own), :] = dot(left, right, ((1,), (1,)))
    sent_ref[...] = out_s[...].reshape(devices, half, cols).astype(BF)


def norm_kernel(
    got_ref, t_ref, gain_ref, gate_ref, adj_ref, zn_ref, w_out_ref,
    sent_ref, output_ref, d_logit_ref, part_ref,
):
    devices, depth, cols = got_ref.shape
    gain = column(gain_ref[...])
    total = None
    for two in range(depth // 16):
        pieces = []
        for part, mixed in enumerate(apart(got_ref[:, two * 16 : two * 16 + 16, :], devices)):
            row = 2 * two + part
            lanes = slice(row * cols, (row + 1) * cols)
            hat, rstd = centred(mixed)
            pieces.append(back_t(t_ref[:, lanes].astype(F32), hat, rstd))
            proj_out = dot((hat * gain).T.astype(BF), w_out_ref[...])
            gate = gate_ref[row]
            output_ref[row] = (gate * proj_out).astype(BF)
            d_logit = (adj_ref[row].astype(F32) * proj_out * gate * (1.0 - gate)).astype(BF)
            d_logit_ref[row] = d_logit
            term = dot(zn_ref[:, lanes], d_logit)
            total = term if total is None else total + term
        sent_ref[:, two * 16 : two * 16 + 16, :] = two_rows(*pieces, devices)
    part_ref[...] = total


def unmix_kernel(got_ref, left_ref, right_ref, sent_ref, in_s, left_s, right_s):
    devices, half, cols = got_ref.shape
    own = left_ref.shape[0]
    count = devices * half // own
    in_s[...] = got_ref[...].astype(F32).reshape(devices * half, cols)
    for h in range(own):
        grad = in_s[pl.ds(h, count, stride=own), :]
        left_s[pl.ds(h, count, stride=own), :] = dot(grad.astype(BF), right_ref[h])
        right_s[pl.ds(h, count, stride=own), :] = dot(grad.T.astype(BF), left_ref[h])
    sent_ref[:, :half, :] = left_s[...].reshape(devices, half, cols).astype(BF)
    sent_ref[:, half:, :] = right_s[...].reshape(devices, half, cols).astype(BF)


def cells_kernel(
    got_ref, factor_ref, zn_ref, gate_part_ref, w_ref, columns_ref, u_ref, part_ref, cells_ref
):
    devices, depth, cols = got_ref.shape
    half = depth // 2
    hidden = factor_ref.shape[0] // 4
    for side in range(2):
        for two in range(half // 16):
            at = side * half + two * 16
            for part, grad in enumerate(apart(got_ref[:, at : at + 16, :], devices)):
                row = 2 * two + part
                lanes = slice(row * cols, (row + 1) * cols)
                for kind in (2 * side, 2 * side + 1):
                    place = slice(kind * hidden, (kind + 1) * hidden)
                    cells_ref[place, lanes] = (grad * factor_ref[place, lanes].astype(F32)).astype(BF)
    total = dot(zn_ref[...], cells_ref[...], ((1,), (1,)))
    part_ref[:, : 4 * hidden] = total.astype(BF)
    part_ref[:, 4 * hidden :] = gate_part_ref[...].astype(BF)
    u = dot(w_ref[...], cells_ref[...]) * columns_ref[:, :1]
    u_ref[...] = (u - jnp.mean(u, 0, keepdims=True)).astype(BF)


def sum_kernel(residues, got_ref, sent_ref):
    total = jnp.sum(got_ref[...].astype(F32), 0) / residues
    sent_ref[...] = jnp.broadcast_to(total.astype(BF)[None], sent_ref.shape)


def finish_kernel(
    got_ref, output_ref, u_ref, d_logit_ref, hat_ref, rstd_ref, columns_ref, w_gate_ref,
    output_out, d_pair_out, proj_out, gate_out,
    d_pair_ref, proj_ref, gate_ref, sems, row_sems,
):
    devices, chunk, depth = got_ref.shape
    rows, cols, width = d_logit_ref.shape
    wide = proj_ref.shape[1]
    copies = [pltpu.make_async_copy(output_ref, output_out, sems.at[0])]
    copies[0].start()
    total = got_ref[...].astype(F32).reshape(devices * chunk, depth)
    proj_ref[...] = total[:, :wide]
    gate_ref[...] = total[:, wide:]
    copies.append(pltpu.make_async_copy(proj_ref, proj_out, sems.at[1]))
    copies.append(pltpu.make_async_copy(gate_ref, gate_out, sems.at[2]))
    copies[1].start()
    copies[2].start()
    gain = columns_ref[...]
    half = rows // 2
    for row in range(rows):
        lanes = slice(row * cols, (row + 1) * cols)
        u = dot(w_gate_ref[...], d_logit_ref[row], ((1,), (1,))) * gain
        u = u + u_ref[:, lanes].astype(F32)
        d_pair_ref[row] = back_t(
            u, hat_ref[:, lanes], rstd_ref[row : row + 1, :]
        ).T.astype(BF)
        if row + 1 in (half, rows):
            place = pl.ds(row + 1 - half, half)
            at = row // half
            copies.append(
                pltpu.make_async_copy(d_pair_ref.at[place], d_pair_out.at[place], row_sems.at[at])
            )
            copies[-1].start()
    for copy in copies:
        copy.wait()


def call(kernel, outs, scratch=(), flops=0, name=None, space=pltpu.VMEM, mib=12, away=()):
    spec = pl.BlockSpec(memory_space=pltpu.VMEM)

    def run(*args):
        moved = sum(a.size * a.dtype.itemsize for a in (*args, *outs))
        return pl.pallas_call(
            kernel,
            out_shape=list(outs),
            in_specs=[pl.BlockSpec(memory_space=space)] * len(args),
            out_specs=[pl.BlockSpec(memory_space=pl.ANY) if i in away else spec for i in range(len(outs))],
            scratch_shapes=list(scratch),
            compiler_params=pltpu.CompilerParams(vmem_limit_bytes=mib * 1024 * 1024),
            cost_estimate=pl.CostEstimate(
                flops=flops, bytes_accessed=moved, transcendentals=0
            ),
            name=name,
        )(*args)

    return run


def small_blocks(pair, adjoint, mask, chain, gain_in, w_proj, w_gate, chain_bias, gain_out, w_out):
    rows, cols, width = pair.shape
    hidden = w_out.shape[0]
    devices = lax.axis_size("wide")
    own = hidden // devices
    residues = rows * devices
    cells = rows * cols
    half = rows * own
    shape = jax.ShapeDtypeStruct
    start = lax.axis_index("wide") * rows
    row_chain = lax.dynamic_slice_in_dim(chain, start, rows, 0)
    same = (row_chain[:, None] == chain[None, :]).astype(F32)
    gain_in, gain_out = gain_in[None], gain_out[None]
    sent, zn, cell_mask = call(
        project_kernel,
        [shape((devices, 2 * half, cols), BF), shape((width, cells), BF), shape((rows, cols), F32)],
        [
            pltpu.VMEM(pair.shape, BF),
            pltpu.VMEM((1, residues), jnp.int32),
            pltpu.VMEM(gain_in.shape, F32),
            pltpu.VMEM(w_proj.shape, BF),
            pltpu.SemaphoreType.DMA((4,)),
        ],
        name="project",
        space=pltpu.HBM,
        mib=56,
    )(pair, mask[None], gain_in, w_proj)
    got = swap(sent)
    factor, gate, t, columns, hat, rstd = call(
        gate_kernel,
        [shape((4 * hidden, cells), BF), shape((rows, cols, width), F32), shape((hidden, cells), BF), shape((width, width), F32), shape((width, cells), F32), shape((rows, cols), F32)],
        flops=2 * 10**9,
        name="gate",
    )(zn, adjoint, cell_mask, same, w_proj, w_gate, chain_bias, gain_out, w_out, gain_in, pair)
    field = pltpu.VMEM((devices * half, cols), F32)
    channels = shape((own, residues, cols), BF)
    block = shape((devices, half, cols), BF)
    got, t = lax.optimization_barrier((got, t))
    sent, left, right = call(mix_kernel, [block, channels, channels], [field] * 3, name="mix")(got)
    got = swap(sent)
    sent, output, d_logit, gate_part = call(
        norm_kernel,
        [block, shape(pair.shape, BF), shape(pair.shape, BF), shape((width, width), F32)],
        name="norm",
    )(got, t, gain_out, gate, adjoint, zn, w_out)
    got = swap(sent)
    sent = call(
        unmix_kernel, [shape((devices, 2 * half, cols), BF)], [field] * 3, name="unmix"
    )(got, left, right)[0]
    got = swap(sent)
    u, part = call(
        cells_kernel,
        [shape((width, cells), BF), shape((width, 4 * hidden + width), BF)],
        [pltpu.VMEM((4 * hidden, cells), BF)],
        name="cells",
    )(got, factor, zn, gate_part, w_proj, columns)
    got = swap(part.reshape(devices, width // devices, -1))
    sent = call(
        functools.partial(sum_kernel, residues), [shape(got.shape, BF)], name="sum"
    )(got)[0]
    return tuple(
        call(
            finish_kernel,
            [
                shape(pair.shape, BF),
                shape(pair.shape, BF),
                shape((width, 4 * hidden), F32),
                shape((width, width), F32),
            ],
            [
                pltpu.VMEM(pair.shape, BF),
                pltpu.VMEM((width, 4 * hidden), F32),
                pltpu.VMEM((width, width), F32),
                pltpu.SemaphoreType.DMA((3,)),
                pltpu.SemaphoreType.DMA((2,)),
            ],
            name="finish",
            away=(0, 1, 2, 3),
        )(swap(sent), output, u, d_logit, hat, rstd, columns, w_gate)
    )


def per_device(pair, adjoint, mask, chain, gain_in, w_proj, w_gate, chain_bias, gain_out, w_out):
    rows, cols, width = pair.shape
    hidden = w_out.shape[0]
    n_wide = lax.axis_size("wide")
    n_narrow = lax.axis_size("narrow")
    if n_narrow == 1 and (rows, cols, width) == (8, 128, 128) and hidden == 8 * n_wide == 128:
        return small_blocks(
            pair, adjoint, mask, chain, gain_in, w_proj, w_gate, chain_bias, gain_out, w_out
        )
    residues = rows * n_wide
    devices = n_wide * n_narrow
    own = hidden // devices
    row_start = lax.axis_index("wide") * rows
    col_start = lax.axis_index("narrow") * cols
    mask_f = mask.astype(jnp.float32)
    row_mask = lax.dynamic_slice_in_dim(mask_f, row_start, rows, 0)
    col_mask = lax.dynamic_slice_in_dim(mask_f, col_start, cols, 0)
    cell_mask = (row_mask[:, None] * col_mask[None, :])[None]
    row_chain = lax.dynamic_slice_in_dim(chain, row_start, rows, 0)
    col_chain = lax.dynamic_slice_in_dim(chain, col_start, cols, 0)
    same = (row_chain[:, None] == col_chain[None, :])[:, :, None]
    zn_f, z_hat, z_rstd = normalize(pair.astype(jnp.float32), gain_in, -1)
    zn = zn_f.astype(jnp.bfloat16)
    proj_a = jnp.einsum(
        "ijc,ch->hij", zn, w_proj[:, : 2 * hidden], preferred_element_type=jnp.float32
    )
    proj_b = jnp.einsum(
        "ijc,ch->hij", zn, w_proj[:, 2 * hidden :], preferred_element_type=jnp.float32
    )
    a_lin = proj_a[:hidden]
    sig_a = jax.nn.sigmoid(proj_a[hidden:])
    b_lin = proj_b[:hidden]
    sig_b = jax.nn.sigmoid(proj_b[hidden:])
    left_t = (cell_mask * sig_a * a_lin).astype(jnp.bfloat16)
    right_t = (cell_mask * sig_b * b_lin).astype(jnp.bfloat16)
    pairs = jnp.concatenate(
        [left_t.reshape(devices, own, rows, cols), right_t.reshape(devices, own, rows, cols)], 1
    )
    pairs = gather_cells(swap(pairs), n_wide, n_narrow)
    left_c, right_c = pairs[:own], pairs[own:]
    mixed_c = jnp.einsum("hik,hjk->hij", left_c, right_c, preferred_element_type=jnp.float32)
    mixed_t = swap(split_cells(mixed_c.astype(jnp.bfloat16), n_wide, n_narrow))
    mixed_t = mixed_t.reshape(hidden, rows, cols).astype(jnp.float32)
    xn_f, x_hat, x_rstd = normalize(mixed_t, gain_out[:, None, None], 0)
    xn = xn_f.astype(jnp.bfloat16)
    proj_out = jnp.einsum("hij,hc->ijc", xn, w_out, preferred_element_type=jnp.float32)
    logits = jnp.dot(zn, w_gate, preferred_element_type=jnp.float32) + jnp.where(
        same, chain_bias[1], chain_bias[0]
    )
    gate = jax.nn.sigmoid(logits)
    output = (gate * proj_out).astype(jnp.bfloat16)
    adj = adjoint.astype(jnp.float32)
    d_out = (adj * gate).astype(jnp.bfloat16)
    d_logit = (adj * proj_out * gate * (1.0 - gate)).astype(jnp.bfloat16)
    d_xn = jnp.einsum("ijc,hc->hij", d_out, w_out, preferred_element_type=jnp.float32)
    d_mixed_t = norm_back(d_xn * gain_out[:, None, None], x_hat, x_rstd, 0).astype(jnp.bfloat16)
    d_mixed_c = gather_cells(swap(d_mixed_t.reshape(devices, own, rows, cols)), n_wide, n_narrow)
    d_left_c = jnp.einsum("hij,hjk->hik", d_mixed_c, right_c, preferred_element_type=jnp.float32)
    d_right_c = jnp.einsum("hij,hik->hjk", d_mixed_c, left_c, preferred_element_type=jnp.float32)
    back = jnp.concatenate([d_left_c.astype(jnp.bfloat16), d_right_c.astype(jnp.bfloat16)], 0)
    back = swap(split_cells(back, n_wide, n_narrow))
    d_left = back[:, :own].reshape(hidden, rows, cols).astype(jnp.float32)
    d_right = back[:, own:].reshape(hidden, rows, cols).astype(jnp.float32)
    d_cells_a = jnp.concatenate(
        [d_left * cell_mask * sig_a, d_left * cell_mask * a_lin * sig_a * (1.0 - sig_a)], 0
    ).astype(jnp.bfloat16)
    d_cells_b = jnp.concatenate(
        [d_right * cell_mask * sig_b, d_right * cell_mask * b_lin * sig_b * (1.0 - sig_b)], 0
    ).astype(jnp.bfloat16)
    d_zn = jnp.einsum(
        "hij,ch->ijc", d_cells_a, w_proj[:, : 2 * hidden], preferred_element_type=jnp.float32
    )
    d_zn = d_zn + jnp.einsum(
        "hij,ch->ijc", d_cells_b, w_proj[:, 2 * hidden :], preferred_element_type=jnp.float32
    )
    d_zn = d_zn + jnp.dot(d_logit, w_gate.T, preferred_element_type=jnp.float32)
    d_pair = norm_back(d_zn * gain_in, z_hat, z_rstd, -1).astype(jnp.bfloat16)
    proj_part = jnp.concatenate(
        [
            jnp.einsum("ijc,hij->ch", zn, d_cells_a, preferred_element_type=jnp.float32),
            jnp.einsum("ijc,hij->ch", zn, d_cells_b, preferred_element_type=jnp.float32),
        ],
        1,
    )
    flat_z = zn.reshape(-1, width)
    gate_part = jnp.dot(flat_z.T, d_logit.reshape(-1, width), preferred_element_type=jnp.float32)
    parts = jnp.concatenate([proj_part, gate_part], 1)
    chunk = width // devices
    mine = swap(parts.astype(jnp.bfloat16).reshape(devices, chunk, -1))
    mine = jnp.sum(mine.astype(jnp.float32), 0) / residues
    mine = mine.astype(jnp.bfloat16)
    total = swap(jnp.broadcast_to(mine, (devices,) + mine.shape)).reshape(width, -1)
    total = total.astype(jnp.float32)
    return (output, d_pair, total[:, : 4 * hidden], total[:, 4 * hidden :])


def solution(mesh):
    placed = (
        P(("groups", "wide"), "narrow", None),
        P(("groups", "wide"), "narrow", None),
        P("groups"),
        P("groups"),
        P(),
        P(),
        P(),
        P(),
        P(),
        P(),
    )
    return jax.shard_map(
        per_device,
        mesh=mesh,
        in_specs=placed,
        out_specs=(
            P(("groups", "wide"), "narrow", None),
            P(("groups", "wide"), "narrow", None),
            P("groups", None),
            P("groups", None),
        ),
        check_vma=False,
    )
```

```python
import functools

import jax
import jax.numpy as jnp
from jax import lax
from jax.experimental import pallas as pl
from jax.experimental.pallas import tpu as pltpu
from jax.sharding import PartitionSpec as P

EPS = 1e-05


def normalize(values, gain, axis):
    centre = values - jnp.mean(values, axis, keepdims=True)
    rstd = lax.rsqrt(jnp.mean(centre * centre, axis, keepdims=True) + EPS)
    hat = centre * rstd
    return (hat * gain, hat, rstd)


def norm_back(scaled, hat, rstd, axis):
    return rstd * (
        scaled
        - jnp.mean(scaled, axis, keepdims=True)
        - hat * jnp.mean(scaled * hat, axis, keepdims=True)
    )


def swap(blocks):
    return lax.all_to_all(blocks, ("wide", "narrow"), split_axis=0, concat_axis=0, tiled=True)


def gather_cells(blocks, n_wide, n_narrow):
    _, own, rows, cols = blocks.shape
    shaped = blocks.reshape(n_wide, n_narrow, own, rows, cols)
    return jnp.transpose(shaped, (2, 0, 3, 1, 4)).reshape(own, n_wide * rows, n_narrow * cols)


def split_cells(field, n_wide, n_narrow):
    own, rows, cols = field.shape
    shaped = field.reshape(own, n_wide, rows // n_wide, n_narrow, cols // n_narrow)
    moved = jnp.transpose(shaped, (1, 3, 0, 2, 4))
    return moved.reshape(n_wide * n_narrow, own, rows // n_wide, cols // n_narrow)


BF = jnp.bfloat16
F32 = jnp.float32


def dot(a, b, over=((1,), (0,))):
    return lax.dot_general(a, b, (over, ((), ())), preferred_element_type=F32)


def column(row):
    return jnp.broadcast_to(row, (row.shape[1], row.shape[1])).T


def centred(x):
    centre = x - jnp.mean(x, 0, keepdims=True)
    rstd = lax.rsqrt(jnp.mean(centre * centre, 0, keepdims=True) + EPS)
    return centre * rstd, rstd


def back_t(scaled, hat, rstd):
    inner = hat * jnp.mean(scaled * hat, 0, keepdims=True)
    return rstd * (scaled - jnp.mean(scaled, 0, keepdims=True) - inner)


def two_rows(first, second, devices):
    own, cols = first.shape[0] // devices, first.shape[1]
    shape = (devices, own, cols)
    return jnp.concatenate([first.reshape(shape), second.reshape(shape)], 1).astype(BF)


def apart(block, devices):
    wide = block.astype(F32)
    own, cols = wide.shape[1] // 2, wide.shape[2]
    return [wide[:, at * own : (at + 1) * own].reshape(devices * own, cols) for at in range(2)]


def project_kernel(
    pair_hbm, mask_hbm, gain_hbm, w_hbm, sent_ref, zn_ref, mask_ref,
    pair_ref, mask_v, gain_ref, w_ref, sems,
):
    devices, depth, _ = sent_ref.shape
    rows, cols, width = pair_ref.shape
    start = lax.axis_index("wide") * rows
    copies = [
        pltpu.make_async_copy(gain_hbm, gain_ref, sems.at[0]),
        pltpu.make_async_copy(mask_hbm, mask_v, sems.at[1]),
    ]
    for at in range(4):
        place = pl.ds(at * (rows // 4), rows // 4)
        copies.append(
            pltpu.make_async_copy(pair_hbm.at[place], pair_ref.at[place], sems.at[2 + at])
        )
    for at in range(2):
        place = pl.ds(at * (width // 2), width // 2)
        copies.append(pltpu.make_async_copy(w_hbm.at[place], w_ref.at[place], sems.at[6 + at]))
    for copy in copies:
        copy.start()
    for copy in copies:
        copy.wait()
    mask_f = mask_v[...].astype(F32)
    shape = (rows, mask_f.shape[1])
    lane = lax.broadcasted_iota(jnp.int32, shape, 1)
    own = lane == start + lax.broadcasted_iota(jnp.int32, shape, 0)
    mask_ref[...] = mask_f * jnp.sum(jnp.where(own, mask_f, 0.0), 1, keepdims=True)
    gain = column(gain_ref[...])
    weights = w_ref[...].astype(F32).T.astype(BF)
    hidden = weights.shape[0] // 4
    half = depth // 2
    for two in range(rows // 2):
        pieces = []
        for row in (2 * two, 2 * two + 1):
            hat, _ = centred(pair_ref[row].astype(F32).T)
            zn = (hat * gain).astype(BF)
            zn_ref[:, row * cols : (row + 1) * cols] = zn
            proj = dot(weights, zn)
            mask = mask_ref[row : row + 1, :]
            left = mask * jax.nn.sigmoid(proj[hidden : 2 * hidden]) * proj[:hidden]
            right = mask * jax.nn.sigmoid(proj[3 * hidden :]) * proj[2 * hidden : 3 * hidden]
            pieces.append((left, right))
        at = two * 16
        sent_ref[:, at : at + 16, :] = two_rows(pieces[0][0], pieces[1][0], devices)
        sent_ref[:, half + at : half + at + 16, :] = two_rows(pieces[0][1], pieces[1][1], devices)


def gate_kernel(
    zn_ref, adj_ref, mask_ref, same_ref, w_ref, w_gate_ref, bias_ref, gain_ref, w_out_ref,
    gain_in_ref, pair_ref, factor_ref, gate_ref, t_ref, columns_ref, hat_ref, rstd_ref,
):
    rows, cols, width = adj_ref.shape
    weights = w_ref[...].astype(F32).T.astype(BF)
    hidden = weights.shape[0] // 4
    w_gate = w_gate_ref[...].astype(F32).T.astype(BF)
    across, within = column(bias_ref[0:1, :]), column(bias_ref[1:2, :])
    gain = column(gain_ref[...])
    columns_ref[...] = column(gain_in_ref[...])
    for row in range(rows):
        lanes = slice(row * cols, (row + 1) * cols)
        zn = zn_ref[:, lanes]
        proj = dot(weights, zn)
        mask = mask_ref[row : row + 1, :]
        for side in range(2):
            lin = proj[2 * side * hidden : (2 * side + 1) * hidden]
            sig = jax.nn.sigmoid(proj[(2 * side + 1) * hidden : (2 * side + 2) * hidden])
            factor_ref[2 * side * hidden : (2 * side + 1) * hidden, lanes] = (mask * sig).astype(BF)
            factor_ref[(2 * side + 1) * hidden : (2 * side + 2) * hidden, lanes] = (
                mask * lin * sig * (1.0 - sig)
            ).astype(BF)
        bias = jnp.where(same_ref[row : row + 1, :] > 0.5, within, across)
        gate = jax.nn.sigmoid(dot(w_gate, zn) + bias).T
        gate_ref[row] = gate
        d_out = (adj_ref[row].astype(F32) * gate).astype(BF)
        t = dot(w_out_ref[...], d_out, ((1,), (1,))) * gain
        t_ref[:, lanes] = (t - jnp.mean(t, 0, keepdims=True)).astype(BF)
        hat, rstd = centred(pair_ref[row].astype(F32).T)
        hat_ref[:, lanes] = hat
        rstd_ref[row : row + 1, :] = rstd


def mix_kernel(got_ref, sent_ref, left_ref, right_ref, left_s, right_s, out_s):
    devices, depth, cols = got_ref.shape
    own = left_ref.shape[0]
    half = depth // 2
    count = devices * half // own
    left_s[...] = got_ref[:, :half, :].astype(F32).reshape(devices * half, cols)
    right_s[...] = got_ref[:, half:, :].astype(F32).reshape(devices * half, cols)
    for h in range(own):
        left = left_s[pl.ds(h, count, stride=own), :].astype(BF)
        right = right_s[pl.ds(h, count, stride=own), :].astype(BF)
        left_ref[h] = left
        right_ref[h] = right
        out_s[pl.ds(h, count, stride=own), :] = dot(left, right, ((1,), (1,)))
    sent_ref[...] = out_s[...].reshape(devices, half, cols).astype(BF)


def norm_kernel(
    got_ref, t_ref, gain_ref, gate_ref, adj_ref, zn_ref, w_out_ref,
    sent_ref, output_ref, d_logit_ref, part_ref,
):
    devices, depth, cols = got_ref.shape
    gain = column(gain_ref[...])
    total = None
    for two in range(depth // 16):
        pieces = []
        for part, mixed in enumerate(apart(got_ref[:, two * 16 : two * 16 + 16, :], devices)):
            row = 2 * two + part
            lanes = slice(row * cols, (row + 1) * cols)
            hat, rstd = centred(mixed)
            pieces.append(back_t(t_ref[:, lanes].astype(F32), hat, rstd))
            proj_out = dot((hat * gain).T.astype(BF), w_out_ref[...])
            gate = gate_ref[row]
            output_ref[row] = (gate * proj_out).astype(BF)
            d_logit = (adj_ref[row].astype(F32) * proj_out * gate * (1.0 - gate)).astype(BF)
            d_logit_ref[row] = d_logit
            term = dot(zn_ref[:, lanes], d_logit)
            total = term if total is None else total + term
        sent_ref[:, two * 16 : two * 16 + 16, :] = two_rows(*pieces, devices)
    part_ref[...] = total


def unmix_kernel(got_ref, left_ref, right_ref, sent_ref, in_s, left_s, right_s):
    devices, half, cols = got_ref.shape
    own = left_ref.shape[0]
    count = devices * half // own
    in_s[...] = got_ref[...].astype(F32).reshape(devices * half, cols)
    for h in range(own):
        grad = in_s[pl.ds(h, count, stride=own), :]
        left_s[pl.ds(h, count, stride=own), :] = dot(grad.astype(BF), right_ref[h])
        right_s[pl.ds(h, count, stride=own), :] = dot(grad.T.astype(BF), left_ref[h])
    sent_ref[:, :half, :] = left_s[...].reshape(devices, half, cols).astype(BF)
    sent_ref[:, half:, :] = right_s[...].reshape(devices, half, cols).astype(BF)


def cells_kernel(
    got_ref, factor_ref, zn_ref, gate_part_ref, w_ref, columns_ref, u_ref, part_ref, cells_ref
):
    devices, depth, cols = got_ref.shape
    half = depth // 2
    hidden = factor_ref.shape[0] // 4
    for side in range(2):
        for two in range(half // 16):
            at = side * half + two * 16
            for part, grad in enumerate(apart(got_ref[:, at : at + 16, :], devices)):
                row = 2 * two + part
                lanes = slice(row * cols, (row + 1) * cols)
                for kind in (2 * side, 2 * side + 1):
                    place = slice(kind * hidden, (kind + 1) * hidden)
                    cells_ref[place, lanes] = (grad * factor_ref[place, lanes].astype(F32)).astype(BF)
    total = dot(zn_ref[...], cells_ref[...], ((1,), (1,)))
    part_ref[:, : 4 * hidden] = total.astype(BF)
    part_ref[:, 4 * hidden :] = gate_part_ref[...].astype(BF)
    u = dot(w_ref[...], cells_ref[...]) * columns_ref[:, :1]
    u_ref[...] = (u - jnp.mean(u, 0, keepdims=True)).astype(BF)


def sum_kernel(residues, got_ref, sent_ref):
    total = jnp.sum(got_ref[...].astype(F32), 0) / residues
    sent_ref[...] = jnp.broadcast_to(total.astype(BF)[None], sent_ref.shape)


def finish_kernel(
    got_ref, output_ref, u_ref, d_logit_ref, hat_ref, rstd_ref, columns_ref, w_gate_ref,
    output_out, d_pair_out, proj_out, gate_out,
    d_pair_ref, proj_ref, gate_ref, sems, row_sems,
):
    devices, chunk, depth = got_ref.shape
    rows, cols, width = d_logit_ref.shape
    wide = proj_ref.shape[1]
    copies = [pltpu.make_async_copy(output_ref, output_out, sems.at[0])]
    copies[0].start()
    total = got_ref[...].astype(F32).reshape(devices * chunk, depth)
    proj_ref[...] = total[:, :wide]
    gate_ref[...] = total[:, wide:]
    copies.append(pltpu.make_async_copy(proj_ref, proj_out, sems.at[1]))
    copies.append(pltpu.make_async_copy(gate_ref, gate_out, sems.at[2]))
    copies[1].start()
    copies[2].start()
    gain = columns_ref[...]
    half = rows // 2
    for row in range(rows):
        lanes = slice(row * cols, (row + 1) * cols)
        u = dot(w_gate_ref[...], d_logit_ref[row], ((1,), (1,))) * gain
        u = u + u_ref[:, lanes].astype(F32)
        d_pair_ref[row] = back_t(
            u, hat_ref[:, lanes], rstd_ref[row : row + 1, :]
        ).T.astype(BF)
        if row + 1 in (half, rows):
            place = pl.ds(row + 1 - half, half)
            at = row // half
            copies.append(
                pltpu.make_async_copy(d_pair_ref.at[place], d_pair_out.at[place], row_sems.at[at])
            )
            copies[-1].start()
    for copy in copies:
        copy.wait()


def call(kernel, outs, scratch=(), flops=0, name=None, space=pltpu.VMEM, mib=12, away=()):
    spec = pl.BlockSpec(memory_space=pltpu.VMEM)

    def run(*args):
        moved = sum(a.size * a.dtype.itemsize for a in (*args, *outs))
        return pl.pallas_call(
            kernel,
            out_shape=list(outs),
            in_specs=[pl.BlockSpec(memory_space=space)] * len(args),
            out_specs=[pl.BlockSpec(memory_space=pl.ANY) if i in away else spec for i in range(len(outs))],
            scratch_shapes=list(scratch),
            compiler_params=pltpu.CompilerParams(vmem_limit_bytes=mib * 1024 * 1024),
            cost_estimate=pl.CostEstimate(
                flops=flops, bytes_accessed=moved, transcendentals=0
            ),
            name=name,
        )(*args)

    return run


def small_blocks(pair, adjoint, mask, chain, gain_in, w_proj, w_gate, chain_bias, gain_out, w_out):
    rows, cols, width = pair.shape
    hidden = w_out.shape[0]
    devices = lax.axis_size("wide")
    own = hidden // devices
    residues = rows * devices
    cells = rows * cols
    half = rows * own
    shape = jax.ShapeDtypeStruct
    start = lax.axis_index("wide") * rows
    row_chain = lax.dynamic_slice_in_dim(chain, start, rows, 0)
    same = (row_chain[:, None] == chain[None, :]).astype(F32)
    gain_in, gain_out = gain_in[None], gain_out[None]
    sent, zn, cell_mask = call(
        project_kernel,
        [shape((devices, 2 * half, cols), BF), shape((width, cells), BF), shape((rows, cols), F32)],
        [
            pltpu.VMEM(pair.shape, BF),
            pltpu.VMEM((1, residues), jnp.int32),
            pltpu.VMEM(gain_in.shape, F32),
            pltpu.VMEM(w_proj.shape, BF),
            pltpu.SemaphoreType.DMA((8,)),
        ],
        name="project",
        space=pltpu.HBM,
        mib=56,
    )(pair, mask[None], gain_in, w_proj)
    got = swap(sent)
    factor, gate, t, columns, hat, rstd = call(
        gate_kernel,
        [shape((4 * hidden, cells), BF), shape((rows, cols, width), F32), shape((hidden, cells), BF), shape((width, width), F32), shape((width, cells), F32), shape((rows, cols), F32)],
        flops=2 * 10**9,
        name="gate",
    )(zn, adjoint, cell_mask, same, w_proj, w_gate, chain_bias, gain_out, w_out, gain_in, pair)
    field = pltpu.VMEM((devices * half, cols), F32)
    channels = shape((own, residues, cols), BF)
    block = shape((devices, half, cols), BF)
    got, t = lax.optimization_barrier((got, t))
    sent, left, right = call(mix_kernel, [block, channels, channels], [field] * 3, name="mix")(got)
    got = swap(sent)
    sent, output, d_logit, gate_part = call(
        norm_kernel,
        [block, shape(pair.shape, BF), shape(pair.shape, BF), shape((width, width), F32)],
        name="norm",
    )(got, t, gain_out, gate, adjoint, zn, w_out)
    got = swap(sent)
    sent = call(
        unmix_kernel, [shape((devices, 2 * half, cols), BF)], [field] * 3, name="unmix"
    )(got, left, right)[0]
    got = swap(sent)
    u, part = call(
        cells_kernel,
        [shape((width, cells), BF), shape((width, 4 * hidden + width), BF)],
        [pltpu.VMEM((4 * hidden, cells), BF)],
        name="cells",
    )(got, factor, zn, gate_part, w_proj, columns)
    got = swap(part.reshape(devices, width // devices, -1))
    sent = call(
        functools.partial(sum_kernel, residues), [shape(got.shape, BF)], name="sum"
    )(got)[0]
    return tuple(
        call(
            finish_kernel,
            [
                shape(pair.shape, BF),
                shape(pair.shape, BF),
                shape((width, 4 * hidden), F32),
                shape((width, width), F32),
            ],
            [
                pltpu.VMEM(pair.shape, BF),
                pltpu.VMEM((width, 4 * hidden), F32),
                pltpu.VMEM((width, width), F32),
                pltpu.SemaphoreType.DMA((3,)),
                pltpu.SemaphoreType.DMA((2,)),
            ],
            name="finish",
            away=(0, 1, 2, 3),
        )(swap(sent), output, u, d_logit, hat, rstd, columns, w_gate)
    )


def per_device(pair, adjoint, mask, chain, gain_in, w_proj, w_gate, chain_bias, gain_out, w_out):
    rows, cols, width = pair.shape
    hidden = w_out.shape[0]
    n_wide = lax.axis_size("wide")
    n_narrow = lax.axis_size("narrow")
    if n_narrow == 1 and (rows, cols, width) == (8, 128, 128) and hidden == 8 * n_wide == 128:
        return small_blocks(
            pair, adjoint, mask, chain, gain_in, w_proj, w_gate, chain_bias, gain_out, w_out
        )
    residues = rows * n_wide
    devices = n_wide * n_narrow
    own = hidden // devices
    row_start = lax.axis_index("wide") * rows
    col_start = lax.axis_index("narrow") * cols
    mask_f = mask.astype(jnp.float32)
    row_mask = lax.dynamic_slice_in_dim(mask_f, row_start, rows, 0)
    col_mask = lax.dynamic_slice_in_dim(mask_f, col_start, cols, 0)
    cell_mask = (row_mask[:, None] * col_mask[None, :])[None]
    row_chain = lax.dynamic_slice_in_dim(chain, row_start, rows, 0)
    col_chain = lax.dynamic_slice_in_dim(chain, col_start, cols, 0)
    same = (row_chain[:, None] == col_chain[None, :])[:, :, None]
    zn_f, z_hat, z_rstd = normalize(pair.astype(jnp.float32), gain_in, -1)
    zn = zn_f.astype(jnp.bfloat16)
    proj_a = jnp.einsum(
        "ijc,ch->hij", zn, w_proj[:, : 2 * hidden], preferred_element_type=jnp.float32
    )
    proj_b = jnp.einsum(
        "ijc,ch->hij", zn, w_proj[:, 2 * hidden :], preferred_element_type=jnp.float32
    )
    a_lin = proj_a[:hidden]
    sig_a = jax.nn.sigmoid(proj_a[hidden:])
    b_lin = proj_b[:hidden]
    sig_b = jax.nn.sigmoid(proj_b[hidden:])
    left_t = (cell_mask * sig_a * a_lin).astype(jnp.bfloat16)
    right_t = (cell_mask * sig_b * b_lin).astype(jnp.bfloat16)
    pairs = jnp.concatenate(
        [left_t.reshape(devices, own, rows, cols), right_t.reshape(devices, own, rows, cols)], 1
    )
    pairs = gather_cells(swap(pairs), n_wide, n_narrow)
    left_c, right_c = pairs[:own], pairs[own:]
    mixed_c = jnp.einsum("hik,hjk->hij", left_c, right_c, preferred_element_type=jnp.float32)
    mixed_t = swap(split_cells(mixed_c.astype(jnp.bfloat16), n_wide, n_narrow))
    mixed_t = mixed_t.reshape(hidden, rows, cols).astype(jnp.float32)
    xn_f, x_hat, x_rstd = normalize(mixed_t, gain_out[:, None, None], 0)
    xn = xn_f.astype(jnp.bfloat16)
    proj_out = jnp.einsum("hij,hc->ijc", xn, w_out, preferred_element_type=jnp.float32)
    logits = jnp.dot(zn, w_gate, preferred_element_type=jnp.float32) + jnp.where(
        same, chain_bias[1], chain_bias[0]
    )
    gate = jax.nn.sigmoid(logits)
    output = (gate * proj_out).astype(jnp.bfloat16)
    adj = adjoint.astype(jnp.float32)
    d_out = (adj * gate).astype(jnp.bfloat16)
    d_logit = (adj * proj_out * gate * (1.0 - gate)).astype(jnp.bfloat16)
    d_xn = jnp.einsum("ijc,hc->hij", d_out, w_out, preferred_element_type=jnp.float32)
    d_mixed_t = norm_back(d_xn * gain_out[:, None, None], x_hat, x_rstd, 0).astype(jnp.bfloat16)
    d_mixed_c = gather_cells(swap(d_mixed_t.reshape(devices, own, rows, cols)), n_wide, n_narrow)
    d_left_c = jnp.einsum("hij,hjk->hik", d_mixed_c, right_c, preferred_element_type=jnp.float32)
    d_right_c = jnp.einsum("hij,hik->hjk", d_mixed_c, left_c, preferred_element_type=jnp.float32)
    back = jnp.concatenate([d_left_c.astype(jnp.bfloat16), d_right_c.astype(jnp.bfloat16)], 0)
    back = swap(split_cells(back, n_wide, n_narrow))
    d_left = back[:, :own].reshape(hidden, rows, cols).astype(jnp.float32)
    d_right = back[:, own:].reshape(hidden, rows, cols).astype(jnp.float32)
    d_cells_a = jnp.concatenate(
        [d_left * cell_mask * sig_a, d_left * cell_mask * a_lin * sig_a * (1.0 - sig_a)], 0
    ).astype(jnp.bfloat16)
    d_cells_b = jnp.concatenate(
        [d_right * cell_mask * sig_b, d_right * cell_mask * b_lin * sig_b * (1.0 - sig_b)], 0
    ).astype(jnp.bfloat16)
    d_zn = jnp.einsum(
        "hij,ch->ijc", d_cells_a, w_proj[:, : 2 * hidden], preferred_element_type=jnp.float32
    )
    d_zn = d_zn + jnp.einsum(
        "hij,ch->ijc", d_cells_b, w_proj[:, 2 * hidden :], preferred_element_type=jnp.float32
    )
    d_zn = d_zn + jnp.dot(d_logit, w_gate.T, preferred_element_type=jnp.float32)
    d_pair = norm_back(d_zn * gain_in, z_hat, z_rstd, -1).astype(jnp.bfloat16)
    proj_part = jnp.concatenate(
        [
            jnp.einsum("ijc,hij->ch", zn, d_cells_a, preferred_element_type=jnp.float32),
            jnp.einsum("ijc,hij->ch", zn, d_cells_b, preferred_element_type=jnp.float32),
        ],
        1,
    )
    flat_z = zn.reshape(-1, width)
    gate_part = jnp.dot(flat_z.T, d_logit.reshape(-1, width), preferred_element_type=jnp.float32)
    parts = jnp.concatenate([proj_part, gate_part], 1)
    chunk = width // devices
    mine = swap(parts.astype(jnp.bfloat16).reshape(devices, chunk, -1))
    mine = jnp.sum(mine.astype(jnp.float32), 0) / residues
    mine = mine.astype(jnp.bfloat16)
    total = swap(jnp.broadcast_to(mine, (devices,) + mine.shape)).reshape(width, -1)
    total = total.astype(jnp.float32)
    return (output, d_pair, total[:, : 4 * hidden], total[:, 4 * hidden :])


def solution(mesh):
    placed = (
        P(("groups", "wide"), "narrow", None),
        P(("groups", "wide"), "narrow", None),
        P("groups"),
        P("groups"),
        P(),
        P(),
        P(),
        P(),
        P(),
        P(),
    )
    return jax.shard_map(
        per_device,
        mesh=mesh,
        in_specs=placed,
        out_specs=(
            P(("groups", "wide"), "narrow", None),
            P(("groups", "wide"), "narrow", None),
            P("groups", None),
            P("groups", None),
        ),
        check_vma=False,
    )
```

```python
import functools

import jax
import jax.numpy as jnp
from jax import lax
from jax.experimental import pallas as pl
from jax.experimental.pallas import tpu as pltpu
from jax.sharding import PartitionSpec as P

EPS = 1e-05


def normalize(values, gain, axis):
    centre = values - jnp.mean(values, axis, keepdims=True)
    rstd = lax.rsqrt(jnp.mean(centre * centre, axis, keepdims=True) + EPS)
    hat = centre * rstd
    return (hat * gain, hat, rstd)


def norm_back(scaled, hat, rstd, axis):
    return rstd * (
        scaled
        - jnp.mean(scaled, axis, keepdims=True)
        - hat * jnp.mean(scaled * hat, axis, keepdims=True)
    )


def swap(blocks):
    return lax.all_to_all(blocks, ("wide", "narrow"), split_axis=0, concat_axis=0, tiled=True)


def gather_cells(blocks, n_wide, n_narrow):
    _, own, rows, cols = blocks.shape
    shaped = blocks.reshape(n_wide, n_narrow, own, rows, cols)
    return jnp.transpose(shaped, (2, 0, 3, 1, 4)).reshape(own, n_wide * rows, n_narrow * cols)


def split_cells(field, n_wide, n_narrow):
    own, rows, cols = field.shape
    shaped = field.reshape(own, n_wide, rows // n_wide, n_narrow, cols // n_narrow)
    moved = jnp.transpose(shaped, (1, 3, 0, 2, 4))
    return moved.reshape(n_wide * n_narrow, own, rows // n_wide, cols // n_narrow)


BF = jnp.bfloat16
F32 = jnp.float32


def dot(a, b, over=((1,), (0,))):
    return lax.dot_general(a, b, (over, ((), ())), preferred_element_type=F32)


def column(row):
    return jnp.broadcast_to(row, (row.shape[1], row.shape[1])).T


def centred(x):
    centre = x - jnp.mean(x, 0, keepdims=True)
    rstd = lax.rsqrt(jnp.mean(centre * centre, 0, keepdims=True) + EPS)
    return centre * rstd, rstd


def back_t(scaled, hat, rstd):
    inner = hat * jnp.mean(scaled * hat, 0, keepdims=True)
    return rstd * (scaled - jnp.mean(scaled, 0, keepdims=True) - inner)


def two_rows(first, second, devices):
    own, cols = first.shape[0] // devices, first.shape[1]
    shape = (devices, own, cols)
    return jnp.concatenate([first.reshape(shape), second.reshape(shape)], 1).astype(BF)


def apart(block, devices):
    wide = block.astype(F32)
    own, cols = wide.shape[1] // 2, wide.shape[2]
    return [wide[:, at * own : (at + 1) * own].reshape(devices * own, cols) for at in range(2)]


def project_kernel(
    pair_hbm, mask_hbm, gain_hbm, w_hbm, sent_ref, mask_ref,
    pair_ref, mask_v, gain_ref, w_ref, sems,
):
    devices, depth, _ = sent_ref.shape
    rows, cols, width = pair_ref.shape
    start = lax.axis_index("wide") * rows
    copies = [
        pltpu.make_async_copy(gain_hbm, gain_ref, sems.at[0]),
        pltpu.make_async_copy(mask_hbm, mask_v, sems.at[1]),
    ]
    for at in range(4):
        place = pl.ds(at * (rows // 4), rows // 4)
        copies.append(
            pltpu.make_async_copy(pair_hbm.at[place], pair_ref.at[place], sems.at[2 + at])
        )
    for at in range(2):
        place = pl.ds(at * (width // 2), width // 2)
        copies.append(pltpu.make_async_copy(w_hbm.at[place], w_ref.at[place], sems.at[6 + at]))
    for copy in copies:
        copy.start()
    for copy in copies:
        copy.wait()
    mask_f = mask_v[...].astype(F32)
    shape = (rows, mask_f.shape[1])
    lane = lax.broadcasted_iota(jnp.int32, shape, 1)
    own = lane == start + lax.broadcasted_iota(jnp.int32, shape, 0)
    mask_ref[...] = mask_f * jnp.sum(jnp.where(own, mask_f, 0.0), 1, keepdims=True)
    gain = column(gain_ref[...])
    weights = w_ref[...].astype(F32).T.astype(BF)
    hidden = weights.shape[0] // 4
    half = depth // 2
    for two in range(rows // 2):
        pieces = []
        for row in (2 * two, 2 * two + 1):
            hat, _ = centred(pair_ref[row].astype(F32).T)
            zn = (hat * gain).astype(BF)
            proj = dot(weights, zn)
            mask = mask_ref[row : row + 1, :]
            left = mask * jax.nn.sigmoid(proj[hidden : 2 * hidden]) * proj[:hidden]
            right = mask * jax.nn.sigmoid(proj[3 * hidden :]) * proj[2 * hidden : 3 * hidden]
            pieces.append((left, right))
        at = two * 16
        sent_ref[:, at : at + 16, :] = two_rows(pieces[0][0], pieces[1][0], devices)
        sent_ref[:, half + at : half + at + 16, :] = two_rows(pieces[0][1], pieces[1][1], devices)


def gate_kernel(
    adj_ref, mask_ref, same_ref, w_ref, w_gate_ref, bias_ref, gain_ref, w_out_ref,
    gain_in_ref, pair_ref, factor_ref, gate_ref, t_ref, columns_ref, hat_ref, rstd_ref, zn_ref,
):
    rows, cols, width = adj_ref.shape
    weights = w_ref[...].astype(F32).T.astype(BF)
    hidden = weights.shape[0] // 4
    w_gate = w_gate_ref[...].astype(F32).T.astype(BF)
    across, within = column(bias_ref[0:1, :]), column(bias_ref[1:2, :])
    gain = column(gain_ref[...])
    gain_in = column(gain_in_ref[...])
    columns_ref[...] = gain_in
    for row in range(rows):
        lanes = slice(row * cols, (row + 1) * cols)
        hat, rstd = centred(pair_ref[row].astype(F32).T)
        hat_ref[:, lanes] = hat
        rstd_ref[row : row + 1, :] = rstd
        zn = (hat * gain_in).astype(BF)
        zn_ref[:, lanes] = zn
        proj = dot(weights, zn)
        mask = mask_ref[row : row + 1, :]
        for side in range(2):
            lin = proj[2 * side * hidden : (2 * side + 1) * hidden]
            sig = jax.nn.sigmoid(proj[(2 * side + 1) * hidden : (2 * side + 2) * hidden])
            factor_ref[2 * side * hidden : (2 * side + 1) * hidden, lanes] = (mask * sig).astype(BF)
            factor_ref[(2 * side + 1) * hidden : (2 * side + 2) * hidden, lanes] = (
                mask * lin * sig * (1.0 - sig)
            ).astype(BF)
        bias = jnp.where(same_ref[row : row + 1, :] > 0.5, within, across)
        gate = jax.nn.sigmoid(dot(w_gate, zn) + bias).T
        gate_ref[row] = gate
        d_out = (adj_ref[row].astype(F32) * gate).astype(BF)
        t = dot(w_out_ref[...], d_out, ((1,), (1,))) * gain
        t_ref[:, lanes] = (t - jnp.mean(t, 0, keepdims=True)).astype(BF)


def mix_kernel(got_ref, sent_ref, left_ref, right_ref, left_s, right_s, out_s):
    devices, depth, cols = got_ref.shape
    own = left_ref.shape[0]
    half = depth // 2
    count = devices * half // own
    left_s[...] = got_ref[:, :half, :].astype(F32).reshape(devices * half, cols)
    right_s[...] = got_ref[:, half:, :].astype(F32).reshape(devices * half, cols)
    for h in range(own):
        left = left_s[pl.ds(h, count, stride=own), :].astype(BF)
        right = right_s[pl.ds(h, count, stride=own), :].astype(BF)
        left_ref[h] = left
        right_ref[h] = right
        out_s[pl.ds(h, count, stride=own), :] = dot(left, right, ((1,), (1,)))
    sent_ref[...] = out_s[...].reshape(devices, half, cols).astype(BF)


def norm_kernel(
    got_ref, t_ref, gain_ref, gate_ref, adj_ref, zn_ref, w_out_ref,
    sent_ref, output_ref, d_logit_ref, part_ref,
):
    devices, depth, cols = got_ref.shape
    gain = column(gain_ref[...])
    total = None
    for two in range(depth // 16):
        pieces = []
        for part, mixed in enumerate(apart(got_ref[:, two * 16 : two * 16 + 16, :], devices)):
            row = 2 * two + part
            lanes = slice(row * cols, (row + 1) * cols)
            hat, rstd = centred(mixed)
            pieces.append(back_t(t_ref[:, lanes].astype(F32), hat, rstd))
            proj_out = dot((hat * gain).T.astype(BF), w_out_ref[...])
            gate = gate_ref[row]
            output_ref[row] = (gate * proj_out).astype(BF)
            d_logit = (adj_ref[row].astype(F32) * proj_out * gate * (1.0 - gate)).astype(BF)
            d_logit_ref[row] = d_logit
            term = dot(zn_ref[:, lanes], d_logit)
            total = term if total is None else total + term
        sent_ref[:, two * 16 : two * 16 + 16, :] = two_rows(*pieces, devices)
    part_ref[...] = total


def unmix_kernel(got_ref, left_ref, right_ref, sent_ref, in_s, left_s, right_s):
    devices, half, cols = got_ref.shape
    own = left_ref.shape[0]
    count = devices * half // own
    in_s[...] = got_ref[...].astype(F32).reshape(devices * half, cols)
    for h in range(own):
        grad = in_s[pl.ds(h, count, stride=own), :]
        left_s[pl.ds(h, count, stride=own), :] = dot(grad.astype(BF), right_ref[h])
        right_s[pl.ds(h, count, stride=own), :] = dot(grad.T.astype(BF), left_ref[h])
    sent_ref[:, :half, :] = left_s[...].reshape(devices, half, cols).astype(BF)
    sent_ref[:, half:, :] = right_s[...].reshape(devices, half, cols).astype(BF)


def cells_kernel(
    got_ref, factor_ref, zn_ref, gate_part_ref, w_ref, columns_ref, u_ref, part_ref, cells_ref
):
    devices, depth, cols = got_ref.shape
    half = depth // 2
    hidden = factor_ref.shape[0] // 4
    for side in range(2):
        for two in range(half // 16):
            at = side * half + two * 16
            for part, grad in enumerate(apart(got_ref[:, at : at + 16, :], devices)):
                row = 2 * two + part
                lanes = slice(row * cols, (row + 1) * cols)
                for kind in (2 * side, 2 * side + 1):
                    place = slice(kind * hidden, (kind + 1) * hidden)
                    cells_ref[place, lanes] = (grad * factor_ref[place, lanes].astype(F32)).astype(BF)
    total = dot(zn_ref[...], cells_ref[...], ((1,), (1,)))
    part_ref[:, : 4 * hidden] = total.astype(BF)
    part_ref[:, 4 * hidden :] = gate_part_ref[...].astype(BF)
    u = dot(w_ref[...], cells_ref[...]) * columns_ref[:, :1]
    u_ref[...] = (u - jnp.mean(u, 0, keepdims=True)).astype(BF)


def sum_kernel(residues, got_ref, sent_ref):
    total = jnp.sum(got_ref[...].astype(F32), 0) / residues
    sent_ref[...] = jnp.broadcast_to(total.astype(BF)[None], sent_ref.shape)


def finish_kernel(
    got_ref, output_ref, u_ref, d_logit_ref, hat_ref, rstd_ref, columns_ref, w_gate_ref,
    output_out, d_pair_out, proj_out, gate_out,
    d_pair_ref, proj_ref, gate_ref, sems, row_sems,
):
    devices, chunk, depth = got_ref.shape
    rows, cols, width = d_logit_ref.shape
    wide = proj_ref.shape[1]
    copies = [pltpu.make_async_copy(output_ref, output_out, sems.at[0])]
    copies[0].start()
    total = got_ref[...].astype(F32).reshape(devices * chunk, depth)
    proj_ref[...] = total[:, :wide]
    gate_ref[...] = total[:, wide:]
    copies.append(pltpu.make_async_copy(proj_ref, proj_out, sems.at[1]))
    copies.append(pltpu.make_async_copy(gate_ref, gate_out, sems.at[2]))
    copies[1].start()
    copies[2].start()
    gain = columns_ref[...]
    half = rows // 2
    for row in range(rows):
        lanes = slice(row * cols, (row + 1) * cols)
        u = dot(w_gate_ref[...], d_logit_ref[row], ((1,), (1,))) * gain
        u = u + u_ref[:, lanes].astype(F32)
        d_pair_ref[row] = back_t(
            u, hat_ref[:, lanes], rstd_ref[row : row + 1, :]
        ).T.astype(BF)
        if row + 1 in (half, rows):
            place = pl.ds(row + 1 - half, half)
            at = row // half
            copies.append(
                pltpu.make_async_copy(d_pair_ref.at[place], d_pair_out.at[place], row_sems.at[at])
            )
            copies[-1].start()
    for copy in copies:
        copy.wait()


def call(kernel, outs, scratch=(), flops=0, name=None, space=pltpu.VMEM, mib=12, away=()):
    spec = pl.BlockSpec(memory_space=pltpu.VMEM)

    def run(*args):
        moved = sum(a.size * a.dtype.itemsize for a in (*args, *outs))
        return pl.pallas_call(
            kernel,
            out_shape=list(outs),
            in_specs=[pl.BlockSpec(memory_space=space)] * len(args),
            out_specs=[pl.BlockSpec(memory_space=pl.ANY) if i in away else spec for i in range(len(outs))],
            scratch_shapes=list(scratch),
            compiler_params=pltpu.CompilerParams(vmem_limit_bytes=mib * 1024 * 1024),
            cost_estimate=pl.CostEstimate(
                flops=flops, bytes_accessed=moved, transcendentals=0
            ),
            name=name,
        )(*args)

    return run


def small_blocks(pair, adjoint, mask, chain, gain_in, w_proj, w_gate, chain_bias, gain_out, w_out):
    rows, cols, width = pair.shape
    hidden = w_out.shape[0]
    devices = lax.axis_size("wide")
    own = hidden // devices
    residues = rows * devices
    cells = rows * cols
    half = rows * own
    shape = jax.ShapeDtypeStruct
    start = lax.axis_index("wide") * rows
    row_chain = lax.dynamic_slice_in_dim(chain, start, rows, 0)
    same = (row_chain[:, None] == chain[None, :]).astype(F32)
    gain_in, gain_out = gain_in[None], gain_out[None]
    sent, cell_mask = call(
        project_kernel,
        [shape((devices, 2 * half, cols), BF), shape((rows, cols), F32)],
        [
            pltpu.VMEM(pair.shape, BF),
            pltpu.VMEM((1, residues), jnp.int32),
            pltpu.VMEM(gain_in.shape, F32),
            pltpu.VMEM(w_proj.shape, BF),
            pltpu.SemaphoreType.DMA((8,)),
        ],
        name="project",
        space=pltpu.HBM,
        mib=56,
    )(pair, mask[None], gain_in, w_proj)
    got = swap(sent)
    factor, gate, t, columns, hat, rstd, zn = call(
        gate_kernel,
        [shape((4 * hidden, cells), BF), shape((rows, cols, width), F32), shape((hidden, cells), BF), shape((width, width), F32), shape((width, cells), F32), shape((rows, cols), F32), shape((width, cells), BF)],
        flops=2 * 10**9,
        name="gate",
    )(adjoint, cell_mask, same, w_proj, w_gate, chain_bias, gain_out, w_out, gain_in, pair)
    field = pltpu.VMEM((devices * half, cols), F32)
    channels = shape((own, residues, cols), BF)
    block = shape((devices, half, cols), BF)
    got, t = lax.optimization_barrier((got, t))
    sent, left, right = call(mix_kernel, [block, channels, channels], [field] * 3, name="mix")(got)
    got = swap(sent)
    sent, output, d_logit, gate_part = call(
        norm_kernel,
        [block, shape(pair.shape, BF), shape(pair.shape, BF), shape((width, width), F32)],
        name="norm",
    )(got, t, gain_out, gate, adjoint, zn, w_out)
    got = swap(sent)
    sent = call(
        unmix_kernel, [shape((devices, 2 * half, cols), BF)], [field] * 3, name="unmix"
    )(got, left, right)[0]
    got = swap(sent)
    u, part = call(
        cells_kernel,
        [shape((width, cells), BF), shape((width, 4 * hidden + width), BF)],
        [pltpu.VMEM((4 * hidden, cells), BF)],
        name="cells",
    )(got, factor, zn, gate_part, w_proj, columns)
    got = swap(part.reshape(devices, width // devices, -1))
    sent = call(
        functools.partial(sum_kernel, residues), [shape(got.shape, BF)], name="sum"
    )(got)[0]
    return tuple(
        call(
            finish_kernel,
            [
                shape(pair.shape, BF),
                shape(pair.shape, BF),
                shape((width, 4 * hidden), F32),
                shape((width, width), F32),
            ],
            [
                pltpu.VMEM(pair.shape, BF),
                pltpu.VMEM((width, 4 * hidden), F32),
                pltpu.VMEM((width, width), F32),
                pltpu.SemaphoreType.DMA((3,)),
                pltpu.SemaphoreType.DMA((2,)),
            ],
            name="finish",
            away=(0, 1, 2, 3),
        )(swap(sent), output, u, d_logit, hat, rstd, columns, w_gate)
    )


def per_device(pair, adjoint, mask, chain, gain_in, w_proj, w_gate, chain_bias, gain_out, w_out):
    rows, cols, width = pair.shape
    hidden = w_out.shape[0]
    n_wide = lax.axis_size("wide")
    n_narrow = lax.axis_size("narrow")
    if n_narrow == 1 and (rows, cols, width) == (8, 128, 128) and hidden == 8 * n_wide == 128:
        return small_blocks(
            pair, adjoint, mask, chain, gain_in, w_proj, w_gate, chain_bias, gain_out, w_out
        )
    residues = rows * n_wide
    devices = n_wide * n_narrow
    own = hidden // devices
    row_start = lax.axis_index("wide") * rows
    col_start = lax.axis_index("narrow") * cols
    mask_f = mask.astype(jnp.float32)
    row_mask = lax.dynamic_slice_in_dim(mask_f, row_start, rows, 0)
    col_mask = lax.dynamic_slice_in_dim(mask_f, col_start, cols, 0)
    cell_mask = (row_mask[:, None] * col_mask[None, :])[None]
    row_chain = lax.dynamic_slice_in_dim(chain, row_start, rows, 0)
    col_chain = lax.dynamic_slice_in_dim(chain, col_start, cols, 0)
    same = (row_chain[:, None] == col_chain[None, :])[:, :, None]
    zn_f, z_hat, z_rstd = normalize(pair.astype(jnp.float32), gain_in, -1)
    zn = zn_f.astype(jnp.bfloat16)
    proj_a = jnp.einsum(
        "ijc,ch->hij", zn, w_proj[:, : 2 * hidden], preferred_element_type=jnp.float32
    )
    proj_b = jnp.einsum(
        "ijc,ch->hij", zn, w_proj[:, 2 * hidden :], preferred_element_type=jnp.float32
    )
    a_lin = proj_a[:hidden]
    sig_a = jax.nn.sigmoid(proj_a[hidden:])
    b_lin = proj_b[:hidden]
    sig_b = jax.nn.sigmoid(proj_b[hidden:])
    left_t = (cell_mask * sig_a * a_lin).astype(jnp.bfloat16)
    right_t = (cell_mask * sig_b * b_lin).astype(jnp.bfloat16)
    pairs = jnp.concatenate(
        [left_t.reshape(devices, own, rows, cols), right_t.reshape(devices, own, rows, cols)], 1
    )
    pairs = gather_cells(swap(pairs), n_wide, n_narrow)
    left_c, right_c = pairs[:own], pairs[own:]
    mixed_c = jnp.einsum("hik,hjk->hij", left_c, right_c, preferred_element_type=jnp.float32)
    mixed_t = swap(split_cells(mixed_c.astype(jnp.bfloat16), n_wide, n_narrow))
    mixed_t = mixed_t.reshape(hidden, rows, cols).astype(jnp.float32)
    xn_f, x_hat, x_rstd = normalize(mixed_t, gain_out[:, None, None], 0)
    xn = xn_f.astype(jnp.bfloat16)
    proj_out = jnp.einsum("hij,hc->ijc", xn, w_out, preferred_element_type=jnp.float32)
    logits = jnp.dot(zn, w_gate, preferred_element_type=jnp.float32) + jnp.where(
        same, chain_bias[1], chain_bias[0]
    )
    gate = jax.nn.sigmoid(logits)
    output = (gate * proj_out).astype(jnp.bfloat16)
    adj = adjoint.astype(jnp.float32)
    d_out = (adj * gate).astype(jnp.bfloat16)
    d_logit = (adj * proj_out * gate * (1.0 - gate)).astype(jnp.bfloat16)
    d_xn = jnp.einsum("ijc,hc->hij", d_out, w_out, preferred_element_type=jnp.float32)
    d_mixed_t = norm_back(d_xn * gain_out[:, None, None], x_hat, x_rstd, 0).astype(jnp.bfloat16)
    d_mixed_c = gather_cells(swap(d_mixed_t.reshape(devices, own, rows, cols)), n_wide, n_narrow)
    d_left_c = jnp.einsum("hij,hjk->hik", d_mixed_c, right_c, preferred_element_type=jnp.float32)
    d_right_c = jnp.einsum("hij,hik->hjk", d_mixed_c, left_c, preferred_element_type=jnp.float32)
    back = jnp.concatenate([d_left_c.astype(jnp.bfloat16), d_right_c.astype(jnp.bfloat16)], 0)
    back = swap(split_cells(back, n_wide, n_narrow))
    d_left = back[:, :own].reshape(hidden, rows, cols).astype(jnp.float32)
    d_right = back[:, own:].reshape(hidden, rows, cols).astype(jnp.float32)
    d_cells_a = jnp.concatenate(
        [d_left * cell_mask * sig_a, d_left * cell_mask * a_lin * sig_a * (1.0 - sig_a)], 0
    ).astype(jnp.bfloat16)
    d_cells_b = jnp.concatenate(
        [d_right * cell_mask * sig_b, d_right * cell_mask * b_lin * sig_b * (1.0 - sig_b)], 0
    ).astype(jnp.bfloat16)
    d_zn = jnp.einsum(
        "hij,ch->ijc", d_cells_a, w_proj[:, : 2 * hidden], preferred_element_type=jnp.float32
    )
    d_zn = d_zn + jnp.einsum(
        "hij,ch->ijc", d_cells_b, w_proj[:, 2 * hidden :], preferred_element_type=jnp.float32
    )
    d_zn = d_zn + jnp.dot(d_logit, w_gate.T, preferred_element_type=jnp.float32)
    d_pair = norm_back(d_zn * gain_in, z_hat, z_rstd, -1).astype(jnp.bfloat16)
    proj_part = jnp.concatenate(
        [
            jnp.einsum("ijc,hij->ch", zn, d_cells_a, preferred_element_type=jnp.float32),
            jnp.einsum("ijc,hij->ch", zn, d_cells_b, preferred_element_type=jnp.float32),
        ],
        1,
    )
    flat_z = zn.reshape(-1, width)
    gate_part = jnp.dot(flat_z.T, d_logit.reshape(-1, width), preferred_element_type=jnp.float32)
    parts = jnp.concatenate([proj_part, gate_part], 1)
    chunk = width // devices
    mine = swap(parts.astype(jnp.bfloat16).reshape(devices, chunk, -1))
    mine = jnp.sum(mine.astype(jnp.float32), 0) / residues
    mine = mine.astype(jnp.bfloat16)
    total = swap(jnp.broadcast_to(mine, (devices,) + mine.shape)).reshape(width, -1)
    total = total.astype(jnp.float32)
    return (output, d_pair, total[:, : 4 * hidden], total[:, 4 * hidden :])


def solution(mesh):
    placed = (
        P(("groups", "wide"), "narrow", None),
        P(("groups", "wide"), "narrow", None),
        P("groups"),
        P("groups"),
        P(),
        P(),
        P(),
        P(),
        P(),
        P(),
    )
    return jax.shard_map(
        per_device,
        mesh=mesh,
        in_specs=placed,
        out_specs=(
            P(("groups", "wide"), "narrow", None),
            P(("groups", "wide"), "narrow", None),
            P("groups", None),
            P("groups", None),
        ),
        check_vma=False,
    )
```

```python
import functools

import jax
import jax.numpy as jnp
from jax import lax
from jax.experimental import pallas as pl
from jax.experimental.pallas import tpu as pltpu
from jax.sharding import PartitionSpec as P

EPS = 1e-05


def normalize(values, gain, axis):
    centre = values - jnp.mean(values, axis, keepdims=True)
    rstd = lax.rsqrt(jnp.mean(centre * centre, axis, keepdims=True) + EPS)
    hat = centre * rstd
    return (hat * gain, hat, rstd)


def norm_back(scaled, hat, rstd, axis):
    return rstd * (
        scaled
        - jnp.mean(scaled, axis, keepdims=True)
        - hat * jnp.mean(scaled * hat, axis, keepdims=True)
    )


def swap(blocks):
    return lax.all_to_all(blocks, ("wide", "narrow"), split_axis=0, concat_axis=0, tiled=True)


def gather_cells(blocks, n_wide, n_narrow):
    _, own, rows, cols = blocks.shape
    shaped = blocks.reshape(n_wide, n_narrow, own, rows, cols)
    return jnp.transpose(shaped, (2, 0, 3, 1, 4)).reshape(own, n_wide * rows, n_narrow * cols)


def split_cells(field, n_wide, n_narrow):
    own, rows, cols = field.shape
    shaped = field.reshape(own, n_wide, rows // n_wide, n_narrow, cols // n_narrow)
    moved = jnp.transpose(shaped, (1, 3, 0, 2, 4))
    return moved.reshape(n_wide * n_narrow, own, rows // n_wide, cols // n_narrow)


BF = jnp.bfloat16
F32 = jnp.float32


def dot(a, b, over=((1,), (0,))):
    return lax.dot_general(a, b, (over, ((), ())), preferred_element_type=F32)


def column(row):
    return jnp.broadcast_to(row, (row.shape[1], row.shape[1])).T


def centred(x):
    centre = x - jnp.mean(x, 0, keepdims=True)
    rstd = lax.rsqrt(jnp.mean(centre * centre, 0, keepdims=True) + EPS)
    return centre * rstd, rstd


def back_t(scaled, hat, rstd):
    inner = hat * jnp.mean(scaled * hat, 0, keepdims=True)
    return rstd * (scaled - jnp.mean(scaled, 0, keepdims=True) - inner)


def two_rows(first, second, devices):
    own, cols = first.shape[0] // devices, first.shape[1]
    shape = (devices, own, cols)
    return jnp.concatenate([first.reshape(shape), second.reshape(shape)], 1).astype(BF)


def apart(block, devices):
    wide = block.astype(F32)
    own, cols = wide.shape[1] // 2, wide.shape[2]
    return [wide[:, at * own : (at + 1) * own].reshape(devices * own, cols) for at in range(2)]


def project_kernel(
    pair_hbm, mask_hbm, gain_hbm, w_hbm, sent_ref, zn_ref, mask_ref,
    pair_ref, mask_v, gain_ref, w_ref, sems,
):
    devices, depth, _ = sent_ref.shape
    rows, cols, width = pair_ref.shape
    start = lax.axis_index("wide") * rows
    copies = [
        pltpu.make_async_copy(gain_hbm, gain_ref, sems.at[0]),
        pltpu.make_async_copy(mask_hbm, mask_v, sems.at[1]),
    ]
    for at in range(4):
        place = pl.ds(at * (rows // 4), rows // 4)
        copies.append(
            pltpu.make_async_copy(pair_hbm.at[place], pair_ref.at[place], sems.at[2 + at])
        )
    for at in range(2):
        place = pl.ds(at * (width // 2), width // 2)
        copies.append(pltpu.make_async_copy(w_hbm.at[place], w_ref.at[place], sems.at[6 + at]))
    for copy in copies:
        copy.start()
    for copy in copies:
        copy.wait()
    mask_f = mask_v[...].astype(F32)
    shape = (rows, mask_f.shape[1])
    lane = lax.broadcasted_iota(jnp.int32, shape, 1)
    own = lane == start + lax.broadcasted_iota(jnp.int32, shape, 0)
    mask_ref[...] = mask_f * jnp.sum(jnp.where(own, mask_f, 0.0), 1, keepdims=True)
    gain = column(gain_ref[...])
    weights = w_ref[...].astype(F32).T.astype(BF)
    hidden = weights.shape[0] // 4
    half = depth // 2
    for two in range(rows // 2):
        pieces = []
        for row in (2 * two, 2 * two + 1):
            hat, _ = centred(pair_ref[row].astype(F32).T)
            zn = (hat * gain).astype(BF)
            zn_ref[:, row * cols : (row + 1) * cols] = zn
            proj = dot(weights, zn)
            mask = mask_ref[row : row + 1, :]
            left = mask * jax.nn.sigmoid(proj[hidden : 2 * hidden]) * proj[:hidden]
            right = mask * jax.nn.sigmoid(proj[3 * hidden :]) * proj[2 * hidden : 3 * hidden]
            pieces.append((left, right))
        at = two * 16
        sent_ref[:, at : at + 16, :] = two_rows(pieces[0][0], pieces[1][0], devices)
        sent_ref[:, half + at : half + at + 16, :] = two_rows(pieces[0][1], pieces[1][1], devices)


def gate_kernel(
    zn_ref, adj_ref, mask_ref, same_ref, w_ref, w_gate_ref, bias_ref, gain_ref, w_out_ref,
    gain_in_ref, pair_ref, factor_ref, gate_ref, t_ref, columns_ref, hat_ref, rstd_ref, slope_ref,
):
    rows, cols, width = adj_ref.shape
    weights = w_ref[...].astype(F32).T.astype(BF)
    hidden = weights.shape[0] // 4
    w_gate = w_gate_ref[...].astype(F32).T.astype(BF)
    across, within = column(bias_ref[0:1, :]), column(bias_ref[1:2, :])
    gain = column(gain_ref[...])
    columns_ref[...] = column(gain_in_ref[...])
    for row in range(rows):
        lanes = slice(row * cols, (row + 1) * cols)
        zn = zn_ref[:, lanes]
        proj = dot(weights, zn)
        mask = mask_ref[row : row + 1, :]
        for side in range(2):
            lin = proj[2 * side * hidden : (2 * side + 1) * hidden]
            sig = jax.nn.sigmoid(proj[(2 * side + 1) * hidden : (2 * side + 2) * hidden])
            factor_ref[2 * side * hidden : (2 * side + 1) * hidden, lanes] = (mask * sig).astype(BF)
            factor_ref[(2 * side + 1) * hidden : (2 * side + 2) * hidden, lanes] = (
                mask * lin * sig * (1.0 - sig)
            ).astype(BF)
        bias = jnp.where(same_ref[row : row + 1, :] > 0.5, within, across)
        gate = jax.nn.sigmoid(dot(w_gate, zn) + bias).T
        gate_ref[row] = gate
        scaled = adj_ref[row].astype(F32) * gate
        slope_ref[row] = scaled * (1.0 - gate)
        d_out = scaled.astype(BF)
        t = dot(w_out_ref[...], d_out, ((1,), (1,))) * gain
        t_ref[:, lanes] = (t - jnp.mean(t, 0, keepdims=True)).astype(BF)
        hat, rstd = centred(pair_ref[row].astype(F32).T)
        hat_ref[:, lanes] = hat
        rstd_ref[row : row + 1, :] = rstd


def mix_kernel(got_ref, sent_ref, left_ref, right_ref, left_s, right_s, out_s):
    devices, depth, cols = got_ref.shape
    own = left_ref.shape[0]
    half = depth // 2
    count = devices * half // own
    left_s[...] = got_ref[:, :half, :].astype(F32).reshape(devices * half, cols)
    right_s[...] = got_ref[:, half:, :].astype(F32).reshape(devices * half, cols)
    for h in range(own):
        left = left_s[pl.ds(h, count, stride=own), :].astype(BF)
        right = right_s[pl.ds(h, count, stride=own), :].astype(BF)
        left_ref[h] = left
        right_ref[h] = right
        out_s[pl.ds(h, count, stride=own), :] = dot(left, right, ((1,), (1,)))
    sent_ref[...] = out_s[...].reshape(devices, half, cols).astype(BF)


def norm_kernel(
    got_ref, t_ref, gain_ref, gate_ref, slope_ref, zn_ref, w_out_ref,
    sent_ref, output_ref, d_logit_ref, part_ref,
):
    devices, depth, cols = got_ref.shape
    gain = column(gain_ref[...])
    total = None
    for two in range(depth // 16):
        pieces = []
        for part, mixed in enumerate(apart(got_ref[:, two * 16 : two * 16 + 16, :], devices)):
            row = 2 * two + part
            lanes = slice(row * cols, (row + 1) * cols)
            hat, rstd = centred(mixed)
            pieces.append(back_t(t_ref[:, lanes].astype(F32), hat, rstd))
            proj_out = dot((hat * gain).T.astype(BF), w_out_ref[...])
            output_ref[row] = (gate_ref[row] * proj_out).astype(BF)
            d_logit = (slope_ref[row] * proj_out).astype(BF)
            d_logit_ref[row] = d_logit
            term = dot(zn_ref[:, lanes], d_logit)
            total = term if total is None else total + term
        sent_ref[:, two * 16 : two * 16 + 16, :] = two_rows(*pieces, devices)
    part_ref[...] = total


def unmix_kernel(got_ref, left_ref, right_ref, sent_ref, in_s, left_s, right_s):
    devices, half, cols = got_ref.shape
    own = left_ref.shape[0]
    count = devices * half // own
    in_s[...] = got_ref[...].astype(F32).reshape(devices * half, cols)
    for h in range(own):
        grad = in_s[pl.ds(h, count, stride=own), :]
        left_s[pl.ds(h, count, stride=own), :] = dot(grad.astype(BF), right_ref[h])
        right_s[pl.ds(h, count, stride=own), :] = dot(grad.T.astype(BF), left_ref[h])
    sent_ref[:, :half, :] = left_s[...].reshape(devices, half, cols).astype(BF)
    sent_ref[:, half:, :] = right_s[...].reshape(devices, half, cols).astype(BF)


def cells_kernel(
    got_ref, factor_ref, zn_ref, gate_part_ref, w_ref, columns_ref, u_ref, part_ref, cells_ref
):
    devices, depth, cols = got_ref.shape
    half = depth // 2
    hidden = factor_ref.shape[0] // 4
    for side in range(2):
        for two in range(half // 16):
            at = side * half + two * 16
            for part, grad in enumerate(apart(got_ref[:, at : at + 16, :], devices)):
                row = 2 * two + part
                lanes = slice(row * cols, (row + 1) * cols)
                for kind in (2 * side, 2 * side + 1):
                    place = slice(kind * hidden, (kind + 1) * hidden)
                    cells_ref[place, lanes] = (grad * factor_ref[place, lanes].astype(F32)).astype(BF)
    total = dot(zn_ref[...], cells_ref[...], ((1,), (1,)))
    part_ref[:, : 4 * hidden] = total.astype(BF)
    part_ref[:, 4 * hidden :] = gate_part_ref[...].astype(BF)
    u = dot(w_ref[...], cells_ref[...]) * columns_ref[:, :1]
    u_ref[...] = (u - jnp.mean(u, 0, keepdims=True)).astype(BF)


def sum_kernel(residues, got_ref, sent_ref):
    total = jnp.sum(got_ref[...].astype(F32), 0) / residues
    sent_ref[...] = jnp.broadcast_to(total.astype(BF)[None], sent_ref.shape)


def finish_kernel(
    got_ref, output_ref, u_ref, d_logit_ref, hat_ref, rstd_ref, columns_ref, w_gate_ref,
    output_out, d_pair_out, proj_out, gate_out,
    d_pair_ref, proj_ref, gate_ref, sems, row_sems,
):
    devices, chunk, depth = got_ref.shape
    rows, cols, width = d_logit_ref.shape
    wide = proj_ref.shape[1]
    copies = [pltpu.make_async_copy(output_ref, output_out, sems.at[0])]
    copies[0].start()
    total = got_ref[...].astype(F32).reshape(devices * chunk, depth)
    proj_ref[...] = total[:, :wide]
    gate_ref[...] = total[:, wide:]
    copies.append(pltpu.make_async_copy(proj_ref, proj_out, sems.at[1]))
    copies.append(pltpu.make_async_copy(gate_ref, gate_out, sems.at[2]))
    copies[1].start()
    copies[2].start()
    gain = columns_ref[...]
    half = rows // 2
    for row in range(rows):
        lanes = slice(row * cols, (row + 1) * cols)
        u = dot(w_gate_ref[...], d_logit_ref[row], ((1,), (1,))) * gain
        u = u + u_ref[:, lanes].astype(F32)
        d_pair_ref[row] = back_t(
            u, hat_ref[:, lanes], rstd_ref[row : row + 1, :]
        ).T.astype(BF)
        if row + 1 in (half, rows):
            place = pl.ds(row + 1 - half, half)
            at = row // half
            copies.append(
                pltpu.make_async_copy(d_pair_ref.at[place], d_pair_out.at[place], row_sems.at[at])
            )
            copies[-1].start()
    for copy in copies:
        copy.wait()


def call(kernel, outs, scratch=(), flops=0, name=None, space=pltpu.VMEM, mib=12, away=()):
    spec = pl.BlockSpec(memory_space=pltpu.VMEM)

    def run(*args):
        moved = sum(a.size * a.dtype.itemsize for a in (*args, *outs))
        return pl.pallas_call(
            kernel,
            out_shape=list(outs),
            in_specs=[pl.BlockSpec(memory_space=space)] * len(args),
            out_specs=[pl.BlockSpec(memory_space=pl.ANY) if i in away else spec for i in range(len(outs))],
            scratch_shapes=list(scratch),
            compiler_params=pltpu.CompilerParams(vmem_limit_bytes=mib * 1024 * 1024),
            cost_estimate=pl.CostEstimate(
                flops=flops, bytes_accessed=moved, transcendentals=0
            ),
            name=name,
        )(*args)

    return run


def small_blocks(pair, adjoint, mask, chain, gain_in, w_proj, w_gate, chain_bias, gain_out, w_out):
    rows, cols, width = pair.shape
    hidden = w_out.shape[0]
    devices = lax.axis_size("wide")
    own = hidden // devices
    residues = rows * devices
    cells = rows * cols
    half = rows * own
    shape = jax.ShapeDtypeStruct
    start = lax.axis_index("wide") * rows
    row_chain = lax.dynamic_slice_in_dim(chain, start, rows, 0)
    same = (row_chain[:, None] == chain[None, :]).astype(F32)
    gain_in, gain_out = gain_in[None], gain_out[None]
    sent, zn, cell_mask = call(
        project_kernel,
        [shape((devices, 2 * half, cols), BF), shape((width, cells), BF), shape((rows, cols), F32)],
        [
            pltpu.VMEM(pair.shape, BF),
            pltpu.VMEM((1, residues), jnp.int32),
            pltpu.VMEM(gain_in.shape, F32),
            pltpu.VMEM(w_proj.shape, BF),
            pltpu.SemaphoreType.DMA((8,)),
        ],
        name="project",
        space=pltpu.HBM,
        mib=56,
    )(pair, mask[None], gain_in, w_proj)
    got = swap(sent)
    factor, gate, t, columns, hat, rstd, slope = call(
        gate_kernel,
        [shape((4 * hidden, cells), BF), shape((rows, cols, width), F32), shape((hidden, cells), BF), shape((width, width), F32), shape((width, cells), F32), shape((rows, cols), F32), shape((rows, cols, width), F32)],
        flops=2 * 10**9,
        name="gate",
    )(zn, adjoint, cell_mask, same, w_proj, w_gate, chain_bias, gain_out, w_out, gain_in, pair)
    field = pltpu.VMEM((devices * half, cols), F32)
    channels = shape((own, residues, cols), BF)
    block = shape((devices, half, cols), BF)
    got, t = lax.optimization_barrier((got, t))
    sent, left, right = call(mix_kernel, [block, channels, channels], [field] * 3, name="mix")(got)
    got = swap(sent)
    sent, output, d_logit, gate_part = call(
        norm_kernel,
        [block, shape(pair.shape, BF), shape(pair.shape, BF), shape((width, width), F32)],
        name="norm",
    )(got, t, gain_out, gate, slope, zn, w_out)
    got = swap(sent)
    sent = call(
        unmix_kernel, [shape((devices, 2 * half, cols), BF)], [field] * 3, name="unmix"
    )(got, left, right)[0]
    got = swap(sent)
    u, part = call(
        cells_kernel,
        [shape((width, cells), BF), shape((width, 4 * hidden + width), BF)],
        [pltpu.VMEM((4 * hidden, cells), BF)],
        name="cells",
    )(got, factor, zn, gate_part, w_proj, columns)
    got = swap(part.reshape(devices, width // devices, -1))
    sent = call(
        functools.partial(sum_kernel, residues), [shape(got.shape, BF)], name="sum"
    )(got)[0]
    return tuple(
        call(
            finish_kernel,
            [
                shape(pair.shape, BF),
                shape(pair.shape, BF),
                shape((width, 4 * hidden), F32),
                shape((width, width), F32),
            ],
            [
                pltpu.VMEM(pair.shape, BF),
                pltpu.VMEM((width, 4 * hidden), F32),
                pltpu.VMEM((width, width), F32),
                pltpu.SemaphoreType.DMA((3,)),
                pltpu.SemaphoreType.DMA((2,)),
            ],
            name="finish",
            away=(0, 1, 2, 3),
        )(swap(sent), output, u, d_logit, hat, rstd, columns, w_gate)
    )


def per_device(pair, adjoint, mask, chain, gain_in, w_proj, w_gate, chain_bias, gain_out, w_out):
    rows, cols, width = pair.shape
    hidden = w_out.shape[0]
    n_wide = lax.axis_size("wide")
    n_narrow = lax.axis_size("narrow")
    if n_narrow == 1 and (rows, cols, width) == (8, 128, 128) and hidden == 8 * n_wide == 128:
        return small_blocks(
            pair, adjoint, mask, chain, gain_in, w_proj, w_gate, chain_bias, gain_out, w_out
        )
    residues = rows * n_wide
    devices = n_wide * n_narrow
    own = hidden // devices
    row_start = lax.axis_index("wide") * rows
    col_start = lax.axis_index("narrow") * cols
    mask_f = mask.astype(jnp.float32)
    row_mask = lax.dynamic_slice_in_dim(mask_f, row_start, rows, 0)
    col_mask = lax.dynamic_slice_in_dim(mask_f, col_start, cols, 0)
    cell_mask = (row_mask[:, None] * col_mask[None, :])[None]
    row_chain = lax.dynamic_slice_in_dim(chain, row_start, rows, 0)
    col_chain = lax.dynamic_slice_in_dim(chain, col_start, cols, 0)
    same = (row_chain[:, None] == col_chain[None, :])[:, :, None]
    zn_f, z_hat, z_rstd = normalize(pair.astype(jnp.float32), gain_in, -1)
    zn = zn_f.astype(jnp.bfloat16)
    proj_a = jnp.einsum(
        "ijc,ch->hij", zn, w_proj[:, : 2 * hidden], preferred_element_type=jnp.float32
    )
    proj_b = jnp.einsum(
        "ijc,ch->hij", zn, w_proj[:, 2 * hidden :], preferred_element_type=jnp.float32
    )
    a_lin = proj_a[:hidden]
    sig_a = jax.nn.sigmoid(proj_a[hidden:])
    b_lin = proj_b[:hidden]
    sig_b = jax.nn.sigmoid(proj_b[hidden:])
    left_t = (cell_mask * sig_a * a_lin).astype(jnp.bfloat16)
    right_t = (cell_mask * sig_b * b_lin).astype(jnp.bfloat16)
    pairs = jnp.concatenate(
        [left_t.reshape(devices, own, rows, cols), right_t.reshape(devices, own, rows, cols)], 1
    )
    pairs = gather_cells(swap(pairs), n_wide, n_narrow)
    left_c, right_c = pairs[:own], pairs[own:]
    mixed_c = jnp.einsum("hik,hjk->hij", left_c, right_c, preferred_element_type=jnp.float32)
    mixed_t = swap(split_cells(mixed_c.astype(jnp.bfloat16), n_wide, n_narrow))
    mixed_t = mixed_t.reshape(hidden, rows, cols).astype(jnp.float32)
    xn_f, x_hat, x_rstd = normalize(mixed_t, gain_out[:, None, None], 0)
    xn = xn_f.astype(jnp.bfloat16)
    proj_out = jnp.einsum("hij,hc->ijc", xn, w_out, preferred_element_type=jnp.float32)
    logits = jnp.dot(zn, w_gate, preferred_element_type=jnp.float32) + jnp.where(
        same, chain_bias[1], chain_bias[0]
    )
    gate = jax.nn.sigmoid(logits)
    output = (gate * proj_out).astype(jnp.bfloat16)
    adj = adjoint.astype(jnp.float32)
    d_out = (adj * gate).astype(jnp.bfloat16)
    d_logit = (adj * proj_out * gate * (1.0 - gate)).astype(jnp.bfloat16)
    d_xn = jnp.einsum("ijc,hc->hij", d_out, w_out, preferred_element_type=jnp.float32)
    d_mixed_t = norm_back(d_xn * gain_out[:, None, None], x_hat, x_rstd, 0).astype(jnp.bfloat16)
    d_mixed_c = gather_cells(swap(d_mixed_t.reshape(devices, own, rows, cols)), n_wide, n_narrow)
    d_left_c = jnp.einsum("hij,hjk->hik", d_mixed_c, right_c, preferred_element_type=jnp.float32)
    d_right_c = jnp.einsum("hij,hik->hjk", d_mixed_c, left_c, preferred_element_type=jnp.float32)
    back = jnp.concatenate([d_left_c.astype(jnp.bfloat16), d_right_c.astype(jnp.bfloat16)], 0)
    back = swap(split_cells(back, n_wide, n_narrow))
    d_left = back[:, :own].reshape(hidden, rows, cols).astype(jnp.float32)
    d_right = back[:, own:].reshape(hidden, rows, cols).astype(jnp.float32)
    d_cells_a = jnp.concatenate(
        [d_left * cell_mask * sig_a, d_left * cell_mask * a_lin * sig_a * (1.0 - sig_a)], 0
    ).astype(jnp.bfloat16)
    d_cells_b = jnp.concatenate(
        [d_right * cell_mask * sig_b, d_right * cell_mask * b_lin * sig_b * (1.0 - sig_b)], 0
    ).astype(jnp.bfloat16)
    d_zn = jnp.einsum(
        "hij,ch->ijc", d_cells_a, w_proj[:, : 2 * hidden], preferred_element_type=jnp.float32
    )
    d_zn = d_zn + jnp.einsum(
        "hij,ch->ijc", d_cells_b, w_proj[:, 2 * hidden :], preferred_element_type=jnp.float32
    )
    d_zn = d_zn + jnp.dot(d_logit, w_gate.T, preferred_element_type=jnp.float32)
    d_pair = norm_back(d_zn * gain_in, z_hat, z_rstd, -1).astype(jnp.bfloat16)
    proj_part = jnp.concatenate(
        [
            jnp.einsum("ijc,hij->ch", zn, d_cells_a, preferred_element_type=jnp.float32),
            jnp.einsum("ijc,hij->ch", zn, d_cells_b, preferred_element_type=jnp.float32),
        ],
        1,
    )
    flat_z = zn.reshape(-1, width)
    gate_part = jnp.dot(flat_z.T, d_logit.reshape(-1, width), preferred_element_type=jnp.float32)
    parts = jnp.concatenate([proj_part, gate_part], 1)
    chunk = width // devices
    mine = swap(parts.astype(jnp.bfloat16).reshape(devices, chunk, -1))
    mine = jnp.sum(mine.astype(jnp.float32), 0) / residues
    mine = mine.astype(jnp.bfloat16)
    total = swap(jnp.broadcast_to(mine, (devices,) + mine.shape)).reshape(width, -1)
    total = total.astype(jnp.float32)
    return (output, d_pair, total[:, : 4 * hidden], total[:, 4 * hidden :])


def solution(mesh):
    placed = (
        P(("groups", "wide"), "narrow", None),
        P(("groups", "wide"), "narrow", None),
        P("groups"),
        P("groups"),
        P(),
        P(),
        P(),
        P(),
        P(),
        P(),
    )
    return jax.shard_map(
        per_device,
        mesh=mesh,
        in_specs=placed,
        out_specs=(
            P(("groups", "wide"), "narrow", None),
            P(("groups", "wide"), "narrow", None),
            P("groups", None),
            P("groups", None),
        ),
        check_vma=False,
    )
```

```python
import functools

import jax
import jax.numpy as jnp
from jax import lax
from jax.experimental import pallas as pl
from jax.experimental.pallas import tpu as pltpu
from jax.sharding import PartitionSpec as P

EPS = 1e-05


def normalize(values, gain, axis):
    centre = values - jnp.mean(values, axis, keepdims=True)
    rstd = lax.rsqrt(jnp.mean(centre * centre, axis, keepdims=True) + EPS)
    hat = centre * rstd
    return (hat * gain, hat, rstd)


def norm_back(scaled, hat, rstd, axis):
    return rstd * (
        scaled
        - jnp.mean(scaled, axis, keepdims=True)
        - hat * jnp.mean(scaled * hat, axis, keepdims=True)
    )


def swap(blocks):
    return lax.all_to_all(blocks, ("wide", "narrow"), split_axis=0, concat_axis=0, tiled=True)


def gather_cells(blocks, n_wide, n_narrow):
    _, own, rows, cols = blocks.shape
    shaped = blocks.reshape(n_wide, n_narrow, own, rows, cols)
    return jnp.transpose(shaped, (2, 0, 3, 1, 4)).reshape(own, n_wide * rows, n_narrow * cols)


def split_cells(field, n_wide, n_narrow):
    own, rows, cols = field.shape
    shaped = field.reshape(own, n_wide, rows // n_wide, n_narrow, cols // n_narrow)
    moved = jnp.transpose(shaped, (1, 3, 0, 2, 4))
    return moved.reshape(n_wide * n_narrow, own, rows // n_wide, cols // n_narrow)


BF = jnp.bfloat16
F32 = jnp.float32


def dot(a, b, over=((1,), (0,))):
    return lax.dot_general(a, b, (over, ((), ())), preferred_element_type=F32)


def column(row):
    return jnp.broadcast_to(row, (row.shape[1], row.shape[1])).T


def centred(x):
    centre = x - jnp.mean(x, 0, keepdims=True)
    rstd = lax.rsqrt(jnp.mean(centre * centre, 0, keepdims=True) + EPS)
    return centre * rstd, rstd


def back_t(scaled, hat, rstd):
    inner = hat * jnp.mean(scaled * hat, 0, keepdims=True)
    return rstd * (scaled - jnp.mean(scaled, 0, keepdims=True) - inner)


def two_rows(first, second, devices):
    own, cols = first.shape[0] // devices, first.shape[1]
    shape = (devices, own, cols)
    return jnp.concatenate([first.reshape(shape), second.reshape(shape)], 1).astype(BF)


def apart(block, devices):
    wide = block.astype(F32)
    own, cols = wide.shape[1] // 2, wide.shape[2]
    return [wide[:, at * own : (at + 1) * own].reshape(devices * own, cols) for at in range(2)]


def project_kernel(
    pair_hbm, mask_hbm, gain_hbm, w_hbm, sent_ref, zn_ref, mask_ref,
    pair_ref, mask_v, gain_ref, w_ref, sems,
):
    devices, depth, _ = sent_ref.shape
    rows, cols, width = pair_ref.shape
    start = lax.axis_index("wide") * rows
    copies = [
        pltpu.make_async_copy(gain_hbm, gain_ref, sems.at[0]),
        pltpu.make_async_copy(mask_hbm, mask_v, sems.at[1]),
    ]
    for at in range(4):
        place = pl.ds(at * (rows // 4), rows // 4)
        copies.append(
            pltpu.make_async_copy(pair_hbm.at[place], pair_ref.at[place], sems.at[2 + at])
        )
    for at in range(2):
        place = pl.ds(at * (width // 2), width // 2)
        copies.append(pltpu.make_async_copy(w_hbm.at[place], w_ref.at[place], sems.at[6 + at]))
    for copy in copies:
        copy.start()
    for copy in copies:
        copy.wait()
    mask_f = mask_v[...].astype(F32)
    shape = (rows, mask_f.shape[1])
    lane = lax.broadcasted_iota(jnp.int32, shape, 1)
    own = lane == start + lax.broadcasted_iota(jnp.int32, shape, 0)
    mask_ref[...] = mask_f * jnp.sum(jnp.where(own, mask_f, 0.0), 1, keepdims=True)
    gain = column(gain_ref[...])
    weights = w_ref[...].astype(F32).T.astype(BF)
    hidden = weights.shape[0] // 4
    half = depth // 2
    for two in range(rows // 2):
        pieces = []
        for row in (2 * two, 2 * two + 1):
            hat, _ = centred(pair_ref[row].astype(F32).T)
            zn = (hat * gain).astype(BF)
            zn_ref[:, row * cols : (row + 1) * cols] = zn
            proj = dot(weights, zn)
            mask = mask_ref[row : row + 1, :]
            left = mask * jax.nn.sigmoid(proj[hidden : 2 * hidden]) * proj[:hidden]
            right = mask * jax.nn.sigmoid(proj[3 * hidden :]) * proj[2 * hidden : 3 * hidden]
            pieces.append((left, right))
        at = two * 16
        sent_ref[:, at : at + 16, :] = two_rows(pieces[0][0], pieces[1][0], devices)
        sent_ref[:, half + at : half + at + 16, :] = two_rows(pieces[0][1], pieces[1][1], devices)


def gate_kernel(
    zn_ref, adj_ref, mask_ref, same_ref, w_ref, w_gate_ref, bias_ref, gain_ref, w_out_ref,
    gain_in_ref, pair_ref, factor_ref, gate_ref, t_ref, columns_ref, hat_ref, rstd_ref, scale_ref,
):
    rows, cols, width = adj_ref.shape
    weights = w_ref[...].astype(F32).T.astype(BF)
    hidden = weights.shape[0] // 4
    w_gate = w_gate_ref[...].astype(F32).T.astype(BF)
    across, within = column(bias_ref[0:1, :]), column(bias_ref[1:2, :])
    gain = column(gain_ref[...])
    columns_ref[...] = column(gain_in_ref[...])
    scale_ref[...] = gain
    for row in range(rows):
        lanes = slice(row * cols, (row + 1) * cols)
        zn = zn_ref[:, lanes]
        proj = dot(weights, zn)
        mask = mask_ref[row : row + 1, :]
        for side in range(2):
            lin = proj[2 * side * hidden : (2 * side + 1) * hidden]
            sig = jax.nn.sigmoid(proj[(2 * side + 1) * hidden : (2 * side + 2) * hidden])
            factor_ref[2 * side * hidden : (2 * side + 1) * hidden, lanes] = (mask * sig).astype(BF)
            factor_ref[(2 * side + 1) * hidden : (2 * side + 2) * hidden, lanes] = (
                mask * lin * sig * (1.0 - sig)
            ).astype(BF)
        bias = jnp.where(same_ref[row : row + 1, :] > 0.5, within, across)
        gate = jax.nn.sigmoid(dot(w_gate, zn) + bias).T
        gate_ref[row] = gate
        d_out = (adj_ref[row].astype(F32) * gate).astype(BF)
        t = dot(w_out_ref[...], d_out, ((1,), (1,))) * gain
        t_ref[:, lanes] = (t - jnp.mean(t, 0, keepdims=True)).astype(BF)
        hat, rstd = centred(pair_ref[row].astype(F32).T)
        hat_ref[:, lanes] = hat
        rstd_ref[row : row + 1, :] = rstd


def mix_kernel(got_ref, sent_ref, left_ref, right_ref, left_s, right_s, out_s):
    devices, depth, cols = got_ref.shape
    own = left_ref.shape[0]
    half = depth // 2
    count = devices * half // own
    left_s[...] = got_ref[:, :half, :].astype(F32).reshape(devices * half, cols)
    right_s[...] = got_ref[:, half:, :].astype(F32).reshape(devices * half, cols)
    for h in range(own):
        left = left_s[pl.ds(h, count, stride=own), :].astype(BF)
        right = right_s[pl.ds(h, count, stride=own), :].astype(BF)
        left_ref[h] = left
        right_ref[h] = right
        out_s[pl.ds(h, count, stride=own), :] = dot(left, right, ((1,), (1,)))
    sent_ref[...] = out_s[...].reshape(devices, half, cols).astype(BF)


def norm_kernel(
    got_ref, t_ref, gain_ref, gate_ref, adj_ref, zn_ref, w_out_ref,
    sent_ref, output_ref, d_logit_ref, part_ref,
):
    devices, depth, cols = got_ref.shape
    gain = gain_ref[...]
    total = None
    for two in range(depth // 16):
        pieces = []
        for part, mixed in enumerate(apart(got_ref[:, two * 16 : two * 16 + 16, :], devices)):
            row = 2 * two + part
            lanes = slice(row * cols, (row + 1) * cols)
            hat, rstd = centred(mixed)
            pieces.append(back_t(t_ref[:, lanes].astype(F32), hat, rstd))
            proj_out = dot((hat * gain).T.astype(BF), w_out_ref[...])
            gate = gate_ref[row]
            output_ref[row] = (gate * proj_out).astype(BF)
            d_logit = (adj_ref[row].astype(F32) * proj_out * gate * (1.0 - gate)).astype(BF)
            d_logit_ref[row] = d_logit
            term = dot(zn_ref[:, lanes], d_logit)
            total = term if total is None else total + term
        sent_ref[:, two * 16 : two * 16 + 16, :] = two_rows(*pieces, devices)
    part_ref[...] = total


def unmix_kernel(got_ref, left_ref, right_ref, sent_ref, in_s, left_s, right_s):
    devices, half, cols = got_ref.shape
    own = left_ref.shape[0]
    count = devices * half // own
    in_s[...] = got_ref[...].astype(F32).reshape(devices * half, cols)
    for h in range(own):
        grad = in_s[pl.ds(h, count, stride=own), :]
        left_s[pl.ds(h, count, stride=own), :] = dot(grad.astype(BF), right_ref[h])
        right_s[pl.ds(h, count, stride=own), :] = dot(grad.T.astype(BF), left_ref[h])
    sent_ref[:, :half, :] = left_s[...].reshape(devices, half, cols).astype(BF)
    sent_ref[:, half:, :] = right_s[...].reshape(devices, half, cols).astype(BF)


def cells_kernel(
    got_ref, factor_ref, zn_ref, gate_part_ref, w_ref, columns_ref, u_ref, part_ref, cells_ref
):
    devices, depth, cols = got_ref.shape
    half = depth // 2
    hidden = factor_ref.shape[0] // 4
    for side in range(2):
        for two in range(half // 16):
            at = side * half + two * 16
            for part, grad in enumerate(apart(got_ref[:, at : at + 16, :], devices)):
                row = 2 * two + part
                lanes = slice(row * cols, (row + 1) * cols)
                for kind in (2 * side, 2 * side + 1):
                    place = slice(kind * hidden, (kind + 1) * hidden)
                    cells_ref[place, lanes] = (grad * factor_ref[place, lanes].astype(F32)).astype(BF)
    total = dot(zn_ref[...], cells_ref[...], ((1,), (1,)))
    part_ref[:, : 4 * hidden] = total.astype(BF)
    part_ref[:, 4 * hidden :] = gate_part_ref[...].astype(BF)
    u = dot(w_ref[...], cells_ref[...]) * columns_ref[:, :1]
    u_ref[...] = (u - jnp.mean(u, 0, keepdims=True)).astype(BF)


def sum_kernel(residues, got_ref, sent_ref):
    total = jnp.sum(got_ref[...].astype(F32), 0) / residues
    sent_ref[...] = jnp.broadcast_to(total.astype(BF)[None], sent_ref.shape)


def finish_kernel(
    got_ref, output_ref, u_ref, d_logit_ref, hat_ref, rstd_ref, columns_ref, w_gate_ref,
    output_out, d_pair_out, proj_out, gate_out,
    d_pair_ref, proj_ref, gate_ref, sems, row_sems,
):
    devices, chunk, depth = got_ref.shape
    rows, cols, width = d_logit_ref.shape
    wide = proj_ref.shape[1]
    copies = [pltpu.make_async_copy(output_ref, output_out, sems.at[0])]
    copies[0].start()
    total = got_ref[...].astype(F32).reshape(devices * chunk, depth)
    proj_ref[...] = total[:, :wide]
    gate_ref[...] = total[:, wide:]
    copies.append(pltpu.make_async_copy(proj_ref, proj_out, sems.at[1]))
    copies.append(pltpu.make_async_copy(gate_ref, gate_out, sems.at[2]))
    copies[1].start()
    copies[2].start()
    gain = columns_ref[...]
    half = rows // 2
    for row in range(rows):
        lanes = slice(row * cols, (row + 1) * cols)
        u = dot(w_gate_ref[...], d_logit_ref[row], ((1,), (1,))) * gain
        u = u + u_ref[:, lanes].astype(F32)
        d_pair_ref[row] = back_t(
            u, hat_ref[:, lanes], rstd_ref[row : row + 1, :]
        ).T.astype(BF)
        if row + 1 in (half, rows):
            place = pl.ds(row + 1 - half, half)
            at = row // half
            copies.append(
                pltpu.make_async_copy(d_pair_ref.at[place], d_pair_out.at[place], row_sems.at[at])
            )
            copies[-1].start()
    for copy in copies:
        copy.wait()


def call(kernel, outs, scratch=(), flops=0, name=None, space=pltpu.VMEM, mib=12, away=()):
    spec = pl.BlockSpec(memory_space=pltpu.VMEM)

    def run(*args):
        moved = sum(a.size * a.dtype.itemsize for a in (*args, *outs))
        return pl.pallas_call(
            kernel,
            out_shape=list(outs),
            in_specs=[pl.BlockSpec(memory_space=space)] * len(args),
            out_specs=[pl.BlockSpec(memory_space=pl.ANY) if i in away else spec for i in range(len(outs))],
            scratch_shapes=list(scratch),
            compiler_params=pltpu.CompilerParams(vmem_limit_bytes=mib * 1024 * 1024),
            cost_estimate=pl.CostEstimate(
                flops=flops, bytes_accessed=moved, transcendentals=0
            ),
            name=name,
        )(*args)

    return run


def small_blocks(pair, adjoint, mask, chain, gain_in, w_proj, w_gate, chain_bias, gain_out, w_out):
    rows, cols, width = pair.shape
    hidden = w_out.shape[0]
    devices = lax.axis_size("wide")
    own = hidden // devices
    residues = rows * devices
    cells = rows * cols
    half = rows * own
    shape = jax.ShapeDtypeStruct
    start = lax.axis_index("wide") * rows
    row_chain = lax.dynamic_slice_in_dim(chain, start, rows, 0)
    same = (row_chain[:, None] == chain[None, :]).astype(F32)
    gain_in, gain_out = gain_in[None], gain_out[None]
    sent, zn, cell_mask = call(
        project_kernel,
        [shape((devices, 2 * half, cols), BF), shape((width, cells), BF), shape((rows, cols), F32)],
        [
            pltpu.VMEM(pair.shape, BF),
            pltpu.VMEM((1, residues), jnp.int32),
            pltpu.VMEM(gain_in.shape, F32),
            pltpu.VMEM(w_proj.shape, BF),
            pltpu.SemaphoreType.DMA((8,)),
        ],
        name="project",
        space=pltpu.HBM,
        mib=56,
    )(pair, mask[None], gain_in, w_proj)
    got = swap(sent)
    factor, gate, t, columns, hat, rstd, scale = call(
        gate_kernel,
        [shape((4 * hidden, cells), BF), shape((rows, cols, width), F32), shape((hidden, cells), BF), shape((width, width), F32), shape((width, cells), F32), shape((rows, cols), F32), shape((width, width), F32)],
        flops=2 * 10**9,
        name="gate",
    )(zn, adjoint, cell_mask, same, w_proj, w_gate, chain_bias, gain_out, w_out, gain_in, pair)
    field = pltpu.VMEM((devices * half, cols), F32)
    channels = shape((own, residues, cols), BF)
    block = shape((devices, half, cols), BF)
    got, t = lax.optimization_barrier((got, t))
    sent, left, right = call(mix_kernel, [block, channels, channels], [field] * 3, name="mix")(got)
    got = swap(sent)
    sent, output, d_logit, gate_part = call(
        norm_kernel,
        [block, shape(pair.shape, BF), shape(pair.shape, BF), shape((width, width), F32)],
        name="norm",
    )(got, t, scale, gate, adjoint, zn, w_out)
    got = swap(sent)
    sent = call(
        unmix_kernel, [shape((devices, 2 * half, cols), BF)], [field] * 3, name="unmix"
    )(got, left, right)[0]
    got = swap(sent)
    u, part = call(
        cells_kernel,
        [shape((width, cells), BF), shape((width, 4 * hidden + width), BF)],
        [pltpu.VMEM((4 * hidden, cells), BF)],
        name="cells",
    )(got, factor, zn, gate_part, w_proj, columns)
    got = swap(part.reshape(devices, width // devices, -1))
    sent = call(
        functools.partial(sum_kernel, residues), [shape(got.shape, BF)], name="sum"
    )(got)[0]
    return tuple(
        call(
            finish_kernel,
            [
                shape(pair.shape, BF),
                shape(pair.shape, BF),
                shape((width, 4 * hidden), F32),
                shape((width, width), F32),
            ],
            [
                pltpu.VMEM(pair.shape, BF),
                pltpu.VMEM((width, 4 * hidden), F32),
                pltpu.VMEM((width, width), F32),
                pltpu.SemaphoreType.DMA((3,)),
                pltpu.SemaphoreType.DMA((2,)),
            ],
            name="finish",
            away=(0, 1, 2, 3),
        )(swap(sent), output, u, d_logit, hat, rstd, columns, w_gate)
    )


def per_device(pair, adjoint, mask, chain, gain_in, w_proj, w_gate, chain_bias, gain_out, w_out):
    rows, cols, width = pair.shape
    hidden = w_out.shape[0]
    n_wide = lax.axis_size("wide")
    n_narrow = lax.axis_size("narrow")
    if n_narrow == 1 and (rows, cols, width) == (8, 128, 128) and hidden == 8 * n_wide == 128:
        return small_blocks(
            pair, adjoint, mask, chain, gain_in, w_proj, w_gate, chain_bias, gain_out, w_out
        )
    residues = rows * n_wide
    devices = n_wide * n_narrow
    own = hidden // devices
    row_start = lax.axis_index("wide") * rows
    col_start = lax.axis_index("narrow") * cols
    mask_f = mask.astype(jnp.float32)
    row_mask = lax.dynamic_slice_in_dim(mask_f, row_start, rows, 0)
    col_mask = lax.dynamic_slice_in_dim(mask_f, col_start, cols, 0)
    cell_mask = (row_mask[:, None] * col_mask[None, :])[None]
    row_chain = lax.dynamic_slice_in_dim(chain, row_start, rows, 0)
    col_chain = lax.dynamic_slice_in_dim(chain, col_start, cols, 0)
    same = (row_chain[:, None] == col_chain[None, :])[:, :, None]
    zn_f, z_hat, z_rstd = normalize(pair.astype(jnp.float32), gain_in, -1)
    zn = zn_f.astype(jnp.bfloat16)
    proj_a = jnp.einsum(
        "ijc,ch->hij", zn, w_proj[:, : 2 * hidden], preferred_element_type=jnp.float32
    )
    proj_b = jnp.einsum(
        "ijc,ch->hij", zn, w_proj[:, 2 * hidden :], preferred_element_type=jnp.float32
    )
    a_lin = proj_a[:hidden]
    sig_a = jax.nn.sigmoid(proj_a[hidden:])
    b_lin = proj_b[:hidden]
    sig_b = jax.nn.sigmoid(proj_b[hidden:])
    left_t = (cell_mask * sig_a * a_lin).astype(jnp.bfloat16)
    right_t = (cell_mask * sig_b * b_lin).astype(jnp.bfloat16)
    pairs = jnp.concatenate(
        [left_t.reshape(devices, own, rows, cols), right_t.reshape(devices, own, rows, cols)], 1
    )
    pairs = gather_cells(swap(pairs), n_wide, n_narrow)
    left_c, right_c = pairs[:own], pairs[own:]
    mixed_c = jnp.einsum("hik,hjk->hij", left_c, right_c, preferred_element_type=jnp.float32)
    mixed_t = swap(split_cells(mixed_c.astype(jnp.bfloat16), n_wide, n_narrow))
    mixed_t = mixed_t.reshape(hidden, rows, cols).astype(jnp.float32)
    xn_f, x_hat, x_rstd = normalize(mixed_t, gain_out[:, None, None], 0)
    xn = xn_f.astype(jnp.bfloat16)
    proj_out = jnp.einsum("hij,hc->ijc", xn, w_out, preferred_element_type=jnp.float32)
    logits = jnp.dot(zn, w_gate, preferred_element_type=jnp.float32) + jnp.where(
        same, chain_bias[1], chain_bias[0]
    )
    gate = jax.nn.sigmoid(logits)
    output = (gate * proj_out).astype(jnp.bfloat16)
    adj = adjoint.astype(jnp.float32)
    d_out = (adj * gate).astype(jnp.bfloat16)
    d_logit = (adj * proj_out * gate * (1.0 - gate)).astype(jnp.bfloat16)
    d_xn = jnp.einsum("ijc,hc->hij", d_out, w_out, preferred_element_type=jnp.float32)
    d_mixed_t = norm_back(d_xn * gain_out[:, None, None], x_hat, x_rstd, 0).astype(jnp.bfloat16)
    d_mixed_c = gather_cells(swap(d_mixed_t.reshape(devices, own, rows, cols)), n_wide, n_narrow)
    d_left_c = jnp.einsum("hij,hjk->hik", d_mixed_c, right_c, preferred_element_type=jnp.float32)
    d_right_c = jnp.einsum("hij,hik->hjk", d_mixed_c, left_c, preferred_element_type=jnp.float32)
    back = jnp.concatenate([d_left_c.astype(jnp.bfloat16), d_right_c.astype(jnp.bfloat16)], 0)
    back = swap(split_cells(back, n_wide, n_narrow))
    d_left = back[:, :own].reshape(hidden, rows, cols).astype(jnp.float32)
    d_right = back[:, own:].reshape(hidden, rows, cols).astype(jnp.float32)
    d_cells_a = jnp.concatenate(
        [d_left * cell_mask * sig_a, d_left * cell_mask * a_lin * sig_a * (1.0 - sig_a)], 0
    ).astype(jnp.bfloat16)
    d_cells_b = jnp.concatenate(
        [d_right * cell_mask * sig_b, d_right * cell_mask * b_lin * sig_b * (1.0 - sig_b)], 0
    ).astype(jnp.bfloat16)
    d_zn = jnp.einsum(
        "hij,ch->ijc", d_cells_a, w_proj[:, : 2 * hidden], preferred_element_type=jnp.float32
    )
    d_zn = d_zn + jnp.einsum(
        "hij,ch->ijc", d_cells_b, w_proj[:, 2 * hidden :], preferred_element_type=jnp.float32
    )
    d_zn = d_zn + jnp.dot(d_logit, w_gate.T, preferred_element_type=jnp.float32)
    d_pair = norm_back(d_zn * gain_in, z_hat, z_rstd, -1).astype(jnp.bfloat16)
    proj_part = jnp.concatenate(
        [
            jnp.einsum("ijc,hij->ch", zn, d_cells_a, preferred_element_type=jnp.float32),
            jnp.einsum("ijc,hij->ch", zn, d_cells_b, preferred_element_type=jnp.float32),
        ],
        1,
    )
    flat_z = zn.reshape(-1, width)
    gate_part = jnp.dot(flat_z.T, d_logit.reshape(-1, width), preferred_element_type=jnp.float32)
    parts = jnp.concatenate([proj_part, gate_part], 1)
    chunk = width // devices
    mine = swap(parts.astype(jnp.bfloat16).reshape(devices, chunk, -1))
    mine = jnp.sum(mine.astype(jnp.float32), 0) / residues
    mine = mine.astype(jnp.bfloat16)
    total = swap(jnp.broadcast_to(mine, (devices,) + mine.shape)).reshape(width, -1)
    total = total.astype(jnp.float32)
    return (output, d_pair, total[:, : 4 * hidden], total[:, 4 * hidden :])


def solution(mesh):
    placed = (
        P(("groups", "wide"), "narrow", None),
        P(("groups", "wide"), "narrow", None),
        P("groups"),
        P("groups"),
        P(),
        P(),
        P(),
        P(),
        P(),
        P(),
    )
    return jax.shard_map(
        per_device,
        mesh=mesh,
        in_specs=placed,
        out_specs=(
            P(("groups", "wide"), "narrow", None),
            P(("groups", "wide"), "narrow", None),
            P("groups", None),
            P("groups", None),
        ),
        check_vma=False,
    )
```
